32 devices in a mesh: work: 8 (over y, x, core), blk: 4 (over z).
Axes of the slice: x: 2, y: 2, z: 4, core: 2. Of those that a mesh axis runs over, the one named last changes fastest.
Arguments:
- tokens: int32 [8, 3, 1024], P('work'), may hold values from 0 to 31999
- targets: int32 [8, 3, 1024], P('work'), may hold values from 0 to 31999
- seq_counts: int32 [8], P('work'), may hold values from 1 to 3, as said below
- embed_w: float32 [32000, 288], P('blk', 'work'), may hold values from -0.5 to 0.5
- qkv_w: float32 [288, 864], P('blk', 'work'), may hold values from -0.375 to 0.375
- out_w: float32 [288, 288], P('blk', 'work'), may hold values from -1.5 to 1.5
- mlp_w: float32 [2, 288, 768], P(None, 'blk', 'work'), may hold values from -0.375 to 0.375
- gain_w: float32 [3, 288], P(None, 'blk'), may hold values from 0.28 to 2.8
- embed_mom: float32 [32000, 288], P('blk', 'work'), may hold values from -0.09375 to 0.09375
- qkv_mom: float32 [288, 864], P('blk', 'work'), may hold values from -0.09375 to 0.09375
- out_mom: float32 [288, 288], P('blk', 'work'), may hold values from -0.09375 to 0.09375
- mlp_mom: float32 [2, 288, 768], P(None, 'blk', 'work'), may hold values from -0.09375 to 0.09375
- gain_mom: float32 [3, 288], P(None, 'blk'), may hold values from -0.875 to 0.875
- embed_first: float32 [8, 32000, 288], P('work', 'blk'), may hold values from -1.1444092e-05 to 1.1444092e-05
- qkv_first: float32 [8, 288, 864], P('work', 'blk'), may hold values from -1.1444092e-05 to 1.1444092e-05
- out_first: float32 [8, 288, 288], P('work', 'blk'), may hold values from -1.1444092e-05 to 1.1444092e-05
- mlp_first: float32 [8, 2, 288, 768], P('work', None, 'blk'), may hold values from -1.1444092e-05 to 1.1444092e-05
- gain_first: float32 [8, 3, 288], P('work', None, 'blk'), may hold values from -5.340576e-05 to 5.340576e-05
- embed_second: float32 [8, 32000, 288], P('work', 'blk'), may hold values from 1.321188e-11 to 5.264734e-11
- qkv_second: float32 [8, 288, 864], P('work', 'blk'), may hold values from 1.321188e-11 to 5.264734e-11
- out_second: float32 [8, 288, 288], P('work', 'blk'), may hold values from 1.321188e-11 to 5.264734e-11
- mlp_second: float32 [8, 2, 288, 768], P('work', None, 'blk'), may hold values from 1.321188e-11 to 5.264734e-11
- gain_second: float32 [8, 3, 288], P('work', None, 'blk'), may hold values from 3.30297e-10 to 1.321188e-09
Outputs:
- loss_stats: float32 [8, 2], P('work')
- grad_norm: float32 [8], P('work')
- embed_new: float32 [32000, 288], P('blk', 'work')
- qkv_new: float32 [288, 864], P('blk', 'work')
- out_new: float32 [288, 288], P('blk', 'work')
- mlp_new: float32 [2, 288, 768], P(None, 'blk', 'work')
- gain_new: float32 [3, 288], P(None, 'blk')
- embed_mom_new: float32 [32000, 288], P('blk', 'work')
- qkv_mom_new: float32 [288, 864], P('blk', 'work')
- out_mom_new: float32 [288, 288], P('blk', 'work')
- mlp_mom_new: float32 [2, 288, 768], P(None, 'blk', 'work')
- gain_mom_new: float32 [3, 288], P(None, 'blk')
- embed_first_new: float32 [8, 32000, 288], P('work', 'blk')
- qkv_first_new: float32 [8, 288, 864], P('work', 'blk')
- out_first_new: float32 [8, 288, 288], P('work', 'blk')
- mlp_first_new: float32 [8, 2, 288, 768], P('work', None, 'blk')
- gain_first_new: float32 [8, 3, 288], P('work', None, 'blk')
- embed_second_new: float32 [8, 32000, 288], P('work', 'blk')
- qkv_second_new: float32 [8, 288, 864], P('work', 'blk')
- out_second_new: float32 [8, 288, 288], P('work', 'blk')
- mlp_second_new: float32 [8, 2, 288, 768], P('work', None, 'blk')
- gain_second_new: float32 [8, 3, 288], P('work', None, 'blk')
The draws below stay inside these ranges and needn't reach their ends.
Inputs may be any that keep to these rules, and one draw needn't show every extreme that they name: The first seq_counts slots of a worker are real sequences; the first worker holds 1 and the last worker 3.
All inputs are finite; a program needn't handle non-finite values.
Results may differ from the reference program's by a relative error of at most 0.01.
The reference program's roundings to bfloat16 on the way count: a program that leaves them out, or rounds other values in their place, can miss the bound.
Values may be sent and summed in bfloat16 or wider, within the bound.
No kernel may reach another device: no remote copies, remote signals or barrier semaphores. Data moves between devices by JAX's collectives and lax.ppermute only.
A program may use at most 448 MiB of HBM per device.

```python
import math
import jax
import jax.numpy as jnp
import numpy as np
from jax import lax

D = 288
H = 6
HD = 48
FF = 768
V = 32000
SLOTS = 3
STEP = 7
NWORK = 8
SEQ = 1024
PARAMS = 9991008


def draw_seq_counts(key, part):
    key = jax.random.fold_in(key, 11)
    worker_rank = jnp.arange(NWORK)
    base_count = 1 + worker_rank * SLOTS // NWORK
    jitter = jax.random.randint(key, (NWORK,), -1, 2)
    counts = jnp.clip(base_count + jitter, 1, SLOTS)
    counts = counts.at[0].set(1).at[NWORK - 1].set(SLOTS)
    return counts.astype(jnp.int32)


def draw_gain_w(key, part):
    key = jax.random.fold_in(key, 23)
    ramp_line = jnp.arange(D).astype(jnp.float32) / (D - 1)
    low_end = 0.6
    high_end = 1.8
    factor = jax.random.uniform(key, (3, D), jnp.float32, 0.8, 1.25)
    curve = jnp.exp(jnp.log(low_end) + (jnp.log(high_end) - jnp.log(low_end)) * ramp_line)
    return curve[None, :] * factor


def with_ends(entries, rng, least, top_value):
    extent = entries.shape
    place = [jax.random.randint(jax.random.fold_in(rng, axis), (), 0, extent[axis]) for axis in range(len(extent))]
    entries = entries.at[tuple(place)].set(least)
    longest = extent.index(max(extent))
    place[longest] = (place[longest] + 1) % extent[longest]
    return entries.at[tuple(place)].set(top_value)


def level_of(rng, extent, pieces, smallest, top_value):
    def one(position, shards_of):
        steps = jax.random.uniform(jax.random.fold_in(jax.random.fold_in(rng, 6), position), (shards_of,), jnp.float32, smallest / len(pieces), top_value / len(pieces))
        return jnp.repeat(jnp.exp(steps), extent[position] // shards_of).reshape((-1,) + (1,) * (len(extent) - position - 1))

    level = one(*pieces[0])
    for cut in pieces[1:]:
        level = level * one(*cut)
    return level


def rank_bounds(number_of, slope):
    portions = [(1 << 20) // math.isqrt(grade ** slope) + 1 for grade in range(1, number_of + 1)]
    width = 1 + sum(portions) // (1 << 30)
    return np.cumsum(np.array([max(1, weight // width) for weight in portions]))


def skewed_ids(own_key, extent, number_of, skew):
    listing = rank_bounds(number_of, skew)
    ticket = jax.random.randint(jax.random.fold_in(own_key, 1), extent, 0, int(listing[number_of - 1]))
    grade = jnp.searchsorted(jnp.asarray(listing, jnp.int32), ticket, side="right")
    return jax.random.permutation(jax.random.fold_in(own_key, 2), number_of)[grade].astype(jnp.int32)


def scatter_about(stream_key, dims, deviation, limit, shards=(), kind=jnp.bfloat16):
    drawn = deviation * jax.random.normal(stream_key, dims, jnp.float32)
    if shards:
        drawn = drawn * level_of(stream_key, dims, shards, -0.22, 0.18)
    return jnp.clip(drawn, -limit, limit).astype(kind)


def setup_inputs(seed: int = 0) -> dict:
    streams_of = jax.random.split(jax.random.key(seed), 24)
    tokens = with_ends(skewed_ids(streams_of[0], (NWORK, SLOTS, SEQ), V, 2), jax.random.fold_in(streams_of[0], 3), 0, V - 1).astype(jnp.int32)
    targets = with_ends(skewed_ids(streams_of[1], (NWORK, SLOTS, SEQ), V, 2), jax.random.fold_in(streams_of[1], 3), 0, V - 1).astype(jnp.int32)
    seq_counts = draw_seq_counts(jax.random.fold_in(streams_of[23], 71), 0)
    embed_w = scatter_about(streams_of[3], (V, D), 0.09, 0.5, ((0, 4), (1, 8)), jnp.float32)
    qkv_w = scatter_about(streams_of[4], (D, 3 * D), D ** -0.5, 0.375, ((0, 4), (1, 8)), jnp.float32)
    out_w = scatter_about(streams_of[5], (D, D), (D // 16) ** -0.5, 1.5, ((0, 4), (1, 8)), jnp.float32)
    mlp_w = scatter_about(streams_of[6], (2, D, FF), D ** -0.5, 0.375, ((1, 4), (2, 8)), jnp.float32)
    gain_w = draw_gain_w(jax.random.fold_in(streams_of[23], 71), 0)
    embed_mom = scatter_about(streams_of[8], (V, D), 0.015, 0.09375, ((0, 4), (1, 8)), jnp.float32)
    qkv_mom = scatter_about(streams_of[9], (D, 3 * D), 0.015, 0.09375, ((0, 4), (1, 8)), jnp.float32)
    out_mom = scatter_about(streams_of[10], (D, D), 0.015, 0.09375, ((0, 4), (1, 8)), jnp.float32)
    mlp_mom = scatter_about(streams_of[11], (2, D, FF), 0.015, 0.09375, ((1, 4), (2, 8)), jnp.float32)
    gain_mom = scatter_about(streams_of[12], (3, D), 0.15, 0.875, ((1, 4),), jnp.float32)
    embed_first = scatter_about(streams_of[13], (NWORK, V, D), (0.0056 / PARAMS ** 0.5), 1.1444091796875e-05, ((0, 8), (1, 4)), jnp.float32)
    qkv_first = scatter_about(streams_of[14], (NWORK, D, 3 * D), (0.0056 / PARAMS ** 0.5), 1.1444091796875e-05, ((0, 8), (1, 4)), jnp.float32)
    out_first = scatter_about(streams_of[15], (NWORK, D, D), (0.0056 / PARAMS ** 0.5), 1.1444091796875e-05, ((0, 8), (1, 4)), jnp.float32)
    mlp_first = scatter_about(streams_of[16], (NWORK, 2, D, FF), (0.0056 / PARAMS ** 0.5), 1.1444091796875e-05, ((0, 8), (2, 4)), jnp.float32)
    gain_first = scatter_about(streams_of[17], (NWORK, 3, D), (0.028 / PARAMS ** 0.5), 5.340576171875e-05, ((0, 8), (2, 4)), jnp.float32)
    embed_second = jnp.clip(jnp.exp(math.log(5.264734134757809e-11) - 1.3824993 * jax.random.uniform(streams_of[18], (NWORK, V, D), jnp.float32) ** level_of(streams_of[18], (NWORK, V, D), ((0, 8), (1, 4)), -0.2, 0.2)), 1.3211880374452978e-11, 5.264734134757809e-11)
    qkv_second = jnp.clip(jnp.exp(math.log(5.264734134757809e-11) - 1.3824993 * jax.random.uniform(streams_of[19], (NWORK, D, 3 * D), jnp.float32) ** level_of(streams_of[19], (NWORK, D, 3 * D), ((0, 8), (1, 4)), -0.2, 0.2)), 1.3211880374452978e-11, 5.264734134757809e-11)
    out_second = jnp.clip(jnp.exp(math.log(5.264734134757809e-11) - 1.3824993 * jax.random.uniform(streams_of[20], (NWORK, D, D), jnp.float32) ** level_of(streams_of[20], (NWORK, D, D), ((0, 8), (1, 4)), -0.2, 0.2)), 1.3211880374452978e-11, 5.264734134757809e-11)
    mlp_second = jnp.clip(jnp.exp(math.log(5.264734134757809e-11) - 1.3824993 * jax.random.uniform(streams_of[21], (NWORK, 2, D, FF), jnp.float32) ** level_of(streams_of[21], (NWORK, 2, D, FF), ((0, 8), (2, 4)), -0.2, 0.2)), 1.3211880374452978e-11, 5.264734134757809e-11)
    gain_second = jnp.clip(jnp.exp(math.log(1.3211880478536386e-09) - 1.3862944 * jax.random.uniform(streams_of[22], (NWORK, 3, D), jnp.float32) ** level_of(streams_of[22], (NWORK, 3, D), ((0, 8), (2, 4)), -0.2, 0.2)), 3.3029701196340966e-10, 1.3211880478536386e-09)
    return {"tokens": tokens, "targets": targets, "seq_counts": seq_counts, "embed_w": embed_w, "qkv_w": qkv_w, "out_w": out_w, "mlp_w": mlp_w, "gain_w": gain_w, "embed_mom": embed_mom, "qkv_mom": qkv_mom, "out_mom": out_mom, "mlp_mom": mlp_mom, "gain_mom": gain_mom, "embed_first": embed_first, "qkv_first": qkv_first, "out_first": out_first, "mlp_first": mlp_first, "gain_first": gain_first, "embed_second": embed_second, "qkv_second": qkv_second, "out_second": out_second, "mlp_second": mlp_second, "gain_second": gain_second}


norm_eps = 1e-06
zloss_coef = 0.01
clip_limit = 0.05
beta_one = 0.9
beta_two = 0.95
adam_eps = 1e-08
decay_rate = 0.1
matrix_rate = 0.03
gain_rate = 0.3
outer_rate = 0.7
outer_mom = 0.9
rope_base = 10000.0
highest = lax.Precision.HIGHEST

@jax.custom_vjp
def low(v):
    return lax.optimization_barrier(v.astype(jnp.bfloat16)).astype(jnp.float32)

@jax.custom_vjp
def low_back(v):
    return v

def low_keep(v):
    return (low(v), None)

def low_pass(kept, grad):
    return (grad,)

def back_keep(v):
    return (v, None)

def back_low(kept, grad):
    return (low(grad),)
low.defvjp(low_keep, low_pass)
low_back.defvjp(back_keep, back_low)

def rms_norm(stream, gain_row):
    return stream * lax.rsqrt(lax.optimization_barrier(jnp.mean(stream * stream, -1, keepdims=True)) + norm_eps) * gain_row

def rope(stream, positions):
    half_dim = HD // 2
    frequency = rope_base ** (-jnp.arange(half_dim).astype(jnp.float32) * 2.0 / HD)
    angles = positions.astype(jnp.float32)[:, None] * frequency[None, :]
    cosine = jnp.cos(angles)[:, None, :]
    sine_table = jnp.sin(angles)[:, None, :]
    first_half = stream[..., :half_dim]
    second_half = stream[..., half_dim:]
    return jnp.concatenate([first_half * cosine - second_half * sine_table, first_half * sine_table + second_half * cosine], -1)

def seq_terms(weights, tok_ids, tgt_ids, slot_valid):
    embed_tab, qkv_mat, out_mat, mlp_mat, gain_tab = weights
    embedded = embed_tab[tok_ids] * math.sqrt(D)
    first_normalized = low(rms_norm(embedded, gain_tab[0]))
    query_key_value_output = low_back(jnp.dot(first_normalized, qkv_mat, precision=highest))
    positions = jnp.arange(SEQ)
    queries = low(rope(query_key_value_output[:, :D].reshape(SEQ, H, HD), positions))
    key_rows = low(rope(query_key_value_output[:, D:2 * D].reshape(SEQ, H, HD), positions))
    values = low(query_key_value_output[:, 2 * D:].reshape(SEQ, H, HD))
    scores = low_back(jnp.einsum('qhd,khd->hqk', queries, key_rows, precision=highest) * (1.0 / math.sqrt(HD)))
    allowed = positions[None, :] <= positions[:, None]
    scores = jnp.where(allowed[None], scores, -1e+30)
    attn_probs = jnp.exp(scores - lax.optimization_barrier(jnp.max(scores, -1, keepdims=True)))
    attn_probs = attn_probs / lax.optimization_barrier(jnp.sum(attn_probs, -1, keepdims=True))
    attn_mix = jnp.einsum('hqk,khd->qhd', low(attn_probs), values, precision=highest).reshape(SEQ, D)
    attn_mix = low_back(low(attn_mix))
    stream_one = embedded + low_back(jnp.dot(attn_mix, out_mat, precision=highest))
    second_normalized = low(rms_norm(stream_one, gain_tab[1]))
    up_projected = low_back(jnp.dot(second_normalized, mlp_mat[0], precision=highest))
    activated = low(jax.nn.gelu(up_projected))
    stream_two = stream_one + low_back(jnp.dot(activated, mlp_mat[1].T, precision=highest))
    normed_out = low(rms_norm(stream_two, gain_tab[2]))
    logits = low_back(jnp.dot(normed_out, embed_tab.T, precision=highest))
    row_peak = lax.optimization_barrier(jnp.max(logits, -1, keepdims=True))
    log_total = (row_peak + jnp.log(lax.optimization_barrier(jnp.sum(jnp.exp(logits - row_peak), -1, keepdims=True))))[:, 0]
    picked = jnp.take_along_axis(logits, tgt_ids[:, None], axis=-1)[:, 0]
    return slot_valid * jnp.sum(log_total - picked + zloss_coef * log_total * log_total)

def worker_loss(masters, tok_ids, tgt_ids, count_seq):
    weights = tuple((low(master) for master in masters))
    slot_valid = (jnp.arange(SLOTS) < count_seq).astype(jnp.float32)
    seq_fn = jax.checkpoint(seq_terms)

    def add_seq(running, inputs):
        return (running + seq_fn(weights, inputs[0], inputs[1], inputs[2]), None)
    total_sum, _ = lax.scan(add_seq, jnp.zeros((), jnp.float32), (tok_ids, tgt_ids, slot_valid))
    count_tok = (count_seq * SEQ).astype(jnp.float32)
    return (total_sum / count_tok, total_sum)

def reference(tokens, targets, seq_counts, embed_w, qkv_w, out_w, mlp_w, gain_w, embed_mom, qkv_mom, out_mom, mlp_mom, gain_mom, embed_first, qkv_first, out_first, mlp_first, gain_first, embed_second, qkv_second, out_second, mlp_second, gain_second):
    masters = (embed_w, qkv_w, out_w, mlp_w, gain_w)
    step_rates = (matrix_rate,) * 4 + (gain_rate,)
    decays = (decay_rate,) * 4 + (0.0,)

    def per_worker(running, inputs):
        tok_ids, tgt_ids, count_seq, firsts, seconds = inputs
        loss_mean, pullback, total_sum = jax.vjp(lambda wts: worker_loss(wts, tok_ids, tgt_ids, count_seq), masters, has_aux=True)
        gradients = pullback(jnp.ones((), jnp.float32))[0]
        grad_total = sum((jnp.sum(gradient * gradient) for gradient in gradients))
        grad_size = jnp.sqrt(grad_total)
        factor = clip_limit / jnp.maximum(grad_size, clip_limit)
        count_tok = (count_seq * SEQ).astype(jnp.float32)
        new_first, new_second, new_running = ([], [], [])
        for gradient, first_mom, second_mom, step_rate, partial_sum in zip(gradients, firsts, seconds, step_rates, running[:5]):
            gradient = gradient * factor
            first_mom = beta_one * first_mom + (1.0 - beta_one) * gradient
            second_mom = beta_two * second_mom + (1.0 - beta_two) * gradient * gradient
            adam_ratio = first_mom / (1.0 - beta_one ** STEP) / (jnp.sqrt(second_mom / (1.0 - beta_two ** STEP)) + adam_eps)
            new_first.append(first_mom)
            new_second.append(second_mom)
            new_running.append(partial_sum + step_rate * adam_ratio * count_tok)
        new_running.append(running[5] + count_tok)
        loss_row = jnp.stack([total_sum, count_tok])
        return (tuple(new_running), (loss_row, grad_size, tuple(new_first), tuple(new_second)))
    initial = tuple((jnp.zeros_like(master) for master in masters)) + (jnp.zeros((), jnp.float32),)
    inputs = (tokens, targets, seq_counts, (embed_first, qkv_first, out_first, mlp_first, gain_first), (embed_second, qkv_second, out_second, mlp_second, gain_second))
    sums, (loss_stats, norm_list, firsts, seconds) = lax.scan(per_worker, initial, inputs)
    new_masters, new_moms = ([], [])
    moms = (embed_mom, qkv_mom, out_mom, mlp_mom, gain_mom)
    for summed, master, momentum, step_rate, decay in zip(sums[:5], masters, moms, step_rates, decays):
        average = summed / sums[5] + step_rate * decay * master
        momentum = outer_mom * momentum + average
        new_masters.append(master - outer_rate * (average + outer_mom * momentum))
        new_moms.append(momentum)
    return (loss_stats, norm_list, new_masters[0], new_masters[1], new_masters[2], new_masters[3], new_masters[4], new_moms[0], new_moms[1], new_moms[2], new_moms[3], new_moms[4], firsts[0], firsts[1], firsts[2], firsts[3], firsts[4], seconds[0], seconds[1], seconds[2], seconds[3], seconds[4])
```

```python
import functools
import math

import jax
import jax.numpy as jnp
from jax import lax
from jax.experimental import pallas as pl
from jax.experimental.pallas import tpu as pltpu
from jax.sharding import PartitionSpec as P

H = 6
HD = 48
STEP = 7

norm_eps = 1e-06
zloss_coef = 0.01
clip_limit = 0.05
beta_one = 0.9
beta_two = 0.95
adam_eps = 1e-08
decay_rate = 0.1
matrix_rate = 0.03
gain_rate = 0.3
outer_rate = 0.7
outer_mom = 0.9
rope_base = 10000.0

LOG2E = 1.0 / math.log(2.0)
LN2 = math.log(2.0)
SCALE = 1.0 / math.sqrt(HD)
BF = jnp.bfloat16
F32 = jnp.float32
NN = ((1,), (0,))
NT = ((1,), (1,))
CH = 1024
VMEM_BYTES = 58 * 1024 * 1024


def dot(a, b, dims=NN):
    return lax.dot_general(a, b, (dims, ((), ())), preferred_element_type=F32)


def params(n=1):
    return pltpu.CompilerParams(
        dimension_semantics=("arbitrary",) * n, vmem_limit_bytes=VMEM_BYTES
    )


def cost(flops, nbytes):
    return pl.CostEstimate(flops=int(flops), bytes_accessed=int(nbytes), transcendentals=0)


def full(shape):
    return pl.BlockSpec(shape, lambda *_: (0,) * len(shape))


SMEM = pl.BlockSpec(memory_space=pltpu.SMEM)


def lookup_kernel(tok_ref, et_ref, out_ref, acc_ref):
    c = pl.program_id(0)
    nb, _, lt = out_ref.shape

    @pl.when(c == 0)
    def _():
        acc_ref[...] = jnp.zeros_like(acc_ref)

    rows = lax.broadcasted_iota(jnp.int32, (CH, lt), 0) + c * CH
    for j in range(nb):
        hot = jnp.where(rows == tok_ref[:, j * lt : (j + 1) * lt], 1.0, 0.0).astype(BF)
        acc_ref[j] += dot(et_ref[...], hot)

    @pl.when(c == pl.num_programs(0) - 1)
    def _():
        out_ref[...] = acc_ref[...].astype(BF)


def lookup(tok, et, nb):
    width, vpad = et.shape
    full_len = tok.shape[1]
    lt = full_len // nb
    return pl.pallas_call(
        lookup_kernel,
        grid=(vpad // CH,),
        in_specs=[full((1, full_len)), pl.BlockSpec((width, CH), lambda c: (0, c))],
        out_specs=full((nb, width, lt)),
        out_shape=jax.ShapeDtypeStruct((nb, width, lt), BF),
        scratch_shapes=[pltpu.VMEM((nb, width, lt), F32)],
        compiler_params=params(),
        cost_estimate=cost(2 * width * vpad * full_len, width * vpad * 2),
        name="lookup",
    )(tok, et)


def norm_t(x, gain):
    scale = lax.rsqrt(jnp.mean(x * x, 0, keepdims=True) + norm_eps)
    return x * scale * gain, scale


def norm_t_bwd(x, scale, gain, incoming):
    unit = x * scale
    inner = incoming * gain
    return scale * (inner - unit * jnp.mean(inner * unit, 0, keepdims=True)), incoming * unit


def turn(u, cosine, sine):
    rows, lt = u.shape
    half = cosine.shape[0]
    u = u.reshape(rows // (2 * half), 2, half, lt)
    a, b = u[:, 0], u[:, 1]
    return jnp.stack([a * cosine - b * sine, a * sine + b * cosine], 1).reshape(rows, lt)


def causal(lt):
    keys = lax.broadcasted_iota(jnp.int32, (lt, lt), 0)
    queries = lax.broadcasted_iota(jnp.int32, (lt, lt), 1)
    return keys <= queries


def gelu_parts(u):
    k0 = math.sqrt(2.0 / math.pi)
    square = u * u
    th = jnp.tanh(k0 * (u + 0.044715 * u * square))
    act = 0.5 * u * (1.0 + th)
    return act, th, square, k0


def gelu_slope(u, th, square, k0):
    return 0.5 * (1.0 + th) + 0.5 * u * (1.0 - th * th) * k0 * (1.0 + 3.0 * 0.044715 * square)


def trunk_fwd_kernel(nb, me_ref, *refs):
    pieces = refs[:nb]
    (wqkv_t, wo_t, wm0_t, wm1, gains, cos_ref, sin_ref) = refs[nb : nb + 7]
    (x0_out, qkv_out, o_out, lse_out, h1_out, h2_out, af_out, krow) = refs[nb + 7 :]
    me = me_ref[0]
    width, full_len = x0_out.shape
    lt = full_len // nb
    root = math.sqrt(width)
    for k, piece in enumerate(pieces):
        at = pl.multiple_of((me ^ k) * lt, lt)
        x0_out[:, pl.ds(at, lt)] = piece[...]
    for j in range(nb):
        here = slice(j * lt, (j + 1) * lt)
        x = x0_out[:, here].astype(F32) * root
        a1, _ = norm_t(x, gains[:, 0:1])
        y = dot(wqkv_t[...], a1.astype(BF))
        cosine, sine = cos_ref[:, here], sin_ref[:, here]
        q = turn(y[:width], cosine, sine) * (SCALE * LOG2E)
        k = turn(y[width : 2 * width], cosine, sine)
        qkv_out[0:width, here] = q.astype(BF)
        qkv_out[width : 2 * width, here] = k.astype(BF)
        qkv_out[2 * width :, here] = y[2 * width :].astype(BF)
        for h in range(H):
            krow[h, here, :] = k[h * HD : (h + 1) * HD].T.astype(BF)

    def head(h, carry):
        qat = pl.multiple_of(h * HD, 16)
        vat = pl.multiple_of(2 * width + h * HD, 16)
        for j in range(nb):
            here = slice(j * lt, (j + 1) * lt)
            q = qkv_out[pl.ds(qat, HD), here]
            s_diag = jnp.where(causal(lt), dot(krow[h, here, :], q), -1e30)
            peak = jnp.max(s_diag, 0, keepdims=True)
            if j:
                s_off = dot(krow[h, : j * lt, :], q)
                peak = jnp.maximum(peak, jnp.max(s_off, 0, keepdims=True))
            p_diag = jnp.exp2(s_diag - peak)
            total = jnp.sum(p_diag, 0, keepdims=True)
            mix = dot(qkv_out[pl.ds(vat, HD), here], p_diag.astype(BF))
            if j:
                p_off = jnp.exp2(s_off - peak)
                total = total + jnp.sum(p_off, 0, keepdims=True)
                mix = mix + dot(qkv_out[pl.ds(vat, HD), : j * lt], p_off.astype(BF))
            o_out[pl.ds(qat, HD), here] = (mix / total).astype(BF)
            lse_out[pl.ds(h, 1), here] = peak + jnp.log2(total)
        return carry

    lse_out[...] = jnp.zeros_like(lse_out)
    lax.fori_loop(0, H, head, 0)

    for j in range(nb):
        here = slice(j * lt, (j + 1) * lt)
        x = x0_out[:, here].astype(F32) * root
        h1 = x + dot(wo_t[...], o_out[:, here])
        h1_out[:, here] = h1
        a2, _ = norm_t(h1, gains[:, 1:2])
        act = gelu_parts(dot(wm0_t[...], a2.astype(BF)))[0]
        h2 = h1 + dot(wm1[...], act.astype(BF))
        h2_out[:, here] = h2
        af, _ = norm_t(h2, gains[:, 2:3])
        af_out[0:width, here] = (af * LOG2E).astype(BF)
        tail = lax.broadcasted_iota(jnp.int32, (af_out.shape[0] - width, lt), 0)
        af_out[width:, here] = jnp.where(tail == 0, 1.0, 0.0).astype(BF)


def trunk_fwd(me, pieces, weights, gains, cosine, sine):
    nb = len(pieces)
    width, lt = pieces[0].shape
    full_len = nb * lt
    ins = [*weights, gains, cosine, sine]
    ff = weights[2].shape[0]
    flops = 2 * full_len * (width * (4 * width + 2 * ff) + full_len * width * 2)
    shapes = [
        ((width, full_len), BF),
        ((3 * width, full_len), BF),
        ((width, full_len), BF),
        ((8, full_len), F32),
        ((width, full_len), F32),
        ((width, full_len), F32),
        ((width + 16, full_len), BF),
    ]
    return pl.pallas_call(
        functools.partial(trunk_fwd_kernel, nb),
        grid=(1,),
        in_specs=[SMEM] + [full(a.shape) for a in (*pieces, *ins)],
        out_specs=[full(s) for s, _ in shapes],
        out_shape=[jax.ShapeDtypeStruct(s, d) for s, d in shapes],
        scratch_shapes=[pltpu.VMEM((H, full_len, HD), BF)],
        compiler_params=params(),
        cost_estimate=cost(flops, 10e6),
        name="trunk_fwd",
    )(me, *pieces, *ins)


def head_kernel(er_ref, af_ref, tgt_ref, pe_ref, po_ref, m_ref, s_ref, pick_ref, za, zb, ma, mb):
    j = pl.program_id(0)
    last = pl.num_programs(0) - 1
    full_len = af_ref.shape[1]
    lt = 256
    rows = lax.broadcasted_iota(jnp.int32, (CH, lt), 0)

    @pl.when(j == 0)
    def _():
        pick_ref[...] = jnp.zeros_like(pick_ref)

    def product(half, z_ref, peak_ref, t):
        here = slice(t * lt, (t + 1) * lt)
        z = dot(er_ref[half * CH : (half + 1) * CH, :], af_ref[:, here])
        z_ref[:, here] = z
        peak_ref[:, here] = jnp.max(z, 0, keepdims=True)

    def power(chunk, z_ref, peak_ref, p_ref, t):
        here = slice(t * lt, (t + 1) * lt)
        z = z_ref[:, here]
        peak = peak_ref[:, here]
        p = jnp.exp2(z - peak)
        p_ref[:, here] = p.astype(BF)
        m_ref[pl.ds(chunk, 1), here] = peak
        s_ref[pl.ds(chunk, 1), here] = jnp.sum(p, 0, keepdims=True)
        hit = rows == (tgt_ref[:, here] - chunk * CH)
        pick_ref[:, here] += jnp.sum(jnp.where(hit, z, 0.0), 0, keepdims=True)

    tiles = range(full_len // lt)

    @pl.when(j == 0)
    def _():
        for t in tiles:
            product(0, za, ma, t)

    @pl.when((j > 0) & (j < last))
    def _():
        for t in tiles:
            product(0, za, ma, t)
            power(2 * j - 1, zb, mb, po_ref, t)

    @pl.when(j < last)
    def _():
        for t in tiles:
            product(1, zb, mb, t)
            power(2 * j, za, ma, pe_ref, t)

    @pl.when(j == last)
    def _():
        for t in tiles:
            power(2 * j - 1, zb, mb, po_ref, t)


def head_first(er, af, tgt):
    vpad, depth = er.shape
    full_len = af.shape[1]
    pairs = vpad // (2 * CH)
    shapes = [
        ((vpad // 2, full_len), BF),
        ((vpad // 2, full_len), BF),
        ((2 * pairs, full_len), F32),
        ((2 * pairs, full_len), F32),
        ((1, full_len), F32),
    ]
    return pl.pallas_call(
        head_kernel,
        grid=(pairs + 1,),
        in_specs=[
            pl.BlockSpec((2 * CH, depth), lambda j: (jnp.minimum(j, pairs - 1), 0)),
            full(af.shape),
            full(tgt.shape),
        ],
        out_specs=[
            pl.BlockSpec((CH, full_len), lambda j: (jnp.minimum(j, pairs - 1), 0)),
            pl.BlockSpec((CH, full_len), lambda j: (jnp.maximum(j - 1, 0), 0)),
            full(shapes[2][0]),
            full(shapes[3][0]),
            full(shapes[4][0]),
        ],
        out_shape=[jax.ShapeDtypeStruct(s, d) for s, d in shapes],
        scratch_shapes=[
            pltpu.VMEM((CH, full_len), F32),
            pltpu.VMEM((CH, full_len), F32),
            pltpu.VMEM((1, full_len), F32),
            pltpu.VMEM((1, full_len), F32),
        ],
        compiler_params=params(),
        cost_estimate=cost(2 * vpad * depth * full_len, 2 * vpad * full_len),
        name="head_first",
    )(er, af, tgt)


def logit_grad(p, rows, tgt, at_target, scale):
    return jnp.where(rows == tgt, at_target, p.astype(F32) * scale).astype(BF)


def table_back_kernel(pe_ref, po_ref, et_ref, tgt_ref, s_ref, d_ref, out_ref, acc_ref):
    j = pl.program_id(0)
    nb, _, lt = out_ref.shape

    @pl.when(j == 0)
    def _():
        acc_ref[...] = jnp.zeros_like(acc_ref)

    rows = lax.broadcasted_iota(jnp.int32, (CH, lt), 0)
    for half, p_ref in enumerate((pe_ref, po_ref)):
        chunk = 2 * j + half
        for t in range(nb):
            here = slice(t * lt, (t + 1) * lt)
            grad = logit_grad(
                p_ref[:, here],
                rows,
                tgt_ref[:, here] - chunk * CH,
                d_ref[:, here],
                s_ref[pl.ds(chunk, 1), here],
            )
            acc_ref[t] += dot(et_ref[:, half * CH : (half + 1) * CH], grad)

    @pl.when(j == pl.num_programs(0) - 1)
    def _():
        out_ref[...] = acc_ref[...].astype(BF)


def table_back(pe, po, et, tgt, scales, at_target, nb):
    width, vpad = et.shape
    full_len = tgt.shape[1]
    lt = full_len // nb
    return pl.pallas_call(
        table_back_kernel,
        grid=(vpad // (2 * CH),),
        in_specs=[
            pl.BlockSpec((CH, full_len), lambda j: (j, 0)),
            pl.BlockSpec((CH, full_len), lambda j: (j, 0)),
            pl.BlockSpec((width, 2 * CH), lambda j: (0, j)),
            full(tgt.shape),
            full(scales.shape),
            full(at_target.shape),
        ],
        out_specs=full((nb, width, lt)),
        out_shape=jax.ShapeDtypeStruct((nb, width, lt), BF),
        scratch_shapes=[pltpu.VMEM((nb, width, lt), F32)],
        compiler_params=params(),
        cost_estimate=cost(2 * width * vpad * full_len, 2 * vpad * full_len),
        name="table_back",
    )(pe, po, et, tgt, scales, at_target)


def table_grad_kernel(slots, *refs):
    p_refs = refs[: 2 * slots]
    af_refs = refs[2 * slots : 3 * slots]
    tgt_ref, s_ref, d_ref, out_ref = refs[3 * slots :]
    j = pl.program_id(0)
    full_len = tgt_ref.shape[2]
    lt = 256
    width = out_ref.shape[0]
    rows = lax.broadcasted_iota(jnp.int32, (CH, lt), 0)
    for half in range(2):
        chunk = 2 * j + half
        total = jnp.zeros((width, CH), F32)
        for s in range(slots):
            for t in range(full_len // lt):
                here = slice(t * lt, (t + 1) * lt)
                grad = logit_grad(
                    p_refs[2 * s + half][:, here],
                    rows,
                    tgt_ref[s, :, here] - chunk * CH,
                    d_ref[s, :, here],
                    s_ref[s, pl.ds(chunk, 1), here],
                )
                total = total + dot(af_refs[s][0:width, here], grad, NT)
        out_ref[:, half * CH : (half + 1) * CH] = total * LN2


def table_grad(ps, afs, tgt, scales, at_target, width):
    slots = len(afs)
    vpad = 2 * ps[0].shape[0]
    full_len = tgt.shape[2]
    pb = pl.BlockSpec((CH, full_len), lambda j: (j, 0))
    return pl.pallas_call(
        functools.partial(table_grad_kernel, slots),
        grid=(vpad // (2 * CH),),
        in_specs=[pb] * (2 * slots)
        + [full(a.shape) for a in afs]
        + [full(tgt.shape), full(scales.shape), full(at_target.shape)],
        out_specs=pl.BlockSpec((width, 2 * CH), lambda j: (0, j)),
        out_shape=jax.ShapeDtypeStruct((width, vpad), F32),
        compiler_params=params(),
        cost_estimate=cost(2 * width * vpad * full_len * slots, 2 * vpad * full_len * slots),
        name="table_grad",
    )(*ps, *afs, tgt, scales, at_target)


def trunk_bwd_kernel(nb, me_ref, *refs):
    pieces = refs[:nb]
    (x0, qkv, o_ref, lse, h1_ref, h2_ref) = refs[nb : nb + 6]
    (wqkv, wo, wm0, wm0_t, wm1_t, gains, cos_ref, sin_ref) = refs[nb + 6 : nb + 14]
    (dx_out, wg_out, gg_out) = refs[nb + 14 : nb + 17]
    (gin, krow, vrow, dqkv, dqkv_b, dh1_s, dh1_b, a_s, du_s, act_s, df_s, do_s, delta, wg) = refs[
        nb + 17 :
    ]
    me = me_ref[0]
    width, full_len = x0.shape
    ff = du_s.shape[0]
    lt = full_len // nb
    root = math.sqrt(width)
    for k, piece in enumerate(pieces):
        at = pl.multiple_of((me ^ k) * lt, lt)
        gin[:, pl.ds(at, lt)] = piece[...]

    gain_sums = [jnp.zeros((width, 1), F32) for _ in range(3)]
    for j in range(nb):
        here = slice(j * lt, (j + 1) * lt)
        h2 = h2_ref[:, here]
        _, scale = norm_t(h2, 1.0)
        dh2, gg = norm_t_bwd(h2, scale, gains[:, 2:3], gin[:, here].astype(F32))
        gain_sums[2] += jnp.sum(gg, 1, keepdims=True)
        df = dh2.astype(BF)
        df_s[:, here] = df
        h1 = h1_ref[:, here]
        a2, scale = norm_t(h1, gains[:, 1:2])
        a2 = a2.astype(BF)
        a_s[:, here] = a2
        u = dot(wm0_t[...], a2)
        act, th, square, k0 = gelu_parts(u)
        act_s[:, here] = act.astype(BF)
        du = (dot(wm1_t[...], df) * gelu_slope(u, th, square, k0)).astype(BF)
        du_s[:, here] = du
        dmid, gg = norm_t_bwd(h1, scale, gains[:, 1:2], dot(wm0[...], du))
        gain_sums[1] += jnp.sum(gg, 1, keepdims=True)
        dh1 = dh2 + dmid
        dh1_s[:, here] = dh1
        dh1b = dh1.astype(BF)
        dh1_b[:, here] = dh1b
        do = dot(wo[...], dh1b).astype(BF)
        do_s[:, here] = do
        weighed = (do.astype(F32) * o_ref[:, here].astype(F32)).reshape(H, HD, lt)
        delta[0:H, here] = jnp.sum(weighed, 1)
        for h in range(H):
            lo = width + h * HD
            krow[h, here, :] = qkv[lo : lo + HD, here].astype(F32).T.astype(BF)
            vrow[h, here, :] = qkv[lo + width : lo + width + HD, here].astype(F32).T.astype(BF)
    wg[:, 4 * width : 4 * width + ff] = dot(a_s[...], du_s[...], NT)
    wg[:, 4 * width + ff :] = dot(df_s[...], act_s[...], NT)
    wg[:, 3 * width : 4 * width] = dot(o_ref[...], dh1_b[...], NT)

    def head(h, carry):
        qat = pl.multiple_of(h * HD, 16)
        kat = pl.multiple_of(width + h * HD, 16)
        vat = pl.multiple_of(2 * width + h * HD, 16)
        for j in reversed(range(nb)):
            here = slice(j * lt, (j + 1) * lt)
            q = qkv[pl.ds(qat, HD), here]
            do = do_s[pl.ds(qat, HD), here]
            lse_row = lse[pl.ds(h, 1), here]
            delta_row = delta[pl.ds(h, 1), here]
            dq = None
            for there, diagonal in ((here, True), (slice(0, j * lt), False)):
                if there.stop == 0:
                    continue
                p = jnp.exp2(dot(krow[h, there, :], q) - lse_row)
                if diagonal:
                    p = jnp.where(causal(lt), p, 0.0)
                ds = p * (dot(vrow[h, there, :], do) - delta_row)
                pb = p.astype(BF)
                dsb = ds.astype(BF)
                part = dot(qkv[pl.ds(kat, HD), there], dsb)
                dq = part if dq is None else dq + part
                dk = dot(q, dsb, NT)
                dv = dot(do, pb, NT)
                if j == nb - 1:
                    dqkv[pl.ds(kat, HD), there] = dk
                    dqkv[pl.ds(vat, HD), there] = dv
                else:
                    dqkv[pl.ds(kat, HD), there] += dk
                    dqkv[pl.ds(vat, HD), there] += dv
            dqkv[pl.ds(qat, HD), here] = dq
        return carry

    lax.fori_loop(0, H, head, 0)

    for j in range(nb):
        here = slice(j * lt, (j + 1) * lt)
        cosine, sine = cos_ref[:, here], -sin_ref[:, here]
        dq = turn(dqkv[0:width, here], cosine, sine) * SCALE
        dk = turn(dqkv[width : 2 * width, here], cosine, sine) * LN2
        dqkv_b[0:width, here] = dq.astype(BF)
        dqkv_b[width : 2 * width, here] = dk.astype(BF)
        dqkv_b[2 * width :, here] = dqkv[2 * width :, here].astype(BF)
        da1 = dot(wqkv[...], dqkv_b[:, here])
        x = x0[:, here].astype(F32) * root
        a1, scale = norm_t(x, gains[:, 0:1])
        a_s[:, here] = a1.astype(BF)
        dlow, gg = norm_t_bwd(x, scale, gains[:, 0:1], da1)
        gain_sums[0] += jnp.sum(gg, 1, keepdims=True)
        dx_out[:, here] = ((dh1_s[:, here] + dlow) * root).astype(BF)
    wg[:, 0 : 3 * width] = dot(a_s[...], dqkv_b[...], NT)
    own = wg_out.shape[0]
    wg_out[...] = wg[pl.ds(pl.multiple_of(me * own, 8), own), :]
    lane = lax.broadcasted_iota(jnp.int32, gg_out.shape, 1)
    gg_out[...] = jnp.where(
        lane == 0, gain_sums[0], jnp.where(lane == 1, gain_sums[1], gain_sums[2])
    )


def trunk_bwd(me, pieces, saved, weights, gains, cosine, sine):
    nb = len(pieces)
    width, lt = pieces[0].shape
    full_len = nb * lt
    ff = weights[2].shape[1]
    ins = [*saved, *weights, gains, cosine, sine]
    cols = 4 * width + 2 * ff
    shapes = [((width, full_len), BF), ((width // nb, cols), F32), ((width, 128), F32)]
    flops = 2 * full_len * (2 * width * (4 * width + 2 * ff) + full_len * width * 4)
    return pl.pallas_call(
        functools.partial(trunk_bwd_kernel, nb),
        grid=(1,),
        in_specs=[SMEM] + [full(a.shape) for a in (*pieces, *ins)],
        out_specs=[full(s) for s, _ in shapes],
        out_shape=[jax.ShapeDtypeStruct(s, d) for s, d in shapes],
        scratch_shapes=[
            pltpu.VMEM((width, full_len), BF),
            pltpu.VMEM((H, full_len, HD), BF),
            pltpu.VMEM((H, full_len, HD), BF),
            pltpu.VMEM((3 * width, full_len), F32),
            pltpu.VMEM((3 * width, full_len), BF),
            pltpu.VMEM((width, full_len), F32),
            pltpu.VMEM((width, full_len), BF),
            pltpu.VMEM((width, full_len), BF),
            pltpu.VMEM((ff, full_len), BF),
            pltpu.VMEM((ff, full_len), BF),
            pltpu.VMEM((width, full_len), BF),
            pltpu.VMEM((width, full_len), BF),
            pltpu.VMEM((8, full_len), F32),
            pltpu.VMEM((width, cols), F32),
        ],
        compiler_params=params(),
        cost_estimate=cost(flops, 10e6),
        name="trunk_bwd",
    )(me, *pieces, *ins)


def token_grad_kernel(slots, de_ref, tok_ref, *refs):
    dx_refs = refs[:slots]
    out_ref, sq_ref = refs[slots:]
    j = pl.program_id(0)
    full_len = tok_ref.shape[2]
    lt = 256
    rows = lax.broadcasted_iota(jnp.int32, (CH, lt), 0) + j * CH
    total = de_ref[...]
    for s in range(slots):
        for t in range(full_len // lt):
            here = slice(t * lt, (t + 1) * lt)
            hot = jnp.where(rows == tok_ref[s, :, here], 1.0, 0.0).astype(BF)
            total = total + dot(dx_refs[s][:, here], hot, NT)
    out_ref[...] = total
    width = total.shape[0]
    squares = jnp.sum((total * total).reshape(width // 8, 8, CH), 0)

    @pl.when(j == 0)
    def _():
        sq_ref[...] = jnp.zeros_like(sq_ref)

    sq_ref[...] += squares


def token_grad(de, tok, dxs):
    slots = len(dxs)
    width, vpad = de.shape
    full_len = tok.shape[2]
    blk = pl.BlockSpec((width, CH), lambda j: (0, j))
    return pl.pallas_call(
        functools.partial(token_grad_kernel, slots),
        grid=(vpad // CH,),
        in_specs=[blk, full(tok.shape)] + [full(a.shape) for a in dxs],
        out_specs=[blk, full((8, CH))],
        out_shape=[
            jax.ShapeDtypeStruct((width, vpad), F32),
            jax.ShapeDtypeStruct((8, CH), F32),
        ],
        input_output_aliases={0: 0},
        compiler_params=params(),
        cost_estimate=cost(2 * width * vpad * full_len * slots, 8 * width * vpad),
        name="token_grad",
    )(de, tok, *dxs)


def adam(gradient, first, second, weight):
    first = beta_one * first + (1.0 - beta_one) * gradient
    second = beta_two * second + (1.0 - beta_two) * gradient * gradient
    ratio = (first * (weight / (1.0 - beta_one**STEP))) / (
        jnp.sqrt(second * (1.0 / (1.0 - beta_two**STEP))) + adam_eps
    )
    return first, second, ratio


def adam_kernel(sc_ref, g_ref, f_ref, s_ref, f_out, s_out, r_out):
    first, second, ratio = adam(g_ref[...] * sc_ref[0], f_ref[...], s_ref[...], sc_ref[1])
    f_out[...] = first
    s_out[...] = second
    r_out[...] = ratio.astype(BF)


def adam_table(scalars, de, first, second):
    width, rows = first.shape
    blk = pl.BlockSpec((width, CH), lambda j: (0, j))
    return pl.pallas_call(
        adam_kernel,
        grid=(pl.cdiv(rows, CH),),
        in_specs=[SMEM, blk, blk, blk],
        out_specs=[blk, blk, blk],
        out_shape=[
            jax.ShapeDtypeStruct((width, rows), F32),
            jax.ShapeDtypeStruct((width, rows), F32),
            jax.ShapeDtypeStruct((width, rows), BF),
        ],
        compiler_params=params(),
        cost_estimate=cost(20 * width * rows, 22 * width * rows),
        name="adam_table",
    )(scalars, de, first, second)


def swap(value, axis, size, k):
    return lax.ppermute(value, axis, [(i, i ^ k) for i in range(size)])


def share(value, axis, size):
    return [value] + [swap(value, axis, size, k) for k in range(1, size)]


def sum_pieces(stack, axis, size, me):
    total = lax.dynamic_index_in_dim(stack, me, 0, False).astype(F32)
    for k in range(1, size):
        piece = lax.dynamic_index_in_dim(stack, me ^ k, 0, False)
        total = total + swap(piece, axis, size, k).astype(F32)
    return total


def outer_update(summed, total_tok, master, momentum, step_rate, decay):
    average = summed / total_tok + step_rate * decay * master
    momentum = outer_mom * momentum + average
    return (master - outer_rate * (average + outer_mom * momentum), momentum)


def local(
    tokens,
    targets,
    seq_counts,
    embed_w,
    qkv_w,
    out_w,
    mlp_w,
    gain_w,
    embed_mom,
    qkv_mom,
    out_mom,
    mlp_mom,
    gain_mom,
    embed_first,
    qkv_first,
    out_first,
    mlp_first,
    gain_first,
    embed_second,
    qkv_second,
    out_second,
    mlp_second,
    gain_second,
):
    nb = lax.axis_size("blk")
    nw = lax.axis_size("work")
    me = lax.axis_index("blk")
    me_arr = me.astype(jnp.int32).reshape(1)
    slots, full_len = tokens.shape[1:]
    vrows = embed_w.shape[0]
    width = embed_first.shape[2]
    ff = mlp_first.shape[3]
    vpad = pl.cdiv(vrows, 2 * CH) * 2 * CH
    own_rows = width // nb

    et_own = embed_w.T.astype(BF)
    et_all = lax.all_gather(et_own, "work", axis=0, tiled=True)
    et = jnp.pad(et_all, ((0, 0), (0, vpad - vrows)))
    tail = jnp.where(
        (lax.broadcasted_iota(jnp.int32, (vpad, 16), 1) == 0)
        & (lax.broadcasted_iota(jnp.int32, (vpad, 16), 0) >= vrows),
        -60000.0,
        0.0,
    ).astype(BF)
    er = jnp.concatenate([et.T, tail], 1)

    packed = jnp.concatenate([qkv_w, out_w, mlp_w[0], mlp_w[1]], 1).astype(BF)
    packed = lax.all_gather(packed, ("blk", "work"), axis=0, tiled=False)
    cols = packed.shape[2]
    packed = packed.reshape(nb, nw, own_rows, cols).transpose(0, 2, 1, 3)
    packed = packed.reshape(width, nw, cols)
    cq, co, cf = qkv_w.shape[1], out_w.shape[1], mlp_w.shape[2]
    wqkv = packed[:, :, :cq].reshape(width, nw * cq)
    wo = packed[:, :, cq : cq + co].reshape(width, nw * co)
    wm0 = packed[:, :, cq + co : cq + co + cf].reshape(width, nw * cf)
    wm1 = packed[:, :, cq + co + cf :].reshape(width, nw * cf)
    gains = lax.all_gather(gain_w.T.astype(BF), "blk", axis=0, tiled=True).astype(F32)
    counts = lax.all_gather(seq_counts, "work", axis=0, tiled=True)
    total_tok = (jnp.sum(counts) * full_len).astype(F32)

    wqkv_t, wo_t, wm0_t, wm1_t = wqkv.T, wo.T, wm0.T, wm1.T
    half = HD // 2
    frequency = rope_base ** (-jnp.arange(half).astype(F32) * 2.0 / HD)
    angles = frequency[:, None] * jnp.arange(full_len).astype(F32)[None, :]
    cosine, sine = jnp.cos(angles), jnp.sin(angles)

    count_seq = seq_counts[0]
    count_tok = (count_seq * full_len).astype(F32)
    valid = (jnp.arange(slots) < count_seq).astype(F32)

    def local_ids(ids):
        ids = ids[0][:, None, :] - me * vrows
        return jnp.where((ids >= 0) & (ids < vrows), ids, -1)

    tok = local_ids(tokens)
    tgt = local_ids(targets)

    saved, afs, ps, stats = [], [], [], []
    for s in range(slots):
        stack = lookup(tok[s], et, nb)
        mine = sum_pieces(stack, "blk", nb, me).astype(BF)
        pieces = share(mine, "blk", nb)
        x0, qkv, o, lse, h1, h2, af = trunk_fwd(
            me_arr, pieces, (wqkv_t, wo_t, wm0_t, wm1), gains, cosine, sine
        )
        saved.append((x0, qkv, o, lse, h1, h2))
        afs.append(af)
        pe, po, m, total, pick = head_first(er, af, tgt[s])
        ps += [pe, po]
        stats.append((m, total, pick))

    peaks = jnp.stack([m for m, _, _ in stats])
    totals = jnp.stack([t for _, t, _ in stats])
    picks = jnp.stack([p for _, _, p in stats])[:, 0]
    peak = jnp.max(peaks, 1)
    total = jnp.sum(totals * jnp.exp2(peaks - peak[:, None]), 1)
    both = share(jnp.concatenate([peak, total], 0), "blk", nb)
    top = functools.reduce(jnp.maximum, [b[:slots] for b in both])
    total = sum(b[slots:] * jnp.exp2(b[:slots] - top) for b in both)
    lse2 = top + jnp.log2(total)
    lse = lse2 * LN2
    weight = valid[:, None] / count_tok
    boost = 1.0 + 2.0 * zloss_coef * lse
    scales = jnp.exp2(peaks - lse2[:, None]) * (boost * weight)[:, None]
    at_target = ((jnp.exp2(picks - lse2) * boost - 1.0) * weight)[:, None]
    loss_lse = jnp.sum(valid[:, None] * (lse + zloss_coef * lse * lse))
    loss_pick = jnp.sum(valid[:, None] * picks) * LN2

    backs = []
    for s in range(slots):
        stack = table_back(ps[2 * s], ps[2 * s + 1], et, tgt[s], scales[s], at_target[s], nb)
        mine = sum_pieces(stack, "blk", nb, me).astype(BF)
        backs.append(share(mine, "blk", nb))
    de = table_grad(ps, afs, tgt, scales, at_target, width)
    dxs, wgs, ggs = [], [], []
    for s in range(slots):
        dx, wg, gg = trunk_bwd(
            me_arr, backs[s], saved[s], (wqkv, wo, wm0, wm0_t, wm1_t), gains, cosine, sine
        )
        dxs.append(dx)
        wgs.append(wg)
        ggs.append(gg)
    de, squares = token_grad(de, tok, dxs)
    wg = sum(wgs)
    gg = lax.dynamic_slice_in_dim(sum(ggs), me * own_rows, own_rows, 0)[:, :3].T
    square_part = jnp.sum(squares) + jnp.sum(wg * wg) + jnp.sum(gg * gg)
    pair = jnp.stack([loss_pick, square_part]).reshape(1, 2)
    pair = sum(share(pair, "blk", nb))[0]
    loss_total = loss_lse - pair[0]
    grad_size = jnp.sqrt(pair[1])
    factor = clip_limit / jnp.maximum(grad_size, clip_limit)

    weight = matrix_rate * count_tok
    scalars = jnp.stack([factor, weight])
    efirst, esecond, eratio = adam_table(scalars, de, embed_first[0].T, embed_second[0].T)
    c0, c1, c2 = 3 * width, 4 * width, 4 * width + ff
    mgrad = jnp.stack([wg[:, c1:c2], wg[:, c2:]])
    small = [
        adam(g * factor, f[0], s[0], w * count_tok)
        for g, f, s, w in (
            (wg[:, :c0], qkv_first, qkv_second, matrix_rate),
            (wg[:, c0:c1], out_first, out_second, matrix_rate),
            (mgrad, mlp_first, mlp_second, matrix_rate),
            (gg, gain_first, gain_second, gain_rate),
        )
    ]

    ratios = eratio.reshape(nw, width // nw, vrows)
    ratios = lax.all_to_all(ratios, "work", 0, 0, tiled=False)
    embed_sum = jnp.sum(ratios.astype(F32), 0).T
    mratio = small[2][2]
    flat = jnp.concatenate([small[0][2], small[1][2], mratio[0], mratio[1]], 1).astype(BF)
    flat = lax.psum(flat, "work").astype(F32)
    gain_sum = lax.psum(small[3][2], "work")
    wi = lax.axis_index("work")

    def mine_of(lo, size):
        return lax.dynamic_slice_in_dim(flat, lo + wi * size, size, 1)

    sums = (
        embed_sum,
        mine_of(0, cq),
        mine_of(c0, co),
        jnp.stack([mine_of(c1, cf), mine_of(c2, cf)]),
        gain_sum,
    )
    masters = (embed_w, qkv_w, out_w, mlp_w, gain_w)
    moms = (embed_mom, qkv_mom, out_mom, mlp_mom, gain_mom)
    rates = (matrix_rate,) * 4 + (gain_rate,)
    decays = (decay_rate,) * 4 + (0.0,)
    updated = [
        outer_update(g, total_tok, w, m, r, d)
        for g, w, m, r, d in zip(sums, masters, moms, rates, decays)
    ]
    firsts = [efirst.T[None]] + [a[0][None] for a in small]
    seconds = [esecond.T[None]] + [a[1][None] for a in small]
    return (
        jnp.stack([loss_total, count_tok])[None],
        grad_size[None],
        *[u[0] for u in updated],
        *[u[1] for u in updated],
        *firsts,
        *seconds,
    )


def solution(mesh):
    weights = (
        P("blk", "work"),
        P("blk", "work"),
        P("blk", "work"),
        P(None, "blk", "work"),
        P(None, "blk"),
    )
    states = (
        P("work", "blk", None),
        P("work", "blk", None),
        P("work", "blk", None),
        P("work", None, "blk", None),
        P("work", None, "blk"),
    )
    in_specs = (
        P("work", None, None),
        P("work", None, None),
        P("work"),
        *weights,
        *weights,
        *states,
        *states,
    )
    out_specs = (P("work", None), P("work"), *weights, *weights, *states, *states)
    return jax.shard_map(local, mesh=mesh, in_specs=in_specs, out_specs=out_specs, check_vma=False)
```

```python
import functools
import math

import jax
import jax.numpy as jnp
from jax import lax
from jax.experimental import pallas as pl
from jax.experimental.pallas import tpu as pltpu
from jax.sharding import PartitionSpec as P

H = 6
HD = 48
STEP = 7

norm_eps = 1e-06
zloss_coef = 0.01
clip_limit = 0.05
beta_one = 0.9
beta_two = 0.95
adam_eps = 1e-08
decay_rate = 0.1
matrix_rate = 0.03
gain_rate = 0.3
outer_rate = 0.7
outer_mom = 0.9
rope_base = 10000.0

LOG2E = 1.0 / math.log(2.0)
LN2 = math.log(2.0)
SCALE = 1.0 / math.sqrt(HD)
BF = jnp.bfloat16
F32 = jnp.float32
NN = ((1,), (0,))
NT = ((1,), (1,))
CH = 1024
VMEM_BYTES = 58 * 1024 * 1024


def dot(a, b, dims=NN):
    return lax.dot_general(a, b, (dims, ((), ())), preferred_element_type=F32)


def params(n=1):
    return pltpu.CompilerParams(
        dimension_semantics=("arbitrary",) * n, vmem_limit_bytes=VMEM_BYTES
    )


def cost(flops, nbytes):
    return pl.CostEstimate(flops=int(flops), bytes_accessed=int(nbytes), transcendentals=0)


def full(shape):
    return pl.BlockSpec(shape, lambda *_: (0,) * len(shape))


SMEM = pl.BlockSpec(memory_space=pltpu.SMEM)
ANY = pl.BlockSpec(memory_space=pl.ANY)


def call(kernel, ins, deps, **options):
    specs = options.pop("in_specs")

    def body(*refs):
        kernel(*refs[: len(ins)], *refs[len(ins) + len(deps) :])

    return pl.pallas_call(body, in_specs=[*specs, *([ANY] * len(deps))], **options)(*ins, *deps)


def pick_rows(ids_ref, s, tab, got, full_len):
    unroll = 32

    def body(i, carry):
        base = pl.multiple_of(i * unroll, unroll)
        for q in range(0, unroll, 8):
            rows = [tab[pl.ds(ids_ref[s, base + q + u], 1), :] for u in range(8)]
            got[pl.ds(pl.multiple_of(base + q, 8), 8), :] = jnp.concatenate(rows, 0)
        return carry

    lax.fori_loop(0, full_len // unroll, body, 0)


def rows_out(blk, got, outs):
    for k, out in enumerate(outs):
        width, lt = out.shape
        at = pl.multiple_of((blk ^ k) * lt, lt)
        out[...] = got[pl.ds(at, lt), 0:width].T.astype(BF)


def prep_kernel(count, vrows, nb, me_ref, ids_ref, *refs):
    pieces = refs[:count]
    et_ref, er_ref = refs[count : count + 2]
    outs = refs[count + 2 : count + 2 + nb]
    tmp, tab, got = refs[count + 2 + nb :]
    j = pl.program_id(0)
    width, lt = outs[0].shape
    for k, piece in enumerate(pieces):
        tmp[me_ref[0] ^ k] = piece[...].astype(F32)
    e = jnp.concatenate([tmp[w] for w in range(count)], 0)
    lane = lax.broadcasted_iota(jnp.int32, (width, CH), 1) + j * CH
    e = jnp.where(lane < vrows, e, 0.0)
    et_ref[...] = e.astype(BF)
    rows = e.T
    tab[pl.ds(pl.multiple_of(j * CH, CH), CH), 0:width] = rows
    er_ref[:, 0:width] = rows.astype(BF)
    row = lax.broadcasted_iota(jnp.int32, (CH, 16), 0) + j * CH
    col = lax.broadcasted_iota(jnp.int32, (CH, 16), 1)
    er_ref[:, width:] = jnp.where((row >= vrows) & (col == 0), -60000.0, 0.0).astype(BF)

    @pl.when(j == pl.num_programs(0) - 1)
    def _():
        pick_rows(ids_ref, 0, tab, got, nb * lt)
        rows_out(me_ref[1], got, outs)


def prep(me, ids, pieces, vpad, nb):
    count = len(pieces)
    rows, vrows = pieces[0].shape
    width = count * rows
    full_len = ids.shape[1]
    lt = full_len // nb
    padded = pl.cdiv(width, 128) * 128
    et, er, *outs = pl.pallas_call(
        functools.partial(prep_kernel, count, vrows, nb),
        grid=(vpad // CH,),
        in_specs=[SMEM, SMEM] + [pl.BlockSpec((rows, CH), lambda j: (0, j))] * count,
        out_specs=[
            pl.BlockSpec((width, CH), lambda j: (0, j)),
            pl.BlockSpec((CH, width + 16), lambda j: (j, 0)),
            *[full((width, lt))] * nb,
        ],
        out_shape=[
            jax.ShapeDtypeStruct((width, vpad), BF),
            jax.ShapeDtypeStruct((vpad, width + 16), BF),
            *[jax.ShapeDtypeStruct((width, lt), BF)] * nb,
        ],
        scratch_shapes=[
            pltpu.VMEM((count, rows, CH), F32),
            pltpu.VMEM((vpad, padded), F32),
            pltpu.VMEM((full_len, padded), F32),
        ],
        compiler_params=params(),
        cost_estimate=cost(1e6, 30e6),
        name="prep",
    )(me, ids, *pieces)
    return et, er, outs


def rows_kernel(count, me_ref, ids_ref, er_ref, *refs):
    outs, (tab, got) = refs[:-2], refs[-2:]
    nb = len(outs) // count
    width, lt = outs[0].shape

    def fill(c, carry):
        here = pl.ds(pl.multiple_of(c * CH, CH), CH)
        tab[here, 0:width] = er_ref[here, 0:width].astype(F32)
        return carry

    lax.fori_loop(0, er_ref.shape[0] // CH, fill, 0)
    for s in range(count):
        pick_rows(ids_ref, s, tab, got, nb * lt)
        rows_out(me_ref[0], got, outs[s * nb : (s + 1) * nb])


def table_rows(me, ids, er, width, nb, deps=()):
    count, full_len = ids.shape
    lt = full_len // nb
    padded = pl.cdiv(width, 128) * 128
    outs = call(
        functools.partial(rows_kernel, count),
        (me, ids, er),
        deps,
        grid=(1,),
        in_specs=[SMEM, SMEM, full(er.shape)],
        out_specs=[full((width, lt))] * (nb * count),
        out_shape=[jax.ShapeDtypeStruct((width, lt), BF)] * (nb * count),
        scratch_shapes=[
            pltpu.VMEM((er.shape[0], padded), F32),
            pltpu.VMEM((full_len, padded), F32),
        ],
        compiler_params=params(),
        cost_estimate=cost(1e6, 20e6),
        name="table_rows",
    )
    return [outs[s * nb : (s + 1) * nb] for s in range(count)]


def norm_t(x, gain):
    scale = lax.rsqrt(jnp.mean(x * x, 0, keepdims=True) + norm_eps)
    return x * scale * gain, scale


def norm_t_bwd(x, scale, gain, incoming):
    unit = x * scale
    inner = incoming * gain
    return scale * (inner - unit * jnp.mean(inner * unit, 0, keepdims=True)), incoming * unit


def turn(u, cosine, sine):
    rows, lt = u.shape
    half = cosine.shape[0]
    u = u.reshape(rows // (2 * half), 2, half, lt)
    a, b = u[:, 0], u[:, 1]
    return jnp.stack([a * cosine - b * sine, a * sine + b * cosine], 1).reshape(rows, lt)


def causal(lt):
    keys = lax.broadcasted_iota(jnp.int32, (lt, lt), 0)
    queries = lax.broadcasted_iota(jnp.int32, (lt, lt), 1)
    return keys <= queries


def gelu_parts(u):
    k0 = math.sqrt(2.0 / math.pi)
    square = u * u
    th = jnp.tanh(k0 * (u + 0.044715 * u * square))
    act = 0.5 * u * (1.0 + th)
    return act, th, square, k0


def gelu_slope(u, th, square, k0):
    return 0.5 * (1.0 + th) + 0.5 * u * (1.0 - th * th) * k0 * (1.0 + 3.0 * 0.044715 * square)


def trunk_fwd_kernel(nb, me_ref, *refs):
    pieces = refs[:nb]
    wants = refs[nb : 2 * nb]
    (wqkv_t, wo_t, wm0_t, wm1, gains, cos_ref, sin_ref) = refs[2 * nb : 2 * nb + 7]
    (x0_out, qkv_out, o_out, lse_out, af_out, krow) = refs[2 * nb + 7 :]
    me = me_ref[0]
    width, full_len = x0_out.shape
    lt = full_len // nb
    root = math.sqrt(width)
    for k, piece in enumerate(pieces):
        at = pl.multiple_of((me ^ k) * lt, lt)
        x0_out[:, pl.ds(at, lt)] = piece[...]
    for j in range(nb):
        here = slice(j * lt, (j + 1) * lt)
        x = x0_out[:, here].astype(F32) * root
        a1, _ = norm_t(x, gains[:, 0:1])
        y = dot(wqkv_t[...], a1.astype(BF))
        cosine, sine = cos_ref[:, here], sin_ref[:, here]
        q = turn(y[:width], cosine, sine) * (SCALE * LOG2E)
        k = turn(y[width : 2 * width], cosine, sine)
        qkv_out[0:width, here] = q.astype(BF)
        qkv_out[width : 2 * width, here] = k.astype(BF)
        qkv_out[2 * width :, here] = y[2 * width :].astype(BF)
        for h in range(H):
            krow[h, here, :] = k[h * HD : (h + 1) * HD].T.astype(BF)

    def head(h, carry):
        qat = pl.multiple_of(h * HD, 16)
        vat = pl.multiple_of(2 * width + h * HD, 16)
        for j in range(nb):
            here = slice(j * lt, (j + 1) * lt)
            q = qkv_out[pl.ds(qat, HD), here]
            s_diag = jnp.where(causal(lt), dot(krow[h, here, :], q), -1e30)
            peak = jnp.max(s_diag, 0, keepdims=True)
            if j:
                s_off = dot(krow[h, : j * lt, :], q)
                peak = jnp.maximum(peak, jnp.max(s_off, 0, keepdims=True))
            p_diag = jnp.exp2(s_diag - peak)
            total = jnp.sum(p_diag, 0, keepdims=True)
            mix = dot(qkv_out[pl.ds(vat, HD), here], p_diag.astype(BF))
            if j:
                p_off = jnp.exp2(s_off - peak)
                total = total + jnp.sum(p_off, 0, keepdims=True)
                mix = mix + dot(qkv_out[pl.ds(vat, HD), : j * lt], p_off.astype(BF))
            o_out[pl.ds(qat, HD), here] = (mix / total).astype(BF)
            lse_out[pl.ds(h, 1), here] = peak + jnp.log2(total)
        return carry

    lse_out[...] = jnp.zeros_like(lse_out)
    lax.fori_loop(0, H, head, 0)

    for j in range(nb):
        here = slice(j * lt, (j + 1) * lt)
        x = x0_out[:, here].astype(F32) * root
        h1 = x + dot(wo_t[...], o_out[:, here])
        a2, _ = norm_t(h1, gains[:, 1:2])
        act = gelu_parts(dot(wm0_t[...], a2.astype(BF)))[0]
        h2 = h1 + dot(wm1[...], act.astype(BF))
        af, _ = norm_t(h2, gains[:, 2:3])
        af = (af * LOG2E).astype(BF)
        af_out[0:width, here] = af
        tail = lax.broadcasted_iota(jnp.int32, (af_out.shape[0] - width, lt), 0)
        af_out[width:, here] = jnp.where(tail == 0, 1.0, 0.0).astype(BF)
    for k, want in enumerate(wants):
        here = pl.ds(pl.multiple_of((me ^ k) * lt, lt), lt)
        picked = af_out[0:width, here].astype(F32) * want[...].astype(F32)
        lse_out[H : H + 1, here] = jnp.sum(picked, 0, keepdims=True)


def trunk_fwd(me, pieces, wants, weights, gains, cosine, sine, deps=()):
    nb = len(pieces)
    width, lt = pieces[0].shape
    full_len = nb * lt
    ins = [*weights, gains, cosine, sine]
    ff = weights[2].shape[0]
    flops = 2 * full_len * (width * (4 * width + 2 * ff) + full_len * width * 2)
    shapes = [
        ((width, full_len), BF),
        ((3 * width, full_len), BF),
        ((width, full_len), BF),
        ((8, full_len), F32),
        ((width + 16, full_len), BF),
    ]
    ins = [*pieces, *wants, *ins]
    return call(
        functools.partial(trunk_fwd_kernel, nb),
        (me, *ins),
        deps,
        grid=(1,),
        in_specs=[SMEM] + [full(a.shape) for a in ins],
        out_specs=[full(s) for s, _ in shapes],
        out_shape=[jax.ShapeDtypeStruct(s, d) for s, d in shapes],
        scratch_shapes=[pltpu.VMEM((H, full_len, HD), BF)],
        compiler_params=params(),
        cost_estimate=cost(flops, 10e6),
        name="trunk_fwd",
    )


def head_kernel(er_ref, af_ref, pe_ref, po_ref, m_ref, st_ref, s_ref, za, zb, ma, mb):
    j = pl.program_id(0)
    last = pl.num_programs(0) - 1
    full_len = af_ref.shape[1]
    lt = min(512, full_len)

    def tiles(body):
        def step(t, carry):
            body(pl.ds(pl.multiple_of(t * lt, lt), lt))
            return carry

        lax.fori_loop(0, full_len // lt, step, 0)

    def product(half, z_ref, peak_ref, here):
        z = dot(er_ref[half * CH : (half + 1) * CH, :], af_ref[:, here])
        z_ref[:, here] = z
        peak_ref[:, here] = jnp.max(z.reshape(CH // 8, 8, lt), 0)

    def power(chunk, z_ref, peak_ref, p_ref, here):
        peak = jnp.max(peak_ref[:, here], 0, keepdims=True)
        p = jnp.exp2(z_ref[:, here] - peak)
        p_ref[:, here] = p.astype(BF)
        total = jnp.sum(p.reshape(CH // 8, 8, lt), 0)
        m_ref[pl.ds(chunk, 1), here] = peak
        s_ref[pl.ds(chunk, 1), here] = jnp.sum(total, 0, keepdims=True)

    @pl.when(j == 0)
    def _():
        tiles(lambda here: product(0, za, ma, here))

    @pl.when((j > 0) & (j < last))
    def _():
        def body(here):
            power(2 * j - 1, zb, mb, po_ref, here)
            product(0, za, ma, here)

        tiles(body)

    @pl.when(j < last)
    def _():
        def body(here):
            power(2 * j, za, ma, pe_ref, here)
            product(1, zb, mb, here)

        tiles(body)

    @pl.when(j == last)
    def _():
        tiles(lambda here: power(2 * j - 1, zb, mb, po_ref, here))
        peaks = m_ref[...]
        peak = jnp.max(peaks, 0, keepdims=True)
        total = jnp.sum(s_ref[...] * jnp.exp2(peaks - peak), 0, keepdims=True)
        st_ref[...] = jnp.zeros_like(st_ref)
        st_ref[0:1, :] = peak
        st_ref[1:2, :] = total


def head_first(er, af, deps=()):
    vpad, depth = er.shape
    full_len = af.shape[1]
    pairs = vpad // (2 * CH)
    shapes = [
        ((vpad // 2, full_len), BF),
        ((vpad // 2, full_len), BF),
        ((2 * pairs, full_len), F32),
        ((8, full_len), F32),
    ]
    return call(
        head_kernel,
        (er, af),
        deps,
        grid=(pairs + 1,),
        in_specs=[
            pl.BlockSpec((2 * CH, depth), lambda j: (jnp.minimum(j, pairs - 1), 0)),
            full(af.shape),
        ],
        out_specs=[
            pl.BlockSpec((CH, full_len), lambda j: (jnp.minimum(j, pairs - 1), 0)),
            pl.BlockSpec((CH, full_len), lambda j: (jnp.maximum(j - 1, 0), 0)),
            full(shapes[2][0]),
            full(shapes[3][0]),
        ],
        out_shape=[jax.ShapeDtypeStruct(s, d) for s, d in shapes],
        scratch_shapes=[
            pltpu.VMEM((2 * pairs, full_len), F32),
            pltpu.VMEM((CH, full_len), F32),
            pltpu.VMEM((CH, full_len), F32),
            pltpu.VMEM((8, full_len), F32),
            pltpu.VMEM((8, full_len), F32),
        ],
        compiler_params=params(),
        cost_estimate=cost(2 * vpad * depth * full_len, 2 * vpad * full_len),
        name="head_first",
    )


def head_back_kernel(nb, sc_ref, *refs):
    (pe_ref, po_ref, et_ref, af_ref, tgt_ref, m_ref, pick_ref) = refs[:7]
    stats = refs[7 : 7 + nb]
    outs = refs[7 + nb : 7 + 2 * nb]
    (de_ref, loss_ref, acc, s_ref, d_ref) = refs[7 + 2 * nb :]
    j = pl.program_id(0)
    width, lt = outs[0].shape

    @pl.when(j == 0)
    def _():
        acc[...] = jnp.zeros_like(acc)
        top = functools.reduce(jnp.maximum, [b[0:1, :] for b in stats])
        total = sum(b[1:2, :] * jnp.exp2(b[0:1, :] - top) for b in stats)
        lse2 = top + jnp.log2(total)
        lse = lse2 * LN2
        boost = (1.0 + 2.0 * zloss_coef * lse) * sc_ref[0]
        pick = pick_ref[H : H + 1, :]
        s_ref[...] = jnp.exp2(m_ref[...] - lse2) * boost
        d_ref[0:1, :] = jnp.exp2(pick - lse2) * boost - sc_ref[0]
        loss_ref[...] = jnp.zeros_like(loss_ref)
        loss_ref[0:1, :] = (lse + zloss_coef * lse * lse) * sc_ref[1]
        loss_ref[1:2, :] = pick * LN2 * sc_ref[1]

    rows = lax.broadcasted_iota(jnp.int32, (CH, lt), 0)
    for half, p_ref in enumerate((pe_ref, po_ref)):
        chunk = 2 * j + half
        there = slice(half * CH, (half + 1) * CH)
        total = None
        for t in range(nb):
            here = slice(t * lt, (t + 1) * lt)
            grad = jnp.where(
                rows == tgt_ref[:, here] - chunk * CH,
                d_ref[0:1, here],
                p_ref[:, here].astype(F32) * s_ref[pl.ds(chunk, 1), here],
            ).astype(BF)
            acc[t] += dot(et_ref[:, there], grad)
            part = dot(af_ref[0:width, here], grad, NT)
            total = part if total is None else total + part
        de_ref[:, there] = (total * LN2).astype(BF)

    @pl.when(j == pl.num_programs(0) - 1)
    def _():
        for k, out in enumerate(outs):
            out[...] = acc[sc_ref[2].astype(jnp.int32) ^ k].astype(BF)


def head_back(scalars, pe, po, et, af, tgt, peaks, picks, stats, deps=()):
    nb = len(stats)
    width, vpad = et.shape
    full_len = tgt.shape[1]
    lt = full_len // nb
    half = pl.BlockSpec((CH, full_len), lambda j: (j, 0))
    wide = pl.BlockSpec((width, 2 * CH), lambda j: (0, j))
    rest = (af, tgt, peaks, picks, *stats)
    *outs, de, loss = call(
        functools.partial(head_back_kernel, nb),
        (scalars, pe, po, et, *rest),
        deps,
        grid=(vpad // (2 * CH),),
        in_specs=[SMEM, half, half, wide] + [full(a.shape) for a in rest],
        out_specs=[full((width, lt))] * nb + [wide, full((8, full_len))],
        out_shape=[jax.ShapeDtypeStruct((width, lt), BF)] * nb
        + [
            jax.ShapeDtypeStruct((width, vpad), BF),
            jax.ShapeDtypeStruct((8, full_len), F32),
        ],
        scratch_shapes=[
            pltpu.VMEM((nb, width, lt), F32),
            pltpu.VMEM(peaks.shape, F32),
            pltpu.VMEM((8, full_len), F32),
        ],
        compiler_params=params(),
        cost_estimate=cost(4 * width * vpad * full_len, 2 * vpad * full_len),
        name="head_back",
    )
    return outs, de, loss


def trunk_bwd_kernel(nb, me_ref, *refs):
    pieces = refs[:nb]
    (x0, qkv, o_ref, lse) = refs[nb : nb + 4]
    (wqkv, wo, wo_t, wm0, wm0_t, wm1, wm1_t, gains, cos_ref, sin_ref) = refs[nb + 4 : nb + 14]
    (dx_out, wg_out, gg_out) = refs[nb + 14 : nb + 17]
    (gin, krow, vrow, dqkv, dqkv_b, dh1_s, dh1_b, a_s, du_s, act_s, df_s, do_s, delta, wg, gg_s) = refs[
        nb + 17 :
    ]
    me = me_ref[0]
    width, full_len = x0.shape
    ff = du_s.shape[0]
    lt = full_len // nb
    root = math.sqrt(width)
    for k, piece in enumerate(pieces):
        at = pl.multiple_of((me ^ k) * lt, lt)
        gin[:, pl.ds(at, lt)] = piece[...]

    gain_sums = [jnp.zeros((width, 1), F32) for _ in range(3)]
    for j in range(nb):
        here = slice(j * lt, (j + 1) * lt)
        h1 = x0[:, here].astype(F32) * root + dot(wo_t[...], o_ref[:, here])
        a2, scale = norm_t(h1, gains[:, 1:2])
        a2 = a2.astype(BF)
        a_s[:, here] = a2
        u = dot(wm0_t[...], a2)
        act, th, square, k0 = gelu_parts(u)
        act = act.astype(BF)
        act_s[:, here] = act
        h2 = h1 + dot(wm1[...], act)
        _, scale2 = norm_t(h2, 1.0)
        dh2, gg = norm_t_bwd(h2, scale2, gains[:, 2:3], gin[:, here].astype(F32))
        gain_sums[2] += jnp.sum(gg, 1, keepdims=True)
        df = dh2.astype(BF)
        df_s[:, here] = df
        du = (dot(wm1_t[...], df) * gelu_slope(u, th, square, k0)).astype(BF)
        du_s[:, here] = du
        dmid, gg = norm_t_bwd(h1, scale, gains[:, 1:2], dot(wm0[...], du))
        gain_sums[1] += jnp.sum(gg, 1, keepdims=True)
        dh1 = dh2 + dmid
        dh1_s[:, here] = dh1
        dh1b = dh1.astype(BF)
        dh1_b[:, here] = dh1b
        do = dot(wo[...], dh1b).astype(BF)
        do_s[:, here] = do
        weighed = (do.astype(F32) * o_ref[:, here].astype(F32)).reshape(H, HD, lt)
        delta[0:H, here] = jnp.sum(weighed, 1)
        for h in range(H):
            lo = width + h * HD
            krow[h, here, :] = qkv[lo : lo + HD, here].astype(F32).T.astype(BF)
            vrow[h, here, :] = qkv[lo + width : lo + width + HD, here].astype(F32).T.astype(BF)
    wg[:, 4 * width : 4 * width + ff] = dot(a_s[...], du_s[...], NT)
    wg[:, 4 * width + ff :] = dot(df_s[...], act_s[...], NT)
    wg[:, 3 * width : 4 * width] = dot(o_ref[...], dh1_b[...], NT)

    def head(h, carry):
        qat = pl.multiple_of(h * HD, 16)
        kat = pl.multiple_of(width + h * HD, 16)
        vat = pl.multiple_of(2 * width + h * HD, 16)
        for j in reversed(range(nb)):
            here = slice(j * lt, (j + 1) * lt)
            q = qkv[pl.ds(qat, HD), here]
            do = do_s[pl.ds(qat, HD), here]
            lse_row = lse[pl.ds(h, 1), here]
            delta_row = delta[pl.ds(h, 1), here]
            dq = None
            for there, diagonal in ((here, True), (slice(0, j * lt), False)):
                if there.stop == 0:
                    continue
                p = jnp.exp2(dot(krow[h, there, :], q) - lse_row)
                if diagonal:
                    p = jnp.where(causal(lt), p, 0.0)
                ds = p * (dot(vrow[h, there, :], do) - delta_row)
                pb = p.astype(BF)
                dsb = ds.astype(BF)
                part = dot(qkv[pl.ds(kat, HD), there], dsb)
                dq = part if dq is None else dq + part
                dk = dot(q, dsb, NT)
                dv = dot(do, pb, NT)
                if j == nb - 1:
                    dqkv[pl.ds(kat, HD), there] = dk
                    dqkv[pl.ds(vat, HD), there] = dv
                else:
                    dqkv[pl.ds(kat, HD), there] += dk
                    dqkv[pl.ds(vat, HD), there] += dv
            dqkv[pl.ds(qat, HD), here] = dq
        return carry

    lax.fori_loop(0, H, head, 0)

    for j in range(nb):
        here = slice(j * lt, (j + 1) * lt)
        cosine, sine = cos_ref[:, here], -sin_ref[:, here]
        dq = turn(dqkv[0:width, here], cosine, sine) * SCALE
        dk = turn(dqkv[width : 2 * width, here], cosine, sine) * LN2
        dqkv_b[0:width, here] = dq.astype(BF)
        dqkv_b[width : 2 * width, here] = dk.astype(BF)
        dqkv_b[2 * width :, here] = dqkv[2 * width :, here].astype(BF)
        da1 = dot(wqkv[...], dqkv_b[:, here])
        x = x0[:, here].astype(F32) * root
        a1, scale = norm_t(x, gains[:, 0:1])
        a_s[:, here] = a1.astype(BF)
        dlow, gg = norm_t_bwd(x, scale, gains[:, 0:1], da1)
        gain_sums[0] += jnp.sum(gg, 1, keepdims=True)
        dx_out[:, here] = ((dh1_s[:, here] + dlow) * root).astype(BF)
    wg[:, 0 : 3 * width] = dot(a_s[...], dqkv_b[...], NT)
    own = wg_out.shape[0]
    wg_out[...] = wg[pl.ds(pl.multiple_of(me * own, 8), own), :]
    lane = lax.broadcasted_iota(jnp.int32, gg_s.shape, 1)
    gg_s[...] = sum(jnp.where(lane == i, gain_sums[i], 0.0) for i in range(3))
    gg_out[...] = gg_s[pl.ds(pl.multiple_of(me * own, 8), own), :]


def trunk_bwd(me, pieces, saved, weights, gains, cosine, sine, deps=()):
    nb = len(pieces)
    width, lt = pieces[0].shape
    full_len = nb * lt
    ff = weights[3].shape[1]
    ins = [*saved, *weights, gains, cosine, sine]
    cols = 4 * width + 2 * ff
    shapes = [((width, full_len), BF), ((width // nb, cols), F32), ((width // nb, 128), F32)]
    flops = 2 * full_len * (2 * width * (4 * width + 2 * ff) + full_len * width * 4)
    return call(
        functools.partial(trunk_bwd_kernel, nb),
        (me, *pieces, *ins),
        deps,
        grid=(1,),
        in_specs=[SMEM] + [full(a.shape) for a in (*pieces, *ins)],
        out_specs=[full(s) for s, _ in shapes],
        out_shape=[jax.ShapeDtypeStruct(s, d) for s, d in shapes],
        scratch_shapes=[
            pltpu.VMEM((width, full_len), BF),
            pltpu.VMEM((H, full_len, HD), BF),
            pltpu.VMEM((H, full_len, HD), BF),
            pltpu.VMEM((3 * width, full_len), F32),
            pltpu.VMEM((3 * width, full_len), BF),
            pltpu.VMEM((width, full_len), F32),
            pltpu.VMEM((width, full_len), BF),
            pltpu.VMEM((width, full_len), BF),
            pltpu.VMEM((ff, full_len), BF),
            pltpu.VMEM((ff, full_len), BF),
            pltpu.VMEM((width, full_len), BF),
            pltpu.VMEM((width, full_len), BF),
            pltpu.VMEM((8, full_len), F32),
            pltpu.VMEM((width, cols), F32),
            pltpu.VMEM((width, 128), F32),
        ],
        compiler_params=params(),
        cost_estimate=cost(flops, 10e6),
        name="trunk_bwd",
    )


def folded(values):
    rows, cols = values.shape
    values = jnp.sum(values.reshape(rows // 8, 8, cols), 0)
    return sum(values[:, c : c + 128] for c in range(0, cols, 128))


def token_grad_kernel(slots, tok_ref, *refs):
    de_refs, dx_refs = refs[:slots], refs[slots : 2 * slots]
    wg_refs, gg_refs = refs[2 * slots : 3 * slots], refs[3 * slots : 4 * slots]
    loss_refs = refs[4 * slots : 5 * slots]
    out_ref, wg_out, gg_out, sum_out, acc = refs[5 * slots :]
    j = pl.program_id(0)
    full_len = tok_ref.shape[2]
    lt = min(512, full_len)

    @pl.when(j == 0)
    def _():
        wg = sum(w[...] for w in wg_refs)
        gg = sum(g[...] for g in gg_refs)
        wg_out[...] = wg
        gg_out[...] = gg
        acc[...] = folded(wg * wg) + folded(gg * gg)

    rows = lax.broadcasted_iota(jnp.int32, (CH, lt), 0) + j * CH
    total = sum(d[...].astype(F32) for d in de_refs)
    for s in range(slots):
        for t in range(full_len // lt):
            here = slice(t * lt, (t + 1) * lt)
            hot = jnp.where(rows == tok_ref[s, :, here], 1.0, 0.0).astype(BF)
            total = total + dot(dx_refs[s][:, here], hot, NT)
    out_ref[...] = total.astype(BF)
    acc[...] += folded(total * total)

    @pl.when(j == pl.num_programs(0) - 1)
    def _():
        lane = lax.broadcasted_iota(jnp.int32, sum_out.shape, 1)
        pick = sum(jnp.sum(r[1:2, :]) for r in loss_refs)
        sum_out[...] = jnp.where(lane == 0, jnp.sum(acc[...]), jnp.where(lane == 1, pick, 0.0))


def token_grad(tok, des, dxs, wgs, ggs, losses):
    slots = len(dxs)
    width, vpad = des[0].shape
    full_len = tok.shape[2]
    blk = pl.BlockSpec((width, CH), lambda j: (0, j))
    rest = (*dxs, *wgs, *ggs, *losses)
    shapes = [(wgs[0].shape, F32), (ggs[0].shape, F32), ((8, 128), F32)]
    return pl.pallas_call(
        functools.partial(token_grad_kernel, slots),
        grid=(vpad // CH,),
        in_specs=[full(tok.shape)] + [blk] * slots + [full(a.shape) for a in rest],
        out_specs=[blk] + [full(s) for s, _ in shapes],
        out_shape=[jax.ShapeDtypeStruct((width, vpad), BF)]
        + [jax.ShapeDtypeStruct(s, d) for s, d in shapes],
        scratch_shapes=[pltpu.VMEM((8, 128), F32)],
        compiler_params=params(),
        cost_estimate=cost(2 * width * vpad * full_len * slots, 8 * width * vpad),
        name="token_grad",
    )(tok, *des, *rest)


def clip_factor(sums):
    total = sum(s[0:1, 0:1] for s in sums)
    return clip_limit / jnp.maximum(jnp.sqrt(total), clip_limit)


def adam(gradient, first, second, weight):
    first = beta_one * first + (1.0 - beta_one) * gradient
    second = beta_two * second + (1.0 - beta_two) * gradient * gradient
    ratio = (first * (weight / (1.0 - beta_one**STEP))) / (
        jnp.sqrt(second * (1.0 / (1.0 - beta_two**STEP))) + adam_eps
    )
    return first, second, ratio


def adam_small_kernel(nb, sc_ref, *refs):
    factor = clip_factor(refs[:nb])
    (wg, gg, qf, of, mf, gf, qs, os_, ms, gs) = refs[nb : nb + 10]
    (qf2, of2, mf2, gf2, qs2, os2, ms2, gs2, flat) = refs[nb + 10 :]
    weight = sc_ref[0] * matrix_rate
    at = 0
    for f, s, f2, s2 in (
        (qf, qs, qf2, qs2),
        (of, os_, of2, os2),
        (mf.at[0], ms.at[0], mf2.at[0], ms2.at[0]),
        (mf.at[1], ms.at[1], mf2.at[1], ms2.at[1]),
    ):
        here = slice(at, at + f.shape[1])
        f2[...], s2[...], flat[:, here] = adam(wg[:, here] * factor, f[...], s[...], weight)
        at = here.stop
    f2, s2, ratio = adam(gg[:, 0:3] * factor, gf[...], gs[...], sc_ref[0] * gain_rate)
    gf2[...] = f2
    gs2[...] = s2
    flat[:, at:] = jnp.zeros_like(flat[:, at:])
    flat[:, at : at + 3] = ratio


def adam_small(scalars, sums, wg, gg, firsts, seconds):
    ins = (*sums, wg, gg, *firsts, *seconds)
    shapes = [a.shape for a in (*firsts, *seconds)]
    shapes.append((wg.shape[0], wg.shape[1] + 128))
    return pl.pallas_call(
        functools.partial(adam_small_kernel, len(sums)),
        grid=(1,),
        in_specs=[SMEM] + [full(a.shape) for a in ins],
        out_specs=[full(s) for s in shapes],
        out_shape=[jax.ShapeDtypeStruct(s, F32) for s in shapes],
        compiler_params=params(),
        cost_estimate=cost(1e6, 6e6),
        name="adam_small",
    )(scalars, *ins)


def adam_kernel(nb, grouped, kept, sc_ref, me_ref, *refs):
    sums, (g_ref, f_ref, s_ref) = refs[:nb], refs[nb : nb + 3]
    f_out, s_out, *r_out = refs[nb + 3 + kept :]
    factor = clip_factor(sums)
    first, second, ratio = adam(
        g_ref[...].astype(F32) * factor, f_ref[...], s_ref[...], sc_ref[0] * matrix_rate
    )
    f_out[...] = first
    s_out[...] = second
    if not grouped:
        r_out[0][...] = ratio.astype(BF)
        return
    groups = 2 * r_out[0].shape[0]
    rows = ratio.shape[0] // groups
    padded = r_out[0].shape[1]
    for w in range(groups):
        piece = ratio[w * rows : (w + 1) * rows]
        piece = jnp.concatenate([piece, jnp.zeros((padded - rows, CH), F32)], 0).astype(BF)
        rel = me_ref[0] ^ w
        for core in range(2):

            @pl.when((rel & 1) == core)
            def _():
                r_out[core][rel >> 1] = piece


def adam_table(scalars, me, sums, de, first, second, groups, part, kept, deps=()):
    width, rows = first.shape
    lo, hi = part
    here = min(hi * CH, rows) - lo * CH
    blk = pl.BlockSpec((width, CH), lambda j: (0, j + lo))
    shapes = [((width, rows), F32)] * 2
    specs = [blk, blk]
    if groups:
        stack = (groups // 2, pl.cdiv(width // groups, 8) * 8)
        shapes += [((*stack, here), BF)] * 2
        specs += [pl.BlockSpec((*stack, CH), lambda j: (0, 0, j))] * 2
    else:
        shapes += [((width, here), BF)]
        specs += [pl.BlockSpec((width, CH), lambda j: (0, j))]
    nb = len(sums)
    at = nb + 5
    return call(
        functools.partial(adam_kernel, nb, bool(groups), len(kept)),
        (scalars, me, *sums, de, first, second, *kept),
        deps,
        grid=(hi - lo,),
        in_specs=[SMEM, SMEM] + [full(a.shape) for a in sums] + [blk] * 3 + [ANY] * len(kept),
        out_specs=specs,
        out_shape=[jax.ShapeDtypeStruct(s, d) for s, d in shapes],
        input_output_aliases={at + i: i for i in range(len(kept))},
        compiler_params=params(),
        cost_estimate=cost(20 * width * here, 22 * width * here),
        name="adam_table",
    )


def swap(value, axis, size, k):
    return lax.ppermute(value, axis, [(i, i ^ k) for i in range(size)])


def share(value, axis, size):
    return [value] + [swap(value, axis, size, k) for k in range(1, size)]


def sum_pieces(pieces, axis, size):
    total = pieces[0].astype(F32)
    for k in range(1, size):
        total = total + swap(pieces[k], axis, size, k).astype(F32)
    return total.astype(BF)


def turn_first(i):
    return i ^ (2 if i % 2 == 0 else 4)


def turn_second(i):
    return i ^ (4 if i % 2 == 0 else 2)


def permute(value, axis, size, partner):
    return lax.ppermute(value, axis, [(i, partner(i)) for i in range(size)])


def gather_pieces(own, axis, core):
    x, y = swap(own, axis, 8, 2), swap(own, axis, 8, 4)
    far = permute(jnp.where(core == 0, y, x), axis, 8, turn_first)
    near = [own, x, y, far]
    others = [swap(p, axis, 8, 1) for p in near]
    return [p for pair in zip(near, others) for p in pair]


def reduce_pieces(same, other, axis, core):
    y = (same.astype(F32) + swap(other, axis, 8, 1).astype(F32)).astype(BF)
    sent = jnp.stack([jnp.where(core == 0, y[1], y[2]), y[3]])
    kept = jnp.where(core == 0, y[2], y[1])
    came = permute(sent, axis, 8, turn_first)
    relayed = (kept.astype(F32) + came[1].astype(F32)).astype(BF)
    total = y[0].astype(F32) + came[0].astype(F32)
    return total + permute(relayed, axis, 8, turn_second).astype(F32)


def outer_update(summed, total_tok, master, momentum, step_rate, decay):
    average = summed / total_tok + step_rate * decay * master
    momentum = outer_mom * momentum + average
    return (master - outer_rate * (average + outer_mom * momentum), momentum)


def local(
    tokens,
    targets,
    seq_counts,
    embed_w,
    qkv_w,
    out_w,
    mlp_w,
    gain_w,
    embed_mom,
    qkv_mom,
    out_mom,
    mlp_mom,
    gain_mom,
    embed_first,
    qkv_first,
    out_first,
    mlp_first,
    gain_first,
    embed_second,
    qkv_second,
    out_second,
    mlp_second,
    gain_second,
):
    nb = lax.axis_size("blk")
    nw = lax.axis_size("work")
    me = lax.axis_index("blk")
    wi = lax.axis_index("work")
    core = wi % 2
    me_arr = me.astype(jnp.int32).reshape(1)
    wi_arr = wi.astype(jnp.int32).reshape(1)
    slots, full_len = tokens.shape[1:]
    vrows = embed_w.shape[0]
    width = embed_first.shape[2]
    ff = mlp_first.shape[3]
    vpad = pl.cdiv(vrows, 2 * CH) * 2 * CH
    own_rows = width // nb
    paired = nw == 8

    et_own = embed_w.T.astype(BF)
    if paired:
        pieces = gather_pieces(et_own, "work", core)
    else:
        pieces = [lax.all_gather(et_own, "work", axis=0, tiled=True)]
    wi_prep = wi_arr if paired else jnp.zeros_like(wi_arr)

    cq, co, cf = qkv_w.shape[1], out_w.shape[1], mlp_w.shape[2]
    count_col = jnp.broadcast_to(seq_counts[0].astype(F32), (own_rows, 1))
    packed = jnp.concatenate([qkv_w, out_w, mlp_w[0], mlp_w[1], gain_w.T, count_col], 1)
    packed = lax.all_gather(packed.astype(BF), ("blk", "work"), axis=0, tiled=False)
    cols = packed.shape[2]
    packed = packed.reshape(nb, nw, own_rows, cols).transpose(0, 2, 1, 3)
    packed = packed.reshape(width, nw, cols)
    c1, c2, c3 = cq + co, cq + co + cf, cq + co + 2 * cf
    wqkv = packed[:, :, :cq].reshape(width, nw * cq)
    wo = packed[:, :, cq:c1].reshape(width, nw * co)
    wm0 = packed[:, :, c1:c2].reshape(width, nw * cf)
    wm1 = packed[:, :, c2:c3].reshape(width, nw * cf)
    gains = packed[:, 0, c3 : c3 + 3].astype(F32)
    total_tok = jnp.sum(packed[0, :, c3 + 3].astype(F32)) * full_len

    wqkv_t, wo_t, wm0_t, wm1_t = wqkv.T, wo.T, wm0.T, wm1.T
    half = HD // 2
    frequency = rope_base ** (-jnp.arange(half).astype(F32) * 2.0 / HD)
    angles = frequency[:, None] * jnp.arange(full_len).astype(F32)[None, :]
    cosine, sine = jnp.cos(angles), jnp.sin(angles)

    count_seq = seq_counts[0]
    count_tok = (count_seq * full_len).astype(F32)
    valid = (jnp.arange(slots) < count_seq).astype(F32)

    def local_ids(ids, missing):
        ids = ids[0] - me * vrows
        return jnp.where((ids >= 0) & (ids < vrows), ids, missing)

    tok = local_ids(tokens, -1)[:, None, :]
    tgt = local_ids(targets, -1)[:, None, :]
    tok_rows = local_ids(tokens, vrows)
    tgt_rows = local_ids(targets, vrows)

    prep_ids = jnp.concatenate([wi_prep, me_arr])
    et, er, looked = prep(prep_ids, tok_rows[:1], pieces, vpad, nb)
    mine = [sum_pieces(looked, "blk", nb)]
    wants = table_rows(me_arr, tgt_rows, er, width, nb)
    fwd_weights = (wqkv_t, wo_t, wm0_t, wm1)
    bwd_weights = (wqkv, wo, wo_t, wm0, wm0_t, wm1, wm1_t)
    more = table_rows(me_arr, tok_rows[1:], er, width, nb, (mine[0], *wants[0], *fwd_weights))
    mine += [sum_pieces(m, "blk", nb) for m in more]
    rows = [share(m, "blk", nb) for m in mine]

    saved, heads, stats, backs, sums, des, losses = {}, {}, {}, {}, {}, {}, {}

    def forward(s, *deps):
        *kept, af = trunk_fwd(
            me_arr, rows[s], wants[s], fwd_weights, gains, cosine, sine, deps
        )
        saved[s] = kept
        heads[s] = [af]

    def head(s, *deps):
        pe, po, peaks, stat = head_first(er, heads[s][0], deps)
        heads[s] += [pe, po, peaks]
        stats[s] = share(stat, "blk", nb)

    def back(s, *deps):
        af, pe, po, peaks = heads[s]
        scalars = jnp.stack([valid[s] / count_tok, valid[s], me.astype(F32)])
        outs, des[s], losses[s] = head_back(
            scalars, pe, po, et, af, tgt[s], peaks, saved[s][3], stats[s], deps
        )
        sums[s] = sum_pieces(outs, "blk", nb)
        backs[s] = share(sums[s], "blk", nb)

    last = None
    for s in range(slots):
        forward(s, *([] if s == 0 else [stats[s - 1][0]]))
        if s >= 2:
            back(s - 2, saved[s][3])
        extra = [mine[s + 1]] if s + 1 < slots else []
        head(s, *extra, *([] if s < 2 else [des[s - 2]]))
    for s in range(max(0, slots - 2), slots):
        last = [stats[slots - 1][0]] if s == slots - 2 else [des[s - 1]] if s else []
        back(s, *last)
    dxs, wgs, ggs = [], [], []
    for s in range(slots):
        deps = [des[slots - 1]] if s == 0 else [dxs[-1]]
        deps += [sums[s + 1]] if s + 1 < slots else []
        dx, wg, gg = trunk_bwd(
            me_arr, backs[s], saved[s], bwd_weights, gains, cosine, sine, deps
        )
        dxs.append(dx)
        wgs.append(wg)
        ggs.append(gg)
    des, losses = [des[s] for s in range(slots)], [losses[s] for s in range(slots)]
    de, wg, gg, both = token_grad(tok, des, dxs, wgs, ggs, losses)
    both = share(both, "blk", nb)
    loss_total = sum(jnp.sum(r[0]) for r in losses) - sum(b[0, 1] for b in both)
    grad_size = jnp.sqrt(sum(b[0, 0] for b in both))

    tokens_of = count_tok.reshape(1)
    small = adam_small(
        tokens_of,
        both,
        wg,
        gg,
        (qkv_first[0], out_first[0], mlp_first[0], gain_first[0].T),
        (qkv_second[0], out_second[0], mlp_second[0], gain_second[0].T),
    )
    flat = small[8].astype(BF)
    summed = lax.psum(flat, "work").astype(F32)

    first, second = embed_first[0].T, embed_second[0].T
    chunks = pl.cdiv(vrows, CH)
    parts = [(0, chunks // 2), (chunks // 2, chunks)]
    kept, embed_sums, deps = (), [], [flat]
    for part in parts:
        out = adam_table(
            tokens_of, wi_arr, both, de, first, second, nw if paired else 0, part, kept, deps
        )
        kept, ratios = out[:2], out[2:]
        deps = []
        if paired:
            part_sum = reduce_pieces(*ratios, "work", core)[: width // nw]
        else:
            part_sum = lax.psum_scatter(ratios[0], "work", scatter_dimension=0, tiled=True)
        embed_sums.append(part_sum.astype(F32))
    efirst, esecond = kept

    def mine_of(lo, size):
        return lax.dynamic_slice_in_dim(summed, lo + wi * size, size, 1)

    d1, d2, d3 = 3 * width, 4 * width, 4 * width + ff
    embed_sum = jnp.concatenate(embed_sums, 1).T
    sums = (
        embed_sum,
        mine_of(0, cq),
        mine_of(d1, co),
        jnp.stack([mine_of(d2, cf), mine_of(d3, cf)]),
        summed[:, d3 + ff : d3 + ff + 3].T,
    )
    masters = (embed_w, qkv_w, out_w, mlp_w, gain_w)
    moms = (embed_mom, qkv_mom, out_mom, mlp_mom, gain_mom)
    rates = (matrix_rate,) * 4 + (gain_rate,)
    decays = (decay_rate,) * 4 + (0.0,)
    updated = [
        outer_update(g, total_tok, w, m, r, d)
        for g, w, m, r, d in zip(sums, masters, moms, rates, decays)
    ]
    firsts = [efirst.T, *small[0:3], small[3].T]
    seconds = [esecond.T, *small[4:7], small[7].T]
    return (
        jnp.stack([loss_total, count_tok])[None],
        grad_size[None],
        *[u[0] for u in updated],
        *[u[1] for u in updated],
        *[a[None] for a in firsts],
        *[a[None] for a in seconds],
    )


def solution(mesh):
    weights = (
        P("blk", "work"),
        P("blk", "work"),
        P("blk", "work"),
        P(None, "blk", "work"),
        P(None, "blk"),
    )
    states = (
        P("work", "blk", None),
        P("work", "blk", None),
        P("work", "blk", None),
        P("work", None, "blk", None),
        P("work", None, "blk"),
    )
    in_specs = (
        P("work", None, None),
        P("work", None, None),
        P("work"),
        *weights,
        *weights,
        *states,
        *states,
    )
    out_specs = (P("work", None), P("work"), *weights, *weights, *states, *states)
    return jax.shard_map(local, mesh=mesh, in_specs=in_specs, out_specs=out_specs, check_vma=False)
```

```python
import functools
import math

import jax
import jax.numpy as jnp
from jax import lax
from jax.experimental import pallas as pl
from jax.experimental.pallas import tpu as pltpu
from jax.sharding import PartitionSpec as P

H = 6
HD = 48
STEP = 7

norm_eps = 1e-06
zloss_coef = 0.01
clip_limit = 0.05
beta_one = 0.9
beta_two = 0.95
adam_eps = 1e-08
decay_rate = 0.1
matrix_rate = 0.03
gain_rate = 0.3
outer_rate = 0.7
outer_mom = 0.9
rope_base = 10000.0

LOG2E = 1.0 / math.log(2.0)
LN2 = math.log(2.0)
SCALE = 1.0 / math.sqrt(HD)
BF = jnp.bfloat16
F32 = jnp.float32
NN = ((1,), (0,))
NT = ((1,), (1,))
CH = 1024
MIB = 1024 * 1024


def dot(a, b, dims=NN):
    return lax.dot_general(a, b, (dims, ((), ())), preferred_element_type=F32)


def params(mib, n=1):
    return pltpu.CompilerParams(
        dimension_semantics=("arbitrary",) * n, vmem_limit_bytes=mib * MIB
    )


COST = pl.CostEstimate(flops=1000, bytes_accessed=1000, transcendentals=0)
VMEM = pl.BlockSpec(memory_space=pltpu.VMEM)


def full(shape):
    return pl.BlockSpec(shape, lambda *_: (0,) * len(shape))


SMEM = pl.BlockSpec(memory_space=pltpu.SMEM)
ANY = pl.BlockSpec(memory_space=pl.ANY)


def call(kernel, ins, deps, **options):
    specs = options.pop("in_specs")

    def body(*refs):
        kernel(*refs[: len(ins)], *refs[len(ins) + len(deps) :])

    return pl.pallas_call(body, in_specs=[*specs, *([ANY] * len(deps))], **options)(*ins, *deps)


def pick_rows(ids_ref, s, tab, got, full_len):
    unroll = 32

    def body(i, carry):
        base = pl.multiple_of(i * unroll, unroll)
        for q in range(0, unroll, 8):
            rows = [tab[pl.ds(ids_ref[s, base + q + u], 1), :] for u in range(8)]
            got[pl.ds(pl.multiple_of(base + q, 8), 8), :] = jnp.concatenate(rows, 0)
        return carry

    lax.fori_loop(0, full_len // unroll, body, 0)


def rows_out(blk, got, outs):
    for k, out in enumerate(outs):
        width, lt = out.shape
        at = pl.multiple_of((blk ^ k) * lt, lt)
        out[...] = got[pl.ds(at, lt), 0:width].T.astype(BF)


def prep_kernel(count, vrows, nb, me_ref, ids_ref, *refs):
    pieces = refs[:count]
    et_ref, er_ref = refs[count : count + 2]
    outs = refs[count + 2 : count + 2 + nb]
    tmp, tab, got = refs[count + 2 + nb :]
    j = pl.program_id(0)
    width, lt = outs[0].shape
    for k, piece in enumerate(pieces):
        tmp[me_ref[0] ^ k] = piece[...].astype(F32)
    e = jnp.concatenate([tmp[w] for w in range(count)], 0)
    lane = lax.broadcasted_iota(jnp.int32, (width, CH), 1) + j * CH
    e = jnp.where(lane < vrows, e, 0.0)
    et_ref[...] = e.astype(BF)
    rows = e.T
    tab[pl.ds(pl.multiple_of(j * CH, CH), CH), 0:width] = rows
    er_ref[:, 0:width] = rows.astype(BF)
    row = lax.broadcasted_iota(jnp.int32, (CH, 16), 0) + j * CH
    col = lax.broadcasted_iota(jnp.int32, (CH, 16), 1)
    er_ref[:, width:] = jnp.where((row >= vrows) & (col == 0), -60000.0, 0.0).astype(BF)

    @pl.when(j == pl.num_programs(0) - 1)
    def _():
        pick_rows(ids_ref, 0, tab, got, nb * lt)
        rows_out(me_ref[1], got, outs)


def prep(me, ids, pieces, vpad, nb):
    count = len(pieces)
    rows, vrows = pieces[0].shape
    width = count * rows
    full_len = ids.shape[1]
    lt = full_len // nb
    padded = pl.cdiv(width, 128) * 128
    et, er, *outs = pl.pallas_call(
        functools.partial(prep_kernel, count, vrows, nb),
        grid=(vpad // CH,),
        in_specs=[SMEM, SMEM] + [pl.BlockSpec((rows, CH), lambda j: (0, j))] * count,
        out_specs=[
            pl.BlockSpec((width, CH), lambda j: (0, j)),
            pl.BlockSpec((CH, width + 16), lambda j: (j, 0)),
            *[full((width, lt))] * nb,
        ],
        out_shape=[
            jax.ShapeDtypeStruct((width, vpad), BF),
            jax.ShapeDtypeStruct((vpad, width + 16), BF),
            *[jax.ShapeDtypeStruct((width, lt), BF)] * nb,
        ],
        scratch_shapes=[
            pltpu.VMEM((count, rows, CH), F32),
            pltpu.VMEM((vpad, padded), F32),
            pltpu.VMEM((full_len, padded), F32),
        ],
        compiler_params=params(36),
        cost_estimate=COST,
        name="prep",
    )(me, ids, *pieces)
    return et, er, outs


def rows_kernel(ids_ref, er_ref, *refs):
    outs, (tab, got) = refs[:-2], refs[-2:]
    width = outs[0].shape[0]

    def fill(c, carry):
        here = pl.ds(pl.multiple_of(c * CH, CH), CH)
        tab[here, 0:width] = er_ref[here, 0:width].astype(F32)
        return carry

    lax.fori_loop(0, er_ref.shape[0] // CH, fill, 0)
    for s, out in enumerate(outs):
        pick_rows(ids_ref, s, tab, got, got.shape[0])
        out[...] = got[:, 0:width].T.astype(BF)


def table_rows(ids, er, width, deps=()):
    count, full_len = ids.shape
    padded = pl.cdiv(width, 128) * 128
    return call(
        rows_kernel,
        (ids, er),
        deps,
        grid=(1,),
        in_specs=[SMEM, full(er.shape)],
        out_specs=[full((width, full_len))] * count,
        out_shape=[jax.ShapeDtypeStruct((width, full_len), BF)] * count,
        scratch_shapes=[
            pltpu.VMEM((er.shape[0], padded), F32),
            pltpu.VMEM((full_len, padded), F32),
        ],
        compiler_params=params(40),
        cost_estimate=COST,
        name="table_rows",
    )


def weights_kernel(nb, nw, widths, packed, *outs):
    rows = packed.shape[1]
    straight, turned = outs[:4], outs[4:8]
    for w in range(nw):
        part = [packed[b * nw + w].astype(F32) for b in range(nb)]
        part = jnp.concatenate(part, 0)
        at = 0
        for size, out in zip(widths, straight):
            out[:, w * size : (w + 1) * size] = part[:, at : at + size].astype(BF)
            at += size
        if w == 0:
            outs[8][...] = part[:, at : at + 3]
        outs[9][0:1, w : w + 1] = part[0:1, at + 3 : at + 4]
    for out, flip in zip(straight, turned):
        flip[...] = out[...].astype(F32).T.astype(BF)


def split_weights(packed, nb, nw, widths):
    rows = packed.shape[1]
    width = nb * rows
    shapes = [(width, nw * size) for size in widths]
    outs = [(s, BF) for s in shapes] + [(s[::-1], BF) for s in shapes]
    outs += [((width, 3), F32), ((1, nw), F32)]
    return pl.pallas_call(
        functools.partial(weights_kernel, nb, nw, widths),
        in_specs=[VMEM],
        out_specs=[VMEM] * len(outs),
        out_shape=[jax.ShapeDtypeStruct(s, d) for s, d in outs],
        compiler_params=pltpu.CompilerParams(vmem_limit_bytes=24 * MIB),
        cost_estimate=COST,
        name="split_weights",
    )(packed)


def norm_t(x, gain):
    scale = lax.rsqrt(jnp.mean(x * x, 0, keepdims=True) + norm_eps)
    return x * scale * gain, scale


def norm_t_bwd(x, scale, gain, incoming):
    unit = x * scale
    inner = incoming * gain
    return scale * (inner - unit * jnp.mean(inner * unit, 0, keepdims=True)), incoming * unit


def turn(u, cosine, sine):
    rows, lt = u.shape
    half = cosine.shape[0]
    u = u.reshape(rows // (2 * half), 2, half, lt)
    a, b = u[:, 0], u[:, 1]
    return jnp.stack([a * cosine - b * sine, a * sine + b * cosine], 1).reshape(rows, lt)


def place(me, pieces, out):
    lt = pieces[0].shape[1]
    for k, piece in enumerate(pieces):
        if len(pieces) == 1:
            out[...] = piece[...]
        else:
            out[:, pl.ds(pl.multiple_of((me ^ k) * lt, lt), lt)] = piece[...]


def interleave(parts):
    while parts:
        parts = [p for p in parts if next(p, 1) is None]


def causal(lt):
    keys = lax.broadcasted_iota(jnp.int32, (lt, lt), 0)
    queries = lax.broadcasted_iota(jnp.int32, (lt, lt), 1)
    return keys <= queries


def gelu_parts(u):
    k0 = math.sqrt(2.0 / math.pi)
    square = u * u
    th = jnp.tanh(k0 * (u + 0.044715 * u * square))
    act = 0.5 * u * (1.0 + th)
    return act, th, square, k0


def gelu_slope(u, th, square, k0):
    return 0.5 * (1.0 + th) + 0.5 * u * (1.0 - th * th) * k0 * (1.0 + 3.0 * 0.044715 * square)


def trunk_fwd_kernel(count, me_ref, *refs):
    (want, wqkv_t, wo_t, wm0_t, wm1, gains, cos_ref, sin_ref) = refs[count : count + 8]
    (x0_out, qkv_out, o_out, lse_out, af_out, krow) = refs[count + 8 :]
    width, full_len = x0_out.shape
    lt = min(256, full_len)
    nb = full_len // lt
    root = math.sqrt(width)
    place(me_ref[0], refs[:count], x0_out)
    for j in range(nb):
        here = slice(j * lt, (j + 1) * lt)
        x = x0_out[:, here].astype(F32) * root
        a1, _ = norm_t(x, gains[:, 0:1])
        y = dot(wqkv_t[...], a1.astype(BF))
        cosine, sine = cos_ref[:, here], sin_ref[:, here]
        q = turn(y[:width], cosine, sine) * (SCALE * LOG2E)
        k = turn(y[width : 2 * width], cosine, sine)
        qkv_out[0:width, here] = q.astype(BF)
        qkv_out[width : 2 * width, here] = k.astype(BF)
        qkv_out[2 * width :, here] = y[2 * width :].astype(BF)
        for h in range(H):
            krow[h, here, :] = k[h * HD : (h + 1) * HD].T.astype(BF)

    lse_out[...] = jnp.zeros_like(lse_out)

    def head(h, j):
        rows = slice(h * HD, (h + 1) * HD)
        values = slice(2 * width + h * HD, 2 * width + (h + 1) * HD)
        here, before = slice(j * lt, (j + 1) * lt), slice(0, j * lt)
        q = qkv_out[rows, here]
        s_diag = jnp.where(causal(lt), dot(krow[h, here, :], q), -1e30)
        peak = jnp.max(s_diag, 0, keepdims=True)
        if j:
            s_off = dot(krow[h, before, :], q)
            peak = jnp.maximum(peak, jnp.max(s_off, 0, keepdims=True))
        yield
        p_diag = jnp.exp2(s_diag - peak)
        total = jnp.sum(p_diag, 0, keepdims=True)
        if j:
            p_off = jnp.exp2(s_off - peak)
            total = total + jnp.sum(p_off, 0, keepdims=True)
        yield
        mix = dot(qkv_out[values, here], p_diag.astype(BF))
        if j:
            mix = mix + dot(qkv_out[values, before], p_off.astype(BF))
        o_out[rows, here] = (mix / total).astype(BF)
        lse_out[h : h + 1, here] = peak + jnp.log2(total)

    for j in range(nb):
        interleave([head(h, j) for h in range(H)])

    for j in range(nb):
        here = slice(j * lt, (j + 1) * lt)
        x = x0_out[:, here].astype(F32) * root
        h1 = x + dot(wo_t[...], o_out[:, here])
        a2, _ = norm_t(h1, gains[:, 1:2])
        act = gelu_parts(dot(wm0_t[...], a2.astype(BF)))[0]
        h2 = h1 + dot(wm1[...], act.astype(BF))
        af, _ = norm_t(h2, gains[:, 2:3])
        af = (af * LOG2E).astype(BF)
        af_out[0:width, here] = af
        tail = lax.broadcasted_iota(jnp.int32, (af_out.shape[0] - width, lt), 0)
        af_out[width:, here] = jnp.where(tail == 0, 1.0, 0.0).astype(BF)
    picked = af_out[0:width, :].astype(F32) * want[...].astype(F32)
    lse_out[H : H + 1, :] = jnp.sum(picked, 0, keepdims=True)


def trunk_fwd(me, pieces, want, weights, gains, cosine, sine, deps=()):
    width, full_len = want.shape
    ins = (me, *pieces, want, *weights, gains, cosine, sine)
    shapes = [
        ((width, full_len), BF),
        ((3 * width, full_len), BF),
        ((width, full_len), BF),
        ((8, full_len), F32),
        ((width + 16, full_len), BF),
    ]
    return call(
        functools.partial(trunk_fwd_kernel, len(pieces)),
        ins,
        deps,
        in_specs=[SMEM] + [VMEM] * (len(ins) - 1),
        out_specs=[VMEM] * len(shapes),
        out_shape=[jax.ShapeDtypeStruct(s, d) for s, d in shapes],
        scratch_shapes=[pltpu.VMEM((H, full_len, HD), BF)],
        compiler_params=pltpu.CompilerParams(vmem_limit_bytes=20 * MIB),
        cost_estimate=COST,
        name="trunk_fwd",
    )


def head_kernel(er_ref, af_ref, pe_ref, po_ref, m_ref, st_ref, s_ref, za, zb, ma, mb):
    j = pl.program_id(0)
    last = pl.num_programs(0) - 1
    full_len = af_ref.shape[1]
    lt = min(512, full_len)

    def tiles(body):
        def step(t, carry):
            body(pl.ds(pl.multiple_of(t * lt, lt), lt))
            return carry

        lax.fori_loop(0, full_len // lt, step, 0)

    def product(half, z_ref, peak_ref, here):
        z = dot(er_ref[half * CH : (half + 1) * CH, :], af_ref[:, here])
        z_ref[:, here] = z
        peak_ref[:, here] = jnp.max(z.reshape(CH // 8, 8, lt), 0)

    def power(chunk, z_ref, peak_ref, p_ref, here):
        peak = jnp.max(peak_ref[:, here], 0, keepdims=True)
        p = jnp.exp2(z_ref[:, here] - peak)
        p_ref[:, here] = p.astype(BF)
        total = jnp.sum(p.reshape(CH // 8, 8, lt), 0)
        m_ref[pl.ds(chunk, 1), here] = peak
        s_ref[pl.ds(chunk, 1), here] = jnp.sum(total, 0, keepdims=True)

    @pl.when(j == 0)
    def _():
        tiles(lambda here: product(0, za, ma, here))

    @pl.when((j > 0) & (j < last))
    def _():
        def body(here):
            power(2 * j - 1, zb, mb, po_ref, here)
            product(0, za, ma, here)

        tiles(body)

    @pl.when(j < last)
    def _():
        def body(here):
            power(2 * j, za, ma, pe_ref, here)
            product(1, zb, mb, here)

        tiles(body)

    @pl.when(j == last)
    def _():
        tiles(lambda here: power(2 * j - 1, zb, mb, po_ref, here))
        peaks = m_ref[...]
        peak = jnp.max(peaks, 0, keepdims=True)
        total = jnp.sum(s_ref[...] * jnp.exp2(peaks - peak), 0, keepdims=True)
        st_ref[...] = jnp.zeros_like(st_ref)
        st_ref[0:1, :] = peak
        st_ref[1:2, :] = total


def head_first(er, af, deps=()):
    vpad, depth = er.shape
    full_len = af.shape[1]
    pairs = vpad // (2 * CH)
    shapes = [
        ((vpad // 2, full_len), BF),
        ((vpad // 2, full_len), BF),
        ((2 * pairs, full_len), F32),
        ((8, full_len), F32),
    ]
    return call(
        head_kernel,
        (er, af),
        deps,
        grid=(pairs + 1,),
        in_specs=[
            pl.BlockSpec((2 * CH, depth), lambda j: (jnp.minimum(j, pairs - 1), 0)),
            full(af.shape),
        ],
        out_specs=[
            pl.BlockSpec((CH, full_len), lambda j: (jnp.minimum(j, pairs - 1), 0)),
            pl.BlockSpec((CH, full_len), lambda j: (jnp.maximum(j - 1, 0), 0)),
            full(shapes[2][0]),
            full(shapes[3][0]),
        ],
        out_shape=[jax.ShapeDtypeStruct(s, d) for s, d in shapes],
        scratch_shapes=[
            pltpu.VMEM((2 * pairs, full_len), F32),
            pltpu.VMEM((CH, full_len), F32),
            pltpu.VMEM((CH, full_len), F32),
            pltpu.VMEM((8, full_len), F32),
            pltpu.VMEM((8, full_len), F32),
        ],
        compiler_params=params(34),
        cost_estimate=COST,
        name="head_first",
    )


def head_back_kernel(slot, nb, sc_ref, *refs):
    (pe_ref, po_ref, et_ref, af_ref, tgt_ref, m_ref, pick_ref) = refs[:7]
    stats = refs[7 : 7 + nb]
    (out, de_ref, loss_ref, acc, s_ref, d_ref) = refs[7 + nb :]
    j = pl.program_id(0)
    width, full_len = out.shape
    lt = min(256, full_len)
    valid = sc_ref[1 + slot]
    weight = valid * sc_ref[0]

    @pl.when(j == 0)
    def _():
        acc[...] = jnp.zeros_like(acc)
        top = functools.reduce(jnp.maximum, [b[0:1, :] for b in stats])
        total = sum(b[1:2, :] * jnp.exp2(b[0:1, :] - top) for b in stats)
        lse2 = top + jnp.log2(total)
        lse = lse2 * LN2
        boost = (1.0 + 2.0 * zloss_coef * lse) * weight
        pick = pick_ref[H : H + 1, :]
        s_ref[...] = jnp.exp2(m_ref[...] - lse2) * boost
        d_ref[0:1, :] = jnp.exp2(pick - lse2) * boost - weight
        loss_ref[...] = jnp.zeros_like(loss_ref)
        loss_ref[0:1, :] = (lse + zloss_coef * lse * lse) * valid
        loss_ref[1:2, :] = pick * LN2 * valid

    rows = lax.broadcasted_iota(jnp.int32, (CH, lt), 0)
    for half, p_ref in enumerate((pe_ref, po_ref)):
        chunk = 2 * j + half
        there = slice(half * CH, (half + 1) * CH)
        total = None
        for t in range(full_len // lt):
            here = slice(t * lt, (t + 1) * lt)
            grad = jnp.where(
                rows == tgt_ref[:, here] - chunk * CH,
                d_ref[0:1, here],
                p_ref[:, here].astype(F32) * s_ref[pl.ds(chunk, 1), here],
            ).astype(BF)
            acc[:, here] += dot(et_ref[:, there], grad)
            part = dot(af_ref[0:width, here], grad, NT)
            total = part if total is None else total + part
        de_ref[:, there] = (total * LN2).astype(BF)

    @pl.when(j == pl.num_programs(0) - 1)
    def _():
        out[...] = acc[...].astype(BF)


def head_back(slot, scalars, pe, po, et, af, tgt, peaks, picks, stats, deps=()):
    nb = len(stats)
    width, vpad = et.shape
    full_len = tgt.shape[1]
    half = pl.BlockSpec((CH, full_len), lambda j: (j, 0))
    wide = pl.BlockSpec((width, 2 * CH), lambda j: (0, j))
    rest = (af, tgt, peaks, picks, *stats)
    return call(
        functools.partial(head_back_kernel, slot, nb),
        (scalars, pe, po, et, *rest),
        deps,
        grid=(vpad // (2 * CH),),
        in_specs=[SMEM, half, half, wide] + [full(a.shape) for a in rest],
        out_specs=[full((width, full_len)), wide, full((8, full_len))],
        out_shape=[
            jax.ShapeDtypeStruct((width, full_len), BF),
            jax.ShapeDtypeStruct((width, vpad), BF),
            jax.ShapeDtypeStruct((8, full_len), F32),
        ],
        scratch_shapes=[
            pltpu.VMEM((width, full_len), F32),
            pltpu.VMEM(peaks.shape, F32),
            pltpu.VMEM((8, full_len), F32),
        ],
        compiler_params=params(30),
        cost_estimate=COST,
        name="head_back",
    )


def trunk_bwd_kernel(me_ref, *refs):
    (gin, x0, qkv, o_ref, lse) = refs[:5]
    (wqkv, wo, wo_t, wm0, wm0_t, wm1, wm1_t, gains, cos_ref, sin_ref) = refs[5:15]
    (dx_out, wg_out, gg_out) = refs[15:18]
    (krow, vrow, dqkv, dqkv_b, dh1_s, dh1_b, a_s, du_s, act_s, df_s, do_s, delta, wg, gg_s) = refs[18:]
    me = me_ref[0]
    width, full_len = x0.shape
    ff = du_s.shape[0]
    lt = min(256, full_len)
    nb = full_len // lt
    root = math.sqrt(width)
    gain_sums = [jnp.zeros((width, 1), F32) for _ in range(3)]
    for j in range(nb):
        here = slice(j * lt, (j + 1) * lt)
        h1 = x0[:, here].astype(F32) * root + dot(wo_t[...], o_ref[:, here])
        a2, scale = norm_t(h1, gains[:, 1:2])
        a2 = a2.astype(BF)
        a_s[:, here] = a2
        u = dot(wm0_t[...], a2)
        act, th, square, k0 = gelu_parts(u)
        act = act.astype(BF)
        act_s[:, here] = act
        h2 = h1 + dot(wm1[...], act)
        _, scale2 = norm_t(h2, 1.0)
        dh2, gg = norm_t_bwd(h2, scale2, gains[:, 2:3], gin[:, here].astype(F32))
        gain_sums[2] += jnp.sum(gg, 1, keepdims=True)
        df = dh2.astype(BF)
        df_s[:, here] = df
        du = (dot(wm1_t[...], df) * gelu_slope(u, th, square, k0)).astype(BF)
        du_s[:, here] = du
        dmid, gg = norm_t_bwd(h1, scale, gains[:, 1:2], dot(wm0[...], du))
        gain_sums[1] += jnp.sum(gg, 1, keepdims=True)
        dh1 = dh2 + dmid
        dh1_s[:, here] = dh1
        dh1b = dh1.astype(BF)
        dh1_b[:, here] = dh1b
        do = dot(wo[...], dh1b).astype(BF)
        do_s[:, here] = do
        weighed = (do.astype(F32) * o_ref[:, here].astype(F32)).reshape(H, HD, lt)
        delta[0:H, here] = jnp.sum(weighed, 1)
        for h in range(H):
            lo = width + h * HD
            krow[h, here, :] = qkv[lo : lo + HD, here].astype(F32).T.astype(BF)
            vrow[h, here, :] = qkv[lo + width : lo + width + HD, here].astype(F32).T.astype(BF)
    wg[:, 4 * width : 4 * width + ff] = dot(a_s[...], du_s[...], NT)
    wg[:, 4 * width + ff :] = dot(df_s[...], act_s[...], NT)
    wg[:, 3 * width : 4 * width] = dot(o_ref[...], dh1_b[...], NT)

    def head(h, j):
        qs, ks, vs = (pl.ds(pl.multiple_of(a + h * HD, 16), HD) for a in (0, width, 2 * width))
        here = slice(j * lt, (j + 1) * lt)
        parts = [(here, True)] + ([(slice(0, j * lt), False)] if j else [])
        q, do = qkv[qs, here], do_s[qs, here]
        lse_row, delta_row = lse[pl.ds(h, 1), here], delta[pl.ds(h, 1), here]
        scores = [(dot(krow[h, t, :], q), dot(vrow[h, t, :], do)) for t, _ in parts]
        yield
        grads = []
        for (there, diagonal), (s, dp) in zip(parts, scores):
            p = jnp.exp2(s - lse_row)
            if diagonal:
                p = jnp.where(causal(lt), p, 0.0)
            grads.append((p.astype(BF), (p * (dp - delta_row)).astype(BF)))
        yield
        dq = 0.0
        for (there, _), (pb, dsb) in zip(parts, grads):
            dq = dq + dot(qkv[ks, there], dsb)
            dk, dv = dot(q, dsb, NT), dot(do, pb, NT)
            if j == nb - 1:
                dqkv[ks, there] = dk
                dqkv[vs, there] = dv
            else:
                dqkv[ks, there] += dk
                dqkv[vs, there] += dv
        dqkv[qs, here] = dq

    def heads(i, carry):
        for j in reversed(range(nb)):
            interleave([head(i * 2 + u, j) for u in range(2)])
        return carry

    lax.fori_loop(0, H // 2, heads, 0)

    for j in range(nb):
        here = slice(j * lt, (j + 1) * lt)
        cosine, sine = cos_ref[:, here], -sin_ref[:, here]
        dq = turn(dqkv[0:width, here], cosine, sine) * SCALE
        dk = turn(dqkv[width : 2 * width, here], cosine, sine) * LN2
        dqkv_b[0:width, here] = dq.astype(BF)
        dqkv_b[width : 2 * width, here] = dk.astype(BF)
        dqkv_b[2 * width :, here] = dqkv[2 * width :, here].astype(BF)
        da1 = dot(wqkv[...], dqkv_b[:, here])
        x = x0[:, here].astype(F32) * root
        a1, scale = norm_t(x, gains[:, 0:1])
        a_s[:, here] = a1.astype(BF)
        dlow, gg = norm_t_bwd(x, scale, gains[:, 0:1], da1)
        gain_sums[0] += jnp.sum(gg, 1, keepdims=True)
        dx_out[:, here] = ((dh1_s[:, here] + dlow) * root).astype(BF)
    wg[:, 0 : 3 * width] = dot(a_s[...], dqkv_b[...], NT)
    own = wg_out.shape[0]
    wg_out[...] = wg[pl.ds(pl.multiple_of(me * own, 8), own), :]
    lane = lax.broadcasted_iota(jnp.int32, gg_s.shape, 1)
    gg_s[...] = sum(jnp.where(lane == i, gain_sums[i], 0.0) for i in range(3))
    gg_out[...] = gg_s[pl.ds(pl.multiple_of(me * own, 8), own), :]


def trunk_bwd(me, gin, saved, weights, gains, cosine, sine, own, deps=()):
    width, full_len = gin.shape
    ff = weights[3].shape[1]
    ins = (me, gin, *saved, *weights, gains, cosine, sine)
    cols = 4 * width + 2 * ff
    shapes = [((width, full_len), BF), ((own, cols), F32), ((own, 128), F32)]
    return call(
        trunk_bwd_kernel,
        ins,
        deps,
        in_specs=[SMEM] + [VMEM] * (len(ins) - 1),
        out_specs=[VMEM] * len(shapes),
        out_shape=[jax.ShapeDtypeStruct(s, d) for s, d in shapes],
        scratch_shapes=[
            pltpu.VMEM((H, full_len, HD), BF),
            pltpu.VMEM((H, full_len, HD), BF),
            pltpu.VMEM((3 * width, full_len), F32),
            pltpu.VMEM((3 * width, full_len), BF),
            pltpu.VMEM((width, full_len), F32),
            pltpu.VMEM((width, full_len), BF),
            pltpu.VMEM((width, full_len), BF),
            pltpu.VMEM((ff, full_len), BF),
            pltpu.VMEM((ff, full_len), BF),
            pltpu.VMEM((width, full_len), BF),
            pltpu.VMEM((width, full_len), BF),
            pltpu.VMEM((8, full_len), F32),
            pltpu.VMEM((width, cols), F32),
            pltpu.VMEM((width, 128), F32),
        ],
        compiler_params=pltpu.CompilerParams(vmem_limit_bytes=32 * MIB),
        cost_estimate=COST,
        name="trunk_bwd",
    )


def folded(values):
    rows, cols = values.shape
    values = jnp.sum(values.reshape(rows // 8, 8, cols), 0)
    return sum(values[:, c : c + 128] for c in range(0, cols, 128))


def token_grad_kernel(slots, tok_ref, *refs):
    de_refs, dx_refs = refs[:slots], refs[slots : 2 * slots]
    wg_refs, gg_refs = refs[2 * slots : 3 * slots], refs[3 * slots : 4 * slots]
    loss_refs = refs[4 * slots : 5 * slots]
    out_ref, wg_out, gg_out, sum_out, acc = refs[5 * slots :]
    j = pl.program_id(0)
    full_len = tok_ref.shape[2]
    lt = min(512, full_len)

    @pl.when(j == 0)
    def _():
        wg = sum(w[...] for w in wg_refs)
        gg = sum(g[...] for g in gg_refs)
        wg_out[...] = wg
        gg_out[...] = gg
        acc[...] = folded(wg * wg) + folded(gg * gg)

    rows = lax.broadcasted_iota(jnp.int32, (CH, lt), 0) + j * CH
    total = sum(d[...].astype(F32) for d in de_refs)
    for s in range(slots):
        for t in range(full_len // lt):
            here = slice(t * lt, (t + 1) * lt)
            hot = jnp.where(rows == tok_ref[s, :, here], 1.0, 0.0).astype(BF)
            total = total + dot(dx_refs[s][:, here], hot, NT)
    out_ref[...] = total.astype(BF)
    acc[...] += folded(total * total)

    @pl.when(j == pl.num_programs(0) - 1)
    def _():
        lane = lax.broadcasted_iota(jnp.int32, sum_out.shape, 1)
        pick = jnp.sum(sum(r[1:2, :] for r in loss_refs))
        lse = jnp.sum(sum(r[0:1, :] for r in loss_refs))
        tail = jnp.where(lane == 2, lse, 0.0)
        sum_out[...] = jnp.where(lane == 0, jnp.sum(acc[...]), jnp.where(lane == 1, pick, tail))


def token_grad(tok, des, dxs, wgs, ggs, losses):
    slots = len(dxs)
    width, vpad = des[0].shape
    full_len = tok.shape[2]
    blk = pl.BlockSpec((width, CH), lambda j: (0, j))
    rest = (*dxs, *wgs, *ggs, *losses)
    shapes = [(wgs[0].shape, F32), (ggs[0].shape, F32), ((8, 128), F32)]
    return pl.pallas_call(
        functools.partial(token_grad_kernel, slots),
        grid=(vpad // CH,),
        in_specs=[full(tok.shape)] + [blk] * slots + [full(a.shape) for a in rest],
        out_specs=[blk] + [full(s) for s, _ in shapes],
        out_shape=[jax.ShapeDtypeStruct((width, vpad), BF)]
        + [jax.ShapeDtypeStruct(s, d) for s, d in shapes],
        scratch_shapes=[pltpu.VMEM((8, 128), F32)],
        compiler_params=params(26),
        cost_estimate=COST,
        name="token_grad",
    )(tok, *des, *rest)


def clip_factor(sums):
    total = sum(s[0:1, 0:1] for s in sums)
    return clip_limit / jnp.maximum(jnp.sqrt(total), clip_limit)


def adam(gradient, first, second, weight):
    first = beta_one * first + (1.0 - beta_one) * gradient
    second = beta_two * second + (1.0 - beta_two) * gradient * gradient
    ratio = (first * (weight / (1.0 - beta_one**STEP))) / (
        jnp.sqrt(second * (1.0 / (1.0 - beta_two**STEP))) + adam_eps
    )
    return first, second, ratio


def adam_small_kernel(nb, widths, sc_ref, me_ref, *refs):
    factor = clip_factor(refs[:nb])
    (wg, gg, qf, of, mf, gf, qs, os_, ms, gs) = refs[nb : nb + 10]
    (qf2, of2, mf2, gf2, qs2, os2, ms2, gs2, *r_out) = refs[nb + 10 :]
    weight = sc_ref[0] * matrix_rate
    at = 0
    ratios = []
    for f, s, f2, s2 in (
        (qf, qs, qf2, qs2),
        (of, os_, of2, os2),
        (mf.at[0], ms.at[0], mf2.at[0], ms2.at[0]),
        (mf.at[1], ms.at[1], mf2.at[1], ms2.at[1]),
    ):
        here = slice(at, at + f.shape[1])
        f2[...], s2[...], ratio = adam(wg[:, here] * factor, f[...], s[...], weight)
        ratios.append(ratio)
        at = here.stop
    f2, s2, ratio = adam(gg[:, 0:3] * factor, gf[...], gs[...], sc_ref[0] * gain_rate)
    gf2[...] = f2
    gs2[...] = s2
    if not widths:
        at = 0
        for r in ratios:
            r_out[0][:, at : at + r.shape[1]] = r
            at += r.shape[1]
        r_out[0][:, at:] = jnp.zeros_like(r_out[0][:, at:])
        r_out[0][:, at : at + 3] = ratio
        return
    rows, padded = r_out[0].shape[1:]
    blank = jnp.zeros((rows, padded - sum(widths) - 3), F32)
    for w in range(2 * r_out[0].shape[0]):
        parts = [r[:, w * size : (w + 1) * size] for r, size in zip(ratios, widths)]
        piece = jnp.concatenate([*parts, ratio, blank], 1)
        rel = me_ref[0] ^ w
        for core in range(2):

            @pl.when((rel & 1) == core)
            def _():
                r_out[core][rel >> 1] = piece


def adam_small(scalars, me, sums, wg, gg, firsts, seconds, groups, widths):
    ins = (*sums, wg, gg, *firsts, *seconds)
    shapes = [a.shape for a in (*firsts, *seconds)]
    if groups:
        padded = pl.cdiv(sum(widths) + 3, 128) * 128
        shapes += [(groups // 2, wg.shape[0], padded)] * 2
    else:
        shapes.append((wg.shape[0], wg.shape[1] + 128))
    return pl.pallas_call(
        functools.partial(adam_small_kernel, len(sums), widths if groups else None),
        in_specs=[SMEM, SMEM] + [VMEM] * len(ins),
        out_specs=[VMEM] * len(shapes),
        out_shape=[jax.ShapeDtypeStruct(s, F32) for s in shapes],
        compiler_params=pltpu.CompilerParams(vmem_limit_bytes=16 * MIB),
        cost_estimate=COST,
        name="adam_small",
    )(scalars, me, *ins)


def adam_kernel(nb, grouped, kept, sc_ref, me_ref, *refs):
    sums, (g_ref, f_ref, s_ref) = refs[:nb], refs[nb : nb + 3]
    f_out, s_out, *r_out = refs[nb + 3 + kept :]
    factor = clip_factor(sums)
    first, second, ratio = adam(
        g_ref[...].astype(F32) * factor, f_ref[...], s_ref[...], sc_ref[0] * matrix_rate
    )
    f_out[...] = first
    s_out[...] = second
    if not grouped:
        r_out[0][...] = ratio.astype(BF)
        return
    groups = 2 * r_out[0].shape[0]
    rows = ratio.shape[0] // groups
    padded = r_out[0].shape[1]
    for w in range(groups):
        piece = ratio[w * rows : (w + 1) * rows]
        piece = jnp.concatenate([piece, jnp.zeros((padded - rows, CH), F32)], 0).astype(BF)
        rel = me_ref[0] ^ w
        for core in range(2):

            @pl.when((rel & 1) == core)
            def _():
                r_out[core][rel >> 1] = piece


def adam_table(scalars, me, sums, de, first, second, groups, part, kept, deps=()):
    width, rows = first.shape
    lo, hi = part
    here = min(hi * CH, rows) - lo * CH
    blk = pl.BlockSpec((width, CH), lambda j: (0, j + lo))
    shapes = [((width, rows), F32)] * 2
    specs = [blk, blk]
    if groups:
        stack = (groups // 2, pl.cdiv(width // groups, 8) * 8)
        shapes += [((*stack, here), BF)] * 2
        specs += [pl.BlockSpec((*stack, CH), lambda j: (0, 0, j))] * 2
    else:
        shapes += [((width, here), BF)]
        specs += [pl.BlockSpec((width, CH), lambda j: (0, j))]
    nb = len(sums)
    at = nb + 5
    return call(
        functools.partial(adam_kernel, nb, bool(groups), len(kept)),
        (scalars, me, *sums, de, first, second, *kept),
        deps,
        grid=(hi - lo,),
        in_specs=[SMEM, SMEM] + [full(a.shape) for a in sums] + [blk] * 3 + [ANY] * len(kept),
        out_specs=specs,
        out_shape=[jax.ShapeDtypeStruct(s, d) for s, d in shapes],
        input_output_aliases={at + i: i for i in range(len(kept))},
        compiler_params=params(24),
        cost_estimate=COST,
        name="adam_table",
    )


def swap(value, axis, size, k):
    return lax.ppermute(value, axis, [(i, i ^ k) for i in range(size)])


def share(value, axis, size):
    return [value] + [swap(value, axis, size, k) for k in range(1, size)]


def sum_pieces(pieces, axis, size):
    total = pieces[0].astype(F32)
    for k in range(1, size):
        total = total + swap(pieces[k], axis, size, k).astype(F32)
    return total.astype(BF)


def turn_first(i):
    return i ^ (2 if i % 2 == 0 else 4)


def turn_second(i):
    return i ^ (4 if i % 2 == 0 else 2)


def permute(value, axis, size, partner):
    return lax.ppermute(value, axis, [(i, partner(i)) for i in range(size)])


def gather_pieces(own, axis, core):
    x, y = swap(own, axis, 8, 2), swap(own, axis, 8, 4)
    far = permute(jnp.where(core == 0, y, x), axis, 8, turn_first)
    near = [own, x, y, far]
    others = [swap(p, axis, 8, 1) for p in near]
    return [p for pair in zip(near, others) for p in pair]


def reduce_pieces(same, other, axis, core):
    y = (same.astype(F32) + swap(other, axis, 8, 1).astype(F32)).astype(BF)
    sent = jnp.stack([jnp.where(core == 0, y[1], y[2]), y[3]])
    kept = jnp.where(core == 0, y[2], y[1])
    came = permute(sent, axis, 8, turn_first)
    relayed = (kept.astype(F32) + came[1].astype(F32)).astype(BF)
    total = y[0].astype(F32) + came[0].astype(F32)
    return total + permute(relayed, axis, 8, turn_second).astype(F32)


def outer_update(summed, total_tok, master, momentum, step_rate, decay):
    average = summed / total_tok + step_rate * decay * master
    momentum = outer_mom * momentum + average
    return (master - outer_rate * (average + outer_mom * momentum), momentum)


def local(
    tokens,
    targets,
    seq_counts,
    embed_w,
    qkv_w,
    out_w,
    mlp_w,
    gain_w,
    embed_mom,
    qkv_mom,
    out_mom,
    mlp_mom,
    gain_mom,
    embed_first,
    qkv_first,
    out_first,
    mlp_first,
    gain_first,
    embed_second,
    qkv_second,
    out_second,
    mlp_second,
    gain_second,
):
    nb = lax.axis_size("blk")
    nw = lax.axis_size("work")
    me = lax.axis_index("blk")
    wi = lax.axis_index("work")
    core = wi % 2
    me_arr = me.astype(jnp.int32).reshape(1)
    wi_arr = wi.astype(jnp.int32).reshape(1)
    slots, full_len = tokens.shape[1:]
    vrows = embed_w.shape[0]
    width = embed_first.shape[2]
    ff = mlp_first.shape[3]
    vpad = pl.cdiv(vrows, 2 * CH) * 2 * CH
    own_rows = width // nb
    paired = nw == 8

    et_own = embed_w.T.astype(BF)
    if paired:
        pieces = gather_pieces(et_own, "work", core)
    else:
        pieces = [lax.all_gather(et_own, "work", axis=0, tiled=True)]
    wi_prep = wi_arr if paired else jnp.zeros_like(wi_arr)

    cq, co, cf = qkv_w.shape[1], out_w.shape[1], mlp_w.shape[2]
    count_col = jnp.broadcast_to(seq_counts[0].astype(F32), (own_rows, 1))
    packed = jnp.concatenate([qkv_w, out_w, mlp_w[0], mlp_w[1], gain_w.T, count_col], 1)
    packed = lax.all_gather(packed.astype(BF), ("blk", "work"), axis=0, tiled=False)
    widths = (cq, co, cf, cf)
    c1, c3 = cq + co, cq + co + 2 * cf
    *weights, gains, count_row = split_weights(packed, nb, nw, widths)
    wqkv, wo, wm0, wm1, wqkv_t, wo_t, wm0_t, wm1_t = weights
    total_tok = jnp.sum(count_row) * full_len

    half = HD // 2
    frequency = rope_base ** (-jnp.arange(half).astype(F32) * 2.0 / HD)
    angles = frequency[:, None] * jnp.arange(full_len).astype(F32)[None, :]
    cosine, sine = jnp.cos(angles), jnp.sin(angles)

    count_seq = seq_counts[0]
    count_tok = (count_seq * full_len).astype(F32)
    valid = (jnp.arange(slots) < count_seq).astype(F32)

    def local_ids(ids, missing):
        ids = ids[0] - me * vrows
        return jnp.where((ids >= 0) & (ids < vrows), ids, missing)

    tok = local_ids(tokens, -1)[:, None, :]
    tgt = local_ids(targets, -1)[:, None, :]
    tok_rows = local_ids(tokens, vrows)
    tgt_rows = local_ids(targets, vrows)

    prep_ids = jnp.concatenate([wi_prep, me_arr])
    et, er, looked = prep(prep_ids, tok_rows[:1], pieces, vpad, nb)
    mine = [sum_pieces(looked, "blk", nb)]
    fwd_weights = (wqkv_t, wo_t, wm0_t, wm1)
    bwd_weights = (wqkv, wo, wo_t, wm0, wm0_t, wm1, wm1_t)
    more = table_rows(tok_rows[1:], er, width)
    wants = table_rows(tgt_rows, er, width, (mine[0], more[0], wqkv))

    def sum_blocks(value, turn):
        return lax.psum(value, "blk", axis_index_groups=[[(k + turn) % nb for k in range(nb)]])

    rows = [share(mine[0], "blk", nb)]
    rows += [[sum_blocks(m, s)] for s, m in enumerate(more)]

    saved, heads, stats, backs, des, losses = {}, {}, {}, {}, {}, {}
    scalars = jnp.concatenate([1.0 / count_tok.reshape(1), valid])

    def forward(s, *deps):
        *kept, af = trunk_fwd(
            me_arr, rows[s], wants[s], fwd_weights, gains, cosine, sine, deps
        )
        saved[s] = kept
        heads[s] = [af]

    def head(s, *deps):
        pe, po, peaks, stat = head_first(er, heads[s][0], deps)
        heads[s] += [pe, po, peaks]
        stats[s] = share(stat, "blk", nb)

    def back(s, *deps):
        af, pe, po, peaks = heads[s]
        gin, des[s], losses[s] = head_back(
            s, scalars, pe, po, et, af, tgt[s], peaks, saved[s][3], stats[s], deps
        )
        backs[s] = sum_blocks(gin, s)

    for s in range(slots):
        forward(s, *([] if s == 0 else [des[s - 2]] if s > 1 else [stats[0][0]]))
        head(s)
        if s:
            back(s - 1, stats[s][0])
    back(slots - 1, *([des[slots - 2]] if slots > 1 else []))
    dxs, wgs, ggs = [], [], []
    for s in range(slots):
        dx, wg, gg = trunk_bwd(
            me_arr,
            backs[s],
            saved[s],
            bwd_weights,
            gains,
            cosine,
            sine,
            own_rows,
            [dxs[-1]] if s else [des[slots - 1]],
        )
        dxs.append(dx)
        wgs.append(wg)
        ggs.append(gg)
    des, losses = [des[s] for s in range(slots)], [losses[s] for s in range(slots)]
    de, wg, gg, both = token_grad(tok, des, dxs, wgs, ggs, losses)
    both = share(both, "blk", nb)
    sums = sum(b[0] for b in both)
    loss_total = both[0][0, 2] - sums[1]
    grad_size = jnp.sqrt(sums[0])

    tokens_of = count_tok.reshape(1)
    groups = nw if paired else 0
    *small, = adam_small(
        tokens_of,
        wi_arr,
        both,
        wg,
        gg,
        (qkv_first[0], out_first[0], mlp_first[0], gain_first[0].T),
        (qkv_second[0], out_second[0], mlp_second[0], gain_second[0].T),
        groups,
        widths,
    )
    ratios = [r.astype(BF) for r in small[8:]]
    d1, d2, d3 = 3 * width, 4 * width, 4 * width + ff
    if paired:
        summed = reduce_pieces(*ratios, "work", core)
        parts = [summed[:, :cq], summed[:, cq : cq + co]]
        parts += [summed[:, c1 + i * cf : c1 + (i + 1) * cf] for i in range(2)]
        gain_sum = summed[:, c3 : c3 + 3].T
    else:
        summed = lax.psum(ratios[0], "work").astype(F32)
        parts = [
            lax.dynamic_slice_in_dim(summed, lo + wi * size, size, 1)
            for lo, size in ((0, cq), (d1, co), (d2, cf), (d3, cf))
        ]
        gain_sum = summed[:, d3 + ff : d3 + ff + 3].T

    first, second = embed_first[0].T, embed_second[0].T
    chunks = pl.cdiv(vrows, CH)
    kept, embed_sums, deps = (), [], [ratios[0]]
    for part in ((0, chunks // 2), (chunks // 2, chunks)):
        out = adam_table(
            tokens_of, wi_arr, both, de, first, second, groups, part, kept, deps
        )
        kept, pair = out[:2], out[2:]
        deps = []
        if paired:
            part_sum = reduce_pieces(*pair, "work", core)[: width // nw]
        else:
            part_sum = lax.psum_scatter(pair[0], "work", scatter_dimension=0, tiled=True)
        embed_sums.append(part_sum.astype(F32))
    efirst, esecond = kept

    embed_sum = jnp.concatenate(embed_sums, 1).T
    sums = (embed_sum, parts[0], parts[1], jnp.stack(parts[2:]), gain_sum)
    masters = (embed_w, qkv_w, out_w, mlp_w, gain_w)
    moms = (embed_mom, qkv_mom, out_mom, mlp_mom, gain_mom)
    rates = (matrix_rate,) * 4 + (gain_rate,)
    decays = (decay_rate,) * 4 + (0.0,)
    updated = [
        outer_update(g, total_tok, w, m, r, d)
        for g, w, m, r, d in zip(sums, masters, moms, rates, decays)
    ]
    firsts = [efirst.T, *small[0:3], small[3].T]
    seconds = [esecond.T, *small[4:7], small[7].T]
    return (
        jnp.stack([loss_total, count_tok])[None],
        grad_size[None],
        *[u[0] for u in updated],
        *[u[1] for u in updated],
        *[a[None] for a in firsts],
        *[a[None] for a in seconds],
    )


def solution(mesh):
    weights = (
        P("blk", "work"),
        P("blk", "work"),
        P("blk", "work"),
        P(None, "blk", "work"),
        P(None, "blk"),
    )
    states = (
        P("work", "blk", None),
        P("work", "blk", None),
        P("work", "blk", None),
        P("work", None, "blk", None),
        P("work", None, "blk"),
    )
    in_specs = (
        P("work", None, None),
        P("work", None, None),
        P("work"),
        *weights,
        *weights,
        *states,
        *states,
    )
    out_specs = (P("work", None), P("work"), *weights, *weights, *states, *states)
    return jax.shard_map(local, mesh=mesh, in_specs=in_specs, out_specs=out_specs, check_vma=False)
```

```python
import functools
import math

import jax
import jax.numpy as jnp
from jax import lax
from jax.experimental import pallas as pl
from jax.experimental.pallas import tpu as pltpu
from jax.sharding import PartitionSpec as P

H = 6
HD = 48
STEP = 7

norm_eps = 1e-06
zloss_coef = 0.01
clip_limit = 0.05
beta_one = 0.9
beta_two = 0.95
adam_eps = 1e-08
decay_rate = 0.1
matrix_rate = 0.03
gain_rate = 0.3
outer_rate = 0.7
outer_mom = 0.9
rope_base = 10000.0

LOG2E = 1.0 / math.log(2.0)
LN2 = math.log(2.0)
SCALE = 1.0 / math.sqrt(HD)
BF = jnp.bfloat16
F32 = jnp.float32
NN = ((1,), (0,))
NT = ((1,), (1,))
CH = 1024
MIB = 1024 * 1024


def dot(a, b, dims=NN):
    return lax.dot_general(a, b, (dims, ((), ())), preferred_element_type=F32)


def params():
    return pltpu.CompilerParams(dimension_semantics=("arbitrary",), vmem_limit_bytes=58 * MIB)


def cost(micros):
    return pl.CostEstimate(flops=0, bytes_accessed=int(micros * 1.2e6), transcendentals=0)


def full(shape):
    return pl.BlockSpec(shape, lambda *_: (0,) * len(shape))


SMEM = pl.BlockSpec(memory_space=pltpu.SMEM)
ANY = pl.BlockSpec(memory_space=pl.ANY)


def call(kernel, ins, deps, **options):
    specs = options.pop("in_specs")

    def body(*refs):
        kernel(*refs[: len(ins)], *refs[len(ins) + len(deps) :])

    return pl.pallas_call(body, in_specs=[*specs, *([ANY] * len(deps))], **options)(*ins, *deps)


def pick_rows(ids_ref, s, tab, got, full_len):
    unroll = 32

    def body(i, carry):
        base = pl.multiple_of(i * unroll, unroll)
        for q in range(0, unroll, 8):
            rows = [tab[pl.ds(ids_ref[s, base + q + u], 1), :] for u in range(8)]
            got[pl.ds(pl.multiple_of(base + q, 8), 8), :] = jnp.concatenate(rows, 0)
        return carry

    lax.fori_loop(0, full_len // unroll, body, 0)


def rows_out(blk, got, outs):
    for k, out in enumerate(outs):
        width, lt = out.shape
        at = pl.multiple_of((blk ^ k) * lt, lt)
        out[...] = got[pl.ds(at, lt), 0:width].T.astype(BF)


def prep_kernel(count, vrows, nb, me_ref, ids_ref, *refs):
    pieces = refs[:count]
    et_ref, er_ref = refs[count : count + 2]
    outs = refs[count + 2 : count + 2 + nb]
    tmp, tab, got = refs[count + 2 + nb :]
    j = pl.program_id(0)
    width, lt = outs[0].shape
    for k, piece in enumerate(pieces):
        tmp[me_ref[0] ^ k] = piece[...].astype(F32)
    e = jnp.concatenate([tmp[w] for w in range(count)], 0)
    lane = lax.broadcasted_iota(jnp.int32, (width, CH), 1) + j * CH
    e = jnp.where(lane < vrows, e, 0.0)
    et_ref[...] = e.astype(BF)
    rows = e.T
    tab[pl.ds(pl.multiple_of(j * CH, CH), CH), 0:width] = rows
    er_ref[:, 0:width] = rows.astype(BF)
    row = lax.broadcasted_iota(jnp.int32, (CH, 16), 0) + j * CH
    col = lax.broadcasted_iota(jnp.int32, (CH, 16), 1)
    er_ref[:, width:] = jnp.where((row >= vrows) & (col == 0), -60000.0, 0.0).astype(BF)

    @pl.when(j == pl.num_programs(0) - 1)
    def _():
        pick_rows(ids_ref, 0, tab, got, nb * lt)
        rows_out(me_ref[1], got, outs)


def prep(me, ids, pieces, vpad, nb):
    count = len(pieces)
    rows, vrows = pieces[0].shape
    width = count * rows
    full_len = ids.shape[1]
    lt = full_len // nb
    padded = pl.cdiv(width, 128) * 128
    et, er, *outs = pl.pallas_call(
        functools.partial(prep_kernel, count, vrows, nb),
        grid=(vpad // CH,),
        in_specs=[SMEM, SMEM] + [pl.BlockSpec((rows, CH), lambda j: (0, j))] * count,
        out_specs=[
            pl.BlockSpec((width, CH), lambda j: (0, j)),
            pl.BlockSpec((CH, width + 16), lambda j: (j, 0)),
            *[full((width, lt))] * nb,
        ],
        out_shape=[
            jax.ShapeDtypeStruct((width, vpad), BF),
            jax.ShapeDtypeStruct((vpad, width + 16), BF),
            *[jax.ShapeDtypeStruct((width, lt), BF)] * nb,
        ],
        scratch_shapes=[
            pltpu.VMEM((count, rows, CH), F32),
            pltpu.VMEM((vpad, padded), F32),
            pltpu.VMEM((full_len, padded), F32),
        ],
        compiler_params=params(),
        cost_estimate=cost(12),
        name="prep",
    )(me, ids, *pieces)
    return et, er, outs


def rows_kernel(ids_ref, er_ref, *refs):
    outs, (mark, tab, got) = refs[:-3], refs[-3:]
    width = outs[0].shape[0]
    mark[...] = jnp.zeros_like(mark)

    def fill(c, carry):
        here = pl.ds(pl.multiple_of(c * CH, CH), CH)
        tab[here, 0:width] = er_ref[here, 0:width].astype(F32)
        return carry

    lax.fori_loop(0, er_ref.shape[0] // CH, fill, 0)
    for s, out in enumerate(outs):
        pick_rows(ids_ref, s, tab, got, got.shape[0])
        out[...] = got[:, 0:width].T.astype(BF)


def table_rows(ids, er, width, deps=()):
    count, full_len = ids.shape
    padded = pl.cdiv(width, 128) * 128
    *rows, mark = call(
        rows_kernel,
        (ids, er),
        deps,
        grid=(1,),
        in_specs=[SMEM, full(er.shape)],
        out_specs=[full((width, full_len))] * count + [full((8, 128))],
        out_shape=[jax.ShapeDtypeStruct((width, full_len), BF)] * count
        + [jax.ShapeDtypeStruct((8, 128), F32)],
        scratch_shapes=[
            pltpu.VMEM((er.shape[0], padded), F32),
            pltpu.VMEM((full_len, padded), F32),
        ],
        compiler_params=params(),
        cost_estimate=cost(11),
        name="table_rows",
    )
    return rows, mark


def weights_kernel(nb, nw, widths, packed, *outs):
    rows = packed.shape[1]
    straight, turned = outs[:4], outs[4:8]
    for w in range(nw):
        part = [packed[b * nw + w].astype(F32) for b in range(nb)]
        part = jnp.concatenate(part, 0)
        at = 0
        for size, out in zip(widths, straight):
            out[:, w * size : (w + 1) * size] = part[:, at : at + size].astype(BF)
            at += size
        if w == 0:
            outs[8][...] = part[:, at : at + 3]
        outs[9][0:1, w : w + 1] = part[0:1, at + 3 : at + 4]
    for out, flip in zip(straight, turned):
        flip[...] = out[...].astype(F32).T.astype(BF)


def split_weights(packed, nb, nw, widths):
    rows = packed.shape[1]
    width = nb * rows
    shapes = [(width, nw * size) for size in widths]
    outs = [(s, BF) for s in shapes] + [(s[::-1], BF) for s in shapes]
    outs += [((width, 3), F32), ((1, nw), F32)]
    return pl.pallas_call(
        functools.partial(weights_kernel, nb, nw, widths),
        grid=(1,),
        in_specs=[full(packed.shape)],
        out_specs=[full(s) for s, _ in outs],
        out_shape=[jax.ShapeDtypeStruct(s, d) for s, d in outs],
        compiler_params=params(),
        cost_estimate=cost(3),
        name="split_weights",
    )(packed)


def norm_t(x, gain):
    scale = lax.rsqrt(jnp.mean(x * x, 0, keepdims=True) + norm_eps)
    return x * scale * gain, scale


def norm_t_bwd(x, scale, gain, incoming):
    unit = x * scale
    inner = incoming * gain
    return scale * (inner - unit * jnp.mean(inner * unit, 0, keepdims=True)), incoming * unit


def turn(u, cosine, sine):
    rows, lt = u.shape
    half = cosine.shape[0]
    u = u.reshape(rows // (2 * half), 2, half, lt)
    a, b = u[:, 0], u[:, 1]
    return jnp.stack([a * cosine - b * sine, a * sine + b * cosine], 1).reshape(rows, lt)


def place(me, pieces, out):
    lt = pieces[0].shape[1]
    for k, piece in enumerate(pieces):
        if len(pieces) == 1:
            out[...] = piece[...]
        else:
            out[:, pl.ds(pl.multiple_of((me ^ k) * lt, lt), lt)] = piece[...]


def interleave(parts):
    while parts:
        parts = [p for p in parts if next(p, 1) is None]


def causal(lt):
    keys = lax.broadcasted_iota(jnp.int32, (lt, lt), 0)
    queries = lax.broadcasted_iota(jnp.int32, (lt, lt), 1)
    return keys <= queries


def gelu_parts(u):
    k0 = math.sqrt(2.0 / math.pi)
    square = u * u
    th = jnp.tanh(k0 * (u + 0.044715 * u * square))
    act = 0.5 * u * (1.0 + th)
    return act, th, square, k0


def gelu_slope(u, th, square, k0):
    return 0.5 * (1.0 + th) + 0.5 * u * (1.0 - th * th) * k0 * (1.0 + 3.0 * 0.044715 * square)


def trunk_fwd_kernel(count, me_ref, *refs):
    (want, wqkv_t, wo_t, wm0_t, wm1, gains, cos_ref, sin_ref) = refs[count : count + 8]
    (x0_out, qkv_out, o_out, lse_out, af_out, krow) = refs[count + 8 :]
    width, full_len = x0_out.shape
    lt = min(256, full_len)
    nb = full_len // lt
    root = math.sqrt(width)
    place(me_ref[0], refs[:count], x0_out)
    for j in range(nb):
        here = slice(j * lt, (j + 1) * lt)
        x = x0_out[:, here].astype(F32) * root
        a1, _ = norm_t(x, gains[:, 0:1])
        y = dot(wqkv_t[...], a1.astype(BF))
        cosine, sine = cos_ref[:, here], sin_ref[:, here]
        q = turn(y[:width], cosine, sine) * (SCALE * LOG2E)
        k = turn(y[width : 2 * width], cosine, sine)
        qkv_out[0:width, here] = q.astype(BF)
        qkv_out[width : 2 * width, here] = k.astype(BF)
        qkv_out[2 * width :, here] = y[2 * width :].astype(BF)
        for h in range(H):
            krow[h, here, :] = k[h * HD : (h + 1) * HD].T.astype(BF)

    lse_out[...] = jnp.zeros_like(lse_out)

    def head(h, j):
        rows = slice(h * HD, (h + 1) * HD)
        values = slice(2 * width + h * HD, 2 * width + (h + 1) * HD)
        here, before = slice(j * lt, (j + 1) * lt), slice(0, j * lt)
        q = qkv_out[rows, here]
        s_diag = jnp.where(causal(lt), dot(krow[h, here, :], q), -1e30)
        peak = jnp.max(s_diag, 0, keepdims=True)
        if j:
            s_off = dot(krow[h, before, :], q)
            peak = jnp.maximum(peak, jnp.max(s_off, 0, keepdims=True))
        yield
        p_diag = jnp.exp2(s_diag - peak)
        total = jnp.sum(p_diag, 0, keepdims=True)
        if j:
            p_off = jnp.exp2(s_off - peak)
            total = total + jnp.sum(p_off, 0, keepdims=True)
        yield
        mix = dot(qkv_out[values, here], p_diag.astype(BF))
        if j:
            mix = mix + dot(qkv_out[values, before], p_off.astype(BF))
        o_out[rows, here] = (mix / total).astype(BF)
        lse_out[h : h + 1, here] = peak + jnp.log2(total)

    for j in range(nb):
        interleave([head(h, j) for h in range(H)])

    for j in range(nb):
        here = slice(j * lt, (j + 1) * lt)
        x = x0_out[:, here].astype(F32) * root
        h1 = x + dot(wo_t[...], o_out[:, here])
        a2, _ = norm_t(h1, gains[:, 1:2])
        act = gelu_parts(dot(wm0_t[...], a2.astype(BF)))[0]
        h2 = h1 + dot(wm1[...], act.astype(BF))
        af, _ = norm_t(h2, gains[:, 2:3])
        af = (af * LOG2E).astype(BF)
        af_out[0:width, here] = af
        tail = lax.broadcasted_iota(jnp.int32, (af_out.shape[0] - width, lt), 0)
        af_out[width:, here] = jnp.where(tail == 0, 1.0, 0.0).astype(BF)
    picked = af_out[0:width, :].astype(F32) * want[...].astype(F32)
    lse_out[H : H + 1, :] = jnp.sum(picked, 0, keepdims=True)


def trunk_fwd(me, pieces, want, weights, gains, cosine, sine, deps=()):
    width, full_len = want.shape
    ins = (me, *pieces, want, *weights, gains, cosine, sine)
    shapes = [
        ((width, full_len), BF),
        ((3 * width, full_len), BF),
        ((width, full_len), BF),
        ((8, full_len), F32),
        ((width + 16, full_len), BF),
    ]
    return call(
        functools.partial(trunk_fwd_kernel, len(pieces)),
        ins,
        deps,
        grid=(1,),
        in_specs=[SMEM] + [full(a.shape) for a in ins[1:]],
        out_specs=[full(s) for s, _ in shapes],
        out_shape=[jax.ShapeDtypeStruct(s, d) for s, d in shapes],
        scratch_shapes=[pltpu.VMEM((H, full_len, HD), BF)],
        compiler_params=params(),
        cost_estimate=cost(13),
        name="trunk_fwd",
    )


def head_kernel(er_ref, af_ref, pe_ref, po_ref, m_ref, st_ref, s_ref, za, zb, ma, mb):
    j = pl.program_id(0)
    last = pl.num_programs(0) - 1
    full_len = af_ref.shape[1]
    lt = min(512, full_len)

    def tiles(body):
        def step(t, carry):
            body(pl.ds(pl.multiple_of(t * lt, lt), lt))
            return carry

        lax.fori_loop(0, full_len // lt, step, 0)

    def product(half, z_ref, peak_ref, here):
        z = dot(er_ref[half * CH : (half + 1) * CH, :], af_ref[:, here])
        z_ref[:, here] = z
        peak_ref[:, here] = jnp.max(z.reshape(CH // 8, 8, lt), 0)

    def power(chunk, z_ref, peak_ref, p_ref, here):
        peak = jnp.max(peak_ref[:, here], 0, keepdims=True)
        p = jnp.exp2(z_ref[:, here] - peak)
        p_ref[:, here] = p.astype(BF)
        total = jnp.sum(p.reshape(CH // 8, 8, lt), 0)
        m_ref[pl.ds(chunk, 1), here] = peak
        s_ref[pl.ds(chunk, 1), here] = jnp.sum(total, 0, keepdims=True)

    @pl.when(j == 0)
    def _():
        tiles(lambda here: product(0, za, ma, here))

    @pl.when((j > 0) & (j < last))
    def _():
        def body(here):
            power(2 * j - 1, zb, mb, po_ref, here)
            product(0, za, ma, here)

        tiles(body)

    @pl.when(j < last)
    def _():
        def body(here):
            power(2 * j, za, ma, pe_ref, here)
            product(1, zb, mb, here)

        tiles(body)

    @pl.when(j == last)
    def _():
        tiles(lambda here: power(2 * j - 1, zb, mb, po_ref, here))
        peaks = m_ref[...]
        peak = jnp.max(peaks, 0, keepdims=True)
        total = jnp.sum(s_ref[...] * jnp.exp2(peaks - peak), 0, keepdims=True)
        st_ref[...] = jnp.zeros_like(st_ref)
        st_ref[0:1, :] = peak
        st_ref[1:2, :] = total


def head_first(er, af, deps=()):
    vpad, depth = er.shape
    full_len = af.shape[1]
    pairs = vpad // (2 * CH)
    shapes = [
        ((vpad // 2, full_len), BF),
        ((vpad // 2, full_len), BF),
        ((2 * pairs, full_len), F32),
        ((8, full_len), F32),
    ]
    return call(
        head_kernel,
        (er, af),
        deps,
        grid=(pairs + 1,),
        in_specs=[
            pl.BlockSpec((2 * CH, depth), lambda j: (jnp.minimum(j, pairs - 1), 0)),
            full(af.shape),
        ],
        out_specs=[
            pl.BlockSpec((CH, full_len), lambda j: (jnp.minimum(j, pairs - 1), 0)),
            pl.BlockSpec((CH, full_len), lambda j: (jnp.maximum(j - 1, 0), 0)),
            full(shapes[2][0]),
            full(shapes[3][0]),
        ],
        out_shape=[jax.ShapeDtypeStruct(s, d) for s, d in shapes],
        scratch_shapes=[
            pltpu.VMEM((2 * pairs, full_len), F32),
            pltpu.VMEM((CH, full_len), F32),
            pltpu.VMEM((CH, full_len), F32),
            pltpu.VMEM((8, full_len), F32),
            pltpu.VMEM((8, full_len), F32),
        ],
        compiler_params=params(),
        cost_estimate=cost(16),
        name="head_first",
    )


def head_back_kernel(slot, nb, sc_ref, *refs):
    (pe_ref, po_ref, et_ref, af_ref, tgt_ref, m_ref, pick_ref) = refs[:7]
    stats = refs[7 : 7 + nb]
    (out, de_ref, loss_ref, acc, s_ref, d_ref) = refs[7 + nb :]
    j = pl.program_id(0)
    width, full_len = out.shape
    lt = min(256, full_len)
    valid = sc_ref[1 + slot]
    weight = valid * sc_ref[0]

    @pl.when(j == 0)
    def _():
        acc[...] = jnp.zeros_like(acc)
        top = functools.reduce(jnp.maximum, [b[0:1, :] for b in stats])
        total = sum(b[1:2, :] * jnp.exp2(b[0:1, :] - top) for b in stats)
        lse2 = top + jnp.log2(total)
        lse = lse2 * LN2
        boost = (1.0 + 2.0 * zloss_coef * lse) * weight
        pick = pick_ref[H : H + 1, :]
        s_ref[...] = jnp.exp2(m_ref[...] - lse2) * boost
        d_ref[0:1, :] = jnp.exp2(pick - lse2) * boost - weight
        loss_ref[...] = jnp.zeros_like(loss_ref)
        loss_ref[0:1, :] = (lse + zloss_coef * lse * lse) * valid
        loss_ref[1:2, :] = pick * LN2 * valid

    rows = lax.broadcasted_iota(jnp.int32, (CH, lt), 0)
    for half, p_ref in enumerate((pe_ref, po_ref)):
        chunk = 2 * j + half
        there = slice(half * CH, (half + 1) * CH)
        total = None
        for t in range(full_len // lt):
            here = slice(t * lt, (t + 1) * lt)
            grad = jnp.where(
                rows == tgt_ref[:, here] - chunk * CH,
                d_ref[0:1, here],
                p_ref[:, here].astype(F32) * s_ref[pl.ds(chunk, 1), here],
            ).astype(BF)
            acc[:, here] += dot(et_ref[:, there], grad)
            part = dot(af_ref[0:width, here], grad, NT)
            total = part if total is None else total + part
        de_ref[:, there] = (total * LN2).astype(BF)

    @pl.when(j == pl.num_programs(0) - 1)
    def _():
        out[...] = acc[...].astype(BF)


def head_back(slot, scalars, pe, po, et, af, tgt, peaks, picks, stats, deps=()):
    nb = len(stats)
    width, vpad = et.shape
    full_len = tgt.shape[1]
    half = pl.BlockSpec((CH, full_len), lambda j: (j, 0))
    wide = pl.BlockSpec((width, 2 * CH), lambda j: (0, j))
    rest = (af, tgt, peaks, picks, *stats)
    return call(
        functools.partial(head_back_kernel, slot, nb),
        (scalars, pe, po, et, *rest),
        deps,
        grid=(vpad // (2 * CH),),
        in_specs=[SMEM, half, half, wide] + [full(a.shape) for a in rest],
        out_specs=[full((width, full_len)), wide, full((8, full_len))],
        out_shape=[
            jax.ShapeDtypeStruct((width, full_len), BF),
            jax.ShapeDtypeStruct((width, vpad), BF),
            jax.ShapeDtypeStruct((8, full_len), F32),
        ],
        scratch_shapes=[
            pltpu.VMEM((width, full_len), F32),
            pltpu.VMEM(peaks.shape, F32),
            pltpu.VMEM((8, full_len), F32),
        ],
        compiler_params=params(),
        cost_estimate=cost(15),
        name="head_back",
    )


def trunk_bwd_kernel(me_ref, *refs):
    (gin, x0, qkv, o_ref, lse) = refs[:5]
    (wqkv, wo, wo_t, wm0, wm0_t, wm1, wm1_t, gains, cos_ref, sin_ref) = refs[5:15]
    (dx_out, wg_out, gg_out) = refs[15:18]
    (krow, vrow, dqkv, dqkv_b, dh1_s, dh1_b, a_s, du_s, act_s, df_s, do_s, delta, wg, gg_s) = refs[18:]
    me = me_ref[0]
    width, full_len = x0.shape
    ff = du_s.shape[0]
    lt = min(256, full_len)
    nb = full_len // lt
    root = math.sqrt(width)
    gain_sums = [jnp.zeros((width, 1), F32) for _ in range(3)]
    for j in range(nb):
        here = slice(j * lt, (j + 1) * lt)
        h1 = x0[:, here].astype(F32) * root + dot(wo_t[...], o_ref[:, here])
        a2, scale = norm_t(h1, gains[:, 1:2])
        a2 = a2.astype(BF)
        a_s[:, here] = a2
        u = dot(wm0_t[...], a2)
        act, th, square, k0 = gelu_parts(u)
        act = act.astype(BF)
        act_s[:, here] = act
        h2 = h1 + dot(wm1[...], act)
        _, scale2 = norm_t(h2, 1.0)
        dh2, gg = norm_t_bwd(h2, scale2, gains[:, 2:3], gin[:, here].astype(F32))
        gain_sums[2] += jnp.sum(gg, 1, keepdims=True)
        df = dh2.astype(BF)
        df_s[:, here] = df
        du = (dot(wm1_t[...], df) * gelu_slope(u, th, square, k0)).astype(BF)
        du_s[:, here] = du
        dmid, gg = norm_t_bwd(h1, scale, gains[:, 1:2], dot(wm0[...], du))
        gain_sums[1] += jnp.sum(gg, 1, keepdims=True)
        dh1 = dh2 + dmid
        dh1_s[:, here] = dh1
        dh1b = dh1.astype(BF)
        dh1_b[:, here] = dh1b
        do = dot(wo[...], dh1b).astype(BF)
        do_s[:, here] = do
        weighed = (do.astype(F32) * o_ref[:, here].astype(F32)).reshape(H, HD, lt)
        delta[0:H, here] = jnp.sum(weighed, 1)
        for h in range(H):
            lo = width + h * HD
            krow[h, here, :] = qkv[lo : lo + HD, here].astype(F32).T.astype(BF)
            vrow[h, here, :] = qkv[lo + width : lo + width + HD, here].astype(F32).T.astype(BF)
    wg[:, 4 * width : 4 * width + ff] = dot(a_s[...], du_s[...], NT)
    wg[:, 4 * width + ff :] = dot(df_s[...], act_s[...], NT)
    wg[:, 3 * width : 4 * width] = dot(o_ref[...], dh1_b[...], NT)

    def head(h, j):
        qs, ks, vs = (pl.ds(pl.multiple_of(a + h * HD, 16), HD) for a in (0, width, 2 * width))
        here = slice(j * lt, (j + 1) * lt)
        parts = [(here, True)] + ([(slice(0, j * lt), False)] if j else [])
        q, do = qkv[qs, here], do_s[qs, here]
        lse_row, delta_row = lse[pl.ds(h, 1), here], delta[pl.ds(h, 1), here]
        scores = [(dot(krow[h, t, :], q), dot(vrow[h, t, :], do)) for t, _ in parts]
        yield
        grads = []
        for (there, diagonal), (s, dp) in zip(parts, scores):
            p = jnp.exp2(s - lse_row)
            if diagonal:
                p = jnp.where(causal(lt), p, 0.0)
            grads.append((p.astype(BF), (p * (dp - delta_row)).astype(BF)))
        yield
        dq = 0.0
        for (there, _), (pb, dsb) in zip(parts, grads):
            dq = dq + dot(qkv[ks, there], dsb)
            dk, dv = dot(q, dsb, NT), dot(do, pb, NT)
            if j == nb - 1:
                dqkv[ks, there] = dk
                dqkv[vs, there] = dv
            else:
                dqkv[ks, there] += dk
                dqkv[vs, there] += dv
        dqkv[qs, here] = dq

    def heads(i, carry):
        for j in reversed(range(nb)):
            interleave([head(i * 2 + u, j) for u in range(2)])
        return carry

    lax.fori_loop(0, H // 2, heads, 0)

    for j in range(nb):
        here = slice(j * lt, (j + 1) * lt)
        cosine, sine = cos_ref[:, here], -sin_ref[:, here]
        dq = turn(dqkv[0:width, here], cosine, sine) * SCALE
        dk = turn(dqkv[width : 2 * width, here], cosine, sine) * LN2
        dqkv_b[0:width, here] = dq.astype(BF)
        dqkv_b[width : 2 * width, here] = dk.astype(BF)
        dqkv_b[2 * width :, here] = dqkv[2 * width :, here].astype(BF)
        da1 = dot(wqkv[...], dqkv_b[:, here])
        x = x0[:, here].astype(F32) * root
        a1, scale = norm_t(x, gains[:, 0:1])
        a_s[:, here] = a1.astype(BF)
        dlow, gg = norm_t_bwd(x, scale, gains[:, 0:1], da1)
        gain_sums[0] += jnp.sum(gg, 1, keepdims=True)
        dx_out[:, here] = ((dh1_s[:, here] + dlow) * root).astype(BF)
    wg[:, 0 : 3 * width] = dot(a_s[...], dqkv_b[...], NT)
    own = wg_out.shape[0]
    wg_out[...] = wg[pl.ds(pl.multiple_of(me * own, 8), own), :]
    lane = lax.broadcasted_iota(jnp.int32, gg_s.shape, 1)
    gg_s[...] = sum(jnp.where(lane == i, gain_sums[i], 0.0) for i in range(3))
    gg_out[...] = gg_s[pl.ds(pl.multiple_of(me * own, 8), own), :]


def trunk_bwd(me, gin, saved, weights, gains, cosine, sine, own, deps=()):
    width, full_len = gin.shape
    ff = weights[3].shape[1]
    ins = (me, gin, *saved, *weights, gains, cosine, sine)
    cols = 4 * width + 2 * ff
    shapes = [((width, full_len), BF), ((own, cols), F32), ((own, 128), F32)]
    return call(
        trunk_bwd_kernel,
        ins,
        deps,
        grid=(1,),
        in_specs=[SMEM] + [full(a.shape) for a in ins[1:]],
        out_specs=[full(s) for s, _ in shapes],
        out_shape=[jax.ShapeDtypeStruct(s, d) for s, d in shapes],
        scratch_shapes=[
            pltpu.VMEM((H, full_len, HD), BF),
            pltpu.VMEM((H, full_len, HD), BF),
            pltpu.VMEM((3 * width, full_len), F32),
            pltpu.VMEM((3 * width, full_len), BF),
            pltpu.VMEM((width, full_len), F32),
            pltpu.VMEM((width, full_len), BF),
            pltpu.VMEM((width, full_len), BF),
            pltpu.VMEM((ff, full_len), BF),
            pltpu.VMEM((ff, full_len), BF),
            pltpu.VMEM((width, full_len), BF),
            pltpu.VMEM((width, full_len), BF),
            pltpu.VMEM((8, full_len), F32),
            pltpu.VMEM((width, cols), F32),
            pltpu.VMEM((width, 128), F32),
        ],
        compiler_params=params(),
        cost_estimate=cost(24),
        name="trunk_bwd",
    )


def folded(values):
    rows, cols = values.shape
    values = jnp.sum(values.reshape(rows // 8, 8, cols), 0)
    return sum(values[:, c : c + 128] for c in range(0, cols, 128))


def token_grad_kernel(slots, tok_ref, *refs):
    de_refs, dx_refs = refs[:slots], refs[slots : 2 * slots]
    wg_refs, gg_refs = refs[2 * slots : 3 * slots], refs[3 * slots : 4 * slots]
    loss_refs = refs[4 * slots : 5 * slots]
    out_ref, wg_out, gg_out, sum_out, acc = refs[5 * slots :]
    j = pl.program_id(0)
    full_len = tok_ref.shape[2]
    lt = min(512, full_len)

    @pl.when(j == 0)
    def _():
        wg = sum(w[...] for w in wg_refs)
        gg = sum(g[...] for g in gg_refs)
        wg_out[...] = wg
        gg_out[...] = gg
        acc[...] = folded(wg * wg) + folded(gg * gg)

    rows = lax.broadcasted_iota(jnp.int32, (CH, lt), 0) + j * CH
    total = sum(d[...].astype(F32) for d in de_refs)
    for s in range(slots):
        for t in range(full_len // lt):
            here = slice(t * lt, (t + 1) * lt)
            hot = jnp.where(rows == tok_ref[s, :, here], 1.0, 0.0).astype(BF)
            total = total + dot(dx_refs[s][:, here], hot, NT)
    out_ref[...] = total.astype(BF)
    acc[...] += folded(total * total)

    @pl.when(j == pl.num_programs(0) - 1)
    def _():
        lane = lax.broadcasted_iota(jnp.int32, sum_out.shape, 1)
        pick = jnp.sum(sum(r[1:2, :] for r in loss_refs))
        lse = jnp.sum(sum(r[0:1, :] for r in loss_refs))
        tail = jnp.where(lane == 2, lse, 0.0)
        sum_out[...] = jnp.where(lane == 0, jnp.sum(acc[...]), jnp.where(lane == 1, pick, tail))


def token_grad(tok, des, dxs, wgs, ggs, losses):
    slots = len(dxs)
    width, vpad = des[0].shape
    full_len = tok.shape[2]
    blk = pl.BlockSpec((width, CH), lambda j: (0, j))
    rest = (*dxs, *wgs, *ggs, *losses)
    shapes = [(wgs[0].shape, F32), (ggs[0].shape, F32), ((8, 128), F32)]
    return pl.pallas_call(
        functools.partial(token_grad_kernel, slots),
        grid=(vpad // CH,),
        in_specs=[full(tok.shape)] + [blk] * slots + [full(a.shape) for a in rest],
        out_specs=[blk] + [full(s) for s, _ in shapes],
        out_shape=[jax.ShapeDtypeStruct((width, vpad), BF)]
        + [jax.ShapeDtypeStruct(s, d) for s, d in shapes],
        scratch_shapes=[pltpu.VMEM((8, 128), F32)],
        compiler_params=params(),
        cost_estimate=cost(19),
        name="token_grad",
    )(tok, *des, *rest)


def clip_factor(sums):
    total = sum(s[0:1, 0:1] for s in sums)
    return clip_limit / jnp.maximum(jnp.sqrt(total), clip_limit)


def adam(gradient, first, second, weight):
    first = beta_one * first + (1.0 - beta_one) * gradient
    second = beta_two * second + (1.0 - beta_two) * gradient * gradient
    ratio = (first * (weight / (1.0 - beta_one**STEP))) / (
        jnp.sqrt(second * (1.0 / (1.0 - beta_two**STEP))) + adam_eps
    )
    return first, second, ratio


def adam_small_kernel(nb, widths, sc_ref, me_ref, *refs):
    factor = clip_factor(refs[:nb])
    (wg, gg, qf, of, mf, gf, qs, os_, ms, gs) = refs[nb : nb + 10]
    (qf2, of2, mf2, gf2, qs2, os2, ms2, gs2, *r_out) = refs[nb + 10 :]
    weight = sc_ref[0] * matrix_rate
    at = 0
    ratios = []
    for f, s, f2, s2 in (
        (qf, qs, qf2, qs2),
        (of, os_, of2, os2),
        (mf.at[0], ms.at[0], mf2.at[0], ms2.at[0]),
        (mf.at[1], ms.at[1], mf2.at[1], ms2.at[1]),
    ):
        here = slice(at, at + f.shape[1])
        f2[...], s2[...], ratio = adam(wg[:, here] * factor, f[...], s[...], weight)
        ratios.append(ratio)
        at = here.stop
    f2, s2, ratio = adam(gg[:, 0:3] * factor, gf[...], gs[...], sc_ref[0] * gain_rate)
    gf2[...] = f2
    gs2[...] = s2
    if not widths:
        at = 0
        for r in ratios:
            r_out[0][:, at : at + r.shape[1]] = r
            at += r.shape[1]
        r_out[0][:, at:] = jnp.zeros_like(r_out[0][:, at:])
        r_out[0][:, at : at + 3] = ratio
        return
    rows, cols = ratio.shape[0] // 2, r_out[0].shape[2] // 2
    blank = jnp.zeros((2 * rows, cols - sum(widths) - 3), F32)
    below = jnp.zeros((r_out[0].shape[1] - rows, 2 * cols), F32)
    for w in range(2 * r_out[0].shape[0]):
        parts = [r[:, w * size : (w + 1) * size] for r, size in zip(ratios, widths)]
        piece = jnp.concatenate([*parts, ratio, blank], 1)
        piece = jnp.concatenate([piece[:rows], piece[rows:]], 1)
        piece = jnp.concatenate([piece, below], 0).astype(BF)
        rel = me_ref[0] ^ w
        for core in range(2):

            @pl.when((rel & 1) == core)
            def _():
                r_out[core][rel >> 1] = piece


def adam_small(scalars, me, sums, wg, gg, firsts, seconds, groups, widths, deps=()):
    ins = (*sums, wg, gg, *firsts, *seconds)
    shapes = [(a.shape, F32) for a in (*firsts, *seconds)]
    if groups:
        cols = pl.cdiv(sum(widths) + 3, 128) * 128
        rows = pl.cdiv(wg.shape[0] // 2, 8) * 8
        shapes += [((groups // 2, rows, 2 * cols), BF)] * 2
    else:
        shapes.append(((wg.shape[0], wg.shape[1] + 128), F32))
    return call(
        functools.partial(adam_small_kernel, len(sums), widths if groups else None),
        (scalars, me, *ins),
        deps,
        grid=(1,),
        in_specs=[SMEM, SMEM] + [full(a.shape) for a in ins],
        out_specs=[full(s) for s, _ in shapes],
        out_shape=[jax.ShapeDtypeStruct(s, d) for s, d in shapes],
        compiler_params=params(),
        cost_estimate=cost(3),
        name="adam_small",
    )


def adam_kernel(nb, grouped, kept, through, sc_ref, me_ref, *refs):
    sums, (g_ref, f_ref, s_ref) = refs[:nb], refs[nb : nb + 3]
    f_out, s_out, *r_out = refs[nb + 3 + kept + through : len(refs) - through]
    factor = clip_factor(sums)
    first, second, ratio = adam(
        g_ref[...].astype(F32) * factor, f_ref[...], s_ref[...], sc_ref[0] * matrix_rate
    )
    f_out[...] = first
    s_out[...] = second
    if not grouped:
        r_out[0][...] = ratio.astype(BF)
        return
    groups = 2 * r_out[0].shape[0]
    rows = ratio.shape[0] // groups
    padded = r_out[0].shape[1]
    for w in range(groups):
        piece = ratio[w * rows : (w + 1) * rows]
        piece = jnp.concatenate([piece, jnp.zeros((padded - rows, CH), F32)], 0).astype(BF)
        rel = me_ref[0] ^ w
        for core in range(2):

            @pl.when((rel & 1) == core)
            def _():
                r_out[core][rel >> 1] = piece


def adam_table(scalars, me, sums, de, first, second, groups, part, kept=(), through=(), deps=()):
    width, rows = first.shape
    lo, hi = part
    here = min(hi * CH, rows) - lo * CH
    blk = pl.BlockSpec((width, CH), lambda j: (0, j + lo))
    shapes = [((width, rows), F32)] * 2
    specs = [blk, blk]
    if groups:
        stack = (groups // 2, pl.cdiv(width // groups, 8) * 8)
        shapes += [((*stack, here), BF)] * 2
        specs += [pl.BlockSpec((*stack, CH), lambda j: (0, 0, j))] * 2
    else:
        shapes += [((width, here), BF)]
        specs += [pl.BlockSpec((width, CH), lambda j: (0, j))]
    nb = len(sums)
    at, count = nb + 5, len(shapes)
    aliases = {at + i: i for i in range(len(kept))}
    aliases |= {at + len(kept) + i: count + i for i in range(len(through))}
    shapes += [(a.shape, a.dtype) for a in through]
    unread = [ANY] * (len(kept) + len(through))
    return call(
        functools.partial(adam_kernel, nb, bool(groups), len(kept), len(through)),
        (scalars, me, *sums, de, first, second, *kept, *through),
        deps,
        grid=(hi - lo,),
        in_specs=[SMEM, SMEM] + [full(a.shape) for a in sums] + [blk] * 3 + unread,
        out_specs=specs + [ANY] * len(through),
        out_shape=[jax.ShapeDtypeStruct(s, d) for s, d in shapes],
        input_output_aliases=aliases,
        compiler_params=params(),
        cost_estimate=cost(10),
        name="adam_table",
    )


def swap(value, axis, size, k):
    return lax.ppermute(value, axis, [(i, i ^ k) for i in range(size)])


def share(value, axis, size):
    return [value] + [swap(value, axis, size, k) for k in range(1, size)]


def sum_pieces(pieces, axis, size):
    total = pieces[0].astype(F32)
    for k in range(1, size):
        total = total + swap(pieces[k], axis, size, k).astype(F32)
    return total.astype(BF)


def turn_first(i):
    return i ^ (2 if i % 2 == 0 else 4)


def turn_second(i):
    return i ^ (4 if i % 2 == 0 else 2)


def permute(value, axis, size, partner):
    return lax.ppermute(value, axis, [(i, partner(i)) for i in range(size)])


def gather_pieces(own, axis, core):
    x, y = swap(own, axis, 8, 2), swap(own, axis, 8, 4)
    far = permute(jnp.where(core == 0, y, x), axis, 8, turn_first)
    near = [own, x, y, far]
    others = [swap(p, axis, 8, 1) for p in near]
    return [p for pair in zip(near, others) for p in pair]


def reduce_first(same, other, axis, core):
    y = (same.astype(F32) + swap(other, axis, 8, 1).astype(F32)).astype(BF)
    sent = jnp.stack([jnp.where(core == 0, y[1], y[2]), y[3]])
    return sent, jnp.where(core == 0, y[2], y[1]), y[0]


def reduce_last(sent, kept, own, axis):
    came = permute(sent, axis, 8, turn_first)
    relayed = (kept.astype(F32) + came[1].astype(F32)).astype(BF)
    total = own.astype(F32) + came[0].astype(F32)
    return total + permute(relayed, axis, 8, turn_second).astype(F32)


def outer_update(summed, total_tok, master, momentum, step_rate, decay):
    average = summed / total_tok + step_rate * decay * master
    momentum = outer_mom * momentum + average
    return (master - outer_rate * (average + outer_mom * momentum), momentum)


def local(
    tokens,
    targets,
    seq_counts,
    embed_w,
    qkv_w,
    out_w,
    mlp_w,
    gain_w,
    embed_mom,
    qkv_mom,
    out_mom,
    mlp_mom,
    gain_mom,
    embed_first,
    qkv_first,
    out_first,
    mlp_first,
    gain_first,
    embed_second,
    qkv_second,
    out_second,
    mlp_second,
    gain_second,
):
    nb = lax.axis_size("blk")
    nw = lax.axis_size("work")
    me = lax.axis_index("blk")
    wi = lax.axis_index("work")
    core = wi % 2
    me_arr = me.astype(jnp.int32).reshape(1)
    wi_arr = wi.astype(jnp.int32).reshape(1)
    slots, full_len = tokens.shape[1:]
    vrows = embed_w.shape[0]
    width = embed_first.shape[2]
    ff = mlp_first.shape[3]
    vpad = pl.cdiv(vrows, 2 * CH) * 2 * CH
    own_rows = width // nb
    paired = nw == 8

    et_own = embed_w.T.astype(BF)
    if paired:
        pieces = gather_pieces(et_own, "work", core)
    else:
        pieces = [lax.all_gather(et_own, "work", axis=0, tiled=True)]
    wi_prep = wi_arr if paired else jnp.zeros_like(wi_arr)

    cq, co, cf = qkv_w.shape[1], out_w.shape[1], mlp_w.shape[2]
    count_col = jnp.broadcast_to(seq_counts[0].astype(F32), (own_rows, 1))
    packed = jnp.concatenate([qkv_w, out_w, mlp_w[0], mlp_w[1], gain_w.T, count_col], 1)
    packed = lax.all_gather(packed.astype(BF), ("blk", "work"), axis=0, tiled=False)
    widths = (cq, co, cf, cf)
    c1, c3 = cq + co, cq + co + 2 * cf
    *weights, gains, count_row = split_weights(packed, nb, nw, widths)
    wqkv, wo, wm0, wm1, wqkv_t, wo_t, wm0_t, wm1_t = weights
    total_tok = jnp.sum(count_row) * full_len

    half = HD // 2
    frequency = rope_base ** (-jnp.arange(half).astype(F32) * 2.0 / HD)
    angles = frequency[:, None] * jnp.arange(full_len).astype(F32)[None, :]
    cosine, sine = jnp.cos(angles), jnp.sin(angles)

    count_seq = seq_counts[0]
    count_tok = (count_seq * full_len).astype(F32)
    valid = (jnp.arange(slots) < count_seq).astype(F32)

    def local_ids(ids, missing):
        ids = ids[0] - me * vrows
        return jnp.where((ids >= 0) & (ids < vrows), ids, missing)

    tok = local_ids(tokens, -1)[:, None, :]
    tgt = local_ids(targets, -1)[:, None, :]
    tok_rows = local_ids(tokens, vrows)
    tgt_rows = local_ids(targets, vrows)

    prep_ids = jnp.concatenate([wi_prep, me_arr])
    et, er, looked = prep(prep_ids, tok_rows[:1], pieces, vpad, nb)
    mine = [sum_pieces(looked, "blk", nb)]
    fwd_weights = (wqkv_t, wo_t, wm0_t, wm1)
    bwd_weights = (wqkv, wo, wo_t, wm0, wm0_t, wm1, wm1_t)
    more, mark = table_rows(tok_rows[1:], er, width)
    def sum_blocks(value, turn):
        return lax.psum(value, "blk", axis_index_groups=[[(k + turn) % nb for k in range(nb)]])

    rows = [share(mine[0], "blk", nb)]
    wants, _ = table_rows(tgt_rows, er, width, (mark, wqkv))
    rows += [[sum_blocks(m, s)] for s, m in enumerate(more)]

    saved, heads, stats, backs, des, losses = {}, {}, {}, {}, {}, {}
    scalars = jnp.concatenate([1.0 / count_tok.reshape(1), valid])

    def forward(s, *deps):
        *kept, af = trunk_fwd(
            me_arr, rows[s], wants[s], fwd_weights, gains, cosine, sine, deps
        )
        saved[s] = kept
        heads[s] = [af]

    def head(s, *deps):
        pe, po, peaks, stat = head_first(er, heads[s][0], deps)
        heads[s] += [pe, po, peaks]
        stats[s] = share(stat, "blk", nb)

    def back(s, *deps):
        af, pe, po, peaks = heads[s]
        gin, des[s], losses[s] = head_back(
            s, scalars, pe, po, et, af, tgt[s], peaks, saved[s][3], stats[s], deps
        )
        backs[s] = sum_blocks(gin, s)

    for s in range(slots):
        forward(s, *([] if s == 0 else [des[s - 2]] if s > 1 else [stats[0][0]]))
        head(s)
        if s:
            back(s - 1, stats[s][0])
    back(slots - 1, *([des[slots - 2]] if slots > 1 else []))
    dxs, wgs, ggs = [], [], []
    for s in range(slots):
        dx, wg, gg = trunk_bwd(
            me_arr,
            backs[s],
            saved[s],
            bwd_weights,
            gains,
            cosine,
            sine,
            own_rows,
            [dxs[-1]] if s else [des[slots - 1]],
        )
        dxs.append(dx)
        wgs.append(wg)
        ggs.append(gg)
    des, losses = [des[s] for s in range(slots)], [losses[s] for s in range(slots)]
    de, wg, gg, both = token_grad(tok, des, dxs, wgs, ggs, losses)
    both = share(both, "blk", nb)
    sums = sum(b[0] for b in both)
    loss_total = both[0][0, 2] - sums[1]
    grad_size = jnp.sqrt(sums[0])

    tokens_of = count_tok.reshape(1)
    groups = nw if paired else 0
    first, second = embed_first[0].T, embed_second[0].T
    chunks = pl.cdiv(vrows, CH)
    cut = (5 * chunks + 7) // 8
    f0, s0, *pair = adam_table(
        tokens_of, wi_arr, both, de, first, second, groups, (0, cut)
    )
    p, q = pair[0], pair[-1]
    small = adam_small(
        tokens_of,
        wi_arr,
        both,
        wg,
        gg,
        (qkv_first[0], out_first[0], mlp_first[0], gain_first[0].T),
        (qkv_second[0], out_second[0], mlp_second[0], gain_second[0].T),
        groups,
        widths,
        [p],
    )
    waits, through = [small[8]], ()
    if paired:
        begun = reduce_first(p, q, "work", core)
        through = (begun[2],)
    efirst, esecond, *pair = adam_table(
        tokens_of, wi_arr, both, de, first, second, groups, (cut, chunks), (f0, s0), through, waits
    )
    d1, d2, d3 = 3 * width, 4 * width, 4 * width + ff
    if paired:
        pair, through = pair[:2], pair[2:]
        begun = (*begun[:2], through[0])
        pair = [jnp.concatenate([a, b], 2) for a, b in zip(pair, small[8:])]
        embed_sums = [begun, reduce_first(*pair, "work", core)]
        embed_sums = [reduce_last(*b, "work") for b in embed_sums]
        summed = embed_sums[1][: own_rows // 2, vrows - cut * CH :]
        embed_sums = [e[: width // nw] for e in embed_sums]
        embed_sums[1] = embed_sums[1][:, : vrows - cut * CH]
        summed = jnp.concatenate(jnp.split(summed, 2, 1), 0)
        parts = [summed[:, :cq], summed[:, cq : cq + co]]
        parts += [summed[:, c1 + i * cf : c1 + (i + 1) * cf] for i in range(2)]
        gain_sum = summed[:, c3 : c3 + 3].T
    else:
        embed_sums = [
            lax.psum_scatter(r, "work", scatter_dimension=0, tiled=True).astype(F32)
            for r in (p, pair[0])
        ]
        summed = lax.psum(small[8].astype(BF), "work").astype(F32)
        parts = [
            lax.dynamic_slice_in_dim(summed, lo + wi * size, size, 1)
            for lo, size in ((0, cq), (d1, co), (d2, cf), (d3, cf))
        ]
        gain_sum = summed[:, d3 + ff : d3 + ff + 3].T

    embed_sum = jnp.concatenate(embed_sums, 1).T
    sums = (embed_sum, parts[0], parts[1], jnp.stack(parts[2:]), gain_sum)
    masters = (embed_w, qkv_w, out_w, mlp_w, gain_w)
    moms = (embed_mom, qkv_mom, out_mom, mlp_mom, gain_mom)
    rates = (matrix_rate,) * 4 + (gain_rate,)
    decays = (decay_rate,) * 4 + (0.0,)
    updated = [
        outer_update(g, total_tok, w, m, r, d)
        for g, w, m, r, d in zip(sums, masters, moms, rates, decays)
    ]
    firsts = [efirst.T, *small[0:3], small[3].T]
    seconds = [esecond.T, *small[4:7], small[7].T]
    return (
        jnp.stack([loss_total, count_tok])[None],
        grad_size[None],
        *[u[0] for u in updated],
        *[u[1] for u in updated],
        *[a[None] for a in firsts],
        *[a[None] for a in seconds],
    )


def solution(mesh):
    weights = (
        P("blk", "work"),
        P("blk", "work"),
        P("blk", "work"),
        P(None, "blk", "work"),
        P(None, "blk"),
    )
    states = (
        P("work", "blk", None),
        P("work", "blk", None),
        P("work", "blk", None),
        P("work", None, "blk", None),
        P("work", None, "blk"),
    )
    in_specs = (
        P("work", None, None),
        P("work", None, None),
        P("work"),
        *weights,
        *weights,
        *states,
        *states,
    )
    out_specs = (P("work", None), P("work"), *weights, *weights, *states, *states)
    return jax.shard_map(local, mesh=mesh, in_specs=in_specs, out_specs=out_specs, check_vma=False)
```

```python
import functools
import math

import jax
import jax.numpy as jnp
from jax import lax
from jax.experimental import pallas as pl
from jax.experimental.pallas import tpu as pltpu
from jax.sharding import PartitionSpec as P

H = 6
HD = 48
STEP = 7

norm_eps = 1e-06
zloss_coef = 0.01
clip_limit = 0.05
beta_one = 0.9
beta_two = 0.95
adam_eps = 1e-08
decay_rate = 0.1
matrix_rate = 0.03
gain_rate = 0.3
outer_rate = 0.7
outer_mom = 0.9
rope_base = 10000.0

LOG2E = 1.0 / math.log(2.0)
LN2 = math.log(2.0)
SCALE = 1.0 / math.sqrt(HD)
BF = jnp.bfloat16
F32 = jnp.float32
NN = ((1,), (0,))
NT = ((1,), (1,))
CH = 1024
MIB = 1024 * 1024


def dot(a, b, dims=NN):
    return lax.dot_general(a, b, (dims, ((), ())), preferred_element_type=F32)


def params():
    return pltpu.CompilerParams(dimension_semantics=("arbitrary",), vmem_limit_bytes=58 * MIB)


def cost(micros):
    return pl.CostEstimate(flops=0, bytes_accessed=int(micros * 1.2e6), transcendentals=0)


def full(shape):
    return pl.BlockSpec(shape, lambda *_: (0,) * len(shape))


SMEM = pl.BlockSpec(memory_space=pltpu.SMEM)
ANY = pl.BlockSpec(memory_space=pl.ANY)


def call(kernel, ins, deps, **options):
    specs = options.pop("in_specs")

    def body(*refs):
        kernel(*refs[: len(ins)], *refs[len(ins) + len(deps) :])

    return pl.pallas_call(body, in_specs=[*specs, *([ANY] * len(deps))], **options)(*ins, *deps)


def pick_rows(ids_ref, s, tab, got, full_len):
    unroll = 32

    def body(i, carry):
        base = pl.multiple_of(i * unroll, unroll)
        for q in range(0, unroll, 8):
            rows = [tab[pl.ds(ids_ref[s, base + q + u], 1), :] for u in range(8)]
            got[pl.ds(pl.multiple_of(base + q, 8), 8), :] = jnp.concatenate(rows, 0)
        return carry

    lax.fori_loop(0, full_len // unroll, body, 0)


def rows_out(blk, got, outs):
    for k, out in enumerate(outs):
        width, lt = out.shape
        at = pl.multiple_of((blk ^ k) * lt, lt)
        out[...] = got[pl.ds(at, lt), 0:width].T.astype(BF)


def prep_kernel(count, vrows, nb, me_ref, ids_ref, *refs):
    pieces = refs[:count]
    et_ref, er_ref = refs[count : count + 2]
    outs = refs[count + 2 : count + 2 + nb]
    tmp, tab, got = refs[count + 2 + nb :]
    j = pl.program_id(0)
    width, lt = outs[0].shape
    for k, piece in enumerate(pieces):
        tmp[me_ref[0] ^ k] = piece[...].astype(F32)
    e = jnp.concatenate([tmp[w] for w in range(count)], 0)
    lane = lax.broadcasted_iota(jnp.int32, (width, CH), 1) + j * CH
    e = jnp.where(lane < vrows, e, 0.0)
    et_ref[...] = e.astype(BF)
    rows = e.T
    tab[pl.ds(pl.multiple_of(j * CH, CH), CH), 0:width] = rows
    er_ref[:, 0:width] = rows.astype(BF)
    row = lax.broadcasted_iota(jnp.int32, (CH, 16), 0) + j * CH
    col = lax.broadcasted_iota(jnp.int32, (CH, 16), 1)
    er_ref[:, width:] = jnp.where((row >= vrows) & (col == 0), -60000.0, 0.0).astype(BF)

    @pl.when(j == pl.num_programs(0) - 1)
    def _():
        pick_rows(ids_ref, 0, tab, got, nb * lt)
        rows_out(me_ref[1], got, outs)


def prep(me, ids, pieces, vpad, nb):
    count = len(pieces)
    rows, vrows = pieces[0].shape
    width = count * rows
    full_len = ids.shape[1]
    lt = full_len // nb
    padded = pl.cdiv(width, 128) * 128
    et, er, *outs = pl.pallas_call(
        functools.partial(prep_kernel, count, vrows, nb),
        grid=(vpad // CH,),
        in_specs=[SMEM, SMEM] + [pl.BlockSpec((rows, CH), lambda j: (0, j))] * count,
        out_specs=[
            pl.BlockSpec((width, CH), lambda j: (0, j)),
            pl.BlockSpec((CH, width + 16), lambda j: (j, 0)),
            *[full((width, lt))] * nb,
        ],
        out_shape=[
            jax.ShapeDtypeStruct((width, vpad), BF),
            jax.ShapeDtypeStruct((vpad, width + 16), BF),
            *[jax.ShapeDtypeStruct((width, lt), BF)] * nb,
        ],
        scratch_shapes=[
            pltpu.VMEM((count, rows, CH), F32),
            pltpu.VMEM((vpad, padded), F32),
            pltpu.VMEM((full_len, padded), F32),
        ],
        compiler_params=params(),
        cost_estimate=cost(12),
        name="prep",
    )(me, ids, *pieces)
    return et, er, outs


def rows_kernel(ids_ref, er_ref, *refs):
    outs, (mark, tab, got) = refs[:-3], refs[-3:]
    width = outs[0].shape[0]
    mark[...] = jnp.zeros_like(mark)

    def fill(c, carry):
        here = pl.ds(pl.multiple_of(c * CH, CH), CH)
        tab[here, 0:width] = er_ref[here, 0:width].astype(F32)
        return carry

    lax.fori_loop(0, er_ref.shape[0] // CH, fill, 0)
    for s, out in enumerate(outs):
        pick_rows(ids_ref, s, tab, got, got.shape[0])
        out[...] = got[:, 0:width].T.astype(BF)


def table_rows(ids, er, width, deps=()):
    count, full_len = ids.shape
    padded = pl.cdiv(width, 128) * 128
    *rows, mark = call(
        rows_kernel,
        (ids, er),
        deps,
        grid=(1,),
        in_specs=[SMEM, full(er.shape)],
        out_specs=[full((width, full_len))] * count + [full((8, 128))],
        out_shape=[jax.ShapeDtypeStruct((width, full_len), BF)] * count
        + [jax.ShapeDtypeStruct((8, 128), F32)],
        scratch_shapes=[
            pltpu.VMEM((er.shape[0], padded), F32),
            pltpu.VMEM((full_len, padded), F32),
        ],
        compiler_params=params(),
        cost_estimate=cost(11),
        name="table_rows",
    )
    return rows, mark


def weights_kernel(nb, nw, widths, packed, *outs):
    rows = packed.shape[1]
    straight, turned = outs[:4], outs[4:8]
    for w in range(nw):
        part = [packed[b * nw + w].astype(F32) for b in range(nb)]
        part = jnp.concatenate(part, 0)
        at = 0
        for size, out in zip(widths, straight):
            out[:, w * size : (w + 1) * size] = part[:, at : at + size].astype(BF)
            at += size
        if w == 0:
            outs[8][...] = part[:, at : at + 3]
        outs[9][0:1, w : w + 1] = part[0:1, at + 3 : at + 4]
    for out, flip in zip(straight, turned):
        flip[...] = out[...].astype(F32).T.astype(BF)


def split_weights(packed, nb, nw, widths):
    rows = packed.shape[1]
    width = nb * rows
    shapes = [(width, nw * size) for size in widths]
    outs = [(s, BF) for s in shapes] + [(s[::-1], BF) for s in shapes]
    outs += [((width, 3), F32), ((1, nw), F32)]
    return pl.pallas_call(
        functools.partial(weights_kernel, nb, nw, widths),
        grid=(1,),
        in_specs=[full(packed.shape)],
        out_specs=[full(s) for s, _ in outs],
        out_shape=[jax.ShapeDtypeStruct(s, d) for s, d in outs],
        compiler_params=params(),
        cost_estimate=cost(3),
        name="split_weights",
    )(packed)


def norm_t(x, gain):
    scale = lax.rsqrt(jnp.mean(x * x, 0, keepdims=True) + norm_eps)
    return x * scale * gain, scale


def norm_t_bwd(x, scale, gain, incoming):
    unit = x * scale
    inner = incoming * gain
    return scale * (inner - unit * jnp.mean(inner * unit, 0, keepdims=True)), incoming * unit


def turn(u, cosine, sine):
    rows, lt = u.shape
    half = cosine.shape[0]
    u = u.reshape(rows // (2 * half), 2, half, lt)
    a, b = u[:, 0], u[:, 1]
    return jnp.stack([a * cosine - b * sine, a * sine + b * cosine], 1).reshape(rows, lt)


def place(me, pieces, out):
    lt = pieces[0].shape[1]
    for k, piece in enumerate(pieces):
        if len(pieces) == 1:
            out[...] = piece[...]
        else:
            out[:, pl.ds(pl.multiple_of((me ^ k) * lt, lt), lt)] = piece[...]


def interleave(parts):
    while parts:
        parts = [p for p in parts if next(p, 1) is None]


def causal(lt):
    keys = lax.broadcasted_iota(jnp.int32, (lt, lt), 0)
    queries = lax.broadcasted_iota(jnp.int32, (lt, lt), 1)
    return keys <= queries


def gelu_parts(u):
    k0 = math.sqrt(2.0 / math.pi)
    square = u * u
    th = jnp.tanh(k0 * (u + 0.044715 * u * square))
    act = 0.5 * u * (1.0 + th)
    return act, th, square, k0


def gelu_slope(u, th, square, k0):
    return 0.5 * (1.0 + th) + 0.5 * u * (1.0 - th * th) * k0 * (1.0 + 3.0 * 0.044715 * square)


def trunk_fwd_kernel(count, me_ref, *refs):
    (want, wqkv_t, wo_t, wm0_t, wm1, gains, cos_ref, sin_ref) = refs[count : count + 8]
    (x0_out, qkv_out, o_out, lse_out, af_out, krow) = refs[count + 8 :]
    width, full_len = x0_out.shape
    lt = min(256, full_len)
    nb = full_len // lt
    root = math.sqrt(width)
    place(me_ref[0], refs[:count], x0_out)
    def project(j):
        here = slice(j * lt, (j + 1) * lt)
        x = x0_out[:, here].astype(F32) * root
        a1, _ = norm_t(x, gains[:, 0:1])
        yield
        y = dot(wqkv_t[...], a1.astype(BF))
        yield
        cosine, sine = cos_ref[:, here], sin_ref[:, here]
        q = turn(y[:width], cosine, sine) * (SCALE * LOG2E)
        k = turn(y[width : 2 * width], cosine, sine)
        qkv_out[0:width, here] = q.astype(BF)
        qkv_out[width : 2 * width, here] = k.astype(BF)
        qkv_out[2 * width :, here] = y[2 * width :].astype(BF)
        for h in range(H):
            krow[h, here, :] = k[h * HD : (h + 1) * HD].T.astype(BF)

    interleave([project(j) for j in range(nb)])
    lse_out[...] = jnp.zeros_like(lse_out)

    def head(h, j):
        rows = slice(h * HD, (h + 1) * HD)
        values = slice(2 * width + h * HD, 2 * width + (h + 1) * HD)
        here, before = slice(j * lt, (j + 1) * lt), slice(0, j * lt)
        q = qkv_out[rows, here]
        s_diag = jnp.where(causal(lt), dot(krow[h, here, :], q), -1e30)
        peak = jnp.max(s_diag, 0, keepdims=True)
        if j:
            s_off = dot(krow[h, before, :], q)
            peak = jnp.maximum(peak, jnp.max(s_off, 0, keepdims=True))
        yield
        p_diag = jnp.exp2(s_diag - peak)
        total = jnp.sum(p_diag, 0, keepdims=True)
        if j:
            p_off = jnp.exp2(s_off - peak)
            total = total + jnp.sum(p_off, 0, keepdims=True)
        yield
        mix = dot(qkv_out[values, here], p_diag.astype(BF))
        if j:
            mix = mix + dot(qkv_out[values, before], p_off.astype(BF))
        o_out[rows, here] = (mix / total).astype(BF)
        lse_out[h : h + 1, here] = peak + jnp.log2(total)

    for j in range(nb):
        interleave([head(h, j) for h in range(H)])

    def finish(j):
        here = slice(j * lt, (j + 1) * lt)
        x = x0_out[:, here].astype(F32) * root
        h1 = x + dot(wo_t[...], o_out[:, here])
        yield
        a2, _ = norm_t(h1, gains[:, 1:2])
        yield
        u = dot(wm0_t[...], a2.astype(BF))
        yield
        act = gelu_parts(u)[0].astype(BF)
        yield
        h2 = h1 + dot(wm1[...], act)
        yield
        af, _ = norm_t(h2, gains[:, 2:3])
        af = (af * LOG2E).astype(BF)
        af_out[0:width, here] = af
        tail = lax.broadcasted_iota(jnp.int32, (af_out.shape[0] - width, lt), 0)
        af_out[width:, here] = jnp.where(tail == 0, 1.0, 0.0).astype(BF)

    interleave([finish(j) for j in range(nb)])
    picked = af_out[0:width, :].astype(F32) * want[...].astype(F32)
    lse_out[H : H + 1, :] = jnp.sum(picked, 0, keepdims=True)


def trunk_fwd(me, pieces, want, weights, gains, cosine, sine, deps=()):
    width, full_len = want.shape
    ins = (me, *pieces, want, *weights, gains, cosine, sine)
    shapes = [
        ((width, full_len), BF),
        ((3 * width, full_len), BF),
        ((width, full_len), BF),
        ((8, full_len), F32),
        ((width + 16, full_len), BF),
    ]
    return call(
        functools.partial(trunk_fwd_kernel, len(pieces)),
        ins,
        deps,
        grid=(1,),
        in_specs=[SMEM] + [full(a.shape) for a in ins[1:]],
        out_specs=[full(s) for s, _ in shapes],
        out_shape=[jax.ShapeDtypeStruct(s, d) for s, d in shapes],
        scratch_shapes=[pltpu.VMEM((H, full_len, HD), BF)],
        compiler_params=params(),
        cost_estimate=cost(13),
        name="trunk_fwd",
    )


def head_kernel(er_ref, af_ref, p_ref, m_ref, st_ref, s_ref, run, cur, z_ref):
    j = pl.program_id(0)
    full_len = af_ref.shape[1]
    lt = z_ref.shape[1]
    tiles = [slice(t, t + lt) for t in range(0, full_len, lt)]

    def emit(here, z, peak):
        p = jnp.exp2(z - peak)
        p_ref[:, here] = p.astype(BF)
        m_ref[pl.ds(j, 1), here] = peak
        total = jnp.sum(p.reshape(CH // 8, 8, lt), 0)
        s_ref[pl.ds(j, 1), here] = jnp.sum(total, 0, keepdims=True)

    @pl.when(j == 0)
    def _():
        run[...] = jnp.full_like(run, -1e30)
        cur[...] = jnp.zeros_like(cur)

    @pl.when(j > 0)
    def _():
        for here in tiles:
            z = dot(er_ref[...], af_ref[:, here])
            peak = jnp.max(z.reshape(CH // 8, 8, lt), 0)
            cur[0:1, here] = jnp.max(peak, 0, keepdims=True)
            emit(here, z, run[0:1, here])

    again = (j == 0) | (jnp.max(cur[0:1, :] - run[0:1, :]) > 60.0)

    @pl.when(again)
    def _():
        for here in tiles:
            z_ref[...] = dot(er_ref[...], af_ref[:, here])
            peak = jnp.max(z_ref[...], 0, keepdims=True)
            peak = jnp.maximum(peak, run[0:1, here])
            cur[0:1, here] = peak
            emit(here, z_ref[...], peak)

    run[0:1, :] = jnp.maximum(run[0:1, :], cur[0:1, :])

    @pl.when(j == pl.num_programs(0) - 1)
    def _():
        peak = run[0:1, :]
        total = jnp.sum(s_ref[...] * jnp.exp2(m_ref[...] - peak), 0, keepdims=True)
        st_ref[...] = jnp.zeros_like(st_ref)
        st_ref[0:1, :] = peak
        st_ref[1:2, :] = total


def head_first(er, af, deps=()):
    vpad, depth = er.shape
    full_len = af.shape[1]
    chunks = vpad // CH
    shapes = [((vpad, full_len), BF), ((chunks, full_len), F32), ((8, full_len), F32)]
    return call(
        head_kernel,
        (er, af),
        deps,
        grid=(chunks,),
        in_specs=[pl.BlockSpec((CH, depth), lambda j: (j, 0)), full(af.shape)],
        out_specs=[pl.BlockSpec((CH, full_len), lambda j: (j, 0))]
        + [full(s) for s, _ in shapes[1:]],
        out_shape=[jax.ShapeDtypeStruct(s, d) for s, d in shapes],
        scratch_shapes=[
            pltpu.VMEM((chunks, full_len), F32),
            pltpu.VMEM((8, full_len), F32),
            pltpu.VMEM((8, full_len), F32),
            pltpu.VMEM((CH, min(512, full_len)), F32),
        ],
        compiler_params=params(),
        cost_estimate=cost(16),
        name="head_first",
    )


def head_back_kernel(slot, nb, sc_ref, *refs):
    (p_ref, et_ref, af_ref, tgt_ref, m_ref, pick_ref) = refs[:6]
    stats = refs[6 : 6 + nb]
    (out, de_ref, loss_ref, acc, s_ref, d_ref) = refs[6 + nb :]
    j = pl.program_id(0)
    width, full_len = out.shape
    lt = min(256, full_len)
    valid = sc_ref[1 + slot]
    weight = valid * sc_ref[0]

    @pl.when(j == 0)
    def _():
        acc[...] = jnp.zeros_like(acc)
        top = functools.reduce(jnp.maximum, [b[0:1, :] for b in stats])
        total = sum(b[1:2, :] * jnp.exp2(b[0:1, :] - top) for b in stats)
        lse2 = top + jnp.log2(total)
        lse = lse2 * LN2
        boost = (1.0 + 2.0 * zloss_coef * lse) * weight
        pick = pick_ref[H : H + 1, :]
        s_ref[...] = jnp.exp2(m_ref[...] - lse2) * boost
        d_ref[0:1, :] = jnp.exp2(pick - lse2) * boost - weight
        loss_ref[...] = jnp.zeros_like(loss_ref)
        loss_ref[0:1, :] = (lse + zloss_coef * lse * lse) * valid
        loss_ref[1:2, :] = pick * LN2 * valid

    rows = lax.broadcasted_iota(jnp.int32, (CH, lt), 0)
    for half in range(2):
        chunk = 2 * j + half
        there = slice(half * CH, (half + 1) * CH)
        total = None
        for t in range(full_len // lt):
            here = slice(t * lt, (t + 1) * lt)
            grad = jnp.where(
                rows == tgt_ref[:, here] - chunk * CH,
                d_ref[0:1, here],
                p_ref[there, here].astype(F32) * s_ref[pl.ds(chunk, 1), here],
            ).astype(BF)
            acc[:, here] += dot(et_ref[:, there], grad)
            part = dot(af_ref[0:width, here], grad, NT)
            total = part if total is None else total + part
        de_ref[:, there] = (total * LN2).astype(BF)

    @pl.when(j == pl.num_programs(0) - 1)
    def _():
        out[...] = acc[...].astype(BF)


def head_back(slot, scalars, p, et, af, tgt, peaks, picks, stats, deps=()):
    nb = len(stats)
    width, vpad = et.shape
    full_len = tgt.shape[1]
    tall = pl.BlockSpec((2 * CH, full_len), lambda j: (j, 0))
    wide = pl.BlockSpec((width, 2 * CH), lambda j: (0, j))
    rest = (af, tgt, peaks, picks, *stats)
    return call(
        functools.partial(head_back_kernel, slot, nb),
        (scalars, p, et, *rest),
        deps,
        grid=(vpad // (2 * CH),),
        in_specs=[SMEM, tall, wide] + [full(a.shape) for a in rest],
        out_specs=[full((width, full_len)), wide, full((8, full_len))],
        out_shape=[
            jax.ShapeDtypeStruct((width, full_len), BF),
            jax.ShapeDtypeStruct((width, vpad), BF),
            jax.ShapeDtypeStruct((8, full_len), F32),
        ],
        scratch_shapes=[
            pltpu.VMEM((width, full_len), F32),
            pltpu.VMEM(peaks.shape, F32),
            pltpu.VMEM((8, full_len), F32),
        ],
        compiler_params=params(),
        cost_estimate=cost(15),
        name="head_back",
    )


def trunk_bwd_kernel(me_ref, *refs):
    (gin, x0, qkv, o_ref, lse) = refs[:5]
    (wqkv, wo, wo_t, wm0, wm0_t, wm1, wm1_t, gains, cos_ref, sin_ref) = refs[5:15]
    (dx_out, wg_out, gg_out) = refs[15:18]
    (krow, vrow, dqkv, dqkv_b, dh1_s, dh1_b, a_s, du_s, act_s, df_s, do_s, delta, wg, gg_s) = refs[18:]
    me = me_ref[0]
    width, full_len = x0.shape
    ff = du_s.shape[0]
    lt = min(256, full_len)
    nb = full_len // lt
    root = math.sqrt(width)
    gain_sums = [[None] * nb for _ in range(3)]

    def outer(j):
        here = slice(j * lt, (j + 1) * lt)
        h1 = x0[:, here].astype(F32) * root + dot(wo_t[...], o_ref[:, here])
        yield
        a2, scale = norm_t(h1, gains[:, 1:2])
        a2 = a2.astype(BF)
        a_s[:, here] = a2
        yield
        u = dot(wm0_t[...], a2)
        yield
        act, th, square, k0 = gelu_parts(u)
        slope = gelu_slope(u, th, square, k0)
        act = act.astype(BF)
        act_s[:, here] = act
        yield
        h2 = h1 + dot(wm1[...], act)
        yield
        _, scale2 = norm_t(h2, 1.0)
        dh2, gg = norm_t_bwd(h2, scale2, gains[:, 2:3], gin[:, here].astype(F32))
        gain_sums[2][j] = jnp.sum(gg, 1, keepdims=True)
        df = dh2.astype(BF)
        df_s[:, here] = df
        yield
        du = (dot(wm1_t[...], df) * slope).astype(BF)
        du_s[:, here] = du
        yield
        da2 = dot(wm0[...], du)
        yield
        dmid, gg = norm_t_bwd(h1, scale, gains[:, 1:2], da2)
        gain_sums[1][j] = jnp.sum(gg, 1, keepdims=True)
        dh1 = dh2 + dmid
        dh1_s[:, here] = dh1
        dh1b = dh1.astype(BF)
        dh1_b[:, here] = dh1b
        yield
        do = dot(wo[...], dh1b).astype(BF)
        do_s[:, here] = do
        weighed = (do.astype(F32) * o_ref[:, here].astype(F32)).reshape(H, HD, lt)
        delta[0:H, here] = jnp.sum(weighed, 1)
        yield
        for h in range(H):
            lo = width + h * HD
            krow[h, here, :] = qkv[lo : lo + HD, here].astype(F32).T.astype(BF)
            vrow[h, here, :] = qkv[lo + width : lo + width + HD, here].astype(F32).T.astype(BF)

    interleave([outer(j) for j in range(nb)])
    wg[:, 4 * width : 4 * width + ff] = dot(a_s[...], du_s[...], NT)
    wg[:, 4 * width + ff :] = dot(df_s[...], act_s[...], NT)
    wg[:, 3 * width : 4 * width] = dot(o_ref[...], dh1_b[...], NT)

    def head(h, j):
        qs, ks, vs = (pl.ds(pl.multiple_of(a + h * HD, 16), HD) for a in (0, width, 2 * width))
        here = slice(j * lt, (j + 1) * lt)
        parts = [(here, True)] + ([(slice(0, j * lt), False)] if j else [])
        q, do = qkv[qs, here], do_s[qs, here]
        lse_row, delta_row = lse[pl.ds(h, 1), here], delta[pl.ds(h, 1), here]
        scores = [(dot(krow[h, t, :], q), dot(vrow[h, t, :], do)) for t, _ in parts]
        yield
        grads = []
        for (there, diagonal), (s, dp) in zip(parts, scores):
            p = jnp.exp2(s - lse_row)
            if diagonal:
                p = jnp.where(causal(lt), p, 0.0)
            grads.append((p.astype(BF), (p * (dp - delta_row)).astype(BF)))
        yield
        dq = 0.0
        for (there, _), (pb, dsb) in zip(parts, grads):
            dq = dq + dot(qkv[ks, there], dsb)
            dk, dv = dot(q, dsb, NT), dot(do, pb, NT)
            if j == nb - 1:
                dqkv[ks, there] = dk
                dqkv[vs, there] = dv
            else:
                dqkv[ks, there] += dk
                dqkv[vs, there] += dv
        dqkv[qs, here] = dq

    def heads(i, carry):
        for j in reversed(range(nb)):
            interleave([head(i * 2 + u, j) for u in range(2)])
        return carry

    lax.fori_loop(0, H // 2, heads, 0)

    def inner(j):
        here = slice(j * lt, (j + 1) * lt)
        cosine, sine = cos_ref[:, here], -sin_ref[:, here]
        dq = turn(dqkv[0:width, here], cosine, sine) * SCALE
        dk = turn(dqkv[width : 2 * width, here], cosine, sine) * LN2
        dqkv_b[0:width, here] = dq.astype(BF)
        dqkv_b[width : 2 * width, here] = dk.astype(BF)
        dqkv_b[2 * width :, here] = dqkv[2 * width :, here].astype(BF)
        x = x0[:, here].astype(F32) * root
        a1, scale = norm_t(x, gains[:, 0:1])
        a_s[:, here] = a1.astype(BF)
        yield
        da1 = dot(wqkv[...], dqkv_b[:, here])
        yield
        dlow, gg = norm_t_bwd(x, scale, gains[:, 0:1], da1)
        gain_sums[0][j] = jnp.sum(gg, 1, keepdims=True)
        dx_out[:, here] = ((dh1_s[:, here] + dlow) * root).astype(BF)

    interleave([inner(j) for j in range(nb)])
    wg[:, 0 : 3 * width] = dot(a_s[...], dqkv_b[...], NT)
    own = wg_out.shape[0]
    wg_out[...] = wg[pl.ds(pl.multiple_of(me * own, 8), own), :]
    lane = lax.broadcasted_iota(jnp.int32, gg_s.shape, 1)
    gg_s[...] = sum(jnp.where(lane == i, sum(gain_sums[i]), 0.0) for i in range(3))
    gg_out[...] = gg_s[pl.ds(pl.multiple_of(me * own, 8), own), :]


def trunk_bwd(me, gin, saved, weights, gains, cosine, sine, own, deps=()):
    width, full_len = gin.shape
    ff = weights[3].shape[1]
    ins = (me, gin, *saved, *weights, gains, cosine, sine)
    cols = 4 * width + 2 * ff
    shapes = [((width, full_len), BF), ((own, cols), F32), ((own, 128), F32)]
    return call(
        trunk_bwd_kernel,
        ins,
        deps,
        grid=(1,),
        in_specs=[SMEM] + [full(a.shape) for a in ins[1:]],
        out_specs=[full(s) for s, _ in shapes],
        out_shape=[jax.ShapeDtypeStruct(s, d) for s, d in shapes],
        scratch_shapes=[
            pltpu.VMEM((H, full_len, HD), BF),
            pltpu.VMEM((H, full_len, HD), BF),
            pltpu.VMEM((3 * width, full_len), F32),
            pltpu.VMEM((3 * width, full_len), BF),
            pltpu.VMEM((width, full_len), F32),
            pltpu.VMEM((width, full_len), BF),
            pltpu.VMEM((width, full_len), BF),
            pltpu.VMEM((ff, full_len), BF),
            pltpu.VMEM((ff, full_len), BF),
            pltpu.VMEM((width, full_len), BF),
            pltpu.VMEM((width, full_len), BF),
            pltpu.VMEM((8, full_len), F32),
            pltpu.VMEM((width, cols), F32),
            pltpu.VMEM((width, 128), F32),
        ],
        compiler_params=params(),
        cost_estimate=cost(24),
        name="trunk_bwd",
    )


def folded(values):
    rows, cols = values.shape
    values = jnp.sum(values.reshape(rows // 8, 8, cols), 0)
    return sum(values[:, c : c + 128] for c in range(0, cols, 128))


def token_grad_kernel(slots, tok_ref, *refs):
    de_refs, dx_refs = refs[:slots], refs[slots : 2 * slots]
    wg_refs, gg_refs = refs[2 * slots : 3 * slots], refs[3 * slots : 4 * slots]
    loss_refs = refs[4 * slots : 5 * slots]
    out_ref, wg_out, gg_out, sum_out, acc = refs[5 * slots :]
    j = pl.program_id(0)
    full_len = tok_ref.shape[2]
    lt = min(512, full_len)

    @pl.when(j == 0)
    def _():
        wg = sum(w[...] for w in wg_refs)
        gg = sum(g[...] for g in gg_refs)
        wg_out[...] = wg
        gg_out[...] = gg
        acc[...] = folded(wg * wg) + folded(gg * gg)

    rows = lax.broadcasted_iota(jnp.int32, (CH, lt), 0) + j * CH
    total = sum(d[...].astype(F32) for d in de_refs)
    for s in range(slots):
        for t in range(full_len // lt):
            here = slice(t * lt, (t + 1) * lt)
            hot = jnp.where(rows == tok_ref[s, :, here], 1.0, 0.0).astype(BF)
            total = total + dot(dx_refs[s][:, here], hot, NT)
    out_ref[...] = total.astype(BF)
    acc[...] += folded(total * total)

    @pl.when(j == pl.num_programs(0) - 1)
    def _():
        lane = lax.broadcasted_iota(jnp.int32, sum_out.shape, 1)
        pick = jnp.sum(sum(r[1:2, :] for r in loss_refs))
        lse = jnp.sum(sum(r[0:1, :] for r in loss_refs))
        tail = jnp.where(lane == 2, lse, 0.0)
        sum_out[...] = jnp.where(lane == 0, jnp.sum(acc[...]), jnp.where(lane == 1, pick, tail))


def token_grad(tok, des, dxs, wgs, ggs, losses):
    slots = len(dxs)
    width, vpad = des[0].shape
    full_len = tok.shape[2]
    blk = pl.BlockSpec((width, CH), lambda j: (0, j))
    rest = (*dxs, *wgs, *ggs, *losses)
    shapes = [(wgs[0].shape, F32), (ggs[0].shape, F32), ((8, 128), F32)]
    return pl.pallas_call(
        functools.partial(token_grad_kernel, slots),
        grid=(vpad // CH,),
        in_specs=[full(tok.shape)] + [blk] * slots + [full(a.shape) for a in rest],
        out_specs=[blk] + [full(s) for s, _ in shapes],
        out_shape=[jax.ShapeDtypeStruct((width, vpad), BF)]
        + [jax.ShapeDtypeStruct(s, d) for s, d in shapes],
        scratch_shapes=[pltpu.VMEM((8, 128), F32)],
        compiler_params=params(),
        cost_estimate=cost(19),
        name="token_grad",
    )(tok, *des, *rest)


def clip_factor(sums):
    total = sum(s[0:1, 0:1] for s in sums)
    return clip_limit / jnp.maximum(jnp.sqrt(total), clip_limit)


def adam(gradient, first, second, weight):
    first = beta_one * first + (1.0 - beta_one) * gradient
    second = beta_two * second + (1.0 - beta_two) * gradient * gradient
    ratio = (first * (weight / (1.0 - beta_one**STEP))) / (
        jnp.sqrt(second * (1.0 / (1.0 - beta_two**STEP))) + adam_eps
    )
    return first, second, ratio


def adam_small_kernel(nb, widths, sc_ref, me_ref, *refs):
    factor = clip_factor(refs[:nb])
    (wg, gg, qf, of, mf, gf, qs, os_, ms, gs) = refs[nb : nb + 10]
    (qf2, of2, mf2, gf2, qs2, os2, ms2, gs2, *r_out) = refs[nb + 11 : -1]
    weight = sc_ref[0] * matrix_rate
    at = 0
    ratios = []
    for f, s, f2, s2 in (
        (qf, qs, qf2, qs2),
        (of, os_, of2, os2),
        (mf.at[0], ms.at[0], mf2.at[0], ms2.at[0]),
        (mf.at[1], ms.at[1], mf2.at[1], ms2.at[1]),
    ):
        here = slice(at, at + f.shape[1])
        f2[...], s2[...], ratio = adam(wg[:, here] * factor, f[...], s[...], weight)
        ratios.append(ratio)
        at = here.stop
    f2, s2, ratio = adam(gg[:, 0:3] * factor, gf[...], gs[...], sc_ref[0] * gain_rate)
    gf2[...] = f2
    gs2[...] = s2
    if not widths:
        at = 0
        for r in ratios:
            r_out[0][:, at : at + r.shape[1]] = r
            at += r.shape[1]
        r_out[0][:, at:] = jnp.zeros_like(r_out[0][:, at:])
        r_out[0][:, at : at + 3] = ratio
        return
    rows, cols = ratio.shape[0] // 2, r_out[0].shape[2] // 2
    blank = jnp.zeros((2 * rows, cols - sum(widths) - 3), F32)
    below = jnp.zeros((r_out[0].shape[1] - rows, 2 * cols), F32)
    for w in range(2 * r_out[0].shape[0]):
        parts = [r[:, w * size : (w + 1) * size] for r, size in zip(ratios, widths)]
        piece = jnp.concatenate([*parts, ratio, blank], 1)
        piece = jnp.concatenate([piece[:rows], piece[rows:]], 1)
        piece = jnp.concatenate([piece, below], 0).astype(BF)
        rel = me_ref[0] ^ w
        for core in range(2):

            @pl.when((rel & 1) == core)
            def _():
                r_out[core][rel >> 1] = piece


def adam_small(scalars, me, sums, wg, gg, firsts, seconds, groups, widths, through):
    ins = (*sums, wg, gg, *firsts, *seconds)
    shapes = [(a.shape, F32) for a in (*firsts, *seconds)]
    if groups:
        cols = pl.cdiv(sum(widths) + 3, 128) * 128
        rows = pl.cdiv(wg.shape[0] // 2, 8) * 8
        shapes += [((groups // 2, rows, 2 * cols), BF)] * 2
    else:
        shapes.append(((wg.shape[0], wg.shape[1] + 128), F32))
    return pl.pallas_call(
        functools.partial(adam_small_kernel, len(sums), widths if groups else None),
        grid=(1,),
        in_specs=[SMEM, SMEM] + [full(a.shape) for a in ins] + [ANY],
        out_specs=[full(s) for s, _ in shapes] + [ANY],
        out_shape=[jax.ShapeDtypeStruct(s, d) for s, d in shapes]
        + [jax.ShapeDtypeStruct(through.shape, through.dtype)],
        input_output_aliases={2 + len(ins): len(shapes)},
        compiler_params=params(),
        cost_estimate=cost(3),
        name="adam_small",
    )(scalars, me, *ins, through)


def adam_kernel(nb, grouped, kept, through, sc_ref, me_ref, *refs):
    sums, (g_ref, f_ref, s_ref) = refs[:nb], refs[nb : nb + 3]
    f_out, s_out, *r_out = refs[nb + 3 + kept + through : len(refs) - through]
    factor = clip_factor(sums)
    first, second, ratio = adam(
        g_ref[...].astype(F32) * factor, f_ref[...], s_ref[...], sc_ref[0] * matrix_rate
    )
    f_out[...] = first
    s_out[...] = second
    if not grouped:
        r_out[0][...] = ratio.astype(BF)
        return
    groups = 2 * r_out[0].shape[0]
    rows = ratio.shape[0] // groups
    padded = r_out[0].shape[1]
    for w in range(groups):
        piece = ratio[w * rows : (w + 1) * rows]
        piece = jnp.concatenate([piece, jnp.zeros((padded - rows, CH), F32)], 0).astype(BF)
        rel = me_ref[0] ^ w
        for core in range(2):

            @pl.when((rel & 1) == core)
            def _():
                r_out[core][rel >> 1] = piece


def adam_table(scalars, me, sums, de, first, second, groups, part, kept=(), through=(), deps=()):
    width, rows = first.shape
    lo, hi = part
    here = min(hi * CH, rows) - lo * CH
    blk = pl.BlockSpec((width, CH), lambda j: (0, j + lo))
    shapes = [((width, rows), F32)] * 2
    specs = [blk, blk]
    if groups:
        stack = (groups // 2, pl.cdiv(width // groups, 8) * 8)
        shapes += [((*stack, here), BF)] * 2
        specs += [pl.BlockSpec((*stack, CH), lambda j: (0, 0, j))] * 2
    else:
        shapes += [((width, here), BF)]
        specs += [pl.BlockSpec((width, CH), lambda j: (0, j))]
    nb = len(sums)
    at, count = nb + 5, len(shapes)
    aliases = {at + i: i for i in range(len(kept))}
    aliases |= {at + len(kept) + i: count + i for i in range(len(through))}
    shapes += [(a.shape, a.dtype) for a in through]
    unread = [ANY] * (len(kept) + len(through))
    return call(
        functools.partial(adam_kernel, nb, bool(groups), len(kept), len(through)),
        (scalars, me, *sums, de, first, second, *kept, *through),
        deps,
        grid=(hi - lo,),
        in_specs=[SMEM, SMEM] + [full(a.shape) for a in sums] + [blk] * 3 + unread,
        out_specs=specs + [ANY] * len(through),
        out_shape=[jax.ShapeDtypeStruct(s, d) for s, d in shapes],
        input_output_aliases=aliases,
        compiler_params=params(),
        cost_estimate=cost(10),
        name="adam_table",
    )


def swap(value, axis, size, k):
    return lax.ppermute(value, axis, [(i, i ^ k) for i in range(size)])


def share(value, axis, size):
    return [value] + [swap(value, axis, size, k) for k in range(1, size)]


def sum_kernel(*refs):
    *pieces, out = refs
    out[...] = sum(p[...].astype(F32) for p in pieces).astype(BF)


def sum_pieces(pieces, axis, size, deps=()):
    came = [pieces[0]] + [swap(pieces[k], axis, size, k) for k in range(1, size)]
    return call(
        sum_kernel,
        tuple(came),
        deps,
        grid=(1,),
        in_specs=[full(c.shape) for c in came],
        out_specs=full(came[0].shape),
        out_shape=jax.ShapeDtypeStruct(came[0].shape, BF),
        compiler_params=params(),
        cost_estimate=cost(2),
        name="sum_pieces",
    )


def turn_first(i):
    return i ^ (2 if i % 2 == 0 else 4)


def turn_second(i):
    return i ^ (4 if i % 2 == 0 else 2)


def permute(value, axis, size, partner):
    return lax.ppermute(value, axis, [(i, partner(i)) for i in range(size)])


def gather_pieces(own, axis, core):
    x, y = swap(own, axis, 8, 2), swap(own, axis, 8, 4)
    far = permute(jnp.where(core == 0, y, x), axis, 8, turn_first)
    near = [own, x, y, far]
    others = [swap(p, axis, 8, 1) for p in near]
    return [p for pair in zip(near, others) for p in pair]


def reduce_first(same, other, axis, core):
    y = (same.astype(F32) + swap(other, axis, 8, 1).astype(F32)).astype(BF)
    sent = jnp.stack([jnp.where(core == 0, y[1], y[2]), y[3]])
    return sent, jnp.where(core == 0, y[2], y[1]), y[0]


def reduce_last(sent, kept, own, axis):
    came = permute(sent, axis, 8, turn_first)
    relayed = (kept.astype(F32) + came[1].astype(F32)).astype(BF)
    total = own.astype(F32) + came[0].astype(F32)
    return total + permute(relayed, axis, 8, turn_second).astype(F32)


def outer_update(summed, total_tok, master, momentum, step_rate, decay):
    average = summed / total_tok + step_rate * decay * master
    momentum = outer_mom * momentum + average
    return (master - outer_rate * (average + outer_mom * momentum), momentum)


def local(
    tokens,
    targets,
    seq_counts,
    embed_w,
    qkv_w,
    out_w,
    mlp_w,
    gain_w,
    embed_mom,
    qkv_mom,
    out_mom,
    mlp_mom,
    gain_mom,
    embed_first,
    qkv_first,
    out_first,
    mlp_first,
    gain_first,
    embed_second,
    qkv_second,
    out_second,
    mlp_second,
    gain_second,
):
    nb = lax.axis_size("blk")
    nw = lax.axis_size("work")
    me = lax.axis_index("blk")
    wi = lax.axis_index("work")
    core = wi % 2
    me_arr = me.astype(jnp.int32).reshape(1)
    wi_arr = wi.astype(jnp.int32).reshape(1)
    slots, full_len = tokens.shape[1:]
    vrows = embed_w.shape[0]
    width = embed_first.shape[2]
    ff = mlp_first.shape[3]
    vpad = pl.cdiv(vrows, 2 * CH) * 2 * CH
    own_rows = width // nb
    paired = nw == 8

    et_own = embed_w.T.astype(BF)
    if paired:
        pieces = gather_pieces(et_own, "work", core)
    else:
        pieces = [lax.all_gather(et_own, "work", axis=0, tiled=True)]
    wi_prep = wi_arr if paired else jnp.zeros_like(wi_arr)

    cq, co, cf = qkv_w.shape[1], out_w.shape[1], mlp_w.shape[2]
    count_col = jnp.broadcast_to(seq_counts[0].astype(F32), (own_rows, 1))
    packed = jnp.concatenate([qkv_w, out_w, mlp_w[0], mlp_w[1], gain_w.T, count_col], 1)
    packed = lax.all_gather(packed.astype(BF), ("blk", "work"), axis=0, tiled=False)
    widths = (cq, co, cf, cf)
    c1, c3 = cq + co, cq + co + 2 * cf
    *weights, gains, count_row = split_weights(packed, nb, nw, widths)
    wqkv, wo, wm0, wm1, wqkv_t, wo_t, wm0_t, wm1_t = weights
    total_tok = jnp.sum(count_row) * full_len

    half = HD // 2
    frequency = rope_base ** (-jnp.arange(half).astype(F32) * 2.0 / HD)
    angles = frequency[:, None] * jnp.arange(full_len).astype(F32)[None, :]
    cosine, sine = jnp.cos(angles), jnp.sin(angles)

    count_seq = seq_counts[0]
    count_tok = (count_seq * full_len).astype(F32)
    valid = (jnp.arange(slots) < count_seq).astype(F32)

    def local_ids(ids, missing):
        ids = ids[0] - me * vrows
        return jnp.where((ids >= 0) & (ids < vrows), ids, missing)

    tok = local_ids(tokens, -1)[:, None, :]
    tgt = local_ids(targets, -1)[:, None, :]
    tok_rows = local_ids(tokens, vrows)
    tgt_rows = local_ids(targets, vrows)

    prep_ids = jnp.concatenate([wi_prep, me_arr])
    et, er, looked = prep(prep_ids, tok_rows[:1], pieces, vpad, nb)
    fwd_weights = (wqkv_t, wo_t, wm0_t, wm1)
    bwd_weights = (wqkv, wo, wo_t, wm0, wm0_t, wm1, wm1_t)
    more, mark = table_rows(tok_rows[1:], er, width)
    wants, mark = table_rows(tgt_rows[:-1], er, width, (mark,))
    mine = sum_pieces(looked, "blk", nb, (mark,))
    later, mark = table_rows(tgt_rows[-1:], er, width, (mark, wqkv))
    wants += later
    def sum_blocks(value, turn):
        return lax.psum(value, "blk", axis_index_groups=[[(k + turn) % nb for k in range(nb)]])

    rows = [share(mine, "blk", nb)]
    rows += [[sum_blocks(m, s)] for s, m in enumerate(more)]

    saved, heads, stats, backs, des, losses = {}, {}, {}, {}, {}, {}
    scalars = jnp.concatenate([1.0 / count_tok.reshape(1), valid])

    def forward(s, *deps):
        *kept, af = trunk_fwd(
            me_arr, rows[s], wants[s], fwd_weights, gains, cosine, sine, deps
        )
        saved[s] = kept
        heads[s] = [af]

    def head(s, *deps):
        p, peaks, stat = head_first(er, heads[s][0], deps)
        heads[s] += [p, peaks]
        stats[s] = share(stat, "blk", nb)

    def back(s, *deps):
        af, p, peaks = heads[s]
        gin, des[s], losses[s] = head_back(
            s, scalars, p, et, af, tgt[s], peaks, saved[s][3], stats[s], deps
        )
        backs[s] = sum_blocks(gin, s)

    for s in range(slots):
        forward(s, *([mark] if s == 0 else [des[s - 2]] if s > 1 else [stats[0][0]]))
        head(s)
        if s:
            back(s - 1, stats[s][0])
    back(slots - 1, *([des[slots - 2]] if slots > 1 else []))
    dxs, wgs, ggs = [], [], []
    for s in range(slots):
        dx, wg, gg = trunk_bwd(
            me_arr,
            backs[s],
            saved[s],
            bwd_weights,
            gains,
            cosine,
            sine,
            own_rows,
            [dxs[-1]] if s else [des[slots - 1]],
        )
        dxs.append(dx)
        wgs.append(wg)
        ggs.append(gg)
    des, losses = [des[s] for s in range(slots)], [losses[s] for s in range(slots)]
    de, wg, gg, both = token_grad(tok, des, dxs, wgs, ggs, losses)
    both = share(both, "blk", nb)
    sums = sum(b[0] for b in both)
    loss_total = both[0][0, 2] - sums[1]
    grad_size = jnp.sqrt(sums[0])

    tokens_of = count_tok.reshape(1)
    groups = nw if paired else 0
    first, second = embed_first[0].T, embed_second[0].T
    chunks = pl.cdiv(vrows, CH)
    cut = (5 * chunks + 7) // 8
    f0, s0, *pair = adam_table(
        tokens_of, wi_arr, both, de, first, second, groups, (0, cut)
    )
    p, q = pair[0], pair[-1]
    *small, p = adam_small(
        tokens_of,
        wi_arr,
        both,
        wg,
        gg,
        (qkv_first[0], out_first[0], mlp_first[0], gain_first[0].T),
        (qkv_second[0], out_second[0], mlp_second[0], gain_second[0].T),
        groups,
        widths,
        p,
    )
    waits, through = [small[8]], ()
    if paired:
        begun = reduce_first(p, q, "work", core)
        through = (begun[2],)
    efirst, esecond, *pair = adam_table(
        tokens_of, wi_arr, both, de, first, second, groups, (cut, chunks), (f0, s0), through, waits
    )
    d1, d2, d3 = 3 * width, 4 * width, 4 * width + ff
    if paired:
        pair, through = pair[:2], pair[2:]
        begun = (*begun[:2], through[0])
        pair = [jnp.concatenate([a, b], 2) for a, b in zip(pair, small[8:])]
        embed_sums = [begun, reduce_first(*pair, "work", core)]
        embed_sums = [reduce_last(*b, "work") for b in embed_sums]
        summed = embed_sums[1][: own_rows // 2, vrows - cut * CH :]
        embed_sums = [e[: width // nw] for e in embed_sums]
        embed_sums[1] = embed_sums[1][:, : vrows - cut * CH]
        summed = jnp.concatenate(jnp.split(summed, 2, 1), 0)
        parts = [summed[:, :cq], summed[:, cq : cq + co]]
        parts += [summed[:, c1 + i * cf : c1 + (i + 1) * cf] for i in range(2)]
        gain_sum = summed[:, c3 : c3 + 3].T
    else:
        embed_sums = [
            lax.psum_scatter(r, "work", scatter_dimension=0, tiled=True).astype(F32)
            for r in (p, pair[0])
        ]
        summed = lax.psum(small[8].astype(BF), "work").astype(F32)
        parts = [
            lax.dynamic_slice_in_dim(summed, lo + wi * size, size, 1)
            for lo, size in ((0, cq), (d1, co), (d2, cf), (d3, cf))
        ]
        gain_sum = summed[:, d3 + ff : d3 + ff + 3].T

    embed_sum = jnp.concatenate(embed_sums, 1).T
    sums = (embed_sum, parts[0], parts[1], jnp.stack(parts[2:]), gain_sum)
    masters = (embed_w, qkv_w, out_w, mlp_w, gain_w)
    moms = (embed_mom, qkv_mom, out_mom, mlp_mom, gain_mom)
    rates = (matrix_rate,) * 4 + (gain_rate,)
    decays = (decay_rate,) * 4 + (0.0,)
    updated = [
        outer_update(g, total_tok, w, m, r, d)
        for g, w, m, r, d in zip(sums, masters, moms, rates, decays)
    ]
    firsts = [efirst.T, *small[0:3], small[3].T]
    seconds = [esecond.T, *small[4:7], small[7].T]
    return (
        jnp.stack([loss_total, count_tok])[None],
        grad_size[None],
        *[u[0] for u in updated],
        *[u[1] for u in updated],
        *[a[None] for a in firsts],
        *[a[None] for a in seconds],
    )


def solution(mesh):
    weights = (
        P("blk", "work"),
        P("blk", "work"),
        P("blk", "work"),
        P(None, "blk", "work"),
        P(None, "blk"),
    )
    states = (
        P("work", "blk", None),
        P("work", "blk", None),
        P("work", "blk", None),
        P("work", None, "blk", None),
        P("work", None, "blk"),
    )
    in_specs = (
        P("work", None, None),
        P("work", None, None),
        P("work"),
        *weights,
        *weights,
        *states,
        *states,
    )
    out_specs = (P("work", None), P("work"), *weights, *weights, *states, *states)
    return jax.shard_map(local, mesh=mesh, in_specs=in_specs, out_specs=out_specs, check_vma=False)
```

```python
import functools
import math

import jax
import jax.numpy as jnp
from jax import lax
from jax.experimental import pallas as pl
from jax.experimental.pallas import tpu as pltpu
from jax.sharding import PartitionSpec as P

H = 6
HD = 48
STEP = 7

norm_eps = 1e-06
zloss_coef = 0.01
clip_limit = 0.05
beta_one = 0.9
beta_two = 0.95
adam_eps = 1e-08
decay_rate = 0.1
matrix_rate = 0.03
gain_rate = 0.3
outer_rate = 0.7
outer_mom = 0.9
rope_base = 10000.0

LOG2E = 1.0 / math.log(2.0)
LN2 = math.log(2.0)
SCALE = 1.0 / math.sqrt(HD)
BF = jnp.bfloat16
F32 = jnp.float32
NN = ((1,), (0,))
NT = ((1,), (1,))
CH = 1024
MIB = 1024 * 1024


def dot(a, b, dims=NN):
    return lax.dot_general(a, b, (dims, ((), ())), preferred_element_type=F32)


def params():
    return pltpu.CompilerParams(dimension_semantics=("arbitrary",), vmem_limit_bytes=58 * MIB)


def cost(micros):
    return pl.CostEstimate(flops=0, bytes_accessed=int(micros * 1.2e6), transcendentals=0)


def full(shape):
    return pl.BlockSpec(shape, lambda *_: (0,) * len(shape))


SMEM = pl.BlockSpec(memory_space=pltpu.SMEM)
ANY = pl.BlockSpec(memory_space=pl.ANY)


def call(kernel, ins, deps, **options):
    specs = options.pop("in_specs")

    def body(*refs):
        kernel(*refs[: len(ins)], *refs[len(ins) + len(deps) :])

    return pl.pallas_call(body, in_specs=[*specs, *([ANY] * len(deps))], **options)(*ins, *deps)


def pick_rows(ids_ref, s, tab, got, full_len):
    unroll = 32

    def body(i, carry):
        base = pl.multiple_of(i * unroll, unroll)
        for q in range(0, unroll, 8):
            rows = [tab[pl.ds(ids_ref[s, base + q + u], 1), :] for u in range(8)]
            got[pl.ds(pl.multiple_of(base + q, 8), 8), :] = jnp.concatenate(rows, 0)
        return carry

    lax.fori_loop(0, full_len // unroll, body, 0)


def rows_out(blk, got, outs):
    for k, out in enumerate(outs):
        width, lt = out.shape
        at = pl.multiple_of((blk ^ k) * lt, lt)
        out[...] = got[pl.ds(at, lt), 0:width].T.astype(BF)


def prep_kernel(count, vrows, nb, me_ref, ids_ref, *refs):
    pieces = refs[:count]
    et_ref, er_ref = refs[count : count + 2]
    outs = refs[count + 2 : count + 2 + nb]
    *others, tmp, tab, got = refs[count + 2 + nb :]
    j = pl.program_id(0)
    width, lt = outs[0].shape
    for k, piece in enumerate(pieces):
        tmp[me_ref[0] ^ k] = piece[...].astype(F32)
    e = jnp.concatenate([tmp[w] for w in range(count)], 0)
    lane = lax.broadcasted_iota(jnp.int32, (width, CH), 1) + j * CH
    e = jnp.where(lane < vrows, e, 0.0)
    et_ref[...] = e.astype(BF)
    rows = e.T
    tab[pl.ds(pl.multiple_of(j * CH, CH), CH), 0:width] = rows
    er_ref[:, 0:width] = rows.astype(BF)
    row = lax.broadcasted_iota(jnp.int32, (CH, 16), 0) + j * CH
    col = lax.broadcasted_iota(jnp.int32, (CH, 16), 1)
    er_ref[:, width:] = jnp.where((row >= vrows) & (col == 0), -60000.0, 0.0).astype(BF)

    @pl.when(j == pl.num_programs(0) - 1)
    def _():
        pick_rows(ids_ref, 0, tab, got, nb * lt)
        rows_out(me_ref[1], got, outs)
        for s, other in enumerate(others):
            pick_rows(ids_ref, s + 1, tab, got, nb * lt)
            other[...] = got[:, 0:width].T.astype(BF)


def prep(me, ids, pieces, vpad, nb):
    count = len(pieces)
    rows, vrows = pieces[0].shape
    width = count * rows
    slots, full_len = ids.shape
    lt = full_len // nb
    padded = pl.cdiv(width, 128) * 128
    et, er, *outs = pl.pallas_call(
        functools.partial(prep_kernel, count, vrows, nb),
        grid=(vpad // CH,),
        in_specs=[SMEM, SMEM] + [pl.BlockSpec((rows, CH), lambda j: (0, j))] * count,
        out_specs=[
            pl.BlockSpec((width, CH), lambda j: (0, j)),
            pl.BlockSpec((CH, width + 16), lambda j: (j, 0)),
            *[full((width, lt))] * nb,
            *[full((width, full_len))] * (slots - 1),
        ],
        out_shape=[
            jax.ShapeDtypeStruct((width, vpad), BF),
            jax.ShapeDtypeStruct((vpad, width + 16), BF),
            *[jax.ShapeDtypeStruct((width, lt), BF)] * nb,
            *[jax.ShapeDtypeStruct((width, full_len), BF)] * (slots - 1),
        ],
        scratch_shapes=[
            pltpu.VMEM((count, rows, CH), F32),
            pltpu.VMEM((vpad, padded), F32),
            pltpu.VMEM((full_len, padded), F32),
        ],
        compiler_params=params(),
        cost_estimate=cost(12),
        name="prep",
    )(me, ids, *pieces)
    return et, er, outs[:nb], outs[nb:]


def rows_kernel(ids_ref, er_ref, *refs):
    outs, (mark, tab, got) = refs[:-3], refs[-3:]
    width = outs[0].shape[0]
    mark[...] = jnp.zeros_like(mark)

    def fill(c, carry):
        here = pl.ds(pl.multiple_of(c * CH, CH), CH)
        tab[here, 0:width] = er_ref[here, 0:width].astype(F32)
        return carry

    lax.fori_loop(0, er_ref.shape[0] // CH, fill, 0)
    for s, out in enumerate(outs):
        pick_rows(ids_ref, s, tab, got, got.shape[0])
        out[...] = got[:, 0:width].T.astype(BF)


def table_rows(ids, er, width, deps=()):
    count, full_len = ids.shape
    padded = pl.cdiv(width, 128) * 128
    *rows, mark = call(
        rows_kernel,
        (ids, er),
        deps,
        grid=(1,),
        in_specs=[SMEM, full(er.shape)],
        out_specs=[full((width, full_len))] * count + [full((8, 128))],
        out_shape=[jax.ShapeDtypeStruct((width, full_len), BF)] * count
        + [jax.ShapeDtypeStruct((8, 128), F32)],
        scratch_shapes=[
            pltpu.VMEM((er.shape[0], padded), F32),
            pltpu.VMEM((full_len, padded), F32),
        ],
        compiler_params=params(),
        cost_estimate=cost(11),
        name="table_rows",
    )
    return rows, mark


def weights_kernel(nb, nw, widths, packed, *outs):
    rows = packed.shape[1]
    straight, turned = outs[:4], outs[4:8]
    for w in range(nw):
        part = [packed[b * nw + w].astype(F32) for b in range(nb)]
        part = jnp.concatenate(part, 0)
        at = 0
        for size, out in zip(widths, straight):
            out[:, w * size : (w + 1) * size] = part[:, at : at + size].astype(BF)
            at += size
        if w == 0:
            outs[8][...] = part[:, at : at + 3]
        outs[9][0:1, w : w + 1] = part[0:1, at + 3 : at + 4]
    for out, flip in zip(straight, turned):
        flip[...] = out[...].astype(F32).T.astype(BF)


def split_weights(packed, nb, nw, widths):
    rows = packed.shape[1]
    width = nb * rows
    shapes = [(width, nw * size) for size in widths]
    outs = [(s, BF) for s in shapes] + [(s[::-1], BF) for s in shapes]
    outs += [((width, 3), F32), ((1, nw), F32)]
    return pl.pallas_call(
        functools.partial(weights_kernel, nb, nw, widths),
        grid=(1,),
        in_specs=[full(packed.shape)],
        out_specs=[full(s) for s, _ in outs],
        out_shape=[jax.ShapeDtypeStruct(s, d) for s, d in outs],
        compiler_params=params(),
        cost_estimate=cost(3),
        name="split_weights",
    )(packed)


def norm_t(x, gain):
    scale = lax.rsqrt(jnp.mean(x * x, 0, keepdims=True) + norm_eps)
    return x * scale * gain, scale


def norm_t_bwd(x, scale, gain, incoming):
    unit = x * scale
    inner = incoming * gain
    return scale * (inner - unit * jnp.mean(inner * unit, 0, keepdims=True)), incoming * unit


def turn(u, cosine, sine):
    rows, lt = u.shape
    half = cosine.shape[0]
    u = u.reshape(rows // (2 * half), 2, half, lt)
    a, b = u[:, 0], u[:, 1]
    return jnp.stack([a * cosine - b * sine, a * sine + b * cosine], 1).reshape(rows, lt)


def place(me, pieces, out):
    lt = pieces[0].shape[1]
    for k, piece in enumerate(pieces):
        if len(pieces) == 1:
            out[...] = piece[...]
        else:
            out[:, pl.ds(pl.multiple_of((me ^ k) * lt, lt), lt)] = piece[...]


def interleave(parts):
    while parts:
        parts = [p for p in parts if next(p, 1) is None]


def causal(lt):
    keys = lax.broadcasted_iota(jnp.int32, (lt, lt), 0)
    queries = lax.broadcasted_iota(jnp.int32, (lt, lt), 1)
    return keys <= queries


def gelu_parts(u):
    k0 = math.sqrt(2.0 / math.pi)
    square = u * u
    th = jnp.tanh(k0 * (u + 0.044715 * u * square))
    act = 0.5 * u * (1.0 + th)
    return act, th, square, k0


def gelu_slope(u, th, square, k0):
    return 0.5 * (1.0 + th) + 0.5 * u * (1.0 - th * th) * k0 * (1.0 + 3.0 * 0.044715 * square)


def trunk_fwd_kernel(count, me_ref, *refs):
    (want, wqkv_t, wo_t, wm0_t, wm1, gains, cos_ref, sin_ref) = refs[count : count + 8]
    (x0_out, qkv_out, o_out, lse_out, af_out, krow) = refs[count + 8 :]
    width, full_len = x0_out.shape
    lt = min(256, full_len)
    nb = full_len // lt
    root = math.sqrt(width)
    place(me_ref[0], refs[:count], x0_out)
    def project(j):
        here = slice(j * lt, (j + 1) * lt)
        x = x0_out[:, here].astype(F32) * root
        a1, _ = norm_t(x, gains[:, 0:1])
        yield
        y = dot(wqkv_t[...], a1.astype(BF))
        yield
        cosine, sine = cos_ref[:, here], sin_ref[:, here]
        q = turn(y[:width], cosine, sine) * (SCALE * LOG2E)
        k = turn(y[width : 2 * width], cosine, sine)
        qkv_out[0:width, here] = q.astype(BF)
        qkv_out[width : 2 * width, here] = k.astype(BF)
        qkv_out[2 * width :, here] = y[2 * width :].astype(BF)
        for h in range(H):
            krow[h, here, :] = k[h * HD : (h + 1) * HD].T.astype(BF)

    interleave([project(j) for j in range(nb)])
    lse_out[...] = jnp.zeros_like(lse_out)

    def head(h, j):
        rows = slice(h * HD, (h + 1) * HD)
        values = slice(2 * width + h * HD, 2 * width + (h + 1) * HD)
        here, before = slice(j * lt, (j + 1) * lt), slice(0, j * lt)
        q = qkv_out[rows, here]
        s_diag = jnp.where(causal(lt), dot(krow[h, here, :], q), -1e30)
        peak = jnp.max(s_diag, 0, keepdims=True)
        if j:
            s_off = dot(krow[h, before, :], q)
            peak = jnp.maximum(peak, jnp.max(s_off, 0, keepdims=True))
        yield
        p_diag = jnp.exp2(s_diag - peak)
        total = jnp.sum(p_diag, 0, keepdims=True)
        if j:
            p_off = jnp.exp2(s_off - peak)
            total = total + jnp.sum(p_off, 0, keepdims=True)
        yield
        mix = dot(qkv_out[values, here], p_diag.astype(BF))
        if j:
            mix = mix + dot(qkv_out[values, before], p_off.astype(BF))
        o_out[rows, here] = (mix / total).astype(BF)
        lse_out[h : h + 1, here] = peak + jnp.log2(total)

    for j in range(nb):
        interleave([head(h, j) for h in range(H)])

    def finish(j):
        here = slice(j * lt, (j + 1) * lt)
        x = x0_out[:, here].astype(F32) * root
        h1 = x + dot(wo_t[...], o_out[:, here])
        yield
        a2, _ = norm_t(h1, gains[:, 1:2])
        yield
        u = dot(wm0_t[...], a2.astype(BF))
        yield
        act = gelu_parts(u)[0].astype(BF)
        yield
        h2 = h1 + dot(wm1[...], act)
        yield
        af, _ = norm_t(h2, gains[:, 2:3])
        af = (af * LOG2E).astype(BF)
        af_out[0:width, here] = af
        tail = lax.broadcasted_iota(jnp.int32, (af_out.shape[0] - width, lt), 0)
        af_out[width:, here] = jnp.where(tail == 0, 1.0, 0.0).astype(BF)

    interleave([finish(j) for j in range(nb)])
    picked = af_out[0:width, :].astype(F32) * want[...].astype(F32)
    lse_out[H : H + 1, :] = jnp.sum(picked, 0, keepdims=True)


def trunk_fwd(me, pieces, want, weights, gains, cosine, sine, deps=()):
    width, full_len = want.shape
    ins = (me, *pieces, want, *weights, gains, cosine, sine)
    shapes = [
        ((width, full_len), BF),
        ((3 * width, full_len), BF),
        ((width, full_len), BF),
        ((8, full_len), F32),
        ((width + 16, full_len), BF),
    ]
    return call(
        functools.partial(trunk_fwd_kernel, len(pieces)),
        ins,
        deps,
        grid=(1,),
        in_specs=[SMEM] + [full(a.shape) for a in ins[1:]],
        out_specs=[full(s) for s, _ in shapes],
        out_shape=[jax.ShapeDtypeStruct(s, d) for s, d in shapes],
        scratch_shapes=[pltpu.VMEM((H, full_len, HD), BF)],
        compiler_params=params(),
        cost_estimate=cost(13),
        name="trunk_fwd",
    )


def head_kernel(er_ref, af_ref, p_ref, m_ref, st_ref, s_ref, run, cur, z_ref):
    j = pl.program_id(0)
    full_len = af_ref.shape[1]
    lt = z_ref.shape[1]
    tiles = [slice(t, t + lt) for t in range(0, full_len, lt)]

    def emit(here, z, peak):
        p = jnp.exp2(z - peak)
        p_ref[:, here] = p.astype(BF)
        m_ref[pl.ds(j, 1), here] = peak
        total = jnp.sum(p.reshape(CH // 8, 8, lt), 0)
        s_ref[pl.ds(j, 1), here] = jnp.sum(total, 0, keepdims=True)

    @pl.when(j == 0)
    def _():
        run[...] = jnp.full_like(run, -1e30)
        cur[...] = jnp.zeros_like(cur)

    @pl.when(j > 0)
    def _():
        for here in tiles:
            z = dot(er_ref[...], af_ref[:, here])
            peak = jnp.max(z.reshape(CH // 8, 8, lt), 0)
            cur[0:1, here] = jnp.max(peak, 0, keepdims=True)
            emit(here, z, run[0:1, here])

    again = (j == 0) | (jnp.max(cur[0:1, :] - run[0:1, :]) > 60.0)

    @pl.when(again)
    def _():
        for here in tiles:
            z_ref[...] = dot(er_ref[...], af_ref[:, here])
            peak = jnp.max(z_ref[...], 0, keepdims=True)
            peak = jnp.maximum(peak, run[0:1, here])
            cur[0:1, here] = peak
            emit(here, z_ref[...], peak)

    run[0:1, :] = jnp.maximum(run[0:1, :], cur[0:1, :])

    @pl.when(j == pl.num_programs(0) - 1)
    def _():
        peak = run[0:1, :]
        total = jnp.sum(s_ref[...] * jnp.exp2(m_ref[...] - peak), 0, keepdims=True)
        st_ref[...] = jnp.zeros_like(st_ref)
        st_ref[0:1, :] = peak
        st_ref[1:2, :] = total


def head_first(er, af, deps=()):
    vpad, depth = er.shape
    full_len = af.shape[1]
    chunks = vpad // CH
    shapes = [((vpad, full_len), BF), ((chunks, full_len), F32), ((8, full_len), F32)]
    return call(
        head_kernel,
        (er, af),
        deps,
        grid=(chunks,),
        in_specs=[pl.BlockSpec((CH, depth), lambda j: (j, 0)), full(af.shape)],
        out_specs=[pl.BlockSpec((CH, full_len), lambda j: (j, 0))]
        + [full(s) for s, _ in shapes[1:]],
        out_shape=[jax.ShapeDtypeStruct(s, d) for s, d in shapes],
        scratch_shapes=[
            pltpu.VMEM((chunks, full_len), F32),
            pltpu.VMEM((8, full_len), F32),
            pltpu.VMEM((8, full_len), F32),
            pltpu.VMEM((CH, min(512, full_len)), F32),
        ],
        compiler_params=params(),
        cost_estimate=cost(16),
        name="head_first",
    )


def head_back_kernel(slot, nb, sc_ref, *refs):
    (p_ref, et_ref, af_ref, tgt_ref, m_ref, pick_ref) = refs[:6]
    stats = refs[6 : 6 + nb]
    (out, de_ref, loss_ref, acc, s_ref, d_ref) = refs[6 + nb :]
    j = pl.program_id(0)
    width, full_len = out.shape
    lt = min(256, full_len)
    valid = sc_ref[1 + slot]
    weight = valid * sc_ref[0]

    @pl.when(j == 0)
    def _():
        acc[...] = jnp.zeros_like(acc)
        top = functools.reduce(jnp.maximum, [b[0:1, :] for b in stats])
        total = sum(b[1:2, :] * jnp.exp2(b[0:1, :] - top) for b in stats)
        lse2 = top + jnp.log2(total)
        lse = lse2 * LN2
        boost = (1.0 + 2.0 * zloss_coef * lse) * weight
        pick = pick_ref[H : H + 1, :]
        s_ref[...] = jnp.exp2(m_ref[...] - lse2) * boost
        d_ref[0:1, :] = jnp.exp2(pick - lse2) * boost - weight
        loss_ref[...] = jnp.zeros_like(loss_ref)
        loss_ref[0:1, :] = (lse + zloss_coef * lse * lse) * valid
        loss_ref[1:2, :] = pick * LN2 * valid

    rows = lax.broadcasted_iota(jnp.int32, (CH, lt), 0)
    for half in range(2):
        chunk = 2 * j + half
        there = slice(half * CH, (half + 1) * CH)
        total = None
        for t in range(full_len // lt):
            here = slice(t * lt, (t + 1) * lt)
            grad = jnp.where(
                rows == tgt_ref[:, here] - chunk * CH,
                d_ref[0:1, here],
                p_ref[there, here].astype(F32) * s_ref[pl.ds(chunk, 1), here],
            ).astype(BF)
            acc[:, here] += dot(et_ref[:, there], grad)
            part = dot(af_ref[0:width, here], grad, NT)
            total = part if total is None else total + part
        de_ref[:, there] = (total * LN2).astype(BF)

    @pl.when(j == pl.num_programs(0) - 1)
    def _():
        out[...] = acc[...].astype(BF)


def head_back(slot, scalars, p, et, af, tgt, peaks, picks, stats, deps=()):
    nb = len(stats)
    width, vpad = et.shape
    full_len = tgt.shape[1]
    tall = pl.BlockSpec((2 * CH, full_len), lambda j: (j, 0))
    wide = pl.BlockSpec((width, 2 * CH), lambda j: (0, j))
    rest = (af, tgt, peaks, picks, *stats)
    return call(
        functools.partial(head_back_kernel, slot, nb),
        (scalars, p, et, *rest),
        deps,
        grid=(vpad // (2 * CH),),
        in_specs=[SMEM, tall, wide] + [full(a.shape) for a in rest],
        out_specs=[full((width, full_len)), wide, full((8, full_len))],
        out_shape=[
            jax.ShapeDtypeStruct((width, full_len), BF),
            jax.ShapeDtypeStruct((width, vpad), BF),
            jax.ShapeDtypeStruct((8, full_len), F32),
        ],
        scratch_shapes=[
            pltpu.VMEM((width, full_len), F32),
            pltpu.VMEM(peaks.shape, F32),
            pltpu.VMEM((8, full_len), F32),
        ],
        compiler_params=params(),
        cost_estimate=cost(15),
        name="head_back",
    )


def trunk_bwd_kernel(me_ref, *refs):
    (gin, x0, qkv, o_ref, lse) = refs[:5]
    (wqkv, wo, wo_t, wm0, wm0_t, wm1, wm1_t, gains, cos_ref, sin_ref) = refs[5:15]
    (dx_out, wg_out, gg_out) = refs[15:18]
    (krow, vrow, dqkv, dqkv_b, dh1_s, dh1_b, a_s, du_s, act_s, df_s, do_s, delta, wg, gg_s) = refs[18:]
    me = me_ref[0]
    width, full_len = x0.shape
    ff = du_s.shape[0]
    lt = min(256, full_len)
    nb = full_len // lt
    root = math.sqrt(width)
    gain_sums = [[None] * nb for _ in range(3)]

    def outer(j):
        here = slice(j * lt, (j + 1) * lt)
        h1 = x0[:, here].astype(F32) * root + dot(wo_t[...], o_ref[:, here])
        yield
        a2, scale = norm_t(h1, gains[:, 1:2])
        a2 = a2.astype(BF)
        a_s[:, here] = a2
        yield
        u = dot(wm0_t[...], a2)
        yield
        act, th, square, k0 = gelu_parts(u)
        slope = gelu_slope(u, th, square, k0)
        act = act.astype(BF)
        act_s[:, here] = act
        yield
        h2 = h1 + dot(wm1[...], act)
        yield
        _, scale2 = norm_t(h2, 1.0)
        dh2, gg = norm_t_bwd(h2, scale2, gains[:, 2:3], gin[:, here].astype(F32))
        gain_sums[2][j] = jnp.sum(gg, 1, keepdims=True)
        df = dh2.astype(BF)
        df_s[:, here] = df
        yield
        du = (dot(wm1_t[...], df) * slope).astype(BF)
        du_s[:, here] = du
        yield
        da2 = dot(wm0[...], du)
        yield
        dmid, gg = norm_t_bwd(h1, scale, gains[:, 1:2], da2)
        gain_sums[1][j] = jnp.sum(gg, 1, keepdims=True)
        dh1 = dh2 + dmid
        dh1_s[:, here] = dh1
        dh1b = dh1.astype(BF)
        dh1_b[:, here] = dh1b
        yield
        do = dot(wo[...], dh1b).astype(BF)
        do_s[:, here] = do
        weighed = (do.astype(F32) * o_ref[:, here].astype(F32)).reshape(H, HD, lt)
        delta[0:H, here] = jnp.sum(weighed, 1)
        yield
        for h in range(H):
            lo = width + h * HD
            krow[h, here, :] = qkv[lo : lo + HD, here].astype(F32).T.astype(BF)
            vrow[h, here, :] = qkv[lo + width : lo + width + HD, here].astype(F32).T.astype(BF)

    interleave([outer(j) for j in range(nb)])
    wg[:, 4 * width : 4 * width + ff] = dot(a_s[...], du_s[...], NT)
    wg[:, 4 * width + ff :] = dot(df_s[...], act_s[...], NT)
    wg[:, 3 * width : 4 * width] = dot(o_ref[...], dh1_b[...], NT)

    def head(h, j):
        qs, ks, vs = (pl.ds(pl.multiple_of(a + h * HD, 16), HD) for a in (0, width, 2 * width))
        here = slice(j * lt, (j + 1) * lt)
        parts = [(here, True)] + ([(slice(0, j * lt), False)] if j else [])
        q, do = qkv[qs, here], do_s[qs, here]
        lse_row, delta_row = lse[pl.ds(h, 1), here], delta[pl.ds(h, 1), here]
        scores = [(dot(krow[h, t, :], q), dot(vrow[h, t, :], do)) for t, _ in parts]
        yield
        grads = []
        for (there, diagonal), (s, dp) in zip(parts, scores):
            p = jnp.exp2(s - lse_row)
            if diagonal:
                p = jnp.where(causal(lt), p, 0.0)
            grads.append((p.astype(BF), (p * (dp - delta_row)).astype(BF)))
        yield
        dq = 0.0
        for (there, _), (pb, dsb) in zip(parts, grads):
            dq = dq + dot(qkv[ks, there], dsb)
            dk, dv = dot(q, dsb, NT), dot(do, pb, NT)
            if j == nb - 1:
                dqkv[ks, there] = dk
                dqkv[vs, there] = dv
            else:
                dqkv[ks, there] += dk
                dqkv[vs, there] += dv
        dqkv[qs, here] = dq

    def heads(i, carry):
        for j in reversed(range(nb)):
            interleave([head(i * 2 + u, j) for u in range(2)])
        return carry

    lax.fori_loop(0, H // 2, heads, 0)

    def inner(j):
        here = slice(j * lt, (j + 1) * lt)
        cosine, sine = cos_ref[:, here], -sin_ref[:, here]
        dq = turn(dqkv[0:width, here], cosine, sine) * SCALE
        dk = turn(dqkv[width : 2 * width, here], cosine, sine) * LN2
        dqkv_b[0:width, here] = dq.astype(BF)
        dqkv_b[width : 2 * width, here] = dk.astype(BF)
        dqkv_b[2 * width :, here] = dqkv[2 * width :, here].astype(BF)
        x = x0[:, here].astype(F32) * root
        a1, scale = norm_t(x, gains[:, 0:1])
        a_s[:, here] = a1.astype(BF)
        yield
        da1 = dot(wqkv[...], dqkv_b[:, here])
        yield
        dlow, gg = norm_t_bwd(x, scale, gains[:, 0:1], da1)
        gain_sums[0][j] = jnp.sum(gg, 1, keepdims=True)
        dx_out[:, here] = ((dh1_s[:, here] + dlow) * root).astype(BF)

    interleave([inner(j) for j in range(nb)])
    wg[:, 0 : 3 * width] = dot(a_s[...], dqkv_b[...], NT)
    own = wg_out.shape[0]
    wg_out[...] = wg[pl.ds(pl.multiple_of(me * own, 8), own), :]
    lane = lax.broadcasted_iota(jnp.int32, gg_s.shape, 1)
    gg_s[...] = sum(jnp.where(lane == i, sum(gain_sums[i]), 0.0) for i in range(3))
    gg_out[...] = gg_s[pl.ds(pl.multiple_of(me * own, 8), own), :]


def trunk_bwd(me, gin, saved, weights, gains, cosine, sine, own, deps=()):
    width, full_len = gin.shape
    ff = weights[3].shape[1]
    ins = (me, gin, *saved, *weights, gains, cosine, sine)
    cols = 4 * width + 2 * ff
    shapes = [((width, full_len), BF), ((own, cols), F32), ((own, 128), F32)]
    return call(
        trunk_bwd_kernel,
        ins,
        deps,
        grid=(1,),
        in_specs=[SMEM] + [full(a.shape) for a in ins[1:]],
        out_specs=[full(s) for s, _ in shapes],
        out_shape=[jax.ShapeDtypeStruct(s, d) for s, d in shapes],
        scratch_shapes=[
            pltpu.VMEM((H, full_len, HD), BF),
            pltpu.VMEM((H, full_len, HD), BF),
            pltpu.VMEM((3 * width, full_len), F32),
            pltpu.VMEM((3 * width, full_len), BF),
            pltpu.VMEM((width, full_len), F32),
            pltpu.VMEM((width, full_len), BF),
            pltpu.VMEM((width, full_len), BF),
            pltpu.VMEM((ff, full_len), BF),
            pltpu.VMEM((ff, full_len), BF),
            pltpu.VMEM((width, full_len), BF),
            pltpu.VMEM((width, full_len), BF),
            pltpu.VMEM((8, full_len), F32),
            pltpu.VMEM((width, cols), F32),
            pltpu.VMEM((width, 128), F32),
        ],
        compiler_params=params(),
        cost_estimate=cost(24),
        name="trunk_bwd",
    )


def folded(values):
    rows, cols = values.shape
    values = jnp.sum(values.reshape(rows // 8, 8, cols), 0)
    return sum(values[:, c : c + 128] for c in range(0, cols, 128))


def token_grad_kernel(slots, tok_ref, *refs):
    de_refs, dx_refs = refs[:slots], refs[slots : 2 * slots]
    wg_refs, gg_refs = refs[2 * slots : 3 * slots], refs[3 * slots : 4 * slots]
    loss_refs = refs[4 * slots : 5 * slots]
    out_ref, wg_out, gg_out, sum_out, acc = refs[5 * slots :]
    j = pl.program_id(0)
    full_len = tok_ref.shape[2]
    lt = min(512, full_len)

    @pl.when(j == 0)
    def _():
        wg = sum(w[...] for w in wg_refs)
        gg = sum(g[...] for g in gg_refs)
        wg_out[...] = wg
        gg_out[...] = gg
        acc[...] = folded(wg * wg) + folded(gg * gg)

    rows = lax.broadcasted_iota(jnp.int32, (CH, lt), 0) + j * CH
    total = sum(d[...].astype(F32) for d in de_refs)
    for s in range(slots):
        for t in range(full_len // lt):
            here = slice(t * lt, (t + 1) * lt)
            hot = jnp.where(rows == tok_ref[s, :, here], 1.0, 0.0).astype(BF)
            total = total + dot(dx_refs[s][:, here], hot, NT)
    out_ref[...] = total.astype(BF)
    acc[...] += folded(total * total)

    @pl.when(j == pl.num_programs(0) - 1)
    def _():
        lane = lax.broadcasted_iota(jnp.int32, sum_out.shape, 1)
        pick = jnp.sum(sum(r[1:2, :] for r in loss_refs))
        lse = jnp.sum(sum(r[0:1, :] for r in loss_refs))
        tail = jnp.where(lane == 2, lse, 0.0)
        sum_out[...] = jnp.where(lane == 0, jnp.sum(acc[...]), jnp.where(lane == 1, pick, tail))


def token_grad(tok, des, dxs, wgs, ggs, losses):
    slots = len(dxs)
    width, vpad = des[0].shape
    full_len = tok.shape[2]
    blk = pl.BlockSpec((width, CH), lambda j: (0, j))
    rest = (*dxs, *wgs, *ggs, *losses)
    shapes = [(wgs[0].shape, F32), (ggs[0].shape, F32), ((8, 128), F32)]
    return pl.pallas_call(
        functools.partial(token_grad_kernel, slots),
        grid=(vpad // CH,),
        in_specs=[full(tok.shape)] + [blk] * slots + [full(a.shape) for a in rest],
        out_specs=[blk] + [full(s) for s, _ in shapes],
        out_shape=[jax.ShapeDtypeStruct((width, vpad), BF)]
        + [jax.ShapeDtypeStruct(s, d) for s, d in shapes],
        scratch_shapes=[pltpu.VMEM((8, 128), F32)],
        compiler_params=params(),
        cost_estimate=cost(19),
        name="token_grad",
    )(tok, *des, *rest)


def clip_factor(sums):
    total = sum(s[0:1, 0:1] for s in sums)
    return clip_limit / jnp.maximum(jnp.sqrt(total), clip_limit)


def adam(gradient, first, second, weight):
    first = beta_one * first + (1.0 - beta_one) * gradient
    second = beta_two * second + (1.0 - beta_two) * gradient * gradient
    ratio = (first * (weight / (1.0 - beta_one**STEP))) / (
        jnp.sqrt(second * (1.0 / (1.0 - beta_two**STEP))) + adam_eps
    )
    return first, second, ratio


def adam_small_kernel(nb, widths, sc_ref, me_ref, *refs):
    factor = clip_factor(refs[:nb])
    (wg, gg, qf, of, mf, gf, qs, os_, ms, gs) = refs[nb : nb + 10]
    (qf2, of2, mf2, gf2, qs2, os2, ms2, gs2, *r_out) = refs[nb + 11 : -2]
    res = refs[-2]
    sums = sum(r[...] for r in refs[:nb])
    lane = lax.broadcasted_iota(jnp.int32, res.shape, 1)
    loss = refs[0][:, 2:3] - sums[:, 1:2]
    res[...] = jnp.where(lane == 0, loss, jnp.where(lane == 1, jnp.sqrt(sums[:, 0:1]), 0.0))
    weight = sc_ref[0] * matrix_rate
    at = 0
    ratios = []
    for f, s, f2, s2 in (
        (qf, qs, qf2, qs2),
        (of, os_, of2, os2),
        (mf.at[0], ms.at[0], mf2.at[0], ms2.at[0]),
        (mf.at[1], ms.at[1], mf2.at[1], ms2.at[1]),
    ):
        here = slice(at, at + f.shape[1])
        f2[...], s2[...], ratio = adam(wg[:, here] * factor, f[...], s[...], weight)
        ratios.append(ratio)
        at = here.stop
    f2, s2, ratio = adam(gg[:, 0:3] * factor, gf[...], gs[...], sc_ref[0] * gain_rate)
    gf2[...] = f2
    gs2[...] = s2
    if not widths:
        at = 0
        for r in ratios:
            r_out[0][:, at : at + r.shape[1]] = r
            at += r.shape[1]
        r_out[0][:, at:] = jnp.zeros_like(r_out[0][:, at:])
        r_out[0][:, at : at + 3] = ratio
        return
    rows, cols = ratio.shape[0] // 2, r_out[0].shape[2] // 2
    blank = jnp.zeros((2 * rows, cols - sum(widths) - 3), F32)
    below = jnp.zeros((r_out[0].shape[1] - rows, 2 * cols), F32)
    for w in range(2 * r_out[0].shape[0]):
        parts = [r[:, w * size : (w + 1) * size] for r, size in zip(ratios, widths)]
        piece = jnp.concatenate([*parts, ratio, blank], 1)
        piece = jnp.concatenate([piece[:rows], piece[rows:]], 1)
        piece = jnp.concatenate([piece, below], 0).astype(BF)
        rel = me_ref[0] ^ w
        for core in range(2):

            @pl.when((rel & 1) == core)
            def _():
                r_out[core][rel >> 1] = piece


def adam_small(scalars, me, sums, wg, gg, firsts, seconds, groups, widths, through):
    ins = (*sums, wg, gg, *firsts, *seconds)
    shapes = [(a.shape, F32) for a in (*firsts, *seconds)]
    if groups:
        cols = pl.cdiv(sum(widths) + 3, 128) * 128
        rows = pl.cdiv(wg.shape[0] // 2, 8) * 8
        shapes += [((groups // 2, rows, 2 * cols), BF)] * 2
    else:
        shapes.append(((wg.shape[0], wg.shape[1] + 128), F32))
    shapes.append((sums[0].shape, F32))
    return pl.pallas_call(
        functools.partial(adam_small_kernel, len(sums), widths if groups else None),
        grid=(1,),
        in_specs=[SMEM, SMEM] + [full(a.shape) for a in ins] + [ANY],
        out_specs=[full(s) for s, _ in shapes] + [ANY],
        out_shape=[jax.ShapeDtypeStruct(s, d) for s, d in shapes]
        + [jax.ShapeDtypeStruct(through.shape, through.dtype)],
        input_output_aliases={2 + len(ins): len(shapes)},
        compiler_params=params(),
        cost_estimate=cost(3),
        name="adam_small",
    )(scalars, me, *ins, through)


def adam_kernel(nb, grouped, kept, through, extra, sc_ref, me_ref, *refs):
    r_out = refs[len(refs) - through - (2 if grouped else 1) : len(refs) - through]
    if not extra:
        return adam_chunk(nb, grouped, kept + through, sc_ref, me_ref, refs, r_out)
    j = pl.program_id(0)

    @pl.when(j < pl.num_programs(0) - 1)
    def _():
        adam_chunk(nb, grouped, kept + through + extra, sc_ref, me_ref, refs, r_out)

    @pl.when(j == pl.num_programs(0) - 1)
    def _():
        for e, r in zip(refs[nb + 3 : nb + 3 + extra], r_out):
            r[:, :, 0 : e.shape[2]] = e[...]


def adam_chunk(nb, grouped, skipped, sc_ref, me_ref, refs, r_out):
    sums, (g_ref, f_ref, s_ref) = refs[:nb], refs[nb : nb + 3]
    f_out, s_out = refs[nb + 3 + skipped : nb + 5 + skipped]
    factor = clip_factor(sums)
    first, second, ratio = adam(
        g_ref[...].astype(F32) * factor, f_ref[...], s_ref[...], sc_ref[0] * matrix_rate
    )
    f_out[...] = first
    s_out[...] = second
    if not grouped:
        r_out[0][...] = ratio.astype(BF)
        return
    groups = 2 * r_out[0].shape[0]
    rows = ratio.shape[0] // groups
    padded = r_out[0].shape[1]
    for w in range(groups):
        piece = ratio[w * rows : (w + 1) * rows]
        piece = jnp.concatenate([piece, jnp.zeros((padded - rows, CH), F32)], 0).astype(BF)
        rel = me_ref[0] ^ w
        for core in range(2):

            @pl.when((rel & 1) == core)
            def _():
                r_out[core][rel >> 1] = piece


def adam_table(scalars, me, sums, de, first, second, groups, part, kept=(), through=(), extra=(), deps=()):
    width, rows = first.shape
    lo, hi = part
    here = (hi - lo) * CH + extra[0].shape[2] if extra else min(hi * CH, rows) - lo * CH
    blk = pl.BlockSpec((width, CH), lambda j: (0, jnp.minimum(j + lo, hi - 1)))
    shapes = [((width, rows), F32)] * 2
    specs = [blk, blk]
    if groups:
        stack = (groups // 2, pl.cdiv(width // groups, 8) * 8)
        shapes += [((*stack, here), BF)] * 2
        specs += [pl.BlockSpec((*stack, CH), lambda j: (0, 0, j))] * 2
    else:
        shapes += [((width, here), BF)]
        specs += [pl.BlockSpec((width, CH), lambda j: (0, j))]
    nb = len(sums)
    at, count = nb + 5 + len(extra), len(shapes)
    aliases = {at + i: i for i in range(len(kept))}
    aliases |= {at + len(kept) + i: count + i for i in range(len(through))}
    shapes += [(a.shape, a.dtype) for a in through]
    unread = [ANY] * (len(kept) + len(through))
    return call(
        functools.partial(
            adam_kernel, nb, bool(groups), len(kept), len(through), len(extra)
        ),
        (scalars, me, *sums, de, first, second, *extra, *kept, *through),
        deps,
        grid=(hi - lo + (1 if extra else 0),),
        in_specs=[SMEM, SMEM]
        + [full(a.shape) for a in sums]
        + [blk] * 3
        + [full(a.shape) for a in extra]
        + unread,
        out_specs=specs + [ANY] * len(through),
        out_shape=[jax.ShapeDtypeStruct(s, d) for s, d in shapes],
        input_output_aliases=aliases,
        compiler_params=params(),
        cost_estimate=cost(10),
        name="adam_table",
    )


def swap(value, axis, size, k):
    return lax.ppermute(value, axis, [(i, i ^ k) for i in range(size)])


def share(value, axis, size):
    return [value] + [swap(value, axis, size, k) for k in range(1, size)]


def sum_kernel(count, *refs):
    out = refs[count]
    out[...] = sum(p[...].astype(F32) for p in refs[:count]).astype(BF)


def sum_pieces(pieces, axis, size, through, deps=()):
    came = [pieces[0]] + [swap(pieces[k], axis, size, k) for k in range(1, size)]
    rest = (*through, *deps)

    def body(*refs):
        sum_kernel(size, *refs[:size], refs[size + len(rest)])

    return pl.pallas_call(
        body,
        grid=(1,),
        in_specs=[full(c.shape) for c in came] + [ANY] * len(rest),
        out_specs=[full(came[0].shape)] + [ANY] * len(through),
        out_shape=[jax.ShapeDtypeStruct(a.shape, a.dtype) for a in (came[0], *through)],
        input_output_aliases={size + i: 1 + i for i in range(len(through))},
        compiler_params=params(),
        cost_estimate=cost(2),
        name="sum_pieces",
    )(*came, *rest)


def turn_first(i):
    return i ^ (2 if i % 2 == 0 else 4)


def turn_second(i):
    return i ^ (4 if i % 2 == 0 else 2)


def permute(value, axis, size, partner):
    return lax.ppermute(value, axis, [(i, partner(i)) for i in range(size)])


def gather_pieces(own, axis, core):
    x, y = swap(own, axis, 8, 2), swap(own, axis, 8, 4)
    far = permute(jnp.where(core == 0, y, x), axis, 8, turn_first)
    near = [own, x, y, far]
    others = [swap(p, axis, 8, 1) for p in near]
    return [p for pair in zip(near, others) for p in pair]


def reduce_first(same, other, axis, core):
    y = (same.astype(F32) + swap(other, axis, 8, 1).astype(F32)).astype(BF)
    sent = jnp.stack([jnp.where(core == 0, y[1], y[2]), y[3]])
    return sent, jnp.where(core == 0, y[2], y[1]), y[0]


def reduce_last(sent, kept, own, axis):
    came = permute(sent, axis, 8, turn_first)
    relayed = (kept.astype(F32) + came[1].astype(F32)).astype(BF)
    total = own.astype(F32) + came[0].astype(F32)
    return total + permute(relayed, axis, 8, turn_second).astype(F32)


def outer_update(summed, total_tok, master, momentum, step_rate, decay):
    average = summed / total_tok + step_rate * decay * master
    momentum = outer_mom * momentum + average
    return (master - outer_rate * (average + outer_mom * momentum), momentum)


def local(
    tokens,
    targets,
    seq_counts,
    embed_w,
    qkv_w,
    out_w,
    mlp_w,
    gain_w,
    embed_mom,
    qkv_mom,
    out_mom,
    mlp_mom,
    gain_mom,
    embed_first,
    qkv_first,
    out_first,
    mlp_first,
    gain_first,
    embed_second,
    qkv_second,
    out_second,
    mlp_second,
    gain_second,
):
    nb = lax.axis_size("blk")
    nw = lax.axis_size("work")
    me = lax.axis_index("blk")
    wi = lax.axis_index("work")
    core = wi % 2
    me_arr = me.astype(jnp.int32).reshape(1)
    wi_arr = wi.astype(jnp.int32).reshape(1)
    slots, full_len = tokens.shape[1:]
    vrows = embed_w.shape[0]
    width = embed_first.shape[2]
    ff = mlp_first.shape[3]
    vpad = pl.cdiv(vrows, 2 * CH) * 2 * CH
    own_rows = width // nb
    paired = nw == 8

    et_own = embed_w.T.astype(BF)
    if paired:
        pieces = gather_pieces(et_own, "work", core)
    else:
        pieces = [lax.all_gather(et_own, "work", axis=0, tiled=True)]
    wi_prep = wi_arr if paired else jnp.zeros_like(wi_arr)

    cq, co, cf = qkv_w.shape[1], out_w.shape[1], mlp_w.shape[2]
    count_col = jnp.broadcast_to(seq_counts[0].astype(F32), (own_rows, 1))
    packed = jnp.concatenate([qkv_w, out_w, mlp_w[0], mlp_w[1], gain_w.T, count_col], 1)
    packed = lax.all_gather(packed.astype(BF), ("blk", "work"), axis=0, tiled=False)
    widths = (cq, co, cf, cf)
    c1, c3 = cq + co, cq + co + 2 * cf
    *weights, gains, count_row = split_weights(packed, nb, nw, widths)
    wqkv, wo, wm0, wm1, wqkv_t, wo_t, wm0_t, wm1_t = weights
    total_tok = jnp.sum(count_row) * full_len

    half = HD // 2
    frequency = rope_base ** (-jnp.arange(half).astype(F32) * 2.0 / HD)
    angles = frequency[:, None] * jnp.arange(full_len).astype(F32)[None, :]
    cosine, sine = jnp.cos(angles), jnp.sin(angles)

    count_seq = seq_counts[0]
    count_tok = (count_seq * full_len).astype(F32)
    valid = (jnp.arange(slots) < count_seq).astype(F32)

    def local_ids(ids, missing):
        ids = ids[0] - me * vrows
        return jnp.where((ids >= 0) & (ids < vrows), ids, missing)

    tok = local_ids(tokens, -1)[:, None, :]
    tgt = local_ids(targets, -1)[:, None, :]
    tok_rows = local_ids(tokens, vrows)
    tgt_rows = local_ids(targets, vrows)

    prep_ids = jnp.concatenate([wi_prep, me_arr])
    et, er, looked, more = prep(prep_ids, tok_rows, pieces, vpad, nb)
    fwd_weights = (wqkv_t, wo_t, wm0_t, wm1)
    bwd_weights = (wqkv, wo, wo_t, wm0, wm0_t, wm1, wm1_t)
    wants, mark = table_rows(tgt_rows[:-1], er, width)
    mine, *more = sum_pieces(looked, "blk", nb, more, (mark,))
    later, mark = table_rows(tgt_rows[-1:], er, width, (mark, wqkv))
    wants += later
    def sum_blocks(value, turn):
        return lax.psum(value, "blk", axis_index_groups=[[(k + turn) % nb for k in range(nb)]])

    rows = [share(mine, "blk", nb)]
    rows += [[sum_blocks(m, s)] for s, m in enumerate(more)]

    saved, heads, stats, backs, des, losses = {}, {}, {}, {}, {}, {}
    scalars = jnp.concatenate([1.0 / count_tok.reshape(1), valid])

    def forward(s, *deps):
        *kept, af = trunk_fwd(
            me_arr, rows[s], wants[s], fwd_weights, gains, cosine, sine, deps
        )
        saved[s] = kept
        heads[s] = [af]

    def head(s, *deps):
        p, peaks, stat = head_first(er, heads[s][0], deps)
        heads[s] += [p, peaks]
        stats[s] = share(stat, "blk", nb)

    def back(s, *deps):
        af, p, peaks = heads[s]
        gin, des[s], losses[s] = head_back(
            s, scalars, p, et, af, tgt[s], peaks, saved[s][3], stats[s], deps
        )
        backs[s] = sum_blocks(gin, s)

    for s in range(slots):
        forward(s, *([mark] if s == 0 else [des[s - 2]] if s > 1 else [stats[0][0]]))
        head(s)
        if s:
            back(s - 1, stats[s][0])
    back(slots - 1, *([des[slots - 2]] if slots > 1 else []))
    dxs, wgs, ggs = [], [], []
    for s in range(slots):
        dx, wg, gg = trunk_bwd(
            me_arr,
            backs[s],
            saved[s],
            bwd_weights,
            gains,
            cosine,
            sine,
            own_rows,
            [dxs[-1]] if s else [des[slots - 1]],
        )
        dxs.append(dx)
        wgs.append(wg)
        ggs.append(gg)
    des, losses = [des[s] for s in range(slots)], [losses[s] for s in range(slots)]
    de, wg, gg, both = token_grad(tok, des, dxs, wgs, ggs, losses)
    both = share(both, "blk", nb)

    tokens_of = count_tok.reshape(1)
    groups = nw if paired else 0
    first, second = embed_first[0].T, embed_second[0].T
    chunks = pl.cdiv(vrows, CH)
    cut = (5 * chunks + 7) // 8
    f0, s0, *pair = adam_table(
        tokens_of, wi_arr, both, de, first, second, groups, (0, cut)
    )
    p, q = pair[0], pair[-1]
    *small, result, p = adam_small(
        tokens_of,
        wi_arr,
        both,
        wg,
        gg,
        (qkv_first[0], out_first[0], mlp_first[0], gain_first[0].T),
        (qkv_second[0], out_second[0], mlp_second[0], gain_second[0].T),
        groups,
        widths,
        p,
    )
    waits, through, extra = [small[8]], (), ()
    if paired:
        begun = reduce_first(p, q, "work", core)
        through, extra = (begun[2],), small[8:10]
    efirst, esecond, *pair = adam_table(
        tokens_of, wi_arr, both, de, first, second, groups, (cut, chunks), (f0, s0), through, extra, waits
    )
    d1, d2, d3 = 3 * width, 4 * width, 4 * width + ff
    if paired:
        pair, through = pair[:2], pair[2:]
        begun = (*begun[:2], through[0])
        embed_sums = [begun, reduce_first(*pair, "work", core)]
        embed_sums = [reduce_last(*b, "work") for b in embed_sums]
        summed = embed_sums[1][: own_rows // 2, (chunks - cut) * CH :]
        embed_sums = [e[: width // nw] for e in embed_sums]
        embed_sums[1] = embed_sums[1][:, : vrows - cut * CH]
        summed = jnp.concatenate(jnp.split(summed, 2, 1), 0)
        parts = [summed[:, :cq], summed[:, cq : cq + co]]
        parts += [summed[:, c1 + i * cf : c1 + (i + 1) * cf] for i in range(2)]
        gain_sum = summed[:, c3 : c3 + 3].T
    else:
        embed_sums = [
            lax.psum_scatter(r, "work", scatter_dimension=0, tiled=True).astype(F32)
            for r in (p, pair[0])
        ]
        summed = lax.psum(small[8].astype(BF), "work").astype(F32)
        parts = [
            lax.dynamic_slice_in_dim(summed, lo + wi * size, size, 1)
            for lo, size in ((0, cq), (d1, co), (d2, cf), (d3, cf))
        ]
        gain_sum = summed[:, d3 + ff : d3 + ff + 3].T

    embed_sum = jnp.concatenate(embed_sums, 1).T
    sums = (embed_sum, parts[0], parts[1], jnp.stack(parts[2:]), gain_sum)
    masters = (embed_w, qkv_w, out_w, mlp_w, gain_w)
    moms = (embed_mom, qkv_mom, out_mom, mlp_mom, gain_mom)
    rates = (matrix_rate,) * 4 + (gain_rate,)
    decays = (decay_rate,) * 4 + (0.0,)
    updated = [
        outer_update(g, total_tok, w, m, r, d)
        for g, w, m, r, d in zip(sums, masters, moms, rates, decays)
    ]
    firsts = [efirst.T, *small[0:3], small[3].T]
    seconds = [esecond.T, *small[4:7], small[7].T]
    return (
        jnp.stack([result[0, 0], count_tok])[None],
        result[0, 1:2],
        *[u[0] for u in updated],
        *[u[1] for u in updated],
        *[a[None] for a in firsts],
        *[a[None] for a in seconds],
    )


def solution(mesh):
    weights = (
        P("blk", "work"),
        P("blk", "work"),
        P("blk", "work"),
        P(None, "blk", "work"),
        P(None, "blk"),
    )
    states = (
        P("work", "blk", None),
        P("work", "blk", None),
        P("work", "blk", None),
        P("work", None, "blk", None),
        P("work", None, "blk"),
    )
    in_specs = (
        P("work", None, None),
        P("work", None, None),
        P("work"),
        *weights,
        *weights,
        *states,
        *states,
    )
    out_specs = (P("work", None), P("work"), *weights, *weights, *states, *states)
    return jax.shard_map(local, mesh=mesh, in_specs=in_specs, out_specs=out_specs, check_vma=False)
```

```python
import functools
import math

import jax
import jax.numpy as jnp
from jax import lax
from jax.experimental import pallas as pl
from jax.experimental.pallas import tpu as pltpu
from jax.sharding import PartitionSpec as P

H = 6
HD = 48
STEP = 7

norm_eps = 1e-06
zloss_coef = 0.01
clip_limit = 0.05
beta_one = 0.9
beta_two = 0.95
adam_eps = 1e-08
decay_rate = 0.1
matrix_rate = 0.03
gain_rate = 0.3
outer_rate = 0.7
outer_mom = 0.9
rope_base = 10000.0

LOG2E = 1.0 / math.log(2.0)
LN2 = math.log(2.0)
SCALE = 1.0 / math.sqrt(HD)
BF = jnp.bfloat16
F32 = jnp.float32
NN = ((1,), (0,))
NT = ((1,), (1,))
CH = 1024
MIB = 1024 * 1024


def dot(a, b, dims=NN):
    return lax.dot_general(a, b, (dims, ((), ())), preferred_element_type=F32)


def params():
    return pltpu.CompilerParams(dimension_semantics=("arbitrary",), vmem_limit_bytes=58 * MIB)


def cost(micros):
    return pl.CostEstimate(flops=0, bytes_accessed=int(micros * 1.2e6), transcendentals=0)


def full(shape):
    return pl.BlockSpec(shape, lambda *_: (0,) * len(shape))


SMEM = pl.BlockSpec(memory_space=pltpu.SMEM)
ANY = pl.BlockSpec(memory_space=pl.ANY)


def call(kernel, ins, deps, **options):
    specs = options.pop("in_specs")

    def body(*refs):
        kernel(*refs[: len(ins)], *refs[len(ins) + len(deps) :])

    return pl.pallas_call(body, in_specs=[*specs, *([ANY] * len(deps))], **options)(*ins, *deps)


def pick_rows(ids_ref, s, tab, got, full_len):
    unroll = 32

    def body(i, carry):
        base = pl.multiple_of(i * unroll, unroll)
        for q in range(0, unroll, 8):
            rows = [tab[pl.ds(ids_ref[s, base + q + u], 1), :] for u in range(8)]
            got[pl.ds(pl.multiple_of(base + q, 8), 8), :] = jnp.concatenate(rows, 0)
        return carry

    lax.fori_loop(0, full_len // unroll, body, 0)


def rows_out(blk, got, outs):
    for k, out in enumerate(outs):
        width, lt = out.shape
        at = pl.multiple_of((blk ^ k) * lt, lt)
        out[...] = got[pl.ds(at, lt), 0:width].T.astype(BF)


def prep_kernel(count, vrows, nb, me_ref, ids_ref, *refs):
    pieces = refs[:count]
    et_ref, er_ref = refs[count : count + 2]
    outs = refs[count + 2 : count + 2 + nb]
    *others, tmp, tab, got = refs[count + 2 + nb :]
    j = pl.program_id(0)
    width, lt = outs[0].shape
    for k, piece in enumerate(pieces):
        tmp[me_ref[0] ^ k] = piece[...].astype(F32)
    e = jnp.concatenate([tmp[w] for w in range(count)], 0)
    lane = lax.broadcasted_iota(jnp.int32, (width, CH), 1) + j * CH
    e = jnp.where(lane < vrows, e, 0.0)
    et_ref[...] = e.astype(BF)
    rows = e.T
    tab[pl.ds(pl.multiple_of(j * CH, CH), CH), 0:width] = rows
    er_ref[:, 0:width] = rows.astype(BF)
    row = lax.broadcasted_iota(jnp.int32, (CH, 16), 0) + j * CH
    col = lax.broadcasted_iota(jnp.int32, (CH, 16), 1)
    er_ref[:, width:] = jnp.where((row >= vrows) & (col == 0), -60000.0, 0.0).astype(BF)

    @pl.when(j == pl.num_programs(0) - 1)
    def _():
        pick_rows(ids_ref, 0, tab, got, nb * lt)
        rows_out(me_ref[1], got, outs)
        for s, other in enumerate(others):
            pick_rows(ids_ref, s + 1, tab, got, nb * lt)
            other[...] = got[:, 0:width].T.astype(BF)


def prep(me, ids, pieces, vpad, nb):
    count = len(pieces)
    rows, vrows = pieces[0].shape
    width = count * rows
    slots, full_len = ids.shape
    lt = full_len // nb
    padded = pl.cdiv(width, 128) * 128
    et, er, *outs = pl.pallas_call(
        functools.partial(prep_kernel, count, vrows, nb),
        grid=(vpad // CH,),
        in_specs=[SMEM, SMEM] + [pl.BlockSpec((rows, CH), lambda j: (0, j))] * count,
        out_specs=[
            pl.BlockSpec((width, CH), lambda j: (0, j)),
            pl.BlockSpec((CH, width + 16), lambda j: (j, 0)),
            *[full((width, lt))] * nb,
            *[full((width, full_len))] * (slots - 1),
        ],
        out_shape=[
            jax.ShapeDtypeStruct((width, vpad), BF),
            jax.ShapeDtypeStruct((vpad, width + 16), BF),
            *[jax.ShapeDtypeStruct((width, lt), BF)] * nb,
            *[jax.ShapeDtypeStruct((width, full_len), BF)] * (slots - 1),
        ],
        scratch_shapes=[
            pltpu.VMEM((count, rows, CH), F32),
            pltpu.VMEM((vpad, padded), F32),
            pltpu.VMEM((full_len, padded), F32),
        ],
        compiler_params=params(),
        cost_estimate=cost(12),
        name="prep",
    )(me, ids, *pieces)
    return et, er, outs[:nb], outs[nb:]


def rows_kernel(ids_ref, er_ref, *refs):
    outs, (mark, tab, got) = refs[:-3], refs[-3:]
    width = outs[0].shape[0]
    mark[...] = jnp.zeros_like(mark)

    def fill(c, carry):
        here = pl.ds(pl.multiple_of(c * CH, CH), CH)
        tab[here, 0:width] = er_ref[here, 0:width].astype(F32)
        return carry

    lax.fori_loop(0, er_ref.shape[0] // CH, fill, 0)
    for s, out in enumerate(outs):
        pick_rows(ids_ref, s, tab, got, got.shape[0])
        out[...] = got[:, 0:width].T.astype(BF)


def table_rows(ids, er, width, deps=()):
    count, full_len = ids.shape
    padded = pl.cdiv(width, 128) * 128
    *rows, mark = call(
        rows_kernel,
        (ids, er),
        deps,
        grid=(1,),
        in_specs=[SMEM, full(er.shape)],
        out_specs=[full((width, full_len))] * count + [full((8, 128))],
        out_shape=[jax.ShapeDtypeStruct((width, full_len), BF)] * count
        + [jax.ShapeDtypeStruct((8, 128), F32)],
        scratch_shapes=[
            pltpu.VMEM((er.shape[0], padded), F32),
            pltpu.VMEM((full_len, padded), F32),
        ],
        compiler_params=params(),
        cost_estimate=cost(11),
        name="table_rows",
    )
    return rows, mark


def weights_kernel(nb, nw, widths, packed, *outs):
    straight, turned = outs[:4], outs[4:8]
    counts = jnp.zeros((1, 1), F32)
    for w in range(nw):
        part = [packed[b * nw + w].astype(F32) for b in range(nb)]
        part = jnp.concatenate(part, 0)
        at = 0
        for size, out in zip(widths, straight):
            out[:, w * size : (w + 1) * size] = part[:, at : at + size].astype(BF)
            at += size
        if w == 0:
            outs[8][...] = part[:, at : at + 3]
        counts += part[0:1, at + 3 : at + 4]
    outs[9][...] = counts
    for out, flip in zip(straight, turned):
        flip[...] = out[...].astype(F32).T.astype(BF)


def split_weights(packed, nb, nw, widths):
    rows = packed.shape[1]
    width = nb * rows
    shapes = [(width, nw * size) for size in widths]
    outs = [(s, BF) for s in shapes] + [(s[::-1], BF) for s in shapes]
    outs += [((width, 3), F32), ((1, 1), F32)]
    return pl.pallas_call(
        functools.partial(weights_kernel, nb, nw, widths),
        grid=(1,),
        in_specs=[full(packed.shape)],
        out_specs=[full(s) for s, _ in outs],
        out_shape=[jax.ShapeDtypeStruct(s, d) for s, d in outs],
        compiler_params=params(),
        cost_estimate=cost(3),
        name="split_weights",
    )(packed)


def norm_t(x, gain):
    scale = lax.rsqrt(jnp.mean(x * x, 0, keepdims=True) + norm_eps)
    return x * scale * gain, scale


def norm_t_bwd(x, scale, gain, incoming):
    unit = x * scale
    inner = incoming * gain
    return scale * (inner - unit * jnp.mean(inner * unit, 0, keepdims=True)), incoming * unit


def turn(u, cosine, sine):
    rows, lt = u.shape
    half = cosine.shape[0]
    u = u.reshape(rows // (2 * half), 2, half, lt)
    a, b = u[:, 0], u[:, 1]
    return jnp.stack([a * cosine - b * sine, a * sine + b * cosine], 1).reshape(rows, lt)


def place(me, pieces, out):
    lt = pieces[0].shape[1]
    for k, piece in enumerate(pieces):
        if len(pieces) == 1:
            out[...] = piece[...]
        else:
            out[:, pl.ds(pl.multiple_of((me ^ k) * lt, lt), lt)] = piece[...]


def interleave(parts):
    while parts:
        parts = [p for p in parts if next(p, 1) is None]


def causal(lt):
    keys = lax.broadcasted_iota(jnp.int32, (lt, lt), 0)
    queries = lax.broadcasted_iota(jnp.int32, (lt, lt), 1)
    return keys <= queries


def gelu_parts(u):
    k0 = math.sqrt(2.0 / math.pi)
    square = u * u
    th = jnp.tanh(k0 * (u + 0.044715 * u * square))
    act = 0.5 * u * (1.0 + th)
    return act, th, square, k0


def gelu_slope(u, th, square, k0):
    return 0.5 * (1.0 + th) + 0.5 * u * (1.0 - th * th) * k0 * (1.0 + 3.0 * 0.044715 * square)


def trunk_fwd_kernel(count, me_ref, *refs):
    (want, wqkv_t, wo_t, wm0_t, wm1, gains, cos_ref, sin_ref) = refs[count : count + 8]
    (x0_out, qkv_out, o_out, lse_out, af_out, krow) = refs[count + 8 :]
    width, full_len = x0_out.shape
    lt = min(256, full_len)
    nb = full_len // lt
    root = math.sqrt(width)
    place(me_ref[0], refs[:count], x0_out)
    def project(j):
        here = slice(j * lt, (j + 1) * lt)
        x = x0_out[:, here].astype(F32) * root
        a1, _ = norm_t(x, gains[:, 0:1])
        yield
        y = dot(wqkv_t[...], a1.astype(BF))
        yield
        cosine, sine = cos_ref[:, here], sin_ref[:, here]
        q = turn(y[:width], cosine, sine) * (SCALE * LOG2E)
        k = turn(y[width : 2 * width], cosine, sine)
        qkv_out[0:width, here] = q.astype(BF)
        qkv_out[width : 2 * width, here] = k.astype(BF)
        qkv_out[2 * width :, here] = y[2 * width :].astype(BF)
        for h in range(H):
            krow[h, here, :] = k[h * HD : (h + 1) * HD].T.astype(BF)

    interleave([project(j) for j in range(nb)])
    lse_out[...] = jnp.zeros_like(lse_out)

    def head(h, j):
        rows = slice(h * HD, (h + 1) * HD)
        values = slice(2 * width + h * HD, 2 * width + (h + 1) * HD)
        here, before = slice(j * lt, (j + 1) * lt), slice(0, j * lt)
        q = qkv_out[rows, here]
        s_diag = jnp.where(causal(lt), dot(krow[h, here, :], q), -1e30)
        peak = jnp.max(s_diag, 0, keepdims=True)
        if j:
            s_off = dot(krow[h, before, :], q)
            peak = jnp.maximum(peak, jnp.max(s_off, 0, keepdims=True))
        yield
        p_diag = jnp.exp2(s_diag - peak)
        total = jnp.sum(p_diag, 0, keepdims=True)
        if j:
            p_off = jnp.exp2(s_off - peak)
            total = total + jnp.sum(p_off, 0, keepdims=True)
        yield
        mix = dot(qkv_out[values, here], p_diag.astype(BF))
        if j:
            mix = mix + dot(qkv_out[values, before], p_off.astype(BF))
        o_out[rows, here] = (mix / total).astype(BF)
        lse_out[h : h + 1, here] = peak + jnp.log2(total)

    for j in range(nb):
        interleave([head(h, j) for h in range(H)])

    def finish(j):
        here = slice(j * lt, (j + 1) * lt)
        x = x0_out[:, here].astype(F32) * root
        h1 = x + dot(wo_t[...], o_out[:, here])
        yield
        a2, _ = norm_t(h1, gains[:, 1:2])
        yield
        u = dot(wm0_t[...], a2.astype(BF))
        yield
        act = gelu_parts(u)[0].astype(BF)
        yield
        h2 = h1 + dot(wm1[...], act)
        yield
        af, _ = norm_t(h2, gains[:, 2:3])
        af = (af * LOG2E).astype(BF)
        af_out[0:width, here] = af
        tail = lax.broadcasted_iota(jnp.int32, (af_out.shape[0] - width, lt), 0)
        af_out[width:, here] = jnp.where(tail == 0, 1.0, 0.0).astype(BF)

    interleave([finish(j) for j in range(nb)])
    picked = af_out[0:width, :].astype(F32) * want[...].astype(F32)
    lse_out[H : H + 1, :] = jnp.sum(picked, 0, keepdims=True)


def trunk_fwd(me, pieces, want, weights, gains, cosine, sine, deps=()):
    width, full_len = want.shape
    ins = (me, *pieces, want, *weights, gains, cosine, sine)
    shapes = [
        ((width, full_len), BF),
        ((3 * width, full_len), BF),
        ((width, full_len), BF),
        ((8, full_len), F32),
        ((width + 16, full_len), BF),
    ]
    return call(
        functools.partial(trunk_fwd_kernel, len(pieces)),
        ins,
        deps,
        grid=(1,),
        in_specs=[SMEM] + [full(a.shape) for a in ins[1:]],
        out_specs=[full(s) for s, _ in shapes],
        out_shape=[jax.ShapeDtypeStruct(s, d) for s, d in shapes],
        scratch_shapes=[pltpu.VMEM((H, full_len, HD), BF)],
        compiler_params=params(),
        cost_estimate=cost(13),
        name="trunk_fwd",
    )


def head_kernel(er_ref, af_ref, p_ref, m_ref, st_ref, s_ref, run, cur, z_ref):
    j = pl.program_id(0)
    full_len = af_ref.shape[1]
    lt = z_ref.shape[1]
    tiles = [slice(t, t + lt) for t in range(0, full_len, lt)]

    def emit(here, z, peak):
        p = jnp.exp2(z - peak)
        p_ref[:, here] = p.astype(BF)
        m_ref[pl.ds(j, 1), here] = peak
        total = jnp.sum(p.reshape(CH // 8, 8, lt), 0)
        s_ref[pl.ds(j, 1), here] = jnp.sum(total, 0, keepdims=True)

    @pl.when(j == 0)
    def _():
        run[...] = jnp.full_like(run, -1e30)
        cur[...] = jnp.zeros_like(cur)

    @pl.when(j > 0)
    def _():
        for here in tiles:
            z = dot(er_ref[...], af_ref[:, here])
            peak = jnp.max(z.reshape(CH // 8, 8, lt), 0)
            cur[0:1, here] = jnp.max(peak, 0, keepdims=True)
            emit(here, z, run[0:1, here])

    again = (j == 0) | (jnp.max(cur[0:1, :] - run[0:1, :]) > 60.0)

    @pl.when(again)
    def _():
        for here in tiles:
            z_ref[...] = dot(er_ref[...], af_ref[:, here])
            peak = jnp.max(z_ref[...], 0, keepdims=True)
            peak = jnp.maximum(peak, run[0:1, here])
            cur[0:1, here] = peak
            emit(here, z_ref[...], peak)

    run[0:1, :] = jnp.maximum(run[0:1, :], cur[0:1, :])

    @pl.when(j == pl.num_programs(0) - 1)
    def _():
        peak = run[0:1, :]
        total = jnp.sum(s_ref[...] * jnp.exp2(m_ref[...] - peak), 0, keepdims=True)
        st_ref[...] = jnp.zeros_like(st_ref)
        st_ref[0:1, :] = peak
        st_ref[1:2, :] = total


def head_first(er, af, deps=()):
    vpad, depth = er.shape
    full_len = af.shape[1]
    chunks = vpad // CH
    shapes = [((vpad, full_len), BF), ((chunks, full_len), F32), ((8, full_len), F32)]
    return call(
        head_kernel,
        (er, af),
        deps,
        grid=(chunks,),
        in_specs=[pl.BlockSpec((CH, depth), lambda j: (j, 0)), full(af.shape)],
        out_specs=[pl.BlockSpec((CH, full_len), lambda j: (j, 0))]
        + [full(s) for s, _ in shapes[1:]],
        out_shape=[jax.ShapeDtypeStruct(s, d) for s, d in shapes],
        scratch_shapes=[
            pltpu.VMEM((chunks, full_len), F32),
            pltpu.VMEM((8, full_len), F32),
            pltpu.VMEM((8, full_len), F32),
            pltpu.VMEM((CH, min(512, full_len)), F32),
        ],
        compiler_params=params(),
        cost_estimate=cost(16),
        name="head_first",
    )


def head_back_kernel(slot, nb, sc_ref, *refs):
    (p_ref, et_ref, af_ref, tgt_ref, m_ref, pick_ref) = refs[:6]
    stats = refs[6 : 6 + nb]
    (out, de_ref, loss_ref, acc, s_ref, d_ref) = refs[6 + nb :]
    j = pl.program_id(0)
    width, full_len = out.shape
    lt = min(256, full_len)
    valid = sc_ref[1 + slot]
    weight = valid * sc_ref[0]

    @pl.when(j == 0)
    def _():
        acc[...] = jnp.zeros_like(acc)
        top = functools.reduce(jnp.maximum, [b[0:1, :] for b in stats])
        total = sum(b[1:2, :] * jnp.exp2(b[0:1, :] - top) for b in stats)
        lse2 = top + jnp.log2(total)
        lse = lse2 * LN2
        boost = (1.0 + 2.0 * zloss_coef * lse) * weight
        pick = pick_ref[H : H + 1, :]
        s_ref[...] = jnp.exp2(m_ref[...] - lse2) * boost
        d_ref[0:1, :] = jnp.exp2(pick - lse2) * boost - weight
        loss_ref[...] = jnp.zeros_like(loss_ref)
        loss_ref[0:1, :] = (lse + zloss_coef * lse * lse) * valid
        loss_ref[1:2, :] = pick * LN2 * valid

    rows = lax.broadcasted_iota(jnp.int32, (CH, lt), 0)
    for half in range(2):
        chunk = 2 * j + half
        there = slice(half * CH, (half + 1) * CH)
        total = None
        for t in range(full_len // lt):
            here = slice(t * lt, (t + 1) * lt)
            grad = jnp.where(
                rows == tgt_ref[:, here] - chunk * CH,
                d_ref[0:1, here],
                p_ref[there, here].astype(F32) * s_ref[pl.ds(chunk, 1), here],
            ).astype(BF)
            acc[:, here] += dot(et_ref[:, there], grad)
            part = dot(af_ref[0:width, here], grad, NT)
            total = part if total is None else total + part
        de_ref[:, there] = (total * LN2).astype(BF)

    @pl.when(j == pl.num_programs(0) - 1)
    def _():
        out[...] = acc[...].astype(BF)


def head_back(slot, scalars, p, et, af, tgt, peaks, picks, stats, deps=()):
    nb = len(stats)
    width, vpad = et.shape
    full_len = tgt.shape[1]
    tall = pl.BlockSpec((2 * CH, full_len), lambda j: (j, 0))
    wide = pl.BlockSpec((width, 2 * CH), lambda j: (0, j))
    rest = (af, tgt, peaks, picks, *stats)
    return call(
        functools.partial(head_back_kernel, slot, nb),
        (scalars, p, et, *rest),
        deps,
        grid=(vpad // (2 * CH),),
        in_specs=[SMEM, tall, wide] + [full(a.shape) for a in rest],
        out_specs=[full((width, full_len)), wide, full((8, full_len))],
        out_shape=[
            jax.ShapeDtypeStruct((width, full_len), BF),
            jax.ShapeDtypeStruct((width, vpad), BF),
            jax.ShapeDtypeStruct((8, full_len), F32),
        ],
        scratch_shapes=[
            pltpu.VMEM((width, full_len), F32),
            pltpu.VMEM(peaks.shape, F32),
            pltpu.VMEM((8, full_len), F32),
        ],
        compiler_params=params(),
        cost_estimate=cost(15),
        name="head_back",
    )


def trunk_bwd_kernel(me_ref, *refs):
    (gin, x0, qkv, o_ref, lse) = refs[:5]
    (wqkv, wo, wo_t, wm0, wm0_t, wm1, wm1_t, gains, cos_ref, sin_ref) = refs[5:15]
    (dx_out, wg_out, gg_out) = refs[15:18]
    (krow, vrow, dqkv, dqkv_b, dh1_s, dh1_b, a_s, du_s, act_s, df_s, do_s, delta, wg, gg_s) = refs[18:]
    me = me_ref[0]
    width, full_len = x0.shape
    ff = du_s.shape[0]
    lt = min(256, full_len)
    nb = full_len // lt
    root = math.sqrt(width)
    gain_sums = [[None] * nb for _ in range(3)]

    def outer(j):
        here = slice(j * lt, (j + 1) * lt)
        h1 = x0[:, here].astype(F32) * root + dot(wo_t[...], o_ref[:, here])
        yield
        a2, scale = norm_t(h1, gains[:, 1:2])
        a2 = a2.astype(BF)
        a_s[:, here] = a2
        yield
        u = dot(wm0_t[...], a2)
        yield
        act, th, square, k0 = gelu_parts(u)
        slope = gelu_slope(u, th, square, k0)
        act = act.astype(BF)
        act_s[:, here] = act
        yield
        h2 = h1 + dot(wm1[...], act)
        yield
        _, scale2 = norm_t(h2, 1.0)
        dh2, gg = norm_t_bwd(h2, scale2, gains[:, 2:3], gin[:, here].astype(F32))
        gain_sums[2][j] = jnp.sum(gg, 1, keepdims=True)
        df = dh2.astype(BF)
        df_s[:, here] = df
        yield
        du = (dot(wm1_t[...], df) * slope).astype(BF)
        du_s[:, here] = du
        yield
        da2 = dot(wm0[...], du)
        yield
        dmid, gg = norm_t_bwd(h1, scale, gains[:, 1:2], da2)
        gain_sums[1][j] = jnp.sum(gg, 1, keepdims=True)
        dh1 = dh2 + dmid
        dh1_s[:, here] = dh1
        dh1b = dh1.astype(BF)
        dh1_b[:, here] = dh1b
        yield
        do = dot(wo[...], dh1b).astype(BF)
        do_s[:, here] = do
        weighed = (do.astype(F32) * o_ref[:, here].astype(F32)).reshape(H, HD, lt)
        delta[0:H, here] = jnp.sum(weighed, 1)
        yield
        for h in range(H):
            lo = width + h * HD
            krow[h, here, :] = qkv[lo : lo + HD, here].astype(F32).T.astype(BF)
            vrow[h, here, :] = qkv[lo + width : lo + width + HD, here].astype(F32).T.astype(BF)

    interleave([outer(j) for j in range(nb)])
    wg[:, 4 * width : 4 * width + ff] = dot(a_s[...], du_s[...], NT)
    wg[:, 4 * width + ff :] = dot(df_s[...], act_s[...], NT)
    wg[:, 3 * width : 4 * width] = dot(o_ref[...], dh1_b[...], NT)

    def head(h, j):
        qs, ks, vs = (pl.ds(pl.multiple_of(a + h * HD, 16), HD) for a in (0, width, 2 * width))
        here = slice(j * lt, (j + 1) * lt)
        parts = [(here, True)] + ([(slice(0, j * lt), False)] if j else [])
        q, do = qkv[qs, here], do_s[qs, here]
        lse_row, delta_row = lse[pl.ds(h, 1), here], delta[pl.ds(h, 1), here]
        scores = [(dot(krow[h, t, :], q), dot(vrow[h, t, :], do)) for t, _ in parts]
        yield
        grads = []
        for (there, diagonal), (s, dp) in zip(parts, scores):
            p = jnp.exp2(s - lse_row)
            if diagonal:
                p = jnp.where(causal(lt), p, 0.0)
            grads.append((p.astype(BF), (p * (dp - delta_row)).astype(BF)))
        yield
        dq = 0.0
        for (there, _), (pb, dsb) in zip(parts, grads):
            dq = dq + dot(qkv[ks, there], dsb)
            dk, dv = dot(q, dsb, NT), dot(do, pb, NT)
            if j == nb - 1:
                dqkv[ks, there] = dk
                dqkv[vs, there] = dv
            else:
                dqkv[ks, there] += dk
                dqkv[vs, there] += dv
        dqkv[qs, here] = dq

    def heads(i, carry):
        for j in reversed(range(nb)):
            interleave([head(i * 2 + u, j) for u in range(2)])
        return carry

    lax.fori_loop(0, H // 2, heads, 0)

    def inner(j):
        here = slice(j * lt, (j + 1) * lt)
        cosine, sine = cos_ref[:, here], -sin_ref[:, here]
        dq = turn(dqkv[0:width, here], cosine, sine) * SCALE
        dk = turn(dqkv[width : 2 * width, here], cosine, sine) * LN2
        dqkv_b[0:width, here] = dq.astype(BF)
        dqkv_b[width : 2 * width, here] = dk.astype(BF)
        dqkv_b[2 * width :, here] = dqkv[2 * width :, here].astype(BF)
        x = x0[:, here].astype(F32) * root
        a1, scale = norm_t(x, gains[:, 0:1])
        a_s[:, here] = a1.astype(BF)
        yield
        da1 = dot(wqkv[...], dqkv_b[:, here])
        yield
        dlow, gg = norm_t_bwd(x, scale, gains[:, 0:1], da1)
        gain_sums[0][j] = jnp.sum(gg, 1, keepdims=True)
        dx_out[:, here] = ((dh1_s[:, here] + dlow) * root).astype(BF)

    interleave([inner(j) for j in range(nb)])
    wg[:, 0 : 3 * width] = dot(a_s[...], dqkv_b[...], NT)
    own = wg_out.shape[0]
    wg_out[...] = wg[pl.ds(pl.multiple_of(me * own, 8), own), :]
    lane = lax.broadcasted_iota(jnp.int32, gg_s.shape, 1)
    gg_s[...] = sum(jnp.where(lane == i, sum(gain_sums[i]), 0.0) for i in range(3))
    gg_out[...] = gg_s[pl.ds(pl.multiple_of(me * own, 8), own), :]


def trunk_bwd(me, gin, saved, weights, gains, cosine, sine, own, deps=()):
    width, full_len = gin.shape
    ff = weights[3].shape[1]
    ins = (me, gin, *saved, *weights, gains, cosine, sine)
    cols = 4 * width + 2 * ff
    shapes = [((width, full_len), BF), ((own, cols), F32), ((own, 128), F32)]
    return call(
        trunk_bwd_kernel,
        ins,
        deps,
        grid=(1,),
        in_specs=[SMEM] + [full(a.shape) for a in ins[1:]],
        out_specs=[full(s) for s, _ in shapes],
        out_shape=[jax.ShapeDtypeStruct(s, d) for s, d in shapes],
        scratch_shapes=[
            pltpu.VMEM((H, full_len, HD), BF),
            pltpu.VMEM((H, full_len, HD), BF),
            pltpu.VMEM((3 * width, full_len), F32),
            pltpu.VMEM((3 * width, full_len), BF),
            pltpu.VMEM((width, full_len), F32),
            pltpu.VMEM((width, full_len), BF),
            pltpu.VMEM((width, full_len), BF),
            pltpu.VMEM((ff, full_len), BF),
            pltpu.VMEM((ff, full_len), BF),
            pltpu.VMEM((width, full_len), BF),
            pltpu.VMEM((width, full_len), BF),
            pltpu.VMEM((8, full_len), F32),
            pltpu.VMEM((width, cols), F32),
            pltpu.VMEM((width, 128), F32),
        ],
        compiler_params=params(),
        cost_estimate=cost(24),
        name="trunk_bwd",
    )


def folded(values):
    rows, cols = values.shape
    values = jnp.sum(values.reshape(rows // 8, 8, cols), 0)
    return sum(values[:, c : c + 128] for c in range(0, cols, 128))


def token_sum(first, tok_ref, de_refs, dx_refs):
    full_len = tok_ref.shape[2]
    lt = min(512, full_len)
    rows = lax.broadcasted_iota(jnp.int32, (CH, lt), 0) + pl.program_id(0) * CH
    total = sum(d[...].astype(F32) for d in de_refs)
    for s, dx in enumerate(dx_refs):
        for t in range(full_len // lt):
            here = slice(t * lt, (t + 1) * lt)
            hot = jnp.where(rows == tok_ref[first + s, :, here], 1.0, 0.0).astype(BF)
            total = total + dot(dx[:, here], hot, NT)
    return total


def token_part_kernel(count, tok_ref, *refs):
    *ins, out = refs
    out[...] = token_sum(0, tok_ref, ins[:count], ins[count:]).astype(BF)


def token_part(tok, des, dxs):
    width, vpad = des[0].shape
    blk = pl.BlockSpec((width, CH), lambda j: (0, j))
    return pl.pallas_call(
        functools.partial(token_part_kernel, len(des)),
        grid=(vpad // CH,),
        in_specs=[full(tok.shape)] + [blk] * len(des) + [full(a.shape) for a in dxs],
        out_specs=blk,
        out_shape=jax.ShapeDtypeStruct((width, vpad), BF),
        compiler_params=params(),
        cost_estimate=cost(13),
        name="token_part",
    )(tok, *des, *dxs)


def token_grad_kernel(first, slots, tok_ref, de_ref, *refs):
    count = slots - first
    dx_refs, refs = refs[:count], refs[count:]
    wg_refs, gg_refs, loss_refs = refs[:slots], refs[slots : 2 * slots], refs[2 * slots : 3 * slots]
    out_ref, wg_out, gg_out, sum_out, acc = refs[3 * slots :]
    j = pl.program_id(0)

    @pl.when(j == 0)
    def _():
        wg = sum(w[...] for w in wg_refs)
        gg = sum(g[...] for g in gg_refs)
        wg_out[...] = wg
        gg_out[...] = gg
        acc[...] = folded(wg * wg) + folded(gg * gg)

    total = token_sum(first, tok_ref, [de_ref], dx_refs)
    out_ref[...] = total.astype(BF)
    acc[...] += folded(total * total)

    @pl.when(j == pl.num_programs(0) - 1)
    def _():
        lane = lax.broadcasted_iota(jnp.int32, sum_out.shape, 1)
        pick = jnp.sum(sum(r[1:2, :] for r in loss_refs))
        lse = jnp.sum(sum(r[0:1, :] for r in loss_refs))
        tail = jnp.where(lane == 2, lse, 0.0)
        sum_out[...] = jnp.where(lane == 0, jnp.sum(acc[...]), jnp.where(lane == 1, pick, tail))


def token_grad(tok, de, dxs, wgs, ggs, losses):
    slots = len(wgs)
    width, vpad = de.shape
    blk = pl.BlockSpec((width, CH), lambda j: (0, j))
    rest = (*dxs, *wgs, *ggs, *losses)
    shapes = [(wgs[0].shape, F32), (ggs[0].shape, F32), ((8, 128), F32)]
    return pl.pallas_call(
        functools.partial(token_grad_kernel, slots - len(dxs), slots),
        grid=(vpad // CH,),
        in_specs=[full(tok.shape), blk] + [full(a.shape) for a in rest],
        out_specs=[blk] + [full(s) for s, _ in shapes],
        out_shape=[jax.ShapeDtypeStruct((width, vpad), BF)]
        + [jax.ShapeDtypeStruct(s, d) for s, d in shapes],
        scratch_shapes=[pltpu.VMEM((8, 128), F32)],
        compiler_params=params(),
        cost_estimate=cost(9),
        name="token_grad",
    )(tok, de, *rest)


def clip_factor(sums):
    total = sum(s[0:1, 0:1] for s in sums)
    return clip_limit / jnp.maximum(jnp.sqrt(total), clip_limit)


def adam(gradient, first, second, weight):
    first = beta_one * first + (1.0 - beta_one) * gradient
    second = beta_two * second + (1.0 - beta_two) * gradient * gradient
    ratio = (first * (weight / (1.0 - beta_one**STEP))) / (
        jnp.sqrt(second * (1.0 / (1.0 - beta_two**STEP))) + adam_eps
    )
    return first, second, ratio


def adam_small_kernel(nb, widths, sc_ref, me_ref, *refs):
    factor = clip_factor(refs[:nb])
    (wg, gg, qf, of, mf, gf, qs, os_, ms, gs) = refs[nb : nb + 10]
    (qf2, of2, mf2, gf2, qs2, os2, ms2, gs2, *r_out) = refs[nb + 11 : -2]
    res = refs[-2]
    sums = sum(r[...] for r in refs[:nb])
    lane = lax.broadcasted_iota(jnp.int32, res.shape, 1)
    loss = refs[0][:, 2:3] - sums[:, 1:2]
    res[...] = jnp.where(lane == 0, loss, jnp.where(lane == 1, jnp.sqrt(sums[:, 0:1]), 0.0))
    weight = sc_ref[0] * matrix_rate
    at = 0
    ratios = []
    for f, s, f2, s2 in (
        (qf, qs, qf2, qs2),
        (of, os_, of2, os2),
        (mf.at[0], ms.at[0], mf2.at[0], ms2.at[0]),
        (mf.at[1], ms.at[1], mf2.at[1], ms2.at[1]),
    ):
        here = slice(at, at + f.shape[1])
        f2[...], s2[...], ratio = adam(wg[:, here] * factor, f[...], s[...], weight)
        ratios.append(ratio)
        at = here.stop
    f2, s2, ratio = adam(gg[:, 0:3] * factor, gf[...], gs[...], sc_ref[0] * gain_rate)
    gf2[...] = f2
    gs2[...] = s2
    if not widths:
        at = 0
        for r in ratios:
            r_out[0][:, at : at + r.shape[1]] = r
            at += r.shape[1]
        r_out[0][:, at:] = jnp.zeros_like(r_out[0][:, at:])
        r_out[0][:, at : at + 3] = ratio
        return
    rows, cols = ratio.shape[0] // 2, r_out[0].shape[2] // 2
    blank = jnp.zeros((2 * rows, cols - sum(widths) - 3), F32)
    below = jnp.zeros((r_out[0].shape[1] - rows, 2 * cols), F32)
    for w in range(2 * r_out[0].shape[0]):
        parts = [r[:, w * size : (w + 1) * size] for r, size in zip(ratios, widths)]
        piece = jnp.concatenate([*parts, ratio, blank], 1)
        piece = jnp.concatenate([piece[:rows], piece[rows:]], 1)
        piece = jnp.concatenate([piece, below], 0).astype(BF)
        rel = me_ref[0] ^ w
        for core in range(2):

            @pl.when((rel & 1) == core)
            def _():
                r_out[core][rel >> 1] = piece


def adam_small(scalars, me, sums, wg, gg, firsts, seconds, groups, widths, through):
    ins = (*sums, wg, gg, *firsts, *seconds)
    shapes = [(a.shape, F32) for a in (*firsts, *seconds)]
    if groups:
        cols = pl.cdiv(sum(widths) + 3, 128) * 128
        rows = pl.cdiv(wg.shape[0] // 2, 8) * 8
        shapes += [((groups // 2, rows, 2 * cols), BF)] * 2
    else:
        shapes.append(((wg.shape[0], wg.shape[1] + 128), F32))
    shapes.append((sums[0].shape, F32))
    return pl.pallas_call(
        functools.partial(adam_small_kernel, len(sums), widths if groups else None),
        grid=(1,),
        in_specs=[SMEM, SMEM] + [full(a.shape) for a in ins] + [ANY],
        out_specs=[full(s) for s, _ in shapes] + [ANY],
        out_shape=[jax.ShapeDtypeStruct(s, d) for s, d in shapes]
        + [jax.ShapeDtypeStruct(through.shape, through.dtype)],
        input_output_aliases={2 + len(ins): len(shapes)},
        compiler_params=params(),
        cost_estimate=cost(3),
        name="adam_small",
    )(scalars, me, *ins, through)


def adam_kernel(nb, grouped, kept, through, extra, sc_ref, me_ref, *refs):
    r_out = refs[len(refs) - through - (2 if grouped else 1) : len(refs) - through]
    if not extra:
        return adam_chunk(nb, grouped, kept + through, sc_ref, me_ref, refs, r_out)
    j = pl.program_id(0)

    @pl.when(j < pl.num_programs(0) - 1)
    def _():
        adam_chunk(nb, grouped, kept + through + extra, sc_ref, me_ref, refs, r_out)

    @pl.when(j == pl.num_programs(0) - 1)
    def _():
        for e, r in zip(refs[nb + 3 : nb + 3 + extra], r_out):
            r[:, :, 0 : e.shape[2]] = e[...]


def adam_chunk(nb, grouped, skipped, sc_ref, me_ref, refs, r_out):
    sums, (g_ref, f_ref, s_ref) = refs[:nb], refs[nb : nb + 3]
    f_out, s_out = refs[nb + 3 + skipped : nb + 5 + skipped]
    factor = clip_factor(sums)
    first, second, ratio = adam(
        g_ref[...].astype(F32) * factor, f_ref[...], s_ref[...], sc_ref[0] * matrix_rate
    )
    f_out[...] = first
    s_out[...] = second
    if not grouped:
        r_out[0][...] = ratio.astype(BF)
        return
    groups = 2 * r_out[0].shape[0]
    rows = ratio.shape[0] // groups
    padded = r_out[0].shape[1]
    for w in range(groups):
        piece = ratio[w * rows : (w + 1) * rows]
        piece = jnp.concatenate([piece, jnp.zeros((padded - rows, CH), F32)], 0).astype(BF)
        rel = me_ref[0] ^ w
        for core in range(2):

            @pl.when((rel & 1) == core)
            def _():
                r_out[core][rel >> 1] = piece


def adam_table(scalars, me, sums, de, first, second, groups, part, kept=(), through=(), extra=(), deps=()):
    width, rows = first.shape
    lo, hi = part
    here = (hi - lo) * CH + extra[0].shape[2] if extra else min(hi * CH, rows) - lo * CH
    blk = pl.BlockSpec((width, CH), lambda j: (0, jnp.minimum(j + lo, hi - 1)))
    shapes = [((width, rows), F32)] * 2
    specs = [blk, blk]
    if groups:
        stack = (groups // 2, pl.cdiv(width // groups, 8) * 8)
        shapes += [((*stack, here), BF)] * 2
        specs += [pl.BlockSpec((*stack, CH), lambda j: (0, 0, j))] * 2
    else:
        shapes += [((width, here), BF)]
        specs += [pl.BlockSpec((width, CH), lambda j: (0, j))]
    nb = len(sums)
    at, count = nb + 5 + len(extra), len(shapes)
    aliases = {at + i: i for i in range(len(kept))}
    aliases |= {at + len(kept) + i: count + i for i in range(len(through))}
    shapes += [(a.shape, a.dtype) for a in through]
    unread = [ANY] * (len(kept) + len(through))
    return call(
        functools.partial(
            adam_kernel, nb, bool(groups), len(kept), len(through), len(extra)
        ),
        (scalars, me, *sums, de, first, second, *extra, *kept, *through),
        deps,
        grid=(hi - lo + (1 if extra else 0),),
        in_specs=[SMEM, SMEM]
        + [full(a.shape) for a in sums]
        + [blk] * 3
        + [full(a.shape) for a in extra]
        + unread,
        out_specs=specs + [ANY] * len(through),
        out_shape=[jax.ShapeDtypeStruct(s, d) for s, d in shapes],
        input_output_aliases=aliases,
        compiler_params=params(),
        cost_estimate=cost(10),
        name="adam_table",
    )


def swap(value, axis, size, k):
    return lax.ppermute(value, axis, [(i, i ^ k) for i in range(size)])


def share(value, axis, size):
    return [value] + [swap(value, axis, size, k) for k in range(1, size)]


def sum_kernel(count, *refs):
    out = refs[count]
    out[...] = sum(p[...].astype(F32) for p in refs[:count]).astype(BF)


def sum_pieces(pieces, axis, size, through, deps=()):
    came = [pieces[0]] + [swap(pieces[k], axis, size, k) for k in range(1, size)]
    rest = (*through, *deps)

    def body(*refs):
        sum_kernel(size, *refs[:size], refs[size + len(rest)])

    return pl.pallas_call(
        body,
        grid=(1,),
        in_specs=[full(c.shape) for c in came] + [ANY] * len(rest),
        out_specs=[full(came[0].shape)] + [ANY] * len(through),
        out_shape=[jax.ShapeDtypeStruct(a.shape, a.dtype) for a in (came[0], *through)],
        input_output_aliases={size + i: 1 + i for i in range(len(through))},
        compiler_params=params(),
        cost_estimate=cost(2),
        name="sum_pieces",
    )(*came, *rest)


def turn_first(i):
    return i ^ (2 if i % 2 == 0 else 4)


def turn_second(i):
    return i ^ (4 if i % 2 == 0 else 2)


def permute(value, axis, size, partner):
    return lax.ppermute(value, axis, [(i, partner(i)) for i in range(size)])


def gather_pieces(own, axis, core):
    x, y = swap(own, axis, 8, 2), swap(own, axis, 8, 4)
    far = permute(jnp.where(core == 0, y, x), axis, 8, turn_first)
    near = [own, x, y, far]
    others = [swap(p, axis, 8, 1) for p in near]
    return [p for pair in zip(near, others) for p in pair]


def reduce_first(same, other, axis, core):
    y = (same.astype(F32) + swap(other, axis, 8, 1).astype(F32)).astype(BF)
    sent = jnp.stack([jnp.where(core == 0, y[1], y[2]), y[3]])
    return sent, jnp.where(core == 0, y[2], y[1]), y[0]


def reduce_last(sent, kept, own, axis):
    came = permute(sent, axis, 8, turn_first)
    relayed = (kept.astype(F32) + came[1].astype(F32)).astype(BF)
    total = own.astype(F32) + came[0].astype(F32)
    return total + permute(relayed, axis, 8, turn_second).astype(F32)


def outer_update(summed, total_tok, master, momentum, step_rate, decay):
    average = summed / total_tok + step_rate * decay * master
    momentum = outer_mom * momentum + average
    return (master - outer_rate * (average + outer_mom * momentum), momentum)


def local(
    tokens,
    targets,
    seq_counts,
    embed_w,
    qkv_w,
    out_w,
    mlp_w,
    gain_w,
    embed_mom,
    qkv_mom,
    out_mom,
    mlp_mom,
    gain_mom,
    embed_first,
    qkv_first,
    out_first,
    mlp_first,
    gain_first,
    embed_second,
    qkv_second,
    out_second,
    mlp_second,
    gain_second,
):
    nb = lax.axis_size("blk")
    nw = lax.axis_size("work")
    me = lax.axis_index("blk")
    wi = lax.axis_index("work")
    core = wi % 2
    me_arr = me.astype(jnp.int32).reshape(1)
    wi_arr = wi.astype(jnp.int32).reshape(1)
    slots, full_len = tokens.shape[1:]
    vrows = embed_w.shape[0]
    width = embed_first.shape[2]
    ff = mlp_first.shape[3]
    vpad = pl.cdiv(vrows, 2 * CH) * 2 * CH
    own_rows = width // nb
    paired = nw == 8

    et_own = embed_w.T.astype(BF)
    if paired:
        pieces = gather_pieces(et_own, "work", core)
    else:
        pieces = [lax.all_gather(et_own, "work", axis=0, tiled=True)]
    wi_prep = wi_arr if paired else jnp.zeros_like(wi_arr)

    cq, co, cf = qkv_w.shape[1], out_w.shape[1], mlp_w.shape[2]
    count_col = jnp.broadcast_to(seq_counts[0].astype(F32), (own_rows, 1))
    packed = jnp.concatenate([qkv_w, out_w, mlp_w[0], mlp_w[1], gain_w.T, count_col], 1)
    packed = lax.all_gather(packed.astype(BF), ("blk", "work"), axis=0, tiled=False)
    widths = (cq, co, cf, cf)
    c1, c3 = cq + co, cq + co + 2 * cf
    *weights, gains, count_sum = split_weights(packed, nb, nw, widths)
    wqkv, wo, wm0, wm1, wqkv_t, wo_t, wm0_t, wm1_t = weights
    total_tok = count_sum[0, 0] * full_len

    half = HD // 2
    frequency = rope_base ** (-jnp.arange(half).astype(F32) * 2.0 / HD)
    angles = frequency[:, None] * jnp.arange(full_len).astype(F32)[None, :]
    cosine, sine = jnp.cos(angles), jnp.sin(angles)

    count_seq = seq_counts[0]
    count_tok = (count_seq * full_len).astype(F32)
    valid = (jnp.arange(slots) < count_seq).astype(F32)

    def local_ids(ids, missing):
        ids = ids[0] - me * vrows
        return jnp.where((ids >= 0) & (ids < vrows), ids, missing)

    tok = local_ids(tokens, -1)[:, None, :]
    tgt = local_ids(targets, -1)[:, None, :]
    tok_rows = local_ids(tokens, vrows)
    tgt_rows = local_ids(targets, vrows)

    prep_ids = jnp.concatenate([wi_prep, me_arr])
    et, er, looked, more = prep(prep_ids, tok_rows, pieces, vpad, nb)
    fwd_weights = (wqkv_t, wo_t, wm0_t, wm1)
    bwd_weights = (wqkv, wo, wo_t, wm0, wm0_t, wm1, wm1_t)
    wants, mark = table_rows(tgt_rows[:-1], er, width)
    mine, *more = sum_pieces(looked, "blk", nb, more, (mark,))
    later, mark = table_rows(tgt_rows[-1:], er, width, (mark, wqkv))
    wants += later
    def sum_blocks(value, turn):
        return lax.psum(value, "blk", axis_index_groups=[[(k + turn) % nb for k in range(nb)]])

    rows = [share(mine, "blk", nb)]
    rows += [[sum_blocks(m, s)] for s, m in enumerate(more)]

    saved, heads, stats, backs, des, losses = {}, {}, {}, {}, {}, {}
    scalars = jnp.concatenate([1.0 / count_tok.reshape(1), valid])

    def forward(s, *deps):
        *kept, af = trunk_fwd(
            me_arr, rows[s], wants[s], fwd_weights, gains, cosine, sine, deps
        )
        saved[s] = kept
        heads[s] = [af]

    def head(s, *deps):
        p, peaks, stat = head_first(er, heads[s][0], deps)
        heads[s] += [p, peaks]
        stats[s] = share(stat, "blk", nb)

    def back(s, *deps):
        af, p, peaks = heads[s]
        gin, des[s], losses[s] = head_back(
            s, scalars, p, et, af, tgt[s], peaks, saved[s][3], stats[s], deps
        )
        backs[s] = sum_blocks(gin, s)

    for s in range(slots):
        forward(s, *([mark] if s == 0 else [des[s - 2]] if s > 1 else [stats[0][0]]))
        head(s)
        if s:
            back(s - 1, stats[s][0])
    back(slots - 1, *([des[slots - 2]] if slots > 1 else []))
    dxs, wgs, ggs = [], [], []
    for s in range(slots):
        dx, wg, gg = trunk_bwd(
            me_arr,
            backs[s],
            saved[s],
            bwd_weights,
            gains,
            cosine,
            sine,
            own_rows,
            [part if s == slots - 1 else dxs[-1]] if s else [des[slots - 1]],
        )
        dxs.append(dx)
        wgs.append(wg)
        ggs.append(gg)
        if s == slots - 2:
            part = token_part(tok, [des[t] for t in range(slots)], dxs)
    losses = [losses[s] for s in range(slots)]
    de, wg, gg, both = token_grad(tok, part, dxs[-1:], wgs, ggs, losses)
    both = share(both, "blk", nb)

    tokens_of = count_tok.reshape(1)
    groups = nw if paired else 0
    first, second = embed_first[0].T, embed_second[0].T
    chunks = pl.cdiv(vrows, CH)
    cut = (5 * chunks + 7) // 8
    f0, s0, *pair = adam_table(
        tokens_of, wi_arr, both, de, first, second, groups, (0, cut)
    )
    p, q = pair[0], pair[-1]
    *small, result, p = adam_small(
        tokens_of,
        wi_arr,
        both,
        wg,
        gg,
        (qkv_first[0], out_first[0], mlp_first[0], gain_first[0].T),
        (qkv_second[0], out_second[0], mlp_second[0], gain_second[0].T),
        groups,
        widths,
        p,
    )
    waits, through, extra = [small[8]], (), ()
    if paired:
        begun = reduce_first(p, q, "work", core)
        through, extra = (begun[2], result, small[3], small[7]), small[8:10]
    efirst, esecond, *pair = adam_table(
        tokens_of, wi_arr, both, de, first, second, groups, (cut, chunks), (f0, s0), through, extra, waits
    )
    d1, d2, d3 = 3 * width, 4 * width, 4 * width + ff
    if paired:
        pair, through = pair[:2], pair[2:]
        begun = (*begun[:2], through[0])
        result, small[3], small[7] = through[1:]
        embed_sums = [begun, reduce_first(*pair, "work", core)]
        embed_sums = [reduce_last(*b, "work") for b in embed_sums]
        summed = embed_sums[1][: own_rows // 2, (chunks - cut) * CH :]
        embed_sums = [e[: width // nw] for e in embed_sums]
        embed_sums[1] = embed_sums[1][:, : vrows - cut * CH]
        summed = jnp.concatenate(jnp.split(summed, 2, 1), 0)
        parts = [summed[:, :cq], summed[:, cq : cq + co]]
        parts += [summed[:, c1 + i * cf : c1 + (i + 1) * cf] for i in range(2)]
        gain_sum = summed[:, c3 : c3 + 3].T
    else:
        embed_sums = [
            lax.psum_scatter(r, "work", scatter_dimension=0, tiled=True).astype(F32)
            for r in (p, pair[0])
        ]
        summed = lax.psum(small[8].astype(BF), "work").astype(F32)
        parts = [
            lax.dynamic_slice_in_dim(summed, lo + wi * size, size, 1)
            for lo, size in ((0, cq), (d1, co), (d2, cf), (d3, cf))
        ]
        gain_sum = summed[:, d3 + ff : d3 + ff + 3].T

    embed_sum = jnp.concatenate(embed_sums, 1).T
    sums = (embed_sum, parts[0], parts[1], jnp.stack(parts[2:]), gain_sum)
    masters = (embed_w, qkv_w, out_w, mlp_w, gain_w)
    moms = (embed_mom, qkv_mom, out_mom, mlp_mom, gain_mom)
    rates = (matrix_rate,) * 4 + (gain_rate,)
    decays = (decay_rate,) * 4 + (0.0,)
    updated = [
        outer_update(g, total_tok, w, m, r, d)
        for g, w, m, r, d in zip(sums, masters, moms, rates, decays)
    ]
    firsts = [efirst.T, *small[0:3], small[3].T]
    seconds = [esecond.T, *small[4:7], small[7].T]
    return (
        jnp.stack([result[0, 0], count_tok])[None],
        result[0, 1:2],
        *[u[0] for u in updated],
        *[u[1] for u in updated],
        *[a[None] for a in firsts],
        *[a[None] for a in seconds],
    )


def solution(mesh):
    weights = (
        P("blk", "work"),
        P("blk", "work"),
        P("blk", "work"),
        P(None, "blk", "work"),
        P(None, "blk"),
    )
    states = (
        P("work", "blk", None),
        P("work", "blk", None),
        P("work", "blk", None),
        P("work", None, "blk", None),
        P("work", None, "blk"),
    )
    in_specs = (
        P("work", None, None),
        P("work", None, None),
        P("work"),
        *weights,
        *weights,
        *states,
        *states,
    )
    out_specs = (P("work", None), P("work"), *weights, *weights, *states, *states)
    return jax.shard_map(local, mesh=mesh, in_specs=in_specs, out_specs=out_specs, check_vma=False)
```

```python
import functools
import math

import jax
import jax.numpy as jnp
from jax import lax
from jax.experimental import pallas as pl
from jax.experimental.pallas import tpu as pltpu
from jax.sharding import PartitionSpec as P

H = 6
HD = 48
STEP = 7

norm_eps = 1e-06
zloss_coef = 0.01
clip_limit = 0.05
beta_one = 0.9
beta_two = 0.95
adam_eps = 1e-08
decay_rate = 0.1
matrix_rate = 0.03
gain_rate = 0.3
outer_rate = 0.7
outer_mom = 0.9
rope_base = 10000.0

LOG2E = 1.0 / math.log(2.0)
LN2 = math.log(2.0)
SCALE = 1.0 / math.sqrt(HD)
BF = jnp.bfloat16
F32 = jnp.float32
NN = ((1,), (0,))
NT = ((1,), (1,))
CH = 1024
MIB = 1024 * 1024


def dot(a, b, dims=NN):
    return lax.dot_general(a, b, (dims, ((), ())), preferred_element_type=F32)


def params():
    return pltpu.CompilerParams(dimension_semantics=("arbitrary",), vmem_limit_bytes=58 * MIB)


def cost(micros):
    return pl.CostEstimate(flops=0, bytes_accessed=int(micros * 1.2e6), transcendentals=0)


def full(shape):
    return pl.BlockSpec(shape, lambda *_: (0,) * len(shape))


SMEM = pl.BlockSpec(memory_space=pltpu.SMEM)
ANY = pl.BlockSpec(memory_space=pl.ANY)


def call(kernel, ins, deps, **options):
    specs = options.pop("in_specs")

    def body(*refs):
        kernel(*refs[: len(ins)], *refs[len(ins) + len(deps) :])

    return pl.pallas_call(body, in_specs=[*specs, *([ANY] * len(deps))], **options)(*ins, *deps)


def pick_rows(ids_ref, s, tab, got, full_len):
    unroll = 32

    def body(i, carry):
        base = pl.multiple_of(i * unroll, unroll)
        for q in range(0, unroll, 8):
            rows = [tab[pl.ds(ids_ref[s, base + q + u], 1), :] for u in range(8)]
            got[pl.ds(pl.multiple_of(base + q, 8), 8), :] = jnp.concatenate(rows, 0)
        return carry

    lax.fori_loop(0, full_len // unroll, body, 0)


def rows_out(blk, got, outs):
    for k, out in enumerate(outs):
        width, lt = out.shape
        at = pl.multiple_of((blk ^ k) * lt, lt)
        out[...] = got[pl.ds(at, lt), 0:width].T.astype(BF)


def prep_kernel(count, vrows, nb, me_ref, ids_ref, *refs):
    pieces = refs[:count]
    et_ref, er_ref = refs[count : count + 2]
    outs = refs[count + 2 : count + 2 + nb]
    *others, tmp, tab, got = refs[count + 2 + nb :]
    j = pl.program_id(0)
    width, lt = outs[0].shape
    for k, piece in enumerate(pieces):
        tmp[me_ref[0] ^ k] = piece[...].astype(F32)
    e = jnp.concatenate([tmp[w] for w in range(count)], 0)
    lane = lax.broadcasted_iota(jnp.int32, (width, CH), 1) + j * CH
    e = jnp.where(lane < vrows, e, 0.0)
    et_ref[...] = e.astype(BF)
    rows = e.T
    tab[pl.ds(pl.multiple_of(j * CH, CH), CH), 0:width] = rows
    er_ref[:, 0:width] = rows.astype(BF)
    row = lax.broadcasted_iota(jnp.int32, (CH, 16), 0) + j * CH
    col = lax.broadcasted_iota(jnp.int32, (CH, 16), 1)
    er_ref[:, width:] = jnp.where((row >= vrows) & (col == 0), -60000.0, 0.0).astype(BF)

    @pl.when(j == pl.num_programs(0) - 1)
    def _():
        pick_rows(ids_ref, 0, tab, got, nb * lt)
        rows_out(me_ref[1], got, outs)
        for s, other in enumerate(others):
            pick_rows(ids_ref, s + 1, tab, got, nb * lt)
            other[...] = got[:, 0:width].T.astype(BF)


def prep(me, ids, pieces, vpad, nb):
    count = len(pieces)
    rows, vrows = pieces[0].shape
    width = count * rows
    slots, full_len = ids.shape
    lt = full_len // nb
    padded = pl.cdiv(width, 128) * 128
    et, er, *outs = pl.pallas_call(
        functools.partial(prep_kernel, count, vrows, nb),
        grid=(vpad // CH,),
        in_specs=[SMEM, SMEM] + [pl.BlockSpec((rows, CH), lambda j: (0, j))] * count,
        out_specs=[
            pl.BlockSpec((width, CH), lambda j: (0, j)),
            pl.BlockSpec((CH, width + 16), lambda j: (j, 0)),
            *[full((width, lt))] * nb,
            *[full((width, full_len))] * (slots - 1),
        ],
        out_shape=[
            jax.ShapeDtypeStruct((width, vpad), BF),
            jax.ShapeDtypeStruct((vpad, width + 16), BF),
            *[jax.ShapeDtypeStruct((width, lt), BF)] * nb,
            *[jax.ShapeDtypeStruct((width, full_len), BF)] * (slots - 1),
        ],
        scratch_shapes=[
            pltpu.VMEM((count, rows, CH), F32),
            pltpu.VMEM((vpad, padded), F32),
            pltpu.VMEM((full_len, padded), F32),
        ],
        compiler_params=params(),
        cost_estimate=cost(12),
        name="prep",
    )(me, ids, *pieces)
    return et, er, outs[:nb], outs[nb:]


def rows_kernel(ids_ref, er_ref, *refs):
    outs, (mark, tab, got) = refs[:-3], refs[-3:]
    width = outs[0].shape[0]
    mark[...] = jnp.zeros_like(mark)

    def fill(c, carry):
        here = pl.ds(pl.multiple_of(c * CH, CH), CH)
        tab[here, 0:width] = er_ref[here, 0:width].astype(F32)
        return carry

    lax.fori_loop(0, er_ref.shape[0] // CH, fill, 0)
    for s, out in enumerate(outs):
        pick_rows(ids_ref, s, tab, got, got.shape[0])
        out[...] = got[:, 0:width].T.astype(BF)


def table_rows(ids, er, width, deps=()):
    count, full_len = ids.shape
    padded = pl.cdiv(width, 128) * 128
    *rows, mark = call(
        rows_kernel,
        (ids, er),
        deps,
        grid=(1,),
        in_specs=[SMEM, full(er.shape)],
        out_specs=[full((width, full_len))] * count + [full((8, 128))],
        out_shape=[jax.ShapeDtypeStruct((width, full_len), BF)] * count
        + [jax.ShapeDtypeStruct((8, 128), F32)],
        scratch_shapes=[
            pltpu.VMEM((er.shape[0], padded), F32),
            pltpu.VMEM((full_len, padded), F32),
        ],
        compiler_params=params(),
        cost_estimate=cost(11),
        name="table_rows",
    )
    return rows, mark


def weights_kernel(nb, nw, widths, packed, *outs):
    straight, turned = outs[:4], outs[4:8]
    counts = jnp.zeros((1, 1), F32)
    for w in range(nw):
        part = [packed[b * nw + w].astype(F32) for b in range(nb)]
        part = jnp.concatenate(part, 0)
        at = 0
        for size, out in zip(widths, straight):
            out[:, w * size : (w + 1) * size] = part[:, at : at + size].astype(BF)
            at += size
        if w == 0:
            outs[8][...] = part[:, at : at + 3]
        counts += part[0:1, at + 3 : at + 4]
    outs[9][...] = counts
    for out, flip in zip(straight, turned):
        flip[...] = out[...].astype(F32).T.astype(BF)


def split_weights(packed, nb, nw, widths):
    rows = packed.shape[1]
    width = nb * rows
    shapes = [(width, nw * size) for size in widths]
    outs = [(s, BF) for s in shapes] + [(s[::-1], BF) for s in shapes]
    outs += [((width, 3), F32), ((1, 1), F32)]
    return pl.pallas_call(
        functools.partial(weights_kernel, nb, nw, widths),
        grid=(1,),
        in_specs=[full(packed.shape)],
        out_specs=[full(s) for s, _ in outs],
        out_shape=[jax.ShapeDtypeStruct(s, d) for s, d in outs],
        compiler_params=params(),
        cost_estimate=cost(3),
        name="split_weights",
    )(packed)


def norm_t(x, gain):
    scale = lax.rsqrt(jnp.mean(x * x, 0, keepdims=True) + norm_eps)
    return x * scale * gain, scale


def norm_t_bwd(x, scale, gain, incoming):
    unit = x * scale
    inner = incoming * gain
    return scale * (inner - unit * jnp.mean(inner * unit, 0, keepdims=True)), incoming * unit


def turn(u, cosine, sine):
    rows, lt = u.shape
    half = cosine.shape[0]
    u = u.reshape(rows // (2 * half), 2, half, lt)
    a, b = u[:, 0], u[:, 1]
    return jnp.stack([a * cosine - b * sine, a * sine + b * cosine], 1).reshape(rows, lt)


def place(me, pieces, out):
    lt = pieces[0].shape[1]
    for k, piece in enumerate(pieces):
        if len(pieces) == 1:
            out[...] = piece[...]
        else:
            out[:, pl.ds(pl.multiple_of((me ^ k) * lt, lt), lt)] = piece[...]


def interleave(parts):
    while parts:
        parts = [p for p in parts if next(p, 1) is None]


def causal(lt):
    keys = lax.broadcasted_iota(jnp.int32, (lt, lt), 0)
    queries = lax.broadcasted_iota(jnp.int32, (lt, lt), 1)
    return keys <= queries


def gelu_parts(u):
    k0 = math.sqrt(2.0 / math.pi)
    square = u * u
    th = jnp.tanh(k0 * (u + 0.044715 * u * square))
    act = 0.5 * u * (1.0 + th)
    return act, th, square, k0


def gelu_slope(u, th, square, k0):
    return 0.5 * (1.0 + th) + 0.5 * u * (1.0 - th * th) * k0 * (1.0 + 3.0 * 0.044715 * square)


def trunk_fwd_kernel(count, me_ref, *refs):
    (want, wqkv_t, wo_t, wm0_t, wm1, gains, cos_ref, sin_ref) = refs[count : count + 8]
    (x0_out, qkv_out, o_out, lse_out, af_out, krow) = refs[count + 8 :]
    width, full_len = x0_out.shape
    lt = min(256, full_len)
    nb = full_len // lt
    root = math.sqrt(width)
    place(me_ref[0], refs[:count], x0_out)
    def project(j):
        here = slice(j * lt, (j + 1) * lt)
        x = x0_out[:, here].astype(F32) * root
        a1, _ = norm_t(x, gains[:, 0:1])
        yield
        y = dot(wqkv_t[...], a1.astype(BF))
        yield
        cosine, sine = cos_ref[:, here], sin_ref[:, here]
        q = turn(y[:width], cosine, sine) * (SCALE * LOG2E)
        k = turn(y[width : 2 * width], cosine, sine)
        qkv_out[0:width, here] = q.astype(BF)
        qkv_out[width : 2 * width, here] = k.astype(BF)
        qkv_out[2 * width :, here] = y[2 * width :].astype(BF)
        for h in range(H):
            krow[h, here, :] = k[h * HD : (h + 1) * HD].T.astype(BF)

    interleave([project(j) for j in range(nb)])
    lse_out[...] = jnp.zeros_like(lse_out)

    def head(h, j):
        rows = slice(h * HD, (h + 1) * HD)
        values = slice(2 * width + h * HD, 2 * width + (h + 1) * HD)
        here, before = slice(j * lt, (j + 1) * lt), slice(0, j * lt)
        q = qkv_out[rows, here]
        s_diag = jnp.where(causal(lt), dot(krow[h, here, :], q), -1e30)
        peak = jnp.max(s_diag, 0, keepdims=True)
        if j:
            s_off = dot(krow[h, before, :], q)
            peak = jnp.maximum(peak, jnp.max(s_off, 0, keepdims=True))
        yield
        p_diag = jnp.exp2(s_diag - peak)
        total = jnp.sum(p_diag, 0, keepdims=True)
        if j:
            p_off = jnp.exp2(s_off - peak)
            total = total + jnp.sum(p_off, 0, keepdims=True)
        yield
        mix = dot(qkv_out[values, here], p_diag.astype(BF))
        if j:
            mix = mix + dot(qkv_out[values, before], p_off.astype(BF))
        o_out[rows, here] = (mix / total).astype(BF)
        lse_out[h : h + 1, here] = peak + jnp.log2(total)

    for j in range(nb):
        interleave([head(h, j) for h in range(H)])

    def finish(j):
        here = slice(j * lt, (j + 1) * lt)
        x = x0_out[:, here].astype(F32) * root
        h1 = x + dot(wo_t[...], o_out[:, here])
        yield
        a2, _ = norm_t(h1, gains[:, 1:2])
        yield
        u = dot(wm0_t[...], a2.astype(BF))
        yield
        act = gelu_parts(u)[0].astype(BF)
        yield
        h2 = h1 + dot(wm1[...], act)
        yield
        af, _ = norm_t(h2, gains[:, 2:3])
        af = (af * LOG2E).astype(BF)
        af_out[0:width, here] = af
        tail = lax.broadcasted_iota(jnp.int32, (af_out.shape[0] - width, lt), 0)
        af_out[width:, here] = jnp.where(tail == 0, 1.0, 0.0).astype(BF)

    interleave([finish(j) for j in range(nb)])
    picked = af_out[0:width, :].astype(F32) * want[...].astype(F32)
    lse_out[H : H + 1, :] = jnp.sum(picked, 0, keepdims=True)


def trunk_fwd(me, pieces, want, weights, gains, cosine, sine, deps=()):
    width, full_len = want.shape
    ins = (me, *pieces, want, *weights, gains, cosine, sine)
    shapes = [
        ((width, full_len), BF),
        ((3 * width, full_len), BF),
        ((width, full_len), BF),
        ((8, full_len), F32),
        ((width + 16, full_len), BF),
    ]
    return call(
        functools.partial(trunk_fwd_kernel, len(pieces)),
        ins,
        deps,
        grid=(1,),
        in_specs=[SMEM] + [full(a.shape) for a in ins[1:]],
        out_specs=[full(s) for s, _ in shapes],
        out_shape=[jax.ShapeDtypeStruct(s, d) for s, d in shapes],
        scratch_shapes=[pltpu.VMEM((H, full_len, HD), BF)],
        compiler_params=params(),
        cost_estimate=cost(13),
        name="trunk_fwd",
    )


def head_kernel(er_ref, af_ref, p_ref, m_ref, st_ref, s_ref, run, cur, z_ref):
    j = pl.program_id(0)
    full_len = af_ref.shape[1]
    lt = z_ref.shape[1]
    tiles = [slice(t, t + lt) for t in range(0, full_len, lt)]

    def emit(here, z, peak):
        p = jnp.exp2(z - peak)
        p_ref[:, here] = p.astype(BF)
        m_ref[pl.ds(j, 1), here] = peak
        total = jnp.sum(p.reshape(CH // 8, 8, lt), 0)
        s_ref[pl.ds(j, 1), here] = jnp.sum(total, 0, keepdims=True)

    @pl.when(j == 0)
    def _():
        run[...] = jnp.full_like(run, -1e30)
        cur[...] = jnp.zeros_like(cur)

    @pl.when(j > 0)
    def _():
        for here in tiles:
            z = dot(er_ref[...], af_ref[:, here])
            peak = jnp.max(z.reshape(CH // 8, 8, lt), 0)
            cur[0:1, here] = jnp.max(peak, 0, keepdims=True)
            emit(here, z, run[0:1, here])

    again = (j == 0) | (jnp.max(cur[0:1, :] - run[0:1, :]) > 60.0)

    @pl.when(again)
    def _():
        for here in tiles:
            z_ref[...] = dot(er_ref[...], af_ref[:, here])
            peak = jnp.max(z_ref[...], 0, keepdims=True)
            peak = jnp.maximum(peak, run[0:1, here])
            cur[0:1, here] = peak
            emit(here, z_ref[...], peak)

    run[0:1, :] = jnp.maximum(run[0:1, :], cur[0:1, :])

    @pl.when(j == pl.num_programs(0) - 1)
    def _():
        peak = run[0:1, :]
        total = jnp.sum(s_ref[...] * jnp.exp2(m_ref[...] - peak), 0, keepdims=True)
        st_ref[...] = jnp.zeros_like(st_ref)
        st_ref[0:1, :] = peak
        st_ref[1:2, :] = total


def head_first(er, af, deps=()):
    vpad, depth = er.shape
    full_len = af.shape[1]
    chunks = vpad // CH
    shapes = [((vpad, full_len), BF), ((chunks, full_len), F32), ((8, full_len), F32)]
    return call(
        head_kernel,
        (er, af),
        deps,
        grid=(chunks,),
        in_specs=[pl.BlockSpec((CH, depth), lambda j: (j, 0)), full(af.shape)],
        out_specs=[pl.BlockSpec((CH, full_len), lambda j: (j, 0))]
        + [full(s) for s, _ in shapes[1:]],
        out_shape=[jax.ShapeDtypeStruct(s, d) for s, d in shapes],
        scratch_shapes=[
            pltpu.VMEM((chunks, full_len), F32),
            pltpu.VMEM((8, full_len), F32),
            pltpu.VMEM((8, full_len), F32),
            pltpu.VMEM((CH, min(512, full_len)), F32),
        ],
        compiler_params=params(),
        cost_estimate=cost(16),
        name="head_first",
    )


def head_back_kernel(slot, nb, sc_ref, *refs):
    (p_ref, et_ref, af_ref, tgt_ref, m_ref, pick_ref) = refs[:6]
    stats = refs[6 : 6 + nb]
    (out, de_ref, loss_ref, acc, s_ref, d_ref) = refs[6 + nb :]
    j = pl.program_id(0)
    width, full_len = out.shape
    lt = min(256, full_len)
    valid = sc_ref[1 + slot]
    weight = valid * sc_ref[0]

    @pl.when(j == 0)
    def _():
        acc[...] = jnp.zeros_like(acc)
        top = functools.reduce(jnp.maximum, [b[0:1, :] for b in stats])
        total = sum(b[1:2, :] * jnp.exp2(b[0:1, :] - top) for b in stats)
        lse2 = top + jnp.log2(total)
        lse = lse2 * LN2
        boost = (1.0 + 2.0 * zloss_coef * lse) * weight
        pick = pick_ref[H : H + 1, :]
        s_ref[...] = jnp.exp2(m_ref[...] - lse2) * boost
        d_ref[0:1, :] = jnp.exp2(pick - lse2) * boost - weight
        loss_ref[...] = jnp.zeros_like(loss_ref)
        loss_ref[0:1, :] = (lse + zloss_coef * lse * lse) * valid
        loss_ref[1:2, :] = pick * LN2 * valid

    rows = lax.broadcasted_iota(jnp.int32, (CH, lt), 0)
    for half in range(2):
        chunk = 2 * j + half
        there = slice(half * CH, (half + 1) * CH)
        total = None
        for t in range(full_len // lt):
            here = slice(t * lt, (t + 1) * lt)
            grad = jnp.where(
                rows == tgt_ref[:, here] - chunk * CH,
                d_ref[0:1, here],
                p_ref[there, here].astype(F32) * s_ref[pl.ds(chunk, 1), here],
            ).astype(BF)
            acc[:, here] += dot(et_ref[:, there], grad)
            part = dot(af_ref[0:width, here], grad, NT)
            total = part if total is None else total + part
        de_ref[:, there] = (total * LN2).astype(BF)

    @pl.when(j == pl.num_programs(0) - 1)
    def _():
        out[...] = acc[...].astype(BF)


def head_back(slot, scalars, p, et, af, tgt, peaks, picks, stats, deps=()):
    nb = len(stats)
    width, vpad = et.shape
    full_len = tgt.shape[1]
    tall = pl.BlockSpec((2 * CH, full_len), lambda j: (j, 0))
    wide = pl.BlockSpec((width, 2 * CH), lambda j: (0, j))
    rest = (af, tgt, peaks, picks, *stats)
    return call(
        functools.partial(head_back_kernel, slot, nb),
        (scalars, p, et, *rest),
        deps,
        grid=(vpad // (2 * CH),),
        in_specs=[SMEM, tall, wide] + [full(a.shape) for a in rest],
        out_specs=[full((width, full_len)), wide, full((8, full_len))],
        out_shape=[
            jax.ShapeDtypeStruct((width, full_len), BF),
            jax.ShapeDtypeStruct((width, vpad), BF),
            jax.ShapeDtypeStruct((8, full_len), F32),
        ],
        scratch_shapes=[
            pltpu.VMEM((width, full_len), F32),
            pltpu.VMEM(peaks.shape, F32),
            pltpu.VMEM((8, full_len), F32),
        ],
        compiler_params=params(),
        cost_estimate=cost(15),
        name="head_back",
    )


def trunk_bwd_kernel(me_ref, *refs):
    (gin, x0, qkv, o_ref, lse) = refs[:5]
    (wqkv, wo, wo_t, wm0, wm0_t, wm1, wm1_t, gains, cos_ref, sin_ref) = refs[5:15]
    (dx_out, wg_out, gg_out) = refs[15:18]
    (krow, vrow, dqkv, dqkv_b, dh1_s, dh1_b, a_s, du_s, act_s, df_s, do_s, delta, wg, gg_s) = refs[18:]
    me = me_ref[0]
    width, full_len = x0.shape
    ff = du_s.shape[0]
    lt = min(256, full_len)
    nb = full_len // lt
    root = math.sqrt(width)
    gain_sums = [[None] * nb for _ in range(3)]

    def outer(j):
        here = slice(j * lt, (j + 1) * lt)
        h1 = x0[:, here].astype(F32) * root + dot(wo_t[...], o_ref[:, here])
        yield
        a2, scale = norm_t(h1, gains[:, 1:2])
        a2 = a2.astype(BF)
        a_s[:, here] = a2
        yield
        u = dot(wm0_t[...], a2)
        yield
        act, th, square, k0 = gelu_parts(u)
        slope = gelu_slope(u, th, square, k0)
        act = act.astype(BF)
        act_s[:, here] = act
        yield
        h2 = h1 + dot(wm1[...], act)
        yield
        _, scale2 = norm_t(h2, 1.0)
        dh2, gg = norm_t_bwd(h2, scale2, gains[:, 2:3], gin[:, here].astype(F32))
        gain_sums[2][j] = jnp.sum(gg, 1, keepdims=True)
        df = dh2.astype(BF)
        df_s[:, here] = df
        yield
        du = (dot(wm1_t[...], df) * slope).astype(BF)
        du_s[:, here] = du
        yield
        da2 = dot(wm0[...], du)
        yield
        dmid, gg = norm_t_bwd(h1, scale, gains[:, 1:2], da2)
        gain_sums[1][j] = jnp.sum(gg, 1, keepdims=True)
        dh1 = dh2 + dmid
        dh1_s[:, here] = dh1
        dh1b = dh1.astype(BF)
        dh1_b[:, here] = dh1b
        yield
        do = dot(wo[...], dh1b).astype(BF)
        do_s[:, here] = do
        weighed = (do.astype(F32) * o_ref[:, here].astype(F32)).reshape(H, HD, lt)
        delta[0:H, here] = jnp.sum(weighed, 1)
        yield
        for h in range(H):
            lo = width + h * HD
            krow[h, here, :] = qkv[lo : lo + HD, here].astype(F32).T.astype(BF)
            vrow[h, here, :] = qkv[lo + width : lo + width + HD, here].astype(F32).T.astype(BF)

    interleave([outer(j) for j in range(nb)])
    wg[:, 4 * width : 4 * width + ff] = dot(a_s[...], du_s[...], NT)
    wg[:, 4 * width + ff :] = dot(df_s[...], act_s[...], NT)
    wg[:, 3 * width : 4 * width] = dot(o_ref[...], dh1_b[...], NT)

    def head(h, j):
        qs, ks, vs = (pl.ds(pl.multiple_of(a + h * HD, 16), HD) for a in (0, width, 2 * width))
        here = slice(j * lt, (j + 1) * lt)
        parts = [(here, True)] + ([(slice(0, j * lt), False)] if j else [])
        q, do = qkv[qs, here], do_s[qs, here]
        lse_row, delta_row = lse[pl.ds(h, 1), here], delta[pl.ds(h, 1), here]
        scores = [(dot(krow[h, t, :], q), dot(vrow[h, t, :], do)) for t, _ in parts]
        yield
        grads = []
        for (there, diagonal), (s, dp) in zip(parts, scores):
            p = jnp.exp2(s - lse_row)
            if diagonal:
                p = jnp.where(causal(lt), p, 0.0)
            grads.append((p.astype(BF), (p * (dp - delta_row)).astype(BF)))
        yield
        dq = 0.0
        for (there, _), (pb, dsb) in zip(parts, grads):
            dq = dq + dot(qkv[ks, there], dsb)
            dk, dv = dot(q, dsb, NT), dot(do, pb, NT)
            if j == nb - 1:
                dqkv[ks, there] = dk
                dqkv[vs, there] = dv
            else:
                dqkv[ks, there] += dk
                dqkv[vs, there] += dv
        dqkv[qs, here] = dq

    def heads(i, carry):
        for j in reversed(range(nb)):
            interleave([head(i * 2 + u, j) for u in range(2)])
        return carry

    lax.fori_loop(0, H // 2, heads, 0)

    def inner(j):
        here = slice(j * lt, (j + 1) * lt)
        cosine, sine = cos_ref[:, here], -sin_ref[:, here]
        dq = turn(dqkv[0:width, here], cosine, sine) * SCALE
        dk = turn(dqkv[width : 2 * width, here], cosine, sine) * LN2
        dqkv_b[0:width, here] = dq.astype(BF)
        dqkv_b[width : 2 * width, here] = dk.astype(BF)
        dqkv_b[2 * width :, here] = dqkv[2 * width :, here].astype(BF)
        x = x0[:, here].astype(F32) * root
        a1, scale = norm_t(x, gains[:, 0:1])
        a_s[:, here] = a1.astype(BF)
        yield
        da1 = dot(wqkv[...], dqkv_b[:, here])
        yield
        dlow, gg = norm_t_bwd(x, scale, gains[:, 0:1], da1)
        gain_sums[0][j] = jnp.sum(gg, 1, keepdims=True)
        dx_out[:, here] = ((dh1_s[:, here] + dlow) * root).astype(BF)

    interleave([inner(j) for j in range(nb)])
    wg[:, 0 : 3 * width] = dot(a_s[...], dqkv_b[...], NT)
    own = wg_out.shape[0]
    wg_out[...] = wg[pl.ds(pl.multiple_of(me * own, 8), own), :]
    lane = lax.broadcasted_iota(jnp.int32, gg_s.shape, 1)
    gg_s[...] = sum(jnp.where(lane == i, sum(gain_sums[i]), 0.0) for i in range(3))
    gg_out[...] = gg_s[pl.ds(pl.multiple_of(me * own, 8), own), :]


def trunk_bwd(me, gin, saved, weights, gains, cosine, sine, own, deps=()):
    width, full_len = gin.shape
    ff = weights[3].shape[1]
    ins = (me, gin, *saved, *weights, gains, cosine, sine)
    cols = 4 * width + 2 * ff
    shapes = [((width, full_len), BF), ((own, cols), F32), ((own, 128), F32)]
    return call(
        trunk_bwd_kernel,
        ins,
        deps,
        grid=(1,),
        in_specs=[SMEM] + [full(a.shape) for a in ins[1:]],
        out_specs=[full(s) for s, _ in shapes],
        out_shape=[jax.ShapeDtypeStruct(s, d) for s, d in shapes],
        scratch_shapes=[
            pltpu.VMEM((H, full_len, HD), BF),
            pltpu.VMEM((H, full_len, HD), BF),
            pltpu.VMEM((3 * width, full_len), F32),
            pltpu.VMEM((3 * width, full_len), BF),
            pltpu.VMEM((width, full_len), F32),
            pltpu.VMEM((width, full_len), BF),
            pltpu.VMEM((width, full_len), BF),
            pltpu.VMEM((ff, full_len), BF),
            pltpu.VMEM((ff, full_len), BF),
            pltpu.VMEM((width, full_len), BF),
            pltpu.VMEM((width, full_len), BF),
            pltpu.VMEM((8, full_len), F32),
            pltpu.VMEM((width, cols), F32),
            pltpu.VMEM((width, 128), F32),
        ],
        compiler_params=params(),
        cost_estimate=cost(24),
        name="trunk_bwd",
    )


def folded(values):
    rows, cols = values.shape
    values = jnp.sum(values.reshape(rows // 8, 8, cols), 0)
    return sum(values[:, c : c + 128] for c in range(0, cols, 128))


def token_sum(first, tok_ref, de_refs, dx_refs):
    full_len = tok_ref.shape[2]
    lt = min(512, full_len)
    rows = lax.broadcasted_iota(jnp.int32, (CH, lt), 0) + pl.program_id(0) * CH
    total = sum(d[...].astype(F32) for d in de_refs)
    for s, dx in enumerate(dx_refs):
        for t in range(full_len // lt):
            here = slice(t * lt, (t + 1) * lt)
            hot = jnp.where(rows == tok_ref[first + s, :, here], 1.0, 0.0).astype(BF)
            total = total + dot(dx[:, here], hot, NT)
    return total


def token_part_kernel(count, tok_ref, *refs):
    *ins, out = refs
    out[...] = token_sum(0, tok_ref, ins[:count], ins[count:]).astype(BF)


def token_part(tok, des, dxs):
    width, vpad = des[0].shape
    blk = pl.BlockSpec((width, CH), lambda j: (0, j))
    return pl.pallas_call(
        functools.partial(token_part_kernel, len(des)),
        grid=(vpad // CH,),
        in_specs=[full(tok.shape)] + [blk] * len(des) + [full(a.shape) for a in dxs],
        out_specs=blk,
        out_shape=jax.ShapeDtypeStruct((width, vpad), BF),
        compiler_params=params(),
        cost_estimate=cost(13),
        name="token_part",
    )(tok, *des, *dxs)


def token_grad_kernel(first, slots, tok_ref, de_ref, *refs):
    count = slots - first
    dx_refs, refs = refs[:count], refs[count:]
    wg_refs, gg_refs, loss_refs = refs[:slots], refs[slots : 2 * slots], refs[2 * slots : 3 * slots]
    out_ref, wg_out, gg_out, sum_out, acc = refs[3 * slots :]
    j = pl.program_id(0)

    @pl.when(j == 0)
    def _():
        wg = sum(w[...] for w in wg_refs)
        gg = sum(g[...] for g in gg_refs)
        wg_out[...] = wg
        gg_out[...] = gg
        acc[...] = folded(wg * wg) + folded(gg * gg)

    total = token_sum(first, tok_ref, [de_ref], dx_refs)
    out_ref[...] = total.astype(BF)
    acc[...] += folded(total * total)

    @pl.when(j == pl.num_programs(0) - 1)
    def _():
        lane = lax.broadcasted_iota(jnp.int32, sum_out.shape, 1)
        pick = jnp.sum(sum(r[1:2, :] for r in loss_refs))
        lse = jnp.sum(sum(r[0:1, :] for r in loss_refs))
        tail = jnp.where(lane == 2, lse, 0.0)
        sum_out[...] = jnp.where(lane == 0, jnp.sum(acc[...]), jnp.where(lane == 1, pick, tail))


def token_grad(tok, de, dxs, wgs, ggs, losses):
    slots = len(wgs)
    width, vpad = de.shape
    blk = pl.BlockSpec((width, CH), lambda j: (0, j))
    rest = (*dxs, *wgs, *ggs, *losses)
    shapes = [(wgs[0].shape, F32), (ggs[0].shape, F32), ((8, 128), F32)]
    return pl.pallas_call(
        functools.partial(token_grad_kernel, slots - len(dxs), slots),
        grid=(vpad // CH,),
        in_specs=[full(tok.shape), blk] + [full(a.shape) for a in rest],
        out_specs=[blk] + [full(s) for s, _ in shapes],
        out_shape=[jax.ShapeDtypeStruct((width, vpad), BF)]
        + [jax.ShapeDtypeStruct(s, d) for s, d in shapes],
        scratch_shapes=[pltpu.VMEM((8, 128), F32)],
        compiler_params=params(),
        cost_estimate=cost(9),
        name="token_grad",
    )(tok, de, *rest)


def clip_factor(sums):
    total = sum(s[0:1, 0:1] for s in sums)
    return clip_limit / jnp.maximum(jnp.sqrt(total), clip_limit)


def adam(gradient, first, second, weight):
    first = beta_one * first + (1.0 - beta_one) * gradient
    second = beta_two * second + (1.0 - beta_two) * gradient * gradient
    ratio = (first * (weight / (1.0 - beta_one**STEP))) / (
        jnp.sqrt(second * (1.0 / (1.0 - beta_two**STEP))) + adam_eps
    )
    return first, second, ratio


def adam_small_kernel(nb, widths, sc_ref, me_ref, *refs):
    factor = clip_factor(refs[:nb])
    (wg, gg, qf, of, mf, gf, qs, os_, ms, gs) = refs[nb : nb + 10]
    (qf2, of2, mf2, gf2, qs2, os2, ms2, gs2, *r_out) = refs[nb + 11 : -2]
    res = refs[-2]
    sums = sum(r[...] for r in refs[:nb])
    lane = lax.broadcasted_iota(jnp.int32, res.shape, 1)
    loss = refs[0][:, 2:3] - sums[:, 1:2]
    res[...] = jnp.where(lane == 0, loss, jnp.where(lane == 1, jnp.sqrt(sums[:, 0:1]), 0.0))
    weight = sc_ref[0] * matrix_rate
    at = 0
    ratios = []
    for f, s, f2, s2 in (
        (qf, qs, qf2, qs2),
        (of, os_, of2, os2),
        (mf.at[0], ms.at[0], mf2.at[0], ms2.at[0]),
        (mf.at[1], ms.at[1], mf2.at[1], ms2.at[1]),
    ):
        here = slice(at, at + f.shape[1])
        f2[...], s2[...], ratio = adam(wg[:, here] * factor, f[...], s[...], weight)
        ratios.append(ratio)
        at = here.stop
    f2, s2, ratio = adam(gg[:, 0:3] * factor, gf[...], gs[...], sc_ref[0] * gain_rate)
    gf2[...] = f2
    gs2[...] = s2
    if not widths:
        at = 0
        for r in ratios:
            r_out[0][:, at : at + r.shape[1]] = r
            at += r.shape[1]
        r_out[0][:, at:] = jnp.zeros_like(r_out[0][:, at:])
        r_out[0][:, at : at + 3] = ratio
        return
    rows, cols = ratio.shape[0] // 2, r_out[0].shape[2] // 2
    blank = jnp.zeros((2 * rows, cols - sum(widths) - 3), F32)
    below = jnp.zeros((r_out[0].shape[1] - rows, 2 * cols), F32)
    for w in range(2 * r_out[0].shape[0]):
        parts = [r[:, w * size : (w + 1) * size] for r, size in zip(ratios, widths)]
        piece = jnp.concatenate([*parts, ratio, blank], 1)
        piece = jnp.concatenate([piece[:rows], piece[rows:]], 1)
        piece = jnp.concatenate([piece, below], 0).astype(BF)
        rel = me_ref[0] ^ w
        for core in range(2):

            @pl.when((rel & 1) == core)
            def _():
                r_out[core][rel >> 1] = piece


def adam_small(scalars, me, sums, wg, gg, firsts, seconds, groups, widths, through):
    ins = (*sums, wg, gg, *firsts, *seconds)
    shapes = [(a.shape, F32) for a in (*firsts, *seconds)]
    if groups:
        cols = pl.cdiv(sum(widths) + 3, 128) * 128
        rows = pl.cdiv(wg.shape[0] // 2, 8) * 8
        shapes += [((groups // 2, rows, 2 * cols), BF)] * 2
    else:
        shapes.append(((wg.shape[0], wg.shape[1] + 128), F32))
    shapes.append((sums[0].shape, F32))
    return pl.pallas_call(
        functools.partial(adam_small_kernel, len(sums), widths if groups else None),
        grid=(1,),
        in_specs=[SMEM, SMEM] + [full(a.shape) for a in ins] + [ANY],
        out_specs=[full(s) for s, _ in shapes] + [ANY],
        out_shape=[jax.ShapeDtypeStruct(s, d) for s, d in shapes]
        + [jax.ShapeDtypeStruct(through.shape, through.dtype)],
        input_output_aliases={2 + len(ins): len(shapes)},
        compiler_params=params(),
        cost_estimate=cost(3),
        name="adam_small",
    )(scalars, me, *ins, through)


def adam_kernel(nb, grouped, kept, through, extra, sc_ref, me_ref, *refs):
    r_out = refs[len(refs) - through - (2 if grouped else 1) : len(refs) - through]
    if not extra:
        return adam_chunk(nb, grouped, kept + through, sc_ref, me_ref, refs, r_out)
    j = pl.program_id(0)

    @pl.when(j < pl.num_programs(0) - 1)
    def _():
        adam_chunk(nb, grouped, kept + through + extra, sc_ref, me_ref, refs, r_out)

    @pl.when(j == pl.num_programs(0) - 1)
    def _():
        for e, r in zip(refs[nb + 3 : nb + 3 + extra], r_out):
            r[:, :, 0 : e.shape[2]] = e[...]


def adam_chunk(nb, grouped, skipped, sc_ref, me_ref, refs, r_out):
    sums, (g_ref, f_ref, s_ref) = refs[:nb], refs[nb : nb + 3]
    f_out, s_out = refs[nb + 3 + skipped : nb + 5 + skipped]
    factor = clip_factor(sums)
    first, second, ratio = adam(
        g_ref[...].astype(F32) * factor, f_ref[...], s_ref[...], sc_ref[0] * matrix_rate
    )
    f_out[...] = first
    s_out[...] = second
    if not grouped:
        r_out[0][...] = ratio.astype(BF)
        return
    groups = 2 * r_out[0].shape[0]
    rows = ratio.shape[0] // groups
    padded = r_out[0].shape[1]
    for w in range(groups):
        piece = ratio[w * rows : (w + 1) * rows]
        piece = jnp.concatenate([piece, jnp.zeros((padded - rows, CH), F32)], 0).astype(BF)
        rel = me_ref[0] ^ w
        for core in range(2):

            @pl.when((rel & 1) == core)
            def _():
                r_out[core][rel >> 1] = piece


def adam_table(scalars, me, sums, de, first, second, groups, part, kept=(), through=(), extra=(), deps=()):
    width, rows = first.shape
    lo, hi = part
    here = (hi - lo) * CH + extra[0].shape[2] if extra else min(hi * CH, rows) - lo * CH
    blk = pl.BlockSpec((width, CH), lambda j: (0, jnp.minimum(j + lo, hi - 1)))
    shapes = [((width, rows), F32)] * 2
    specs = [blk, blk]
    if groups:
        stack = (groups // 2, pl.cdiv(width // groups, 8) * 8)
        shapes += [((*stack, here), BF)] * 2
        specs += [pl.BlockSpec((*stack, CH), lambda j: (0, 0, j))] * 2
    else:
        shapes += [((width, here), BF)]
        specs += [pl.BlockSpec((width, CH), lambda j: (0, j))]
    nb = len(sums)
    at, count = nb + 5 + len(extra), len(shapes)
    aliases = {at + i: i for i in range(len(kept))}
    aliases |= {at + len(kept) + i: count + i for i in range(len(through))}
    shapes += [(a.shape, a.dtype) for a in through]
    unread = [ANY] * (len(kept) + len(through))
    return call(
        functools.partial(
            adam_kernel, nb, bool(groups), len(kept), len(through), len(extra)
        ),
        (scalars, me, *sums, de, first, second, *extra, *kept, *through),
        deps,
        grid=(hi - lo + (1 if extra else 0),),
        in_specs=[SMEM, SMEM]
        + [full(a.shape) for a in sums]
        + [blk] * 3
        + [full(a.shape) for a in extra]
        + unread,
        out_specs=specs + [ANY] * len(through),
        out_shape=[jax.ShapeDtypeStruct(s, d) for s, d in shapes],
        input_output_aliases=aliases,
        compiler_params=params(),
        cost_estimate=cost(10),
        name="adam_table",
    )


def swap(value, axis, size, k):
    return lax.ppermute(value, axis, [(i, i ^ k) for i in range(size)])


def share(value, axis, size):
    return [value] + [swap(value, axis, size, k) for k in range(1, size)]


def sum_kernel(count, *refs):
    out = refs[count]
    out[...] = sum(p[...].astype(F32) for p in refs[:count]).astype(BF)


def sum_pieces(pieces, axis, size, through, deps=()):
    came = [pieces[0]] + [swap(pieces[k], axis, size, k) for k in range(1, size)]
    rest = (*through, *deps)

    def body(*refs):
        sum_kernel(size, *refs[:size], refs[size + len(rest)])

    return pl.pallas_call(
        body,
        grid=(1,),
        in_specs=[full(c.shape) for c in came] + [ANY] * len(rest),
        out_specs=[full(came[0].shape)] + [ANY] * len(through),
        out_shape=[jax.ShapeDtypeStruct(a.shape, a.dtype) for a in (came[0], *through)],
        input_output_aliases={size + i: 1 + i for i in range(len(through))},
        compiler_params=params(),
        cost_estimate=cost(2),
        name="sum_pieces",
    )(*came, *rest)


def turn_first(i):
    return i ^ (2 if i % 2 == 0 else 4)


def turn_second(i):
    return i ^ (4 if i % 2 == 0 else 2)


def permute(value, axis, size, partner):
    return lax.ppermute(value, axis, [(i, partner(i)) for i in range(size)])


def gather_pieces(own, axis, core):
    x, y = swap(own, axis, 8, 2), swap(own, axis, 8, 4)
    far = permute(jnp.where(core == 0, y, x), axis, 8, turn_first)
    near = [own, x, y, far]
    others = [swap(p, axis, 8, 1) for p in near]
    return [p for pair in zip(near, others) for p in pair]


def reduce_first(same, other, axis, core):
    y = (same.astype(F32) + swap(other, axis, 8, 1).astype(F32)).astype(BF)
    sent = jnp.stack([jnp.where(core == 0, y[1], y[2]), y[3]])
    return sent, jnp.where(core == 0, y[2], y[1]), y[0]


def reduce_last(sent, kept, own, axis):
    came = permute(sent, axis, 8, turn_first)
    relayed = (kept.astype(F32) + came[1].astype(F32)).astype(BF)
    total = own.astype(F32) + came[0].astype(F32)
    return total + permute(relayed, axis, 8, turn_second).astype(F32)


def outer_update(summed, total_tok, master, momentum, step_rate, decay):
    average = summed / total_tok + step_rate * decay * master
    momentum = outer_mom * momentum + average
    return (master - outer_rate * (average + outer_mom * momentum), momentum)


def local(
    tokens,
    targets,
    seq_counts,
    embed_w,
    qkv_w,
    out_w,
    mlp_w,
    gain_w,
    embed_mom,
    qkv_mom,
    out_mom,
    mlp_mom,
    gain_mom,
    embed_first,
    qkv_first,
    out_first,
    mlp_first,
    gain_first,
    embed_second,
    qkv_second,
    out_second,
    mlp_second,
    gain_second,
):
    nb = lax.axis_size("blk")
    nw = lax.axis_size("work")
    me = lax.axis_index("blk")
    wi = lax.axis_index("work")
    core = wi % 2
    me_arr = me.astype(jnp.int32).reshape(1)
    wi_arr = wi.astype(jnp.int32).reshape(1)
    slots, full_len = tokens.shape[1:]
    vrows = embed_w.shape[0]
    width = embed_first.shape[2]
    ff = mlp_first.shape[3]
    vpad = pl.cdiv(vrows, 2 * CH) * 2 * CH
    own_rows = width // nb
    paired = nw == 8

    et_own = embed_w.T.astype(BF)
    if paired:
        pieces = gather_pieces(et_own, "work", core)
    else:
        pieces = [lax.all_gather(et_own, "work", axis=0, tiled=True)]
    wi_prep = wi_arr if paired else jnp.zeros_like(wi_arr)

    cq, co, cf = qkv_w.shape[1], out_w.shape[1], mlp_w.shape[2]
    count_col = jnp.broadcast_to(seq_counts[0].astype(F32), (own_rows, 1))
    packed = jnp.concatenate([qkv_w, out_w, mlp_w[0], mlp_w[1], gain_w.T, count_col], 1)
    packed = lax.all_gather(packed.astype(BF), ("blk", "work"), axis=0, tiled=False)
    widths = (cq, co, cf, cf)
    c1, c3 = cq + co, cq + co + 2 * cf
    *weights, gains, count_sum = split_weights(packed, nb, nw, widths)
    wqkv, wo, wm0, wm1, wqkv_t, wo_t, wm0_t, wm1_t = weights
    total_tok = count_sum[0, 0] * full_len

    half = HD // 2
    frequency = rope_base ** (-jnp.arange(half).astype(F32) * 2.0 / HD)
    angles = frequency[:, None] * jnp.arange(full_len).astype(F32)[None, :]
    cosine, sine = jnp.cos(angles), jnp.sin(angles)

    count_seq = seq_counts[0]
    count_tok = (count_seq * full_len).astype(F32)
    valid = (jnp.arange(slots) < count_seq).astype(F32)

    def local_ids(ids, missing):
        ids = ids[0] - me * vrows
        return jnp.where((ids >= 0) & (ids < vrows), ids, missing)

    tok = local_ids(tokens, -1)[:, None, :]
    tgt = local_ids(targets, -1)[:, None, :]
    tok_rows = local_ids(tokens, vrows)
    tgt_rows = local_ids(targets, vrows)

    prep_ids = jnp.concatenate([wi_prep, me_arr])
    et, er, looked, more = prep(prep_ids, tok_rows, pieces, vpad, nb)
    fwd_weights = (wqkv_t, wo_t, wm0_t, wm1)
    bwd_weights = (wqkv, wo, wo_t, wm0, wm0_t, wm1, wm1_t)
    wants, mark = table_rows(tgt_rows[:-1], er, width)
    mine, *more = sum_pieces(looked, "blk", nb, more, (mark,))
    later, mark = table_rows(tgt_rows[-1:], er, width, (mark, wqkv))
    wants += later
    def sum_blocks(value, turn):
        return lax.psum(value, "blk", axis_index_groups=[[(k + turn) % nb for k in range(nb)]])

    rows = [share(mine, "blk", nb)]
    rows += [[sum_blocks(m, s)] for s, m in enumerate(more)]

    saved, heads, stats, backs, des, losses = {}, {}, {}, {}, {}, {}
    scalars = jnp.concatenate([1.0 / count_tok.reshape(1), valid])

    def forward(s, *deps):
        *kept, af = trunk_fwd(
            me_arr, rows[s], wants[s], fwd_weights, gains, cosine, sine, deps
        )
        saved[s] = kept
        heads[s] = [af]

    def head(s, *deps):
        p, peaks, stat = head_first(er, heads[s][0], deps)
        heads[s] += [p, peaks]
        stats[s] = share(stat, "blk", nb)

    def back(s, *deps):
        af, p, peaks = heads[s]
        gin, des[s], losses[s] = head_back(
            s, scalars, p, et, af, tgt[s], peaks, saved[s][3], stats[s], deps
        )
        backs[s] = sum_blocks(gin, s)

    for s in range(slots):
        forward(s, *([mark] if s == 0 else [des[s - 2]] if s > 1 else [stats[0][0]]))
        head(s)
        if s:
            back(s - 1, stats[s][0])
    back(slots - 1, *([des[slots - 2]] if slots > 1 else []))
    dxs, wgs, ggs = [], [], []
    for s in range(slots):
        dx, wg, gg = trunk_bwd(
            me_arr,
            backs[s],
            saved[s],
            bwd_weights,
            gains,
            cosine,
            sine,
            own_rows,
            [part if s == slots - 1 else dxs[-1]] if s else [des[slots - 1]],
        )
        dxs.append(dx)
        wgs.append(wg)
        ggs.append(gg)
        if s == slots - 2:
            part = token_part(tok, [des[t] for t in range(slots)], dxs[:1])
    losses = [losses[s] for s in range(slots)]
    de, wg, gg, both = token_grad(tok, part, dxs[1:], wgs, ggs, losses)
    both = share(both, "blk", nb)

    tokens_of = count_tok.reshape(1)
    groups = nw if paired else 0
    first, second = embed_first[0].T, embed_second[0].T
    chunks = pl.cdiv(vrows, CH)
    cut = (5 * chunks + 7) // 8
    f0, s0, *pair = adam_table(
        tokens_of, wi_arr, both, de, first, second, groups, (0, cut)
    )
    p, q = pair[0], pair[-1]
    *small, result, p = adam_small(
        tokens_of,
        wi_arr,
        both,
        wg,
        gg,
        (qkv_first[0], out_first[0], mlp_first[0], gain_first[0].T),
        (qkv_second[0], out_second[0], mlp_second[0], gain_second[0].T),
        groups,
        widths,
        p,
    )
    waits, through, extra = [small[8]], (), ()
    if paired:
        begun = reduce_first(p, q, "work", core)
        through, extra = (begun[2], result, small[3], small[7]), small[8:10]
    efirst, esecond, *pair = adam_table(
        tokens_of, wi_arr, both, de, first, second, groups, (cut, chunks), (f0, s0), through, extra, waits
    )
    d1, d2, d3 = 3 * width, 4 * width, 4 * width + ff
    if paired:
        pair, through = pair[:2], pair[2:]
        begun = (*begun[:2], through[0])
        result, small[3], small[7] = through[1:]
        embed_sums = [begun, reduce_first(*pair, "work", core)]
        embed_sums = [reduce_last(*b, "work") for b in embed_sums]
        summed = embed_sums[1][: own_rows // 2, (chunks - cut) * CH :]
        embed_sums = [e[: width // nw] for e in embed_sums]
        embed_sums[1] = embed_sums[1][:, : vrows - cut * CH]
        summed = jnp.concatenate(jnp.split(summed, 2, 1), 0)
        parts = [summed[:, :cq], summed[:, cq : cq + co]]
        parts += [summed[:, c1 + i * cf : c1 + (i + 1) * cf] for i in range(2)]
        gain_sum = summed[:, c3 : c3 + 3].T
    else:
        embed_sums = [
            lax.psum_scatter(r, "work", scatter_dimension=0, tiled=True).astype(F32)
            for r in (p, pair[0])
        ]
        summed = lax.psum(small[8].astype(BF), "work").astype(F32)
        parts = [
            lax.dynamic_slice_in_dim(summed, lo + wi * size, size, 1)
            for lo, size in ((0, cq), (d1, co), (d2, cf), (d3, cf))
        ]
        gain_sum = summed[:, d3 + ff : d3 + ff + 3].T

    embed_sum = jnp.concatenate(embed_sums, 1).T
    sums = (embed_sum, parts[0], parts[1], jnp.stack(parts[2:]), gain_sum)
    masters = (embed_w, qkv_w, out_w, mlp_w, gain_w)
    moms = (embed_mom, qkv_mom, out_mom, mlp_mom, gain_mom)
    rates = (matrix_rate,) * 4 + (gain_rate,)
    decays = (decay_rate,) * 4 + (0.0,)
    updated = [
        outer_update(g, total_tok, w, m, r, d)
        for g, w, m, r, d in zip(sums, masters, moms, rates, decays)
    ]
    firsts = [efirst.T, *small[0:3], small[3].T]
    seconds = [esecond.T, *small[4:7], small[7].T]
    return (
        jnp.stack([result[0, 0], count_tok])[None],
        result[0, 1:2],
        *[u[0] for u in updated],
        *[u[1] for u in updated],
        *[a[None] for a in firsts],
        *[a[None] for a in seconds],
    )


def solution(mesh):
    weights = (
        P("blk", "work"),
        P("blk", "work"),
        P("blk", "work"),
        P(None, "blk", "work"),
        P(None, "blk"),
    )
    states = (
        P("work", "blk", None),
        P("work", "blk", None),
        P("work", "blk", None),
        P("work", None, "blk", None),
        P("work", None, "blk"),
    )
    in_specs = (
        P("work", None, None),
        P("work", None, None),
        P("work"),
        *weights,
        *weights,
        *states,
        *states,
    )
    out_specs = (P("work", None), P("work"), *weights, *weights, *states, *states)
    return jax.shard_map(local, mesh=mesh, in_specs=in_specs, out_specs=out_specs, check_vma=False)
```

```python
import functools
import math

import jax
import jax.numpy as jnp
from jax import lax
from jax.experimental import pallas as pl
from jax.experimental.pallas import tpu as pltpu
from jax.sharding import PartitionSpec as P

H = 6
HD = 48
STEP = 7

norm_eps = 1e-06
zloss_coef = 0.01
clip_limit = 0.05
beta_one = 0.9
beta_two = 0.95
adam_eps = 1e-08
decay_rate = 0.1
matrix_rate = 0.03
gain_rate = 0.3
outer_rate = 0.7
outer_mom = 0.9
rope_base = 10000.0

LOG2E = 1.0 / math.log(2.0)
LN2 = math.log(2.0)
SCALE = 1.0 / math.sqrt(HD)
BF = jnp.bfloat16
F32 = jnp.float32
NN = ((1,), (0,))
NT = ((1,), (1,))
CH = 1024
MIB = 1024 * 1024


def dot(a, b, dims=NN):
    return lax.dot_general(a, b, (dims, ((), ())), preferred_element_type=F32)


def params():
    return pltpu.CompilerParams(dimension_semantics=("arbitrary",), vmem_limit_bytes=58 * MIB)


def cost(micros):
    return pl.CostEstimate(flops=0, bytes_accessed=int(micros * 1.2e6), transcendentals=0)


def full(shape):
    return pl.BlockSpec(shape, lambda *_: (0,) * len(shape))


SMEM = pl.BlockSpec(memory_space=pltpu.SMEM)
ANY = pl.BlockSpec(memory_space=pl.ANY)


def call(kernel, ins, deps, **options):
    specs = options.pop("in_specs")

    def body(*refs):
        kernel(*refs[: len(ins)], *refs[len(ins) + len(deps) :])

    return pl.pallas_call(body, in_specs=[*specs, *([ANY] * len(deps))], **options)(*ins, *deps)


def pick_rows(ids_ref, s, tab, got, full_len):
    unroll = 32

    def body(i, carry):
        base = pl.multiple_of(i * unroll, unroll)
        for q in range(0, unroll, 8):
            rows = [tab[pl.ds(ids_ref[s, base + q + u], 1), :] for u in range(8)]
            got[pl.ds(pl.multiple_of(base + q, 8), 8), :] = jnp.concatenate(rows, 0)
        return carry

    lax.fori_loop(0, full_len // unroll, body, 0)


def rows_out(blk, got, outs):
    for k, out in enumerate(outs):
        width, lt = out.shape
        at = pl.multiple_of((blk ^ k) * lt, lt)
        out[...] = got[pl.ds(at, lt), 0:width].T.astype(BF)


def prep_kernel(count, vrows, nb, me_ref, ids_ref, *refs):
    pieces = refs[:count]
    et_ref, er_ref = refs[count : count + 2]
    outs = refs[count + 2 : count + 2 + nb]
    *others, tmp, tab, got = refs[count + 2 + nb :]
    j = pl.program_id(0)
    width, lt = outs[0].shape
    for k, piece in enumerate(pieces):
        tmp[me_ref[0] ^ k] = piece[...].astype(F32)
    e = jnp.concatenate([tmp[w] for w in range(count)], 0)
    lane = lax.broadcasted_iota(jnp.int32, (width, CH), 1) + j * CH
    e = jnp.where(lane < vrows, e, 0.0)
    et_ref[...] = e.astype(BF)
    rows = e.T
    tab[pl.ds(pl.multiple_of(j * CH, CH), CH), 0:width] = rows
    er_ref[:, 0:width] = rows.astype(BF)
    row = lax.broadcasted_iota(jnp.int32, (CH, 16), 0) + j * CH
    col = lax.broadcasted_iota(jnp.int32, (CH, 16), 1)
    er_ref[:, width:] = jnp.where((row >= vrows) & (col == 0), -60000.0, 0.0).astype(BF)

    @pl.when(j == pl.num_programs(0) - 1)
    def _():
        pick_rows(ids_ref, 0, tab, got, nb * lt)
        rows_out(me_ref[1], got, outs)
        for s, other in enumerate(others):
            pick_rows(ids_ref, s + 1, tab, got, nb * lt)
            other[...] = got[:, 0:width].T.astype(BF)


def prep(me, ids, pieces, vpad, nb):
    count = len(pieces)
    rows, vrows = pieces[0].shape
    width = count * rows
    slots, full_len = ids.shape
    lt = full_len // nb
    padded = pl.cdiv(width, 128) * 128
    et, er, *outs = pl.pallas_call(
        functools.partial(prep_kernel, count, vrows, nb),
        grid=(vpad // CH,),
        in_specs=[SMEM, SMEM] + [pl.BlockSpec((rows, CH), lambda j: (0, j))] * count,
        out_specs=[
            pl.BlockSpec((width, CH), lambda j: (0, j)),
            pl.BlockSpec((CH, width + 16), lambda j: (j, 0)),
            *[full((width, lt))] * nb,
            *[full((width, full_len))] * (slots - 1),
        ],
        out_shape=[
            jax.ShapeDtypeStruct((width, vpad), BF),
            jax.ShapeDtypeStruct((vpad, width + 16), BF),
            *[jax.ShapeDtypeStruct((width, lt), BF)] * nb,
            *[jax.ShapeDtypeStruct((width, full_len), BF)] * (slots - 1),
        ],
        scratch_shapes=[
            pltpu.VMEM((count, rows, CH), F32),
            pltpu.VMEM((vpad, padded), F32),
            pltpu.VMEM((full_len, padded), F32),
        ],
        compiler_params=params(),
        cost_estimate=cost(12),
        name="prep",
    )(me, ids, *pieces)
    return et, er, outs[:nb], outs[nb:]


def rows_kernel(ids_ref, er_ref, *refs):
    outs, (mark, tab, got) = refs[:-3], refs[-3:]
    width = outs[0].shape[0]
    mark[...] = jnp.zeros_like(mark)

    def fill(c, carry):
        here = pl.ds(pl.multiple_of(c * CH, CH), CH)
        tab[here, 0:width] = er_ref[here, 0:width].astype(F32)
        return carry

    lax.fori_loop(0, er_ref.shape[0] // CH, fill, 0)
    for s, out in enumerate(outs):
        pick_rows(ids_ref, s, tab, got, got.shape[0])
        out[...] = got[:, 0:width].T.astype(BF)


def table_rows(ids, er, width, deps=()):
    count, full_len = ids.shape
    padded = pl.cdiv(width, 128) * 128
    *rows, mark = call(
        rows_kernel,
        (ids, er),
        deps,
        grid=(1,),
        in_specs=[SMEM, full(er.shape)],
        out_specs=[full((width, full_len))] * count + [full((8, 128))],
        out_shape=[jax.ShapeDtypeStruct((width, full_len), BF)] * count
        + [jax.ShapeDtypeStruct((8, 128), F32)],
        scratch_shapes=[
            pltpu.VMEM((er.shape[0], padded), F32),
            pltpu.VMEM((full_len, padded), F32),
        ],
        compiler_params=params(),
        cost_estimate=cost(11),
        name="table_rows",
    )
    return rows, mark


def weights_kernel(nb, nw, widths, packed, *outs):
    straight, turned = outs[:4], outs[4:8]
    counts = jnp.zeros((1, 1), F32)
    for w in range(nw):
        part = [packed[b * nw + w].astype(F32) for b in range(nb)]
        part = jnp.concatenate(part, 0)
        at = 0
        for size, out in zip(widths, straight):
            out[:, w * size : (w + 1) * size] = part[:, at : at + size].astype(BF)
            at += size
        if w == 0:
            outs[8][...] = part[:, at : at + 3]
        counts += part[0:1, at + 3 : at + 4]
    outs[9][...] = counts
    for out, flip in zip(straight, turned):
        flip[...] = out[...].astype(F32).T.astype(BF)


def split_weights(packed, nb, nw, widths):
    rows = packed.shape[1]
    width = nb * rows
    shapes = [(width, nw * size) for size in widths]
    outs = [(s, BF) for s in shapes] + [(s[::-1], BF) for s in shapes]
    outs += [((width, 3), F32), ((1, 1), F32)]
    return pl.pallas_call(
        functools.partial(weights_kernel, nb, nw, widths),
        grid=(1,),
        in_specs=[full(packed.shape)],
        out_specs=[full(s) for s, _ in outs],
        out_shape=[jax.ShapeDtypeStruct(s, d) for s, d in outs],
        compiler_params=params(),
        cost_estimate=cost(3),
        name="split_weights",
    )(packed)


def norm_t(x, gain):
    scale = lax.rsqrt(jnp.mean(x * x, 0, keepdims=True) + norm_eps)
    return x * scale * gain, scale


def norm_t_bwd(x, scale, gain, incoming):
    unit = x * scale
    inner = incoming * gain
    return scale * (inner - unit * jnp.mean(inner * unit, 0, keepdims=True)), incoming * unit


def turn(u, cosine, sine):
    rows, lt = u.shape
    half = cosine.shape[0]
    u = u.reshape(rows // (2 * half), 2, half, lt)
    a, b = u[:, 0], u[:, 1]
    return jnp.stack([a * cosine - b * sine, a * sine + b * cosine], 1).reshape(rows, lt)


def place(me, pieces, out):
    lt = pieces[0].shape[1]
    for k, piece in enumerate(pieces):
        if len(pieces) == 1:
            out[...] = piece[...]
        else:
            out[:, pl.ds(pl.multiple_of((me ^ k) * lt, lt), lt)] = piece[...]


def interleave(parts):
    while parts:
        parts = [p for p in parts if next(p, 1) is None]


def causal(lt):
    keys = lax.broadcasted_iota(jnp.int32, (lt, lt), 0)
    queries = lax.broadcasted_iota(jnp.int32, (lt, lt), 1)
    return keys <= queries


def gelu_parts(u):
    k0 = math.sqrt(2.0 / math.pi)
    square = u * u
    th = jnp.tanh(k0 * (u + 0.044715 * u * square))
    act = 0.5 * u * (1.0 + th)
    return act, th, square, k0


def gelu_slope(u, th, square, k0):
    return 0.5 * (1.0 + th) + 0.5 * u * (1.0 - th * th) * k0 * (1.0 + 3.0 * 0.044715 * square)


def trunk_fwd_kernel(count, me_ref, *refs):
    (want, wqkv_t, wo_t, wm0_t, wm1, gains, cos_ref, sin_ref) = refs[count : count + 8]
    (x0_out, qkv_out, o_out, lse_out, af_out, krow) = refs[count + 8 :]
    width, full_len = x0_out.shape
    lt = min(256, full_len)
    nb = full_len // lt
    root = math.sqrt(width)
    place(me_ref[0], refs[:count], x0_out)
    def project(j):
        here = slice(j * lt, (j + 1) * lt)
        x = x0_out[:, here].astype(F32) * root
        a1, _ = norm_t(x, gains[:, 0:1])
        yield
        y = dot(wqkv_t[...], a1.astype(BF))
        yield
        cosine, sine = cos_ref[:, here], sin_ref[:, here]
        q = turn(y[:width], cosine, sine) * (SCALE * LOG2E)
        k = turn(y[width : 2 * width], cosine, sine)
        qkv_out[0:width, here] = q.astype(BF)
        qkv_out[width : 2 * width, here] = k.astype(BF)
        qkv_out[2 * width :, here] = y[2 * width :].astype(BF)
        for h in range(H):
            krow[h, here, :] = k[h * HD : (h + 1) * HD].T.astype(BF)

    interleave([project(j) for j in range(nb)])
    lse_out[...] = jnp.zeros_like(lse_out)

    def head(h, j):
        rows = slice(h * HD, (h + 1) * HD)
        values = slice(2 * width + h * HD, 2 * width + (h + 1) * HD)
        here, before = slice(j * lt, (j + 1) * lt), slice(0, j * lt)
        q = qkv_out[rows, here]
        s_diag = jnp.where(causal(lt), dot(krow[h, here, :], q), -1e30)
        peak = jnp.max(s_diag, 0, keepdims=True)
        if j:
            s_off = dot(krow[h, before, :], q)
            peak = jnp.maximum(peak, jnp.max(s_off, 0, keepdims=True))
        yield
        p_diag = jnp.exp2(s_diag - peak)
        total = jnp.sum(p_diag, 0, keepdims=True)
        if j:
            p_off = jnp.exp2(s_off - peak)
            total = total + jnp.sum(p_off, 0, keepdims=True)
        yield
        mix = dot(qkv_out[values, here], p_diag.astype(BF))
        if j:
            mix = mix + dot(qkv_out[values, before], p_off.astype(BF))
        o_out[rows, here] = (mix / total).astype(BF)
        lse_out[h : h + 1, here] = peak + jnp.log2(total)

    for j in range(nb):
        interleave([head(h, j) for h in range(H)])

    def finish(j):
        here = slice(j * lt, (j + 1) * lt)
        x = x0_out[:, here].astype(F32) * root
        h1 = x + dot(wo_t[...], o_out[:, here])
        yield
        a2, _ = norm_t(h1, gains[:, 1:2])
        yield
        u = dot(wm0_t[...], a2.astype(BF))
        yield
        act = gelu_parts(u)[0].astype(BF)
        yield
        h2 = h1 + dot(wm1[...], act)
        yield
        af, _ = norm_t(h2, gains[:, 2:3])
        af = (af * LOG2E).astype(BF)
        af_out[0:width, here] = af
        tail = lax.broadcasted_iota(jnp.int32, (af_out.shape[0] - width, lt), 0)
        af_out[width:, here] = jnp.where(tail == 0, 1.0, 0.0).astype(BF)

    interleave([finish(j) for j in range(nb)])
    picked = af_out[0:width, :].astype(F32) * want[...].astype(F32)
    lse_out[H : H + 1, :] = jnp.sum(picked, 0, keepdims=True)


def trunk_fwd(me, pieces, want, weights, gains, cosine, sine, deps=()):
    width, full_len = want.shape
    ins = (me, *pieces, want, *weights, gains, cosine, sine)
    shapes = [
        ((width, full_len), BF),
        ((3 * width, full_len), BF),
        ((width, full_len), BF),
        ((8, full_len), F32),
        ((width + 16, full_len), BF),
    ]
    return call(
        functools.partial(trunk_fwd_kernel, len(pieces)),
        ins,
        deps,
        grid=(1,),
        in_specs=[SMEM] + [full(a.shape) for a in ins[1:]],
        out_specs=[full(s) for s, _ in shapes],
        out_shape=[jax.ShapeDtypeStruct(s, d) for s, d in shapes],
        scratch_shapes=[pltpu.VMEM((H, full_len, HD), BF)],
        compiler_params=params(),
        cost_estimate=cost(13),
        name="trunk_fwd",
    )


def head_kernel(er_ref, af_ref, p_ref, m_ref, st_ref, s_ref, run, cur, z_ref):
    j = pl.program_id(0)
    full_len = af_ref.shape[1]
    lt = z_ref.shape[1]
    tiles = [slice(t, t + lt) for t in range(0, full_len, lt)]

    def emit(here, z, peak):
        p = jnp.exp2(z - peak)
        p_ref[:, here] = p.astype(BF)
        m_ref[pl.ds(j, 1), here] = peak
        total = jnp.sum(p.reshape(CH // 8, 8, lt), 0)
        s_ref[pl.ds(j, 1), here] = jnp.sum(total, 0, keepdims=True)

    @pl.when(j == 0)
    def _():
        run[...] = jnp.full_like(run, -1e30)
        cur[...] = jnp.zeros_like(cur)

    @pl.when(j > 0)
    def _():
        for here in tiles:
            z = dot(er_ref[...], af_ref[:, here])
            peak = jnp.max(z.reshape(CH // 8, 8, lt), 0)
            cur[0:1, here] = jnp.max(peak, 0, keepdims=True)
            emit(here, z, run[0:1, here])

    again = (j == 0) | (jnp.max(cur[0:1, :] - run[0:1, :]) > 60.0)

    @pl.when(again)
    def _():
        for here in tiles:
            z_ref[...] = dot(er_ref[...], af_ref[:, here])
            peak = jnp.max(z_ref[...], 0, keepdims=True)
            peak = jnp.maximum(peak, run[0:1, here])
            cur[0:1, here] = peak
            emit(here, z_ref[...], peak)

    run[0:1, :] = jnp.maximum(run[0:1, :], cur[0:1, :])

    @pl.when(j == pl.num_programs(0) - 1)
    def _():
        peak = run[0:1, :]
        total = jnp.sum(s_ref[...] * jnp.exp2(m_ref[...] - peak), 0, keepdims=True)
        st_ref[...] = jnp.zeros_like(st_ref)
        st_ref[0:1, :] = peak
        st_ref[1:2, :] = total


def head_first(er, af, deps=()):
    vpad, depth = er.shape
    full_len = af.shape[1]
    chunks = vpad // CH
    shapes = [((vpad, full_len), BF), ((chunks, full_len), F32), ((8, full_len), F32)]
    return call(
        head_kernel,
        (er, af),
        deps,
        grid=(chunks,),
        in_specs=[pl.BlockSpec((CH, depth), lambda j: (j, 0)), full(af.shape)],
        out_specs=[pl.BlockSpec((CH, full_len), lambda j: (j, 0))]
        + [full(s) for s, _ in shapes[1:]],
        out_shape=[jax.ShapeDtypeStruct(s, d) for s, d in shapes],
        scratch_shapes=[
            pltpu.VMEM((chunks, full_len), F32),
            pltpu.VMEM((8, full_len), F32),
            pltpu.VMEM((8, full_len), F32),
            pltpu.VMEM((CH, min(512, full_len)), F32),
        ],
        compiler_params=params(),
        cost_estimate=cost(16),
        name="head_first",
    )


def head_back_kernel(slot, nb, sc_ref, *refs):
    (p_ref, et_ref, af_ref, tgt_ref, m_ref, pick_ref) = refs[:6]
    stats = refs[6 : 6 + nb]
    (out, de_ref, loss_ref, acc, s_ref, d_ref) = refs[6 + nb :]
    j = pl.program_id(0)
    width, full_len = out.shape
    lt = min(256, full_len)
    valid = sc_ref[1 + slot]
    weight = valid * sc_ref[0]

    @pl.when(j == 0)
    def _():
        acc[...] = jnp.zeros_like(acc)
        top = functools.reduce(jnp.maximum, [b[0:1, :] for b in stats])
        total = sum(b[1:2, :] * jnp.exp2(b[0:1, :] - top) for b in stats)
        lse2 = top + jnp.log2(total)
        lse = lse2 * LN2
        boost = (1.0 + 2.0 * zloss_coef * lse) * weight
        pick = pick_ref[H : H + 1, :]
        s_ref[...] = jnp.exp2(m_ref[...] - lse2) * boost
        d_ref[0:1, :] = jnp.exp2(pick - lse2) * boost - weight
        loss_ref[...] = jnp.zeros_like(loss_ref)
        loss_ref[0:1, :] = (lse + zloss_coef * lse * lse) * valid
        loss_ref[1:2, :] = pick * LN2 * valid

    rows = lax.broadcasted_iota(jnp.int32, (CH, lt), 0)
    for half in range(2):
        chunk = 2 * j + half
        there = slice(half * CH, (half + 1) * CH)
        total = None
        for t in range(full_len // lt):
            here = slice(t * lt, (t + 1) * lt)
            grad = jnp.where(
                rows == tgt_ref[:, here] - chunk * CH,
                d_ref[0:1, here],
                p_ref[there, here].astype(F32) * s_ref[pl.ds(chunk, 1), here],
            ).astype(BF)
            acc[:, here] += dot(et_ref[:, there], grad)
            part = dot(af_ref[0:width, here], grad, NT)
            total = part if total is None else total + part
        de_ref[:, there] = (total * LN2).astype(BF)

    @pl.when(j == pl.num_programs(0) - 1)
    def _():
        out[...] = acc[...].astype(BF)


def head_back(slot, scalars, p, et, af, tgt, peaks, picks, stats, deps=()):
    nb = len(stats)
    width, vpad = et.shape
    full_len = tgt.shape[1]
    tall = pl.BlockSpec((2 * CH, full_len), lambda j: (j, 0))
    wide = pl.BlockSpec((width, 2 * CH), lambda j: (0, j))
    rest = (af, tgt, peaks, picks, *stats)
    return call(
        functools.partial(head_back_kernel, slot, nb),
        (scalars, p, et, *rest),
        deps,
        grid=(vpad // (2 * CH),),
        in_specs=[SMEM, tall, wide] + [full(a.shape) for a in rest],
        out_specs=[full((width, full_len)), wide, full((8, full_len))],
        out_shape=[
            jax.ShapeDtypeStruct((width, full_len), BF),
            jax.ShapeDtypeStruct((width, vpad), BF),
            jax.ShapeDtypeStruct((8, full_len), F32),
        ],
        scratch_shapes=[
            pltpu.VMEM((width, full_len), F32),
            pltpu.VMEM(peaks.shape, F32),
            pltpu.VMEM((8, full_len), F32),
        ],
        compiler_params=params(),
        cost_estimate=cost(15),
        name="head_back",
    )


def trunk_bwd_kernel(me_ref, *refs):
    (gin, x0, qkv, o_ref, lse) = refs[:5]
    (wqkv, wo, wo_t, wm0, wm0_t, wm1, wm1_t, gains, cos_ref, sin_ref) = refs[5:15]
    (dx_out, wg_out, gg_out) = refs[15:18]
    (krow, vrow, dqkv, dqkv_b, dh1_s, dh1_b, a_s, du_s, act_s, df_s, do_s, delta, wg, gg_s) = refs[18:]
    me = me_ref[0]
    width, full_len = x0.shape
    ff = du_s.shape[0]
    lt = min(256, full_len)
    nb = full_len // lt
    root = math.sqrt(width)
    gain_sums = [[None] * nb for _ in range(3)]

    def outer(j):
        here = slice(j * lt, (j + 1) * lt)
        h1 = x0[:, here].astype(F32) * root + dot(wo_t[...], o_ref[:, here])
        yield
        a2, scale = norm_t(h1, gains[:, 1:2])
        a2 = a2.astype(BF)
        a_s[:, here] = a2
        yield
        u = dot(wm0_t[...], a2)
        yield
        act, th, square, k0 = gelu_parts(u)
        slope = gelu_slope(u, th, square, k0)
        act = act.astype(BF)
        act_s[:, here] = act
        yield
        h2 = h1 + dot(wm1[...], act)
        yield
        _, scale2 = norm_t(h2, 1.0)
        dh2, gg = norm_t_bwd(h2, scale2, gains[:, 2:3], gin[:, here].astype(F32))
        gain_sums[2][j] = jnp.sum(gg, 1, keepdims=True)
        df = dh2.astype(BF)
        df_s[:, here] = df
        yield
        du = (dot(wm1_t[...], df) * slope).astype(BF)
        du_s[:, here] = du
        yield
        da2 = dot(wm0[...], du)
        yield
        dmid, gg = norm_t_bwd(h1, scale, gains[:, 1:2], da2)
        gain_sums[1][j] = jnp.sum(gg, 1, keepdims=True)
        dh1 = dh2 + dmid
        dh1_s[:, here] = dh1
        dh1b = dh1.astype(BF)
        dh1_b[:, here] = dh1b
        yield
        do = dot(wo[...], dh1b).astype(BF)
        do_s[:, here] = do
        weighed = (do.astype(F32) * o_ref[:, here].astype(F32)).reshape(H, HD, lt)
        delta[0:H, here] = jnp.sum(weighed, 1)
        yield
        for h in range(H):
            lo = width + h * HD
            krow[h, here, :] = qkv[lo : lo + HD, here].astype(F32).T.astype(BF)
            vrow[h, here, :] = qkv[lo + width : lo + width + HD, here].astype(F32).T.astype(BF)

    interleave([outer(j) for j in range(nb)])
    wg[:, 4 * width : 4 * width + ff] = dot(a_s[...], du_s[...], NT)
    wg[:, 4 * width + ff :] = dot(df_s[...], act_s[...], NT)
    wg[:, 3 * width : 4 * width] = dot(o_ref[...], dh1_b[...], NT)

    def head(h, j):
        qs, ks, vs = (pl.ds(pl.multiple_of(a + h * HD, 16), HD) for a in (0, width, 2 * width))
        here = slice(j * lt, (j + 1) * lt)
        parts = [(here, True)] + ([(slice(0, j * lt), False)] if j else [])
        q, do = qkv[qs, here], do_s[qs, here]
        lse_row, delta_row = lse[pl.ds(h, 1), here], delta[pl.ds(h, 1), here]
        scores = [(dot(krow[h, t, :], q), dot(vrow[h, t, :], do)) for t, _ in parts]
        yield
        grads = []
        for (there, diagonal), (s, dp) in zip(parts, scores):
            p = jnp.exp2(s - lse_row)
            if diagonal:
                p = jnp.where(causal(lt), p, 0.0)
            grads.append((p.astype(BF), (p * (dp - delta_row)).astype(BF)))
        yield
        dq = 0.0
        for (there, _), (pb, dsb) in zip(parts, grads):
            dq = dq + dot(qkv[ks, there], dsb)
            dk, dv = dot(q, dsb, NT), dot(do, pb, NT)
            if j == nb - 1:
                dqkv[ks, there] = dk
                dqkv[vs, there] = dv
            else:
                dqkv[ks, there] += dk
                dqkv[vs, there] += dv
        dqkv[qs, here] = dq

    def heads(i, carry):
        for j in reversed(range(nb)):
            interleave([head(i * 2 + u, j) for u in range(2)])
        return carry

    lax.fori_loop(0, H // 2, heads, 0)

    def inner(j):
        here = slice(j * lt, (j + 1) * lt)
        cosine, sine = cos_ref[:, here], -sin_ref[:, here]
        dq = turn(dqkv[0:width, here], cosine, sine) * SCALE
        dk = turn(dqkv[width : 2 * width, here], cosine, sine) * LN2
        dqkv_b[0:width, here] = dq.astype(BF)
        dqkv_b[width : 2 * width, here] = dk.astype(BF)
        dqkv_b[2 * width :, here] = dqkv[2 * width :, here].astype(BF)
        x = x0[:, here].astype(F32) * root
        a1, scale = norm_t(x, gains[:, 0:1])
        a_s[:, here] = a1.astype(BF)
        yield
        da1 = dot(wqkv[...], dqkv_b[:, here])
        yield
        dlow, gg = norm_t_bwd(x, scale, gains[:, 0:1], da1)
        gain_sums[0][j] = jnp.sum(gg, 1, keepdims=True)
        dx_out[:, here] = ((dh1_s[:, here] + dlow) * root).astype(BF)

    interleave([inner(j) for j in range(nb)])
    wg[:, 0 : 3 * width] = dot(a_s[...], dqkv_b[...], NT)
    own = wg_out.shape[0]
    wg_out[...] = wg[pl.ds(pl.multiple_of(me * own, 8), own), :]
    lane = lax.broadcasted_iota(jnp.int32, gg_s.shape, 1)
    gg_s[...] = sum(jnp.where(lane == i, sum(gain_sums[i]), 0.0) for i in range(3))
    gg_out[...] = gg_s[pl.ds(pl.multiple_of(me * own, 8), own), :]


def trunk_bwd(me, gin, saved, weights, gains, cosine, sine, own, deps=()):
    width, full_len = gin.shape
    ff = weights[3].shape[1]
    ins = (me, gin, *saved, *weights, gains, cosine, sine)
    cols = 4 * width + 2 * ff
    shapes = [((width, full_len), BF), ((own, cols), F32), ((own, 128), F32)]
    return call(
        trunk_bwd_kernel,
        ins,
        deps,
        grid=(1,),
        in_specs=[SMEM] + [full(a.shape) for a in ins[1:]],
        out_specs=[full(s) for s, _ in shapes],
        out_shape=[jax.ShapeDtypeStruct(s, d) for s, d in shapes],
        scratch_shapes=[
            pltpu.VMEM((H, full_len, HD), BF),
            pltpu.VMEM((H, full_len, HD), BF),
            pltpu.VMEM((3 * width, full_len), F32),
            pltpu.VMEM((3 * width, full_len), BF),
            pltpu.VMEM((width, full_len), F32),
            pltpu.VMEM((width, full_len), BF),
            pltpu.VMEM((width, full_len), BF),
            pltpu.VMEM((ff, full_len), BF),
            pltpu.VMEM((ff, full_len), BF),
            pltpu.VMEM((width, full_len), BF),
            pltpu.VMEM((width, full_len), BF),
            pltpu.VMEM((8, full_len), F32),
            pltpu.VMEM((width, cols), F32),
            pltpu.VMEM((width, 128), F32),
        ],
        compiler_params=params(),
        cost_estimate=cost(24),
        name="trunk_bwd",
    )


def folded(values):
    rows, cols = values.shape
    values = jnp.sum(values.reshape(rows // 8, 8, cols), 0)
    return sum(values[:, c : c + 128] for c in range(0, cols, 128))


def token_sum(first, tok_ref, de_refs, dx_refs):
    full_len = tok_ref.shape[2]
    lt = min(512, full_len)
    rows = lax.broadcasted_iota(jnp.int32, (CH, lt), 0) + pl.program_id(0) * CH
    total = sum(d[...].astype(F32) for d in de_refs)
    for s, dx in enumerate(dx_refs):
        for t in range(full_len // lt):
            here = slice(t * lt, (t + 1) * lt)
            hot = jnp.where(rows == tok_ref[first + s, :, here], 1.0, 0.0).astype(BF)
            total = total + dot(dx[:, here], hot, NT)
    return total


def token_part_kernel(count, tok_ref, *refs):
    *ins, out = refs
    out[...] = token_sum(0, tok_ref, ins[:count], ins[count:]).astype(BF)


def token_part(tok, des, dxs):
    width, vpad = des[0].shape
    blk = pl.BlockSpec((width, CH), lambda j: (0, j))
    return pl.pallas_call(
        functools.partial(token_part_kernel, len(des)),
        grid=(vpad // CH,),
        in_specs=[full(tok.shape)] + [blk] * len(des) + [full(a.shape) for a in dxs],
        out_specs=blk,
        out_shape=jax.ShapeDtypeStruct((width, vpad), BF),
        compiler_params=params(),
        cost_estimate=cost(13),
        name="token_part",
    )(tok, *des, *dxs)


def token_grad_kernel(first, slots, tok_ref, de_ref, *refs):
    count = slots - first
    dx_refs, refs = refs[:count], refs[count:]
    wg_refs, gg_refs, loss_refs = refs[:slots], refs[slots : 2 * slots], refs[2 * slots : 3 * slots]
    out_ref, wg_out, gg_out, sum_out, acc = refs[3 * slots :]
    j = pl.program_id(0)

    @pl.when(j == 0)
    def _():
        wg = sum(w[...] for w in wg_refs)
        gg = sum(g[...] for g in gg_refs)
        wg_out[...] = wg
        gg_out[...] = gg
        acc[...] = folded(wg * wg) + folded(gg * gg)

    total = token_sum(first, tok_ref, [de_ref], dx_refs)
    out_ref[...] = total.astype(BF)
    acc[...] += folded(total * total)

    @pl.when(j == pl.num_programs(0) - 1)
    def _():
        lane = lax.broadcasted_iota(jnp.int32, sum_out.shape, 1)
        pick = jnp.sum(sum(r[1:2, :] for r in loss_refs))
        lse = jnp.sum(sum(r[0:1, :] for r in loss_refs))
        tail = jnp.where(lane == 2, lse, 0.0)
        sum_out[...] = jnp.where(lane == 0, jnp.sum(acc[...]), jnp.where(lane == 1, pick, tail))


def token_grad(tok, de, dxs, wgs, ggs, losses):
    slots = len(wgs)
    width, vpad = de.shape
    blk = pl.BlockSpec((width, CH), lambda j: (0, j))
    rest = (*dxs, *wgs, *ggs, *losses)
    shapes = [(wgs[0].shape, F32), (ggs[0].shape, F32), ((8, 128), F32)]
    return pl.pallas_call(
        functools.partial(token_grad_kernel, slots - len(dxs), slots),
        grid=(vpad // CH,),
        in_specs=[full(tok.shape), blk] + [full(a.shape) for a in rest],
        out_specs=[blk] + [full(s) for s, _ in shapes],
        out_shape=[jax.ShapeDtypeStruct((width, vpad), BF)]
        + [jax.ShapeDtypeStruct(s, d) for s, d in shapes],
        scratch_shapes=[pltpu.VMEM((8, 128), F32)],
        compiler_params=params(),
        cost_estimate=cost(9),
        name="token_grad",
    )(tok, de, *rest)


def clip_factor(sums):
    total = sum(s[0:1, 0:1] for s in sums)
    return clip_limit / jnp.maximum(jnp.sqrt(total), clip_limit)


def adam(gradient, first, second, weight):
    first = beta_one * first + (1.0 - beta_one) * gradient
    second = beta_two * second + (1.0 - beta_two) * gradient * gradient
    ratio = (first * (weight / (1.0 - beta_one**STEP))) / (
        jnp.sqrt(second * (1.0 / (1.0 - beta_two**STEP))) + adam_eps
    )
    return first, second, ratio


def adam_small_kernel(nb, widths, sc_ref, me_ref, *refs):
    factor = clip_factor(refs[:nb])
    (wg, gg, qf, of, mf, gf, qs, os_, ms, gs) = refs[nb : nb + 10]
    (qf2, of2, mf2, gf2, qs2, os2, ms2, gs2, *r_out) = refs[nb + 11 : -2]
    res = refs[-2]
    sums = sum(r[...] for r in refs[:nb])
    lane = lax.broadcasted_iota(jnp.int32, res.shape, 1)
    loss = refs[0][:, 2:3] - sums[:, 1:2]
    res[...] = jnp.where(lane == 0, loss, jnp.where(lane == 1, jnp.sqrt(sums[:, 0:1]), 0.0))
    weight = sc_ref[0] * matrix_rate
    at = 0
    ratios = []
    for f, s, f2, s2 in (
        (qf, qs, qf2, qs2),
        (of, os_, of2, os2),
        (mf.at[0], ms.at[0], mf2.at[0], ms2.at[0]),
        (mf.at[1], ms.at[1], mf2.at[1], ms2.at[1]),
    ):
        here = slice(at, at + f.shape[1])
        f2[...], s2[...], ratio = adam(wg[:, here] * factor, f[...], s[...], weight)
        ratios.append(ratio)
        at = here.stop
    f2, s2, ratio = adam(gg[:, 0:3] * factor, gf[...], gs[...], sc_ref[0] * gain_rate)
    gf2[...] = f2
    gs2[...] = s2
    if not widths:
        at = 0
        for r in ratios:
            r_out[0][:, at : at + r.shape[1]] = r
            at += r.shape[1]
        r_out[0][:, at:] = jnp.zeros_like(r_out[0][:, at:])
        r_out[0][:, at : at + 3] = ratio
        return
    rows, cols = ratio.shape[0] // 2, r_out[0].shape[2] // 2
    blank = jnp.zeros((2 * rows, cols - sum(widths) - 3), F32)
    below = jnp.zeros((r_out[0].shape[1] - rows, 2 * cols), F32)
    for w in range(2 * r_out[0].shape[0]):
        parts = [r[:, w * size : (w + 1) * size] for r, size in zip(ratios, widths)]
        piece = jnp.concatenate([*parts, ratio, blank], 1)
        piece = jnp.concatenate([piece[:rows], piece[rows:]], 1)
        piece = jnp.concatenate([piece, below], 0).astype(BF)
        rel = me_ref[0] ^ w
        for core in range(2):

            @pl.when((rel & 1) == core)
            def _():
                r_out[core][rel >> 1] = piece


def adam_small(scalars, me, sums, wg, gg, firsts, seconds, groups, widths, through):
    ins = (*sums, wg, gg, *firsts, *seconds)
    shapes = [(a.shape, F32) for a in (*firsts, *seconds)]
    if groups:
        cols = pl.cdiv(sum(widths) + 3, 128) * 128
        rows = pl.cdiv(wg.shape[0] // 2, 8) * 8
        shapes += [((groups // 2, rows, 2 * cols), BF)] * 2
    else:
        shapes.append(((wg.shape[0], wg.shape[1] + 128), F32))
    shapes.append((sums[0].shape, F32))
    return pl.pallas_call(
        functools.partial(adam_small_kernel, len(sums), widths if groups else None),
        grid=(1,),
        in_specs=[SMEM, SMEM] + [full(a.shape) for a in ins] + [ANY],
        out_specs=[full(s) for s, _ in shapes] + [ANY],
        out_shape=[jax.ShapeDtypeStruct(s, d) for s, d in shapes]
        + [jax.ShapeDtypeStruct(through.shape, through.dtype)],
        input_output_aliases={2 + len(ins): len(shapes)},
        compiler_params=params(),
        cost_estimate=cost(3),
        name="adam_small",
    )(scalars, me, *ins, through)


def adam_kernel(nb, grouped, kept, through, extra, sc_ref, me_ref, *refs):
    r_out = refs[len(refs) - through - (2 if grouped else 1) : len(refs) - through]
    if not extra:
        return adam_chunk(nb, grouped, kept + through, sc_ref, me_ref, refs, r_out)
    j = pl.program_id(0)

    @pl.when(j < pl.num_programs(0) - 1)
    def _():
        adam_chunk(nb, grouped, kept + through + extra, sc_ref, me_ref, refs, r_out)

    @pl.when(j == pl.num_programs(0) - 1)
    def _():
        for e, r in zip(refs[nb + 3 : nb + 3 + extra], r_out):
            r[:, :, 0 : e.shape[2]] = e[...]


def adam_chunk(nb, grouped, skipped, sc_ref, me_ref, refs, r_out):
    sums, (g_ref, f_ref, s_ref) = refs[:nb], refs[nb : nb + 3]
    f_out, s_out = refs[nb + 3 + skipped : nb + 5 + skipped]
    factor = clip_factor(sums)
    first, second, ratio = adam(
        g_ref[...].astype(F32) * factor, f_ref[...], s_ref[...], sc_ref[0] * matrix_rate
    )
    f_out[...] = first
    s_out[...] = second
    if not grouped:
        r_out[0][...] = ratio.astype(BF)
        return
    groups = 2 * r_out[0].shape[0]
    rows = ratio.shape[0] // groups
    padded = r_out[0].shape[1]
    for w in range(groups):
        piece = ratio[w * rows : (w + 1) * rows]
        piece = jnp.concatenate([piece, jnp.zeros((padded - rows, CH), F32)], 0).astype(BF)
        rel = me_ref[0] ^ w
        for core in range(2):

            @pl.when((rel & 1) == core)
            def _():
                r_out[core][rel >> 1] = piece


def adam_table(scalars, me, sums, de, first, second, groups, part, kept=(), through=(), extra=(), deps=()):
    width, rows = first.shape
    lo, hi = part
    here = (hi - lo) * CH + extra[0].shape[2] if extra else min(hi * CH, rows) - lo * CH
    blk = pl.BlockSpec((width, CH), lambda j: (0, jnp.minimum(j + lo, hi - 1)))
    shapes = [((width, rows), F32)] * 2
    specs = [blk, blk]
    if groups:
        stack = (groups // 2, pl.cdiv(width // groups, 8) * 8)
        shapes += [((*stack, here), BF)] * 2
        specs += [pl.BlockSpec((*stack, CH), lambda j: (0, 0, j))] * 2
    else:
        shapes += [((width, here), BF)]
        specs += [pl.BlockSpec((width, CH), lambda j: (0, j))]
    nb = len(sums)
    at, count = nb + 5 + len(extra), len(shapes)
    aliases = {at + i: i for i in range(len(kept))}
    aliases |= {at + len(kept) + i: count + i for i in range(len(through))}
    shapes += [(a.shape, a.dtype) for a in through]
    unread = [ANY] * (len(kept) + len(through))
    return call(
        functools.partial(
            adam_kernel, nb, bool(groups), len(kept), len(through), len(extra)
        ),
        (scalars, me, *sums, de, first, second, *extra, *kept, *through),
        deps,
        grid=(hi - lo + (1 if extra else 0),),
        in_specs=[SMEM, SMEM]
        + [full(a.shape) for a in sums]
        + [blk] * 3
        + [full(a.shape) for a in extra]
        + unread,
        out_specs=specs + [ANY] * len(through),
        out_shape=[jax.ShapeDtypeStruct(s, d) for s, d in shapes],
        input_output_aliases=aliases,
        compiler_params=params(),
        cost_estimate=cost(10),
        name="adam_table",
    )


def swap(value, axis, size, k):
    return lax.ppermute(value, axis, [(i, i ^ k) for i in range(size)])


def share(value, axis, size):
    return [value] + [swap(value, axis, size, k) for k in range(1, size)]


def sum_kernel(count, *refs):
    out = refs[count]
    out[...] = sum(p[...].astype(F32) for p in refs[:count]).astype(BF)


def sum_pieces(pieces, axis, size, through, deps=()):
    came = [pieces[0]] + [swap(pieces[k], axis, size, k) for k in range(1, size)]
    rest = (*through, *deps)

    def body(*refs):
        sum_kernel(size, *refs[:size], refs[size + len(rest)])

    return pl.pallas_call(
        body,
        grid=(1,),
        in_specs=[full(c.shape) for c in came] + [ANY] * len(rest),
        out_specs=[full(came[0].shape)] + [ANY] * len(through),
        out_shape=[jax.ShapeDtypeStruct(a.shape, a.dtype) for a in (came[0], *through)],
        input_output_aliases={size + i: 1 + i for i in range(len(through))},
        compiler_params=params(),
        cost_estimate=cost(2),
        name="sum_pieces",
    )(*came, *rest)


def mark_kernel(value_ref, out_ref):
    out_ref[...] = jnp.full_like(out_ref, value_ref[0])


def mark_after(value, deps):
    mark = call(
        mark_kernel,
        (value.astype(jnp.int32).reshape(1),),
        deps,
        grid=(1,),
        in_specs=[SMEM],
        out_specs=full((8, 128)),
        out_shape=jax.ShapeDtypeStruct((8, 128), jnp.int32),
        compiler_params=params(),
        cost_estimate=cost(1),
        name="mark_after",
    )
    return mark[0, 0]


def turn_first(i):
    return i ^ (2 if i % 2 == 0 else 4)


def turn_second(i):
    return i ^ (4 if i % 2 == 0 else 2)


def permute(value, axis, size, partner):
    return lax.ppermute(value, axis, [(i, partner(i)) for i in range(size)])


def gather_pieces(own, axis, core):
    x, y = swap(own, axis, 8, 2), swap(own, axis, 8, 4)
    far = permute(jnp.where(core == 0, y, x), axis, 8, turn_first)
    near = [own, x, y, far]
    others = [swap(p, axis, 8, 1) for p in near]
    return [p for pair in zip(near, others) for p in pair]


def reduce_first(same, other, axis, core):
    y = (same.astype(F32) + swap(other, axis, 8, 1).astype(F32)).astype(BF)
    sent = jnp.stack([jnp.where(core == 0, y[1], y[2]), y[3]])
    return sent, jnp.where(core == 0, y[2], y[1]), y[0]


def reduce_last(sent, kept, own, axis):
    came = permute(sent, axis, 8, turn_first)
    relayed = (kept.astype(F32) + came[1].astype(F32)).astype(BF)
    total = own.astype(F32) + came[0].astype(F32)
    return total + permute(relayed, axis, 8, turn_second).astype(F32)


def outer_update(summed, total_tok, master, momentum, step_rate, decay):
    average = summed / total_tok + step_rate * decay * master
    momentum = outer_mom * momentum + average
    return (master - outer_rate * (average + outer_mom * momentum), momentum)


def local(
    tokens,
    targets,
    seq_counts,
    embed_w,
    qkv_w,
    out_w,
    mlp_w,
    gain_w,
    embed_mom,
    qkv_mom,
    out_mom,
    mlp_mom,
    gain_mom,
    embed_first,
    qkv_first,
    out_first,
    mlp_first,
    gain_first,
    embed_second,
    qkv_second,
    out_second,
    mlp_second,
    gain_second,
):
    nb = lax.axis_size("blk")
    nw = lax.axis_size("work")
    me = lax.axis_index("blk")
    wi = lax.axis_index("work")
    core = wi % 2
    me_arr = me.astype(jnp.int32).reshape(1)
    wi_arr = wi.astype(jnp.int32).reshape(1)
    slots, full_len = tokens.shape[1:]
    vrows = embed_w.shape[0]
    width = embed_first.shape[2]
    ff = mlp_first.shape[3]
    vpad = pl.cdiv(vrows, 2 * CH) * 2 * CH
    own_rows = width // nb
    paired = nw == 8

    half = HD // 2
    frequency = rope_base ** (-jnp.arange(half).astype(F32) * 2.0 / HD)
    angles = frequency[:, None] * jnp.arange(full_len).astype(F32)[None, :]
    cosine, sine = jnp.cos(angles), jnp.sin(angles)

    def local_ids(ids, missing):
        ids = ids[0] - me * vrows
        return jnp.where((ids >= 0) & (ids < vrows), ids, missing)

    tok = local_ids(tokens, -1)[:, None, :]
    tgt = local_ids(targets, -1)[:, None, :]
    tok_rows = local_ids(tokens, vrows)
    tgt_rows = local_ids(targets, vrows)
    tgt_parts = (tgt_rows[:-1], tgt_rows[-1:])
    tgts = [tgt[s] for s in range(slots)]

    et_own = embed_w.T.astype(BF)
    if paired:
        early = (cosine, sine, tok, tok_rows, *tgt_parts, *tgts)
        pieces = gather_pieces(et_own, "work", mark_after(core, early))
    else:
        pieces = [lax.all_gather(et_own, "work", axis=0, tiled=True)]
    wi_prep = wi_arr if paired else jnp.zeros_like(wi_arr)

    cq, co, cf = qkv_w.shape[1], out_w.shape[1], mlp_w.shape[2]
    count_col = jnp.broadcast_to(seq_counts[0].astype(F32), (own_rows, 1))
    packed = jnp.concatenate([qkv_w, out_w, mlp_w[0], mlp_w[1], gain_w.T, count_col], 1)
    packed = lax.all_gather(packed.astype(BF), ("blk", "work"), axis=0, tiled=False)
    widths = (cq, co, cf, cf)
    c1, c3 = cq + co, cq + co + 2 * cf
    *weights, gains, count_sum = split_weights(packed, nb, nw, widths)
    wqkv, wo, wm0, wm1, wqkv_t, wo_t, wm0_t, wm1_t = weights
    total_tok = count_sum[0, 0] * full_len

    count_seq = seq_counts[0]
    count_tok = (count_seq * full_len).astype(F32)
    valid = (jnp.arange(slots) < count_seq).astype(F32)

    prep_ids = jnp.concatenate([wi_prep, me_arr])
    et, er, looked, more = prep(prep_ids, tok_rows, pieces, vpad, nb)
    fwd_weights = (wqkv_t, wo_t, wm0_t, wm1)
    bwd_weights = (wqkv, wo, wo_t, wm0, wm0_t, wm1, wm1_t)
    wants, mark = table_rows(tgt_parts[0], er, width)
    mine, *more = sum_pieces(looked, "blk", nb, more, (mark,))
    later, mark = table_rows(tgt_parts[1], er, width, (mark, wqkv))
    wants += later
    def sum_blocks(value, turn):
        return lax.psum(value, "blk", axis_index_groups=[[(k + turn) % nb for k in range(nb)]])

    rows = [share(mine, "blk", nb)]
    rows += [[sum_blocks(m, s)] for s, m in enumerate(more)]

    saved, heads, stats, backs, des, losses = {}, {}, {}, {}, {}, {}
    scalars = jnp.concatenate([1.0 / count_tok.reshape(1), valid])

    def forward(s, *deps):
        *kept, af = trunk_fwd(
            me_arr, rows[s], wants[s], fwd_weights, gains, cosine, sine, deps
        )
        saved[s] = kept
        heads[s] = [af]

    def head(s, *deps):
        p, peaks, stat = head_first(er, heads[s][0], deps)
        heads[s] += [p, peaks]
        stats[s] = share(stat, "blk", nb)

    def back(s, *deps):
        af, p, peaks = heads[s]
        gin, des[s], losses[s] = head_back(
            s, scalars, p, et, af, tgts[s], peaks, saved[s][3], stats[s], deps
        )
        backs[s] = sum_blocks(gin, s)

    for s in range(slots):
        forward(s, *([mark] if s == 0 else [des[s - 2]] if s > 1 else [stats[0][0]]))
        head(s)
        if s:
            back(s - 1, stats[s][0])
    back(slots - 1, *([des[slots - 2]] if slots > 1 else []))
    dxs, wgs, ggs = [], [], []
    for s in range(slots):
        dx, wg, gg = trunk_bwd(
            me_arr,
            backs[s],
            saved[s],
            bwd_weights,
            gains,
            cosine,
            sine,
            own_rows,
            [part if s == slots - 1 else dxs[-1]] if s else [des[slots - 1]],
        )
        dxs.append(dx)
        wgs.append(wg)
        ggs.append(gg)
        if s == slots - 2:
            part = token_part(tok, [des[t] for t in range(slots)], dxs)
    losses = [losses[s] for s in range(slots)]
    de, wg, gg, both = token_grad(tok, part, dxs[-1:], wgs, ggs, losses)
    both = share(both, "blk", nb)

    tokens_of = count_tok.reshape(1)
    groups = nw if paired else 0
    first, second = embed_first[0].T, embed_second[0].T
    chunks = pl.cdiv(vrows, CH)
    cut = (5 * chunks + 7) // 8
    f0, s0, *pair = adam_table(
        tokens_of, wi_arr, both, de, first, second, groups, (0, cut)
    )
    p, q = pair[0], pair[-1]
    *small, result, p = adam_small(
        tokens_of,
        wi_arr,
        both,
        wg,
        gg,
        (qkv_first[0], out_first[0], mlp_first[0], gain_first[0].T),
        (qkv_second[0], out_second[0], mlp_second[0], gain_second[0].T),
        groups,
        widths,
        p,
    )
    waits, through, extra = [small[8]], (), ()
    if paired:
        begun = reduce_first(p, q, "work", core)
        through, extra = (begun[2], result, small[3], small[7]), small[8:10]
    efirst, esecond, *pair = adam_table(
        tokens_of, wi_arr, both, de, first, second, groups, (cut, chunks), (f0, s0), through, extra, waits
    )
    d1, d2, d3 = 3 * width, 4 * width, 4 * width + ff
    if paired:
        pair, through = pair[:2], pair[2:]
        begun = (*begun[:2], through[0])
        result, small[3], small[7] = through[1:]
        embed_sums = [begun, reduce_first(*pair, "work", core)]
        embed_sums = [reduce_last(*b, "work") for b in embed_sums]
        summed = embed_sums[1][: own_rows // 2, (chunks - cut) * CH :]
        embed_sums = [e[: width // nw] for e in embed_sums]
        embed_sums[1] = embed_sums[1][:, : vrows - cut * CH]
        summed = jnp.concatenate(jnp.split(summed, 2, 1), 0)
        parts = [summed[:, :cq], summed[:, cq : cq + co]]
        parts += [summed[:, c1 + i * cf : c1 + (i + 1) * cf] for i in range(2)]
        gain_sum = summed[:, c3 : c3 + 3].T
    else:
        embed_sums = [
            lax.psum_scatter(r, "work", scatter_dimension=0, tiled=True).astype(F32)
            for r in (p, pair[0])
        ]
        summed = lax.psum(small[8].astype(BF), "work").astype(F32)
        parts = [
            lax.dynamic_slice_in_dim(summed, lo + wi * size, size, 1)
            for lo, size in ((0, cq), (d1, co), (d2, cf), (d3, cf))
        ]
        gain_sum = summed[:, d3 + ff : d3 + ff + 3].T

    embed_sum = jnp.concatenate(embed_sums, 1).T
    sums = (embed_sum, parts[0], parts[1], jnp.stack(parts[2:]), gain_sum)
    masters = (embed_w, qkv_w, out_w, mlp_w, gain_w)
    moms = (embed_mom, qkv_mom, out_mom, mlp_mom, gain_mom)
    rates = (matrix_rate,) * 4 + (gain_rate,)
    decays = (decay_rate,) * 4 + (0.0,)
    updated = [
        outer_update(g, total_tok, w, m, r, d)
        for g, w, m, r, d in zip(sums, masters, moms, rates, decays)
    ]
    firsts = [efirst.T, *small[0:3], small[3].T]
    seconds = [esecond.T, *small[4:7], small[7].T]
    return (
        jnp.stack([result[0, 0], count_tok])[None],
        result[0, 1:2],
        *[u[0] for u in updated],
        *[u[1] for u in updated],
        *[a[None] for a in firsts],
        *[a[None] for a in seconds],
    )


def solution(mesh):
    weights = (
        P("blk", "work"),
        P("blk", "work"),
        P("blk", "work"),
        P(None, "blk", "work"),
        P(None, "blk"),
    )
    states = (
        P("work", "blk", None),
        P("work", "blk", None),
        P("work", "blk", None),
        P("work", None, "blk", None),
        P("work", None, "blk"),
    )
    in_specs = (
        P("work", None, None),
        P("work", None, None),
        P("work"),
        *weights,
        *weights,
        *states,
        *states,
    )
    out_specs = (P("work", None), P("work"), *weights, *weights, *states, *states)
    return jax.shard_map(local, mesh=mesh, in_specs=in_specs, out_specs=out_specs, check_vma=False)
```
